32 devices in a mesh: dp: 8 (over z, x), seq: 4 (over y, core).
Axes of the slice: x: 2, y: 2, z: 4, core: 2. Of those that a mesh axis runs over, the one named last changes fastest.
Arguments:
- inputs: bfloat16 [16, 1024, 768], P('dp', 'seq'), may hold values from -6 to 6
- cotangent: bfloat16 [16, 1024, 768], P('dp', 'seq'), may hold values from -6 to 6
- task_table: int32 [16], P('dp'), may hold values from 0 to 3, as said below
- type_counts: int32 [16, 3], P('dp'), may hold values from 1 to 512, 1024 in all within a row
- gain_one: float32 [2, 768], replicated, may hold values from 0.5 to 1.5
- bias_one: float32 [2, 768], replicated, may hold values from -2 to 2
- proj_qkv: bfloat16 [2, 768, 2304], replicated, may hold values from -0.21875 to 0.21875
- proj_out: bfloat16 [2, 768, 768], replicated, may hold values from -0.875 to 0.875
- gain_two: float32 [2, 768], replicated, may hold values from 0.5 to 1.5
- bias_two: float32 [2, 768], replicated, may hold values from -2 to 2
- proj_up: bfloat16 [2, 768, 3072], replicated, may hold values from -0.21875 to 0.21875
- proj_down: bfloat16 [2, 3072, 768], replicated, may hold values from -0.109375 to 0.109375
Outputs:
- outputs: bfloat16 [16, 1024, 768], P('dp', 'seq')
- back_inputs: float32 [16, 1024, 768], P('dp', 'seq')
- grad_gain_one: float32 [2, 768], P(None, ('dp', 'seq'))
- grad_bias_one: float32 [2, 768], P(None, ('dp', 'seq'))
- grad_qkv: float32 [2, 768, 2304], P(None, ('dp', 'seq'))
- grad_out: float32 [2, 768, 768], P(None, ('dp', 'seq'))
- grad_gain_two: float32 [2, 768], P(None, ('dp', 'seq'))
- grad_bias_two: float32 [2, 768], P(None, ('dp', 'seq'))
- grad_up: float32 [2, 768, 3072], P(None, ('dp', 'seq'))
- grad_down: float32 [2, 3072, 768], P(None, ('dp', 'seq'))
The draws below stay inside these ranges and needn't reach their ends.
Inputs may be any that keep to these rules, and one draw needn't show every extreme that they name: `task_table`: the first slot of each index of dp holds a task below 3; every task holds at least one sequence; 3 marks an empty slot. `type_counts`: Image, action and text tokens follow one another in that order and fill the sequence.
All inputs are finite; a program needn't handle non-finite values.
Results may differ from the reference program's by a relative error of at most 0.013.
Values may be sent and summed in bfloat16 or wider, within the bound.
A program may use at most 320 MiB of HBM per device.

```python
import math
import jax
import jax.numpy as jnp
import numpy as np
from jax import lax

D = 768
HEADS = 12
HEAD_DIM = 64
FF = 3072
LAYERS = 2
TASKS = 3
SLOTS = 2
LEN = 1024
SEQS = 16


def draw_task_table(key, part):
    key = jax.random.fold_in(key, 7)
    first_key, second_key, third_key = jax.random.split(key, 3)
    offset = jax.random.randint(first_key, (), 0, TASKS)
    leading = jax.random.randint(second_key, (SEQS,), 0, TASKS)
    picks = jax.random.randint(third_key, (SEQS,), 0, TASKS + 1)
    order = jnp.arange(SEQS)
    group = order // SLOTS
    leading = jnp.where(group < TASKS, (group + offset) % TASKS, leading)
    return jnp.where(order % SLOTS == 0, leading, picks).astype(jnp.int32)


def level_of(own_key, dims, shards, smallest, top_value):
    def one(dim, shards_of):
        draws = jax.random.uniform(jax.random.fold_in(jax.random.fold_in(own_key, 6), dim), (shards_of,), jnp.float32, smallest / len(shards), top_value / len(shards))
        return jnp.repeat(jnp.exp(draws), dims[dim] // shards_of).reshape((-1,) + (1,) * (len(dims) - dim - 1))

    factor_of = one(*shards[0])
    for cut in shards[1:]:
        factor_of = factor_of * one(*cut)
    return factor_of


def split_up(count, total, limit, skew):
    weights = [(1 << 20) // math.isqrt(grade ** skew) + 1 for grade in range(2, count + 1)]
    spare, given = total - limit - (count - 1), [1] * (count - 1)
    while spare > 0:
        candidates = [i for i in range(count - 1) if given[i] < limit]
        mass, budget = sum([weights[i] for i in candidates]), spare
        for i in candidates:
            extra = min(limit - given[i], max(1, budget * weights[i] // mass), spare)
            given[i] = given[i] + extra
            spare = spare - extra
    return np.array([limit] + given)


def uneven_parts(stream_key, number_of, total, bound, lean):
    if number_of == 2:
        one = jax.random.randint(stream_key, (), max(1, total - bound), min(bound, total - 1) + 1)
        return jnp.stack([one, total - one])
    lengths = jnp.asarray(split_up(number_of, total, bound, lean), jnp.int32)
    pairs = (number_of - 1) // 2
    donor, taker = lengths[1:1 + 2 * pairs:2], lengths[2:2 + 2 * pairs:2]
    room = jnp.minimum(donor - 1, bound - taker)
    shifted = jax.random.randint(jax.random.fold_in(stream_key, 1), (pairs,), 0, 1 << 20) % (room + 1)
    lengths = lengths.at[1:1 + 2 * pairs:2].set(donor - shifted).at[2:2 + 2 * pairs:2].set(taker + shifted)
    return lengths[jax.random.permutation(jax.random.fold_in(stream_key, 2), number_of)]


def normal_values(key, dims, scale, most, shards=(), kind=jnp.bfloat16):
    result = jax.random.normal(key, dims, jnp.float32) * scale
    if len(shards) > 0:
        result = level_of(key, dims, shards, -0.22, 0.18) * result
    return jnp.clip(result, min=-most, max=most).astype(kind)


def setup_inputs(seed: int = 0) -> dict:
    key_of = jax.random.split(jax.random.key(seed), 13)
    inputs = normal_values(key_of[0], (SEQS, LEN, D), 1.0, 6.0, ((0, 8), (1, 4)))
    cotangent = normal_values(key_of[1], (SEQS, LEN, D), 1.0, 6.0, ((0, 8), (1, 4)))
    task_table = draw_task_table(jax.random.fold_in(key_of[12], 71), 0)
    type_counts = jax.vmap(lambda own: uneven_parts(own, 3, LEN, LEN // 2, 2))(jax.random.split(key_of[3], SEQS)).reshape((SEQS, 3)).astype(jnp.int32)
    gain_one = jnp.clip(1.0 + 0.1 * jax.random.normal(key_of[4], (LAYERS, D), jnp.float32), 0.5, 1.5)
    bias_one = normal_values(key_of[5], (LAYERS, D), 0.3, 2.0, (), jnp.float32)
    proj_qkv = normal_values(key_of[6], (LAYERS, D, 3 * D), D ** -0.5, 0.21875)
    proj_out = normal_values(key_of[7], (LAYERS, D, D), (D // 16) ** -0.5, 0.875)
    gain_two = jnp.clip(1.0 + 0.1 * jax.random.normal(key_of[8], (LAYERS, D), jnp.float32), 0.5, 1.5)
    bias_two = normal_values(key_of[9], (LAYERS, D), 0.3, 2.0, (), jnp.float32)
    proj_up = normal_values(key_of[10], (LAYERS, D, FF), D ** -0.5, 0.21875)
    proj_down = normal_values(key_of[11], (LAYERS, FF, D), FF ** -0.5, 0.109375)
    return dict(inputs=inputs, cotangent=cotangent, task_table=task_table, type_counts=type_counts, gain_one=gain_one, bias_one=bias_one, proj_qkv=proj_qkv, proj_out=proj_out, gain_two=gain_two, bias_two=bias_two, proj_up=proj_up, proj_down=proj_down)


epsilon = 1e-05
precise = lax.Precision.HIGHEST

@jax.custom_vjp
def low(v):
    return lax.optimization_barrier(v.astype(jnp.bfloat16)).astype(jnp.float32)

@jax.custom_vjp
def low_back(v):
    return v

def low_keep(v):
    return (low(v), None)

def low_pass(kept, grad):
    return (grad,)

def back_keep(v):
    return (v, None)

def back_low(kept, grad):
    return (low(grad),)
low.defvjp(low_keep, low_pass)
low_back.defvjp(back_keep, back_low)

def norm_rows(rows_in, gain_row, shift_row):
    average = lax.optimization_barrier(jnp.mean(rows_in, -1, keepdims=True))
    centred = rows_in - average
    spread = lax.optimization_barrier(jnp.mean(centred * centred, -1, keepdims=True))
    return centred * lax.rsqrt(spread + epsilon) * gain_row + shift_row

def block_forward(stream, weights):
    gain_a, shift_a, matrix_qkv, matrix_out, gain_b, shift_b, matrix_up, matrix_down = weights
    length = stream.shape[0]
    score_scale = 1.0 / math.sqrt(HEAD_DIM)
    hidden = low(norm_rows(stream, gain_a, shift_a))
    projected = low(low_back(jnp.dot(hidden, matrix_qkv, precision=precise)))
    queries = projected[:, :D].reshape(length, HEADS, HEAD_DIM)
    key_rows = projected[:, D:2 * D].reshape(length, HEADS, HEAD_DIM)
    value_rows = projected[:, 2 * D:].reshape(length, HEADS, HEAD_DIM)
    scores = low_back(jnp.einsum('chd,thd->hct', queries, key_rows, precision=precise) * score_scale)
    positions = jnp.arange(length)
    allowed = positions[None, :] <= positions[:, None]
    masked = jnp.where(allowed[None], scores, -1e+30)
    row_peak = lax.optimization_barrier(jnp.max(masked, -1, keepdims=True))
    raised = jnp.exp(masked - row_peak)
    attention = low(raised / lax.optimization_barrier(jnp.sum(raised, -1, keepdims=True)))
    attended = jnp.einsum('hct,thd->chd', attention, value_rows, precision=precise).reshape(length, D)
    attended = low(low_back(attended))
    middle = stream + low_back(jnp.dot(attended, matrix_out, precision=precise))
    normed = low(norm_rows(middle, gain_b, shift_b))
    hidden_up = low_back(jnp.dot(normed, matrix_up, precision=precise))
    active = low(jax.nn.gelu(hidden_up, approximate=False))
    return middle + low_back(jnp.dot(active, matrix_down, precision=precise))

def reference(inputs, cotangent, task_table, type_counts, gain_one, bias_one, proj_qkv, proj_out, gain_two, bias_two, proj_up, proj_down):
    params = (gain_one.astype(jnp.float32), bias_one.astype(jnp.float32), proj_qkv.astype(jnp.float32), proj_out.astype(jnp.float32), gain_two.astype(jnp.float32), bias_two.astype(jnp.float32), proj_up.astype(jnp.float32), proj_down.astype(jnp.float32))
    length = inputs.shape[1]
    choose = (task_table[:, None] == jnp.arange(TASKS, dtype=jnp.int32)[None, :]).astype(jnp.float32)
    targets = (length - type_counts[:, 0]).astype(jnp.float32)
    totals = lax.optimization_barrier(jnp.sum(choose * targets[:, None], 0))
    factor = jnp.sum(totals) / TASKS / totals
    seq_weight = lax.optimization_barrier(jnp.sum(choose * factor[None, :], 1))
    positions = jnp.arange(length, dtype=jnp.int32)
    target_mask = (positions[None, :] >= type_counts[:, 0:1]).astype(jnp.float32)
    scaled = cotangent.astype(jnp.float32) * (seq_weight[:, None] * target_mask)[:, :, None]

    def forward(stream, weights):
        for section_index in range(LAYERS):
            stream = block_forward(stream, tuple((weight[section_index] for weight in weights)))
        return stream

    def one_sequence(running, sequence_pair):
        sequence, upstream = sequence_pair
        output, pullback = jax.vjp(forward, sequence.astype(jnp.float32), params)
        back_input, back_params = pullback(upstream)
        running = jax.tree.map(jnp.add, running, back_params)
        return (running, (output.astype(jnp.bfloat16), back_input))
    empty_grads = jax.tree.map(jnp.zeros_like, params)
    weight_grads, results = lax.scan(one_sequence, empty_grads, (inputs, scaled))
    return (results[0], results[1], weight_grads[0], weight_grads[1], weight_grads[2], weight_grads[3], weight_grads[4], weight_grads[5], weight_grads[6], weight_grads[7])
```

```python
import functools
import math

import jax
import jax.numpy as jnp
import numpy as np
from jax import lax
from jax.experimental import pallas as pl
from jax.experimental.pallas import tpu as pltpu
from jax.sharding import PartitionSpec as P

HEADS = 12
HEAD_DIM = 64
LAYERS = 2
TASKS = 3
AXES = ("dp", "seq")
F32 = jnp.float32
BF16 = jnp.bfloat16
epsilon = 1e-05
VMEM_BYTES = 56 * 1024 * 1024


def dot_nn(a, b):
    return lax.dot_general(a, b, (((1,), (0,)), ((), ())), preferred_element_type=F32)


def dot_nt(a, b):
    return lax.dot_general(a, b, (((1,), (1,)), ((), ())), preferred_element_type=F32)


def dot_tn(a, b):
    return lax.dot_general(a, b, (((0,), (0,)), ((), ())), preferred_element_type=F32)


def norm_rows(rows_in, gain_row, shift_row):
    average = jnp.mean(rows_in, -1, keepdims=True)
    centred = rows_in - average
    spread = jnp.mean(centred * centred, -1, keepdims=True)
    return centred * lax.rsqrt(spread + epsilon) * gain_row + shift_row


def gelu_and_slope(x):
    z = jnp.abs(x) * 0.7071067811865476
    d = 1.0 + 0.3275911 * z
    t = pl.reciprocal(d, approx=True)
    t = t * (2.0 - d * t)
    poly = t * (
        0.254829592
        + t * (-0.284496736 + t * (1.421413741 + t * (-1.453152027 + t * 1.061405429)))
    )
    bell = jnp.exp(-0.5 * x * x)
    tail = 0.5 * poly * bell
    below = jnp.where(x >= 0.0, 1.0 - tail, tail)
    return x * below, below + x * bell * 0.3989422804014327


def pair_lists(variant):
    if variant == 0:
        return [[(0, 0, True)], [(0, 0, False), (1, 0, False), (1, 1, False), (0, 1, True)]]
    return [[(1, 0, False), (0, 0, True)], [(0, 0, False), (1, 0, False), (0, 1, True)]]


def head_masks(scale):
    lane = lax.broadcasted_iota(jnp.int32, (1, 2 * HEAD_DIM), 1)
    first = jnp.where(lane < HEAD_DIM, scale, 0.0)
    return first.astype(BF16), (scale - first).astype(BF16)


def attention_forward_kernel(meta, q_ref, ko_ref, vo_ref, kx_ref, vx_ref, out_ref, lse_ref):
    rows = q_ref.shape[0] // 2
    masks = head_masks(1.0 / math.sqrt(HEAD_DIM))
    keys = (ko_ref, kx_ref)
    values = (vo_ref, vx_ref)

    def run(variant):
        below = lax.broadcasted_iota(jnp.int32, (rows, rows), 1) <= lax.broadcasted_iota(
            jnp.int32, (rows, rows), 0
        )
        lane = lax.broadcasted_iota(jnp.int32, (rows, 2 * HEAD_DIM), 1)
        for block, pairs in enumerate(pair_lists(variant)):
            span = pl.ds(block * rows, rows)
            q = q_ref[span, :]
            results, logs = [], []
            for head in range(2):
                qm = q * masks[head]
                scores = []
                for source, kblock, diagonal in pairs:
                    part = dot_nt(qm, keys[source][pl.ds(kblock * rows, rows), :])
                    scores.append(jnp.where(below, part, -1e30) if diagonal else part)
                peak = functools.reduce(jnp.maximum, scores)
                peak = jnp.max(peak, -1, keepdims=True)
                total, acc = None, None
                for part, (source, kblock, diagonal) in zip(scores, pairs):
                    raised = jnp.exp(part - peak)
                    total = raised if total is None else total + raised
                    term = dot_nn(raised.astype(BF16), values[source][pl.ds(kblock * rows, rows), :])
                    acc = term if acc is None else acc + term
                total = jnp.sum(total, -1, keepdims=True)
                results.append(acc / total)
                logs.append(peak + jnp.log(total))
            out_ref[span, :] = jnp.where(lane < HEAD_DIM, results[0], results[1]).astype(BF16)
            packed = jnp.where(lane == 0, logs[0], logs[1])
            lse_ref[0, :, span] = packed.T[:8, :]

    @pl.when(meta[0] == 0)
    def _():
        run(0)

    @pl.when(meta[0] == 1)
    def _():
        run(1)


def attention_forward(meta, projected, other):
    tokens = projected.shape[0]
    pairs = HEADS // 2
    wide = 2 * HEAD_DIM

    def at(offset):
        return pl.BlockSpec((tokens, wide), lambda g, m: (0, offset + g))

    return pl.pallas_call(
        attention_forward_kernel,
        grid_spec=pltpu.PrefetchScalarGridSpec(
            num_scalar_prefetch=1,
            grid=(pairs,),
            in_specs=[at(0), at(pairs), at(2 * pairs), at(0), at(pairs)],
            out_specs=[at(0), pl.BlockSpec((1, 8, tokens), lambda g, m: (g, 0, 0))],
        ),
        out_shape=[
            jax.ShapeDtypeStruct((tokens, HEADS * HEAD_DIM), BF16),
            jax.ShapeDtypeStruct((pairs, 8, tokens), F32),
        ],
        compiler_params=pltpu.CompilerParams(vmem_limit_bytes=VMEM_BYTES),
        cost_estimate=pl.CostEstimate(flops=8_000_000_000, bytes_accessed=4_000_000, transcendentals=4_000_000),
        name="attention_forward",
    )(meta, projected, projected, projected, other, other)


def attention_backward_kernel(
    meta, q_ref, ko_ref, vo_ref, kx_ref, vx_ref, do_ref, o_ref, lse_ref,
    dq_ref, dko_ref, dvo_ref, dkx_ref, dvx_ref,
):
    rows = q_ref.shape[0] // 2
    scale = 1.0 / math.sqrt(HEAD_DIM)
    scaled = head_masks(scale)
    plain = head_masks(1.0)
    keys = (ko_ref, kx_ref)
    values = (vo_ref, vx_ref)
    dkeys = (dko_ref, dkx_ref)
    dvalues = (dvo_ref, dvx_ref)
    product = (do_ref[...].astype(F32) * o_ref[...].astype(F32)).T
    dots = (
        jnp.sum(product[:HEAD_DIM], 0, keepdims=True),
        jnp.sum(product[HEAD_DIM:], 0, keepdims=True),
    )
    logs = lse_ref[0]

    def run(variant):
        below = lax.broadcasted_iota(jnp.int32, (rows, rows), 0) <= lax.broadcasted_iota(
            jnp.int32, (rows, rows), 1
        )
        dk_acc, dv_acc = {}, {}
        for block, pairs in enumerate(pair_lists(variant)):
            span = slice(block * rows, (block + 1) * rows)
            q, do = q_ref[span, :], do_ref[span, :]
            dq = None
            for head in range(2):
                qm, dom = q * scaled[head], do * plain[head]
                log_row = logs[head : head + 1, span]
                dot_row = dots[head][:, span]
                for source, kblock, diagonal in pairs:
                    where = pl.ds(kblock * rows, rows)
                    k, v = keys[source][where, :], values[source][where, :]
                    raised = jnp.exp(dot_nt(k, qm) - log_row)
                    if diagonal:
                        raised = jnp.where(below, raised, 0.0)
                    slope = (raised * (dot_nt(v, dom) - dot_row)).astype(BF16)
                    term_v = dot_nn(raised.astype(BF16), dom)
                    term_k = dot_nn(slope, qm)
                    term_q = dot_tn(slope, k * scaled[head])
                    slot = (source, kblock)
                    dv_acc[slot] = dv_acc[slot] + term_v if slot in dv_acc else term_v
                    dk_acc[slot] = dk_acc[slot] + term_k if slot in dk_acc else term_k
                    dq = term_q if dq is None else dq + term_q
            dq_ref[span, :] = dq.astype(BF16)
        for source in range(2):
            for kblock in range(2):
                span = slice(kblock * rows, (kblock + 1) * rows)
                slot = (source, kblock)
                if slot in dk_acc:
                    dkeys[source][span, :] = dk_acc[slot].astype(dkeys[source].dtype)
                    dvalues[source][span, :] = dv_acc[slot].astype(dvalues[source].dtype)
                else:
                    dkeys[source][span, :] = jnp.zeros((rows, 2 * HEAD_DIM), dkeys[source].dtype)
                    dvalues[source][span, :] = jnp.zeros((rows, 2 * HEAD_DIM), dvalues[source].dtype)

    @pl.when(meta[0] == 0)
    def _():
        run(0)

    @pl.when(meta[0] == 1)
    def _():
        run(1)


def attention_backward(meta, projected, other, back_attended, attended, logs):
    tokens = projected.shape[0]
    pairs = HEADS // 2
    wide = 2 * HEAD_DIM
    width = HEADS * HEAD_DIM

    def at(offset):
        return pl.BlockSpec((tokens, wide), lambda g, m: (0, offset + g))

    return pl.pallas_call(
        attention_backward_kernel,
        grid_spec=pltpu.PrefetchScalarGridSpec(
            num_scalar_prefetch=1,
            grid=(pairs,),
            in_specs=[at(0), at(pairs), at(2 * pairs), at(0), at(pairs), at(0), at(0),
                      pl.BlockSpec((1, 8, tokens), lambda g, m: (g, 0, 0))],
            out_specs=[at(0)] * 5,
        ),
        out_shape=[
            jax.ShapeDtypeStruct((tokens, width), BF16),
            jax.ShapeDtypeStruct((tokens, width), F32),
            jax.ShapeDtypeStruct((tokens, width), F32),
            jax.ShapeDtypeStruct((tokens, width), BF16),
            jax.ShapeDtypeStruct((tokens, width), BF16),
        ],
        compiler_params=pltpu.CompilerParams(vmem_limit_bytes=VMEM_BYTES),
        cost_estimate=pl.CostEstimate(flops=16_000_000_000, bytes_accessed=9_000_000, transcendentals=4_000_000),
        name="attention_backward",
    )(meta, projected, projected, projected, other, other, back_attended, attended, logs)


def feed_forward_kernel(normed_ref, middle_ref, up_ref, down_ref, active_ref, slope_ref, out_ref):
    @pl.when(pl.program_id(0) == 0)
    def _():
        out_ref[...] = middle_ref[...]

    active, slope = gelu_and_slope(dot_nn(normed_ref[...], up_ref[...]))
    active = active.astype(BF16)
    active_ref[...] = active
    slope_ref[...] = slope.astype(BF16)
    out_ref[...] += dot_nn(active, down_ref[...])


def feed_forward(normed, middle, matrix_up, matrix_down):
    tokens, width = normed.shape
    hidden = matrix_up.shape[1]
    tile = 512
    whole = pl.BlockSpec((tokens, width), lambda j: (0, 0))
    part = pl.BlockSpec((tokens, tile), lambda j: (0, j))
    return pl.pallas_call(
        feed_forward_kernel,
        grid=(hidden // tile,),
        in_specs=[whole, whole, pl.BlockSpec((width, tile), lambda j: (0, j)),
                  pl.BlockSpec((tile, width), lambda j: (j, 0))],
        out_specs=[part, part, whole],
        out_shape=[
            jax.ShapeDtypeStruct((tokens, hidden), BF16),
            jax.ShapeDtypeStruct((tokens, hidden), BF16),
            jax.ShapeDtypeStruct((tokens, width), F32),
        ],
        compiler_params=pltpu.CompilerParams(vmem_limit_bytes=VMEM_BYTES),
        cost_estimate=pl.CostEstimate(flops=9_600_000_000, bytes_accessed=20_000_000, transcendentals=3_000_000),
        name="feed_forward",
    )(normed, middle, matrix_up, matrix_down)


def feed_back_kernel(back_ref, slope_ref, up_ref, down_ref, back_up_ref, back_normed_ref):
    back_up = (dot_nt(back_ref[...], down_ref[...]) * slope_ref[...].astype(F32)).astype(BF16)
    back_up_ref[0] = back_up

    @pl.when(pl.program_id(0) == 0)
    def _():
        back_normed_ref[...] = jnp.zeros_like(back_normed_ref)

    back_normed_ref[...] += dot_nt(back_up, up_ref[...])


def feed_back(back_out, slope, matrix_up, matrix_down):
    tokens, width = back_out.shape
    hidden = matrix_up.shape[1]
    tile = 512
    half = hidden // tile // 2
    whole = pl.BlockSpec((tokens, width), lambda j: (0, 0))
    return pl.pallas_call(
        feed_back_kernel,
        grid=(hidden // tile,),
        in_specs=[whole, pl.BlockSpec((tokens, tile), lambda j: (0, j)),
                  pl.BlockSpec((width, tile), lambda j: (0, j)),
                  pl.BlockSpec((tile, width), lambda j: (j, 0))],
        out_specs=[pl.BlockSpec((1, tokens, tile), lambda j: (j // half, 0, j % half)), whole],
        out_shape=[
            jax.ShapeDtypeStruct((2, tokens, hidden // 2), BF16),
            jax.ShapeDtypeStruct((tokens, width), F32),
        ],
        compiler_params=pltpu.CompilerParams(vmem_limit_bytes=VMEM_BYTES),
        cost_estimate=pl.CostEstimate(flops=9_600_000_000, bytes_accessed=20_000_000, transcendentals=0),
        name="feed_back",
    )(back_out, slope, matrix_up, matrix_down)


def grad_up_kernel(chips, meta, ao, ax, bo, bx, keep, send, acc):
    rows = keep.shape[1]
    acc[...] = (dot_tn(ao[...], bo[0]) + dot_tn(ax[...], bx[...])).astype(BF16)
    for position in range(chips):
        chunk = acc[pl.ds(pl.multiple_of(meta[2 + position] * rows, 16), rows), :]
        if position < chips // 2:
            keep[position] = chunk
        else:
            send[position - chips // 2] = chunk


def grad_down_kernel(chips, meta, ao, ax, bo, bx, keep_in, send_in, keep, send):
    rows = keep.shape[1]
    each = ao.shape[1] // rows
    total = (dot_tn(ao[...], bo[...]) + dot_tn(ax[...], bx[...])).astype(BF16)
    for local in range(each):
        position = meta[2 + chips + pl.program_id(0) * each + local]
        chunk = total[local * rows : (local + 1) * rows]

        @pl.when(position < chips // 2)
        def _():
            keep[position] = chunk

        @pl.when(position >= chips // 2)
        def _():
            send[position - chips // 2] = chunk


def grad_branch_kernel(chips, meta, ho, hx, po, px, ao, ax, bo, bx, keep, send, acc):
    rows = keep.shape[1]
    step = pl.program_id(0)

    @pl.when(step < 3)
    def _():
        acc[...] = (dot_tn(ho[...], po[...]) + dot_tn(hx[...], px[...])).astype(BF16)

    @pl.when(step == 3)
    def _():
        acc[...] = (dot_tn(ao[...], bo[...]) + dot_tn(ax[...], bx[...])).astype(BF16)

    for position in range(chips):
        chunk = acc[pl.ds(pl.multiple_of(meta[2 + position] * rows, 16), rows), :]
        if position < chips // 2:
            keep[position] = chunk
        else:
            send[position - chips // 2] = chunk


def ordered(total, ids, chips):
    split = total.astype(BF16).reshape(chips, total.shape[0] // chips, total.shape[1])
    return jnp.take(split, ids, axis=0)


def mlp_gradients(meta, chips, core, normed, normed_x, back_up, back_up_x, active, active_x, back_out, back_out_x):
    tokens, width = normed.shape
    hidden = active.shape[1]
    half = width // 2
    rows = width // chips
    params = pltpu.CompilerParams(vmem_limit_bytes=VMEM_BYTES)
    if rows % 16 != 0:
        ids = meta[2 : 2 + chips]
        up = dot_tn(normed, lax.dynamic_index_in_dim(back_up, core, 0, False)) + dot_tn(normed_x, back_up_x)
        down = dot_tn(active, lax.dynamic_slice_in_dim(back_out, core * half, half, 1)) + dot_tn(active_x, back_out_x)
        up = ordered(up, ids, chips).reshape(chips, rows, 4, half)
        up = up.transpose(0, 2, 1, 3).reshape(chips, 4 * rows, half)
        both = jnp.concatenate([up, ordered(down, ids, chips)], -1)
        return both[: chips // 2], both[chips // 2 :]
    shape = jax.ShapeDtypeStruct((chips // 2, 4 * rows, 2 * half), BF16)
    whole = pl.BlockSpec((tokens, width), lambda j, m: (0, 0))
    keep, send = pl.pallas_call(
        functools.partial(grad_up_kernel, chips),
        grid_spec=pltpu.PrefetchScalarGridSpec(
            num_scalar_prefetch=1,
            grid=(4,),
            in_specs=[whole, whole, pl.BlockSpec((1, tokens, half), lambda j, m: (m[1], 0, j)),
                      pl.BlockSpec((tokens, half), lambda j, m: (0, j))],
            out_specs=[pl.BlockSpec((chips // 2, rows, half), lambda j, m: (0, j, 0))] * 2,
            scratch_shapes=[pltpu.VMEM((width, half), BF16)],
        ),
        out_shape=[shape, shape],
        compiler_params=params,
        cost_estimate=pl.CostEstimate(flops=4_800_000_000, bytes_accessed=7_000_000, transcendentals=0),
        name="gradient_up",
    )(meta, normed, normed_x, back_up, back_up_x)
    steps = hidden // width
    tile = pl.BlockSpec((tokens, width), lambda j, m: (0, j))
    out = pl.BlockSpec((chips // 2, 4 * rows, half), lambda j, m: (0, 0, 1))
    return pl.pallas_call(
        functools.partial(grad_down_kernel, chips),
        grid_spec=pltpu.PrefetchScalarGridSpec(
            num_scalar_prefetch=1,
            grid=(steps,),
            in_specs=[tile, tile, pl.BlockSpec((tokens, half), lambda j, m: (0, m[1])),
                      pl.BlockSpec((tokens, half), lambda j, m: (0, 0)),
                      pl.BlockSpec(memory_space=pl.ANY), pl.BlockSpec(memory_space=pl.ANY)],
            out_specs=[out, out],
        ),
        out_shape=[shape, shape],
        input_output_aliases={5: 0, 6: 1},
        compiler_params=params,
        cost_estimate=pl.CostEstimate(flops=4_800_000_000, bytes_accessed=10_000_000, transcendentals=0),
        name="gradient_down",
    )(meta, active, active_x, back_out, back_out_x, keep, send)


def branch_gradients(meta, chips, core, hidden, hidden_x, back_projected, back_projected_x, attended, attended_x, back_branch, back_branch_x):
    tokens, width = hidden.shape
    half = width // 2
    rows = width // chips
    if rows % 16 != 0:
        ids = meta[2 : 2 + chips]
        own = lax.dynamic_slice_in_dim(back_projected, core * 3 * half, 3 * half, 1)
        qkv = dot_tn(hidden, own) + dot_tn(hidden_x, back_projected_x)
        own = lax.dynamic_slice_in_dim(back_branch, core * half, half, 1)
        out = dot_tn(attended, own) + dot_tn(attended_x, back_branch_x)
        both = ordered(jnp.concatenate([qkv, out], -1), ids, chips)
        return both[: chips // 2], both[chips // 2 :]
    shape = jax.ShapeDtypeStruct((chips // 2, rows, 4 * half), BF16)
    whole = pl.BlockSpec((tokens, width), lambda j, m: (0, 0))
    return pl.pallas_call(
        functools.partial(grad_branch_kernel, chips),
        grid_spec=pltpu.PrefetchScalarGridSpec(
            num_scalar_prefetch=1,
            grid=(4,),
            in_specs=[
                whole, whole,
                pl.BlockSpec((tokens, half), lambda j, m: (0, 3 * m[1] + jnp.minimum(j, 2))),
                pl.BlockSpec((tokens, half), lambda j, m: (0, jnp.minimum(j, 2))),
                whole, whole,
                pl.BlockSpec((tokens, half), lambda j, m: (0, m[1])),
                pl.BlockSpec((tokens, half), lambda j, m: (0, 0)),
            ],
            out_specs=[pl.BlockSpec((chips // 2, rows, half), lambda j, m: (0, 0, j))] * 2,
            scratch_shapes=[pltpu.VMEM((width, half), BF16)],
        ),
        out_shape=[shape, shape],
        compiler_params=pltpu.CompilerParams(vmem_limit_bytes=VMEM_BYTES),
        cost_estimate=pl.CostEstimate(flops=4_800_000_000, bytes_accessed=8_000_000, transcendentals=0),
        name="gradient_branch",
    )(meta, hidden, hidden_x, back_projected, back_projected_x, attended, attended_x, back_branch, back_branch_x)


class Exchange:
    def __init__(self, dp):
        self.dp = dp
        self.chips = 2 * dp
        self.bits = int(math.log2(self.chips))
        self.core_pairs = [(s, s ^ 1) for s in range(4)]
        self.mirror_pairs = [(s, 3 - s) for s in range(4)]
        rest = list(range(2, self.bits))
        self.orders = ([1, 0] + rest, [0, 1] + rest)

    def swap_core(self, value):
        return lax.ppermute(value, "seq", self.core_pairs)

    def mirror(self, value):
        return lax.ppermute(value, "seq", self.mirror_pairs)

    def pairs(self, phase):
        result = []
        for device in range(2 * self.chips):
            chip = (device // 4) * 2 + (device % 4) // 2
            core = device % 2
            other = chip ^ (1 << self.orders[core][phase])
            result.append((device, (other // 2) * 4 + (other % 2) * 2 + core))
        return result

    def tables(self, chip, core):
        index = np.arange(self.chips)
        maps, inverses = [], []
        for order in self.orders:
            value = np.zeros_like(index)
            for phase, bit in enumerate(order):
                value |= ((index >> (self.bits - 1 - phase)) & 1) << bit
            inverse = np.zeros_like(index)
            inverse[value] = index
            maps.append(value.astype(np.int32))
            inverses.append(order)
        ids = chip ^ jnp.where(core == 0, jnp.asarray(maps[0]), jnp.asarray(maps[1]))
        relative = jnp.asarray(index.astype(np.int32)) ^ chip
        places = []
        for order in self.orders:
            place = jnp.zeros_like(relative)
            for phase, bit in enumerate(order):
                place = place | (((relative >> bit) & 1) << (self.bits - 1 - phase))
            places.append(place)
        return ids.astype(jnp.int32), jnp.where(core == 0, places[0], places[1]).astype(jnp.int32)

    def reduce_scatter(self, keep, send, kind):
        parts = [keep]
        for phase in range(self.bits):
            parts.append(lax.ppermute(send, AXES, self.pairs(phase)))
            size = parts[-1].shape[0]
            if phase < self.bits - 1:
                send = sum(part[size // 2 : size].astype(F32) for part in parts).astype(kind)
        return sum(part[0].astype(F32) for part in parts)


def halves(value, core, half):
    return lax.dynamic_slice_in_dim(value, (1 - core) * half, half, 1)


def by_core(core, mine, theirs, axis):
    return jnp.where(
        core == 0,
        jnp.concatenate([mine, theirs], axis),
        jnp.concatenate([theirs, mine], axis),
    )


def layer_forward(stream, weights, flag, exchange):
    gain_a, shift_a, matrix_qkv, matrix_out, gain_b, shift_b, matrix_up, matrix_down = weights
    width = stream.shape[-1]
    hidden = norm_rows(stream, gain_a, shift_a).astype(BF16)
    projected = dot_nn(hidden, matrix_qkv).astype(BF16)
    other = exchange.swap_core(projected[:, width:])
    attended, logs = attention_forward(flag, projected, other)
    middle = stream + dot_nn(attended, matrix_out)
    normed = norm_rows(middle, gain_b, shift_b).astype(BF16)
    active, slope, output = feed_forward(normed, middle, matrix_up, matrix_down)
    remote = tuple(exchange.swap_core(v) for v in (hidden, attended, normed, active))
    kept = (stream, hidden, projected, other, logs, attended, middle, normed, active, slope, remote)
    return output, kept


def layer_backward(upstream, weights, kept, flag, meta, core, exchange):
    gain_a, shift_a, matrix_qkv, matrix_out, gain_b, shift_b, matrix_up, matrix_down = weights
    stream, hidden, projected, other, logs, attended, middle, normed, active, slope, remote = kept
    hidden_x, attended_x, normed_x, active_x = remote
    width = stream.shape[-1]
    chips = exchange.chips
    half = width // 2
    back_out = upstream.astype(BF16)
    back_up, back_normed = feed_back(back_out, slope, matrix_up, matrix_down)
    back_out_x = exchange.swap_core(halves(back_out, core, half))
    back_up_x = exchange.swap_core(lax.dynamic_index_in_dim(back_up, 1 - core, 0, False))
    keep, send = mlp_gradients(
        meta, chips, core, normed, normed_x, back_up, back_up_x, active, active_x, back_out, back_out_x
    )
    mlp_share = exchange.reduce_scatter(keep, send, BF16)
    unused, norm_pull_two = jax.vjp(norm_rows, middle, gain_b, shift_b)
    back_middle, grad_gain_b, grad_shift_b = norm_pull_two(back_normed)
    back_middle = back_middle + upstream
    back_branch = back_middle.astype(BF16)
    back_branch_x = exchange.swap_core(halves(back_branch, core, half))
    back_attended = dot_nt(back_branch, matrix_out).astype(BF16)
    back_q, back_k, back_v, back_kx, back_vx = attention_backward(
        flag, projected, other, back_attended, attended, logs
    )
    back_k = back_k + exchange.swap_core(back_kx).astype(F32)
    back_v = back_v + exchange.swap_core(back_vx).astype(F32)
    back_projected = jnp.concatenate([back_q, back_k.astype(BF16), back_v.astype(BF16)], -1)
    back_projected_x = exchange.swap_core(halves(back_projected, core, 3 * half))
    keep, send = branch_gradients(
        meta, chips, core, hidden, hidden_x, back_projected, back_projected_x,
        attended, attended_x, back_branch, back_branch_x,
    )
    branch_share = exchange.reduce_scatter(keep, send, BF16)
    back_hidden = dot_nt(back_projected, matrix_qkv)
    unused, norm_pull_one = jax.vjp(norm_rows, stream, gain_a, shift_a)
    back_stream, grad_gain_a, grad_shift_a = norm_pull_one(back_hidden)
    rows = jnp.stack([grad_gain_a, grad_shift_a, grad_gain_b, grad_shift_b])
    return back_stream + back_middle, rows, mlp_share, branch_share


def unpack_mlp(share, core, exchange):
    long, wide = share.shape
    rows, half, each = long // 4, wide // 2, long // 8
    up = share[:, :half].reshape(4, 2, each, half)
    down = share[:, half:].reshape(2, 4 * each, half)

    def pick(which):
        return jnp.concatenate(
            [lax.dynamic_index_in_dim(up, which, 1, False).reshape(4 * each, half),
             lax.dynamic_index_in_dim(down, which, 0, False)], -1)

    mine, theirs = pick(core), exchange.swap_core(pick(1 - core))

    def widen(value):
        return value[:, :half].reshape(4, each, half).transpose(1, 0, 2).reshape(each, 4 * half)

    grad_up = by_core(core, widen(mine), widen(theirs), 1)
    grad_down = by_core(core, mine[:, half:], theirs[:, half:], 1)
    return grad_up, grad_down


def unpack_branch(share, core, exchange):
    rows, wide = share.shape
    each, half = rows // 2, wide // 4
    split = share.reshape(2, each, wide)
    mine = lax.dynamic_index_in_dim(split, core, 0, False)
    theirs = exchange.swap_core(lax.dynamic_index_in_dim(split, 1 - core, 0, False))
    grad_qkv = by_core(core, mine[:, : 3 * half], theirs[:, : 3 * half], 1)
    grad_out = by_core(core, mine[:, 3 * half :], theirs[:, 3 * half :], 1)
    return grad_qkv, grad_out


def per_device(
    inputs, cotangent, task_table, type_counts,
    gain_one, bias_one, proj_qkv, proj_out, gain_two, bias_two, proj_up, proj_down,
):
    slots, rows, width = inputs.shape
    length = rows * lax.axis_size("seq")
    exchange = Exchange(lax.axis_size("dp"))
    place = lax.axis_index("seq")
    side, core = place // 2, place % 2
    chip = lax.axis_index("dp") * 2 + side
    low = jnp.minimum(place, 3 - place)
    own_first = place < 2
    ids, places = exchange.tables(chip, core)
    flag = low.astype(jnp.int32).reshape(1)
    meta = jnp.concatenate([flag, core.astype(jnp.int32).reshape(1), ids, places])

    def gather_slot(value):
        own = lax.dynamic_index_in_dim(value, side, 0, False)
        got = exchange.mirror(lax.dynamic_index_in_dim(value, 1 - side, 0, False))
        return jnp.where(own_first, jnp.concatenate([own, got]), jnp.concatenate([got, own]))

    def return_slot(value):
        first, second = value[:rows], value[rows:]
        own = jnp.where(own_first, first, second)
        got = exchange.mirror(jnp.where(own_first, second, first))
        return jnp.where(side == 0, jnp.stack([own, got]), jnp.stack([got, own]))

    stream = gather_slot(inputs).astype(F32)
    cotangent = gather_slot(cotangent)
    choose = (task_table[:, None] == jnp.arange(TASKS, dtype=jnp.int32)[None, :]).astype(F32)
    targets = (length - type_counts[:, 0]).astype(F32)
    totals = lax.psum(jnp.sum(choose * targets[:, None], 0), "dp")
    factor = jnp.sum(totals) / TASKS / totals
    seq_weight = jnp.sum(choose * factor[None, :], 1)
    own_weight = lax.dynamic_index_in_dim(seq_weight, side, 0, False)
    own_start = lax.dynamic_index_in_dim(type_counts[:, 0], side, 0, False)
    steps = jnp.arange(rows, dtype=jnp.int32)
    query_pos = jnp.concatenate([low * rows + steps, (3 - low) * rows + steps])
    scale = jnp.where(query_pos >= own_start, own_weight, 0.0)
    upstream = cotangent.astype(F32) * scale[:, None]

    stacked = (gain_one, bias_one, proj_qkv, proj_out, gain_two, bias_two, proj_up, proj_down)
    kept_all = []
    for section in range(LAYERS):
        weights = tuple(weight[section] for weight in stacked)
        stream, kept = layer_forward(stream, weights, flag, exchange)
        kept_all.append(kept)
    outputs = return_slot(stream.astype(BF16))
    small, mlp, branch = [None] * LAYERS, [None] * LAYERS, [None] * LAYERS
    for section in reversed(range(LAYERS)):
        weights = tuple(weight[section] for weight in stacked)
        upstream, small[section], mlp[section], branch[section] = layer_backward(
            upstream, weights, kept_all[section], flag, meta, core, exchange
        )
    back_inputs = return_slot(upstream.astype(BF16)).astype(F32)

    chips = exchange.chips
    each = width // chips // 2
    table = jnp.concatenate(small).reshape(8, chips, 2, each).transpose(1, 2, 0, 3)
    mine = lax.dynamic_index_in_dim(table, core, 1, False)
    theirs = exchange.swap_core(lax.dynamic_index_in_dim(table, 1 - core, 1, False))
    table = jnp.take(mine + theirs, ids, axis=0)
    table = exchange.reduce_scatter(table[: chips // 2], table[chips // 2 :], F32)
    table = table.reshape(LAYERS, 4, each)
    ups, downs = zip(*(unpack_mlp(share, core, exchange) for share in mlp))
    qkvs, outs = zip(*(unpack_branch(share, core, exchange) for share in branch))
    return (
        outputs, back_inputs, table[:, 0], table[:, 1], jnp.stack(qkvs), jnp.stack(outs),
        table[:, 2], table[:, 3], jnp.stack(ups), jnp.stack(downs),
    )


def solution(mesh):
    tokens = P("dp", "seq", None)
    shared = P(None, AXES)
    in_specs = (tokens, tokens, P("dp"), P("dp", None)) + (P(),) * 8
    out_specs = (
        tokens, tokens, shared, shared, P(None, AXES, None), P(None, AXES, None),
        shared, shared, P(None, AXES, None), P(None, AXES, None),
    )
    return jax.shard_map(
        per_device, mesh=mesh, in_specs=in_specs, out_specs=out_specs, check_vma=False
    )
```

```python
import functools
import math

import jax
import jax.numpy as jnp
import numpy as np
from jax import lax
from jax.experimental import pallas as pl
from jax.experimental.pallas import tpu as pltpu
from jax.sharding import PartitionSpec as P

HEADS = 12
HEAD_DIM = 64
LAYERS = 2
TASKS = 3
AXES = ("dp", "seq")
F32 = jnp.float32
BF16 = jnp.bfloat16
epsilon = 1e-05
VMEM_BYTES = 56 * 1024 * 1024


def dot_nn(a, b):
    return lax.dot_general(a, b, (((1,), (0,)), ((), ())), preferred_element_type=F32)


def dot_nt(a, b):
    return lax.dot_general(a, b, (((1,), (1,)), ((), ())), preferred_element_type=F32)


def dot_tn(a, b):
    return lax.dot_general(a, b, (((0,), (0,)), ((), ())), preferred_element_type=F32)


def gelu_and_slope(x):
    z = jnp.abs(x) * 0.7071067811865476
    d = 1.0 + 0.3275911 * z
    t = pl.reciprocal(d, approx=True)
    t = t * (2.0 - d * t)
    poly = t * (
        0.254829592
        + t * (-0.284496736 + t * (1.421413741 + t * (-1.453152027 + t * 1.061405429)))
    )
    bell = jnp.exp(-0.5 * x * x)
    tail = 0.5 * poly * bell
    below = jnp.where(x >= 0.0, 1.0 - tail, tail)
    return x * below, below + x * bell * 0.3989422804014327


def pair_lists(variant):
    if variant == 0:
        return [[(0, 0, True)], [(0, 0, False), (1, 0, False), (1, 1, False), (0, 1, True)]]
    return [[(1, 0, False), (0, 0, True)], [(0, 0, False), (1, 0, False), (0, 1, True)]]


def head_masks(scale):
    lane = lax.broadcasted_iota(jnp.int32, (1, 2 * HEAD_DIM), 1)
    first = jnp.where(lane < HEAD_DIM, scale, 0.0)
    return first.astype(BF16), (scale - first).astype(BF16)


def attention_forward_kernel(meta, q_ref, ko_ref, vo_ref, kx_ref, vx_ref, out_ref, lse_ref):
    rows = q_ref.shape[0] // 2
    masks = head_masks(1.0 / math.sqrt(HEAD_DIM))
    keys = (ko_ref, kx_ref)
    values = (vo_ref, vx_ref)

    def run(variant):
        below = lax.broadcasted_iota(jnp.int32, (rows, rows), 1) <= lax.broadcasted_iota(
            jnp.int32, (rows, rows), 0
        )
        lane = lax.broadcasted_iota(jnp.int32, (rows, 2 * HEAD_DIM), 1)
        for block, pairs in enumerate(pair_lists(variant)):
            span = pl.ds(block * rows, rows)
            q = q_ref[span, :]
            results, logs = [], []
            for head in range(2):
                qm = q * masks[head]
                scores = []
                for source, kblock, diagonal in pairs:
                    part = dot_nt(qm, keys[source][pl.ds(kblock * rows, rows), :])
                    scores.append(jnp.where(below, part, -1e30) if diagonal else part)
                peak = functools.reduce(jnp.maximum, scores)
                peak = jnp.max(peak, -1, keepdims=True)
                total, acc = None, None
                for part, (source, kblock, diagonal) in zip(scores, pairs):
                    raised = jnp.exp(part - peak)
                    total = raised if total is None else total + raised
                    term = dot_nn(raised.astype(BF16), values[source][pl.ds(kblock * rows, rows), :])
                    acc = term if acc is None else acc + term
                total = jnp.sum(total, -1, keepdims=True)
                results.append(acc / total)
                logs.append(peak + jnp.log(total))
            out_ref[span, :] = jnp.where(lane < HEAD_DIM, results[0], results[1]).astype(BF16)
            packed = jnp.where(lane == 0, logs[0], logs[1])
            lse_ref[0, :, span] = packed.T[:8, :]

    @pl.when(meta[0] == 0)
    def _():
        run(0)

    @pl.when(meta[0] == 1)
    def _():
        run(1)


def attention_forward(meta, queries, own, other):
    tokens = queries.shape[0]
    pairs = HEADS // 2
    wide = 2 * HEAD_DIM

    def at(offset):
        return pl.BlockSpec((tokens, wide), lambda g, m: (0, offset + g))

    return pl.pallas_call(
        attention_forward_kernel,
        grid_spec=pltpu.PrefetchScalarGridSpec(
            num_scalar_prefetch=1,
            grid=(pairs,),
            in_specs=[at(0), at(0), at(pairs), at(0), at(pairs)],
            out_specs=[at(0), pl.BlockSpec((1, 8, tokens), lambda g, m: (g, 0, 0))],
        ),
        out_shape=[
            jax.ShapeDtypeStruct((tokens, HEADS * HEAD_DIM), BF16),
            jax.ShapeDtypeStruct((pairs, 8, tokens), F32),
        ],
        compiler_params=pltpu.CompilerParams(vmem_limit_bytes=VMEM_BYTES),
        cost_estimate=pl.CostEstimate(flops=8_000_000_000, bytes_accessed=4_000_000, transcendentals=4_000_000),
        name="attention_forward",
    )(meta, queries, own, own, other, other)


def attention_backward_kernel(
    meta, q_ref, ko_ref, vo_ref, kx_ref, vx_ref, do_ref, o_ref, lse_ref,
    dq_ref, own_ref, other_ref,
):
    rows = q_ref.shape[0] // 2
    scale = 1.0 / math.sqrt(HEAD_DIM)
    scaled = head_masks(scale)
    plain = head_masks(1.0)
    keys = (ko_ref, kx_ref)
    values = (vo_ref, vx_ref)
    grads = (own_ref, other_ref)
    product = (do_ref[...].astype(F32) * o_ref[...].astype(F32)).T
    dots = (
        jnp.sum(product[:HEAD_DIM], 0, keepdims=True),
        jnp.sum(product[HEAD_DIM:], 0, keepdims=True),
    )
    logs = lse_ref[0]

    def run(variant):
        below = lax.broadcasted_iota(jnp.int32, (rows, rows), 0) <= lax.broadcasted_iota(
            jnp.int32, (rows, rows), 1
        )
        dk_acc, dv_acc = {}, {}
        for block, pairs in enumerate(pair_lists(variant)):
            span = slice(block * rows, (block + 1) * rows)
            q, do = q_ref[span, :], do_ref[span, :]
            dq = None
            for head in range(2):
                qm, dom = q * scaled[head], do * plain[head]
                log_row = logs[head : head + 1, span]
                dot_row = dots[head][:, span]
                for source, kblock, diagonal in pairs:
                    where = pl.ds(kblock * rows, rows)
                    k, v = keys[source][where, :], values[source][where, :]
                    raised = jnp.exp(dot_nt(k, qm) - log_row)
                    if diagonal:
                        raised = jnp.where(below, raised, 0.0)
                    slope = (raised * (dot_nt(v, dom) - dot_row)).astype(BF16)
                    term_v = dot_nn(raised.astype(BF16), dom)
                    term_k = dot_nn(slope, qm)
                    term_q = dot_tn(slope, k * scaled[head])
                    slot = (source, kblock)
                    dv_acc[slot] = dv_acc[slot] + term_v if slot in dv_acc else term_v
                    dk_acc[slot] = dk_acc[slot] + term_k if slot in dk_acc else term_k
                    dq = term_q if dq is None else dq + term_q
            dq_ref[span, :] = dq.astype(BF16)
        for source in range(2):
            for kblock in range(2):
                span = slice(kblock * rows, (kblock + 1) * rows)
                slot = (source, kblock)
                for which, acc in enumerate((dk_acc, dv_acc)):
                    value = acc[slot] if slot in acc else jnp.zeros((rows, 2 * HEAD_DIM), F32)
                    grads[source][which, span, :] = value.astype(grads[source].dtype)

    @pl.when(meta[0] == 0)
    def _():
        run(0)

    @pl.when(meta[0] == 1)
    def _():
        run(1)


def attention_backward(meta, queries, own, other, back_attended, attended, logs):
    tokens = queries.shape[0]
    pairs = HEADS // 2
    wide = 2 * HEAD_DIM
    width = HEADS * HEAD_DIM

    def at(offset):
        return pl.BlockSpec((tokens, wide), lambda g, m: (0, offset + g))

    return pl.pallas_call(
        attention_backward_kernel,
        grid_spec=pltpu.PrefetchScalarGridSpec(
            num_scalar_prefetch=1,
            grid=(pairs,),
            in_specs=[at(0), at(0), at(pairs), at(0), at(pairs), at(0), at(0),
                      pl.BlockSpec((1, 8, tokens), lambda g, m: (g, 0, 0))],
            out_specs=[at(0)] + [pl.BlockSpec((2, tokens, wide), lambda g, m: (0, 0, g))] * 2,
        ),
        out_shape=[
            jax.ShapeDtypeStruct((tokens, width), BF16),
            jax.ShapeDtypeStruct((2, tokens, width), F32),
            jax.ShapeDtypeStruct((2, tokens, width), BF16),
        ],
        compiler_params=pltpu.CompilerParams(vmem_limit_bytes=VMEM_BYTES),
        cost_estimate=pl.CostEstimate(flops=16_000_000_000, bytes_accessed=9_000_000, transcendentals=4_000_000),
        name="attention_backward",
    )(meta, queries, own, own, other, other, back_attended, attended, logs)


def normalised(rows_in):
    average = jnp.mean(rows_in, -1, keepdims=True)
    centred = rows_in - average
    inverse = lax.rsqrt(jnp.mean(centred * centred, -1, keepdims=True) + epsilon)
    return centred * inverse, inverse


def norm_back(rows_in, gain_row, back):
    unit, inverse = normalised(rows_in)
    slope = back * gain_row
    first = jnp.mean(slope, -1, keepdims=True)
    second = jnp.mean(slope * unit, -1, keepdims=True)
    return inverse * (slope - first - unit * second), (
        jnp.sum(back * unit, 0, keepdims=True), jnp.sum(back, 0, keepdims=True))


def with_rows(table, row, sums):
    index = lax.broadcasted_iota(jnp.int32, table.shape, 0)
    return jnp.where(index == row, sums[0], jnp.where(index == row + 1, sums[1], table))


def project_kernel(layer, stream, gain, shift, matrix, hidden, queries, pairs):
    step = pl.program_id(0)

    @pl.when(step == 0)
    def _():
        unit, unused = normalised(stream[...].astype(F32))
        hidden[...] = (unit * gain[layer : layer + 1] + shift[layer : layer + 1]).astype(BF16)

    out = dot_nn(hidden[...], matrix[0]).astype(BF16)

    @pl.when(step < 2)
    def _():
        pairs[...] = out

    @pl.when(step == 2)
    def _():
        queries[...] = out


def project(layer, stream, gain, shift, matrix):
    tokens, width = stream.shape
    whole = pl.BlockSpec((tokens, width), lambda j: (0, 0))
    row = pl.BlockSpec(gain.shape, lambda j: (0, 0))
    return pl.pallas_call(
        functools.partial(project_kernel, layer),
        grid=(3,),
        in_specs=[whole, row, row, pl.BlockSpec((1, width, width), lambda j: (layer, 0, (j + 1) % 3))],
        out_specs=[whole, whole, pl.BlockSpec((tokens, width), lambda j: (0, jnp.minimum(j, 1)))],
        out_shape=[
            jax.ShapeDtypeStruct((tokens, width), BF16),
            jax.ShapeDtypeStruct((tokens, width), BF16),
            jax.ShapeDtypeStruct((tokens, 2 * width), BF16),
        ],
        compiler_params=pltpu.CompilerParams(vmem_limit_bytes=VMEM_BYTES),
        cost_estimate=pl.CostEstimate(flops=2_000_000_000, bytes_accessed=9_000_000, transcendentals=0),
        name="project",
    )(stream, gain, shift, matrix)


def feed_forward_kernel(
    layer, steps, attended, stream, matrix_out, gain, shift, up, down,
    middle, normed, active_ref, slope_ref, out, raw, acc,
):
    step = pl.program_id(0)

    @pl.when(step == 0)
    def _():
        middle[...] = stream[...].astype(F32) + dot_nn(attended[...], matrix_out[0])
        unit, unused = normalised(middle[...])
        normed[...] = (unit * gain[layer : layer + 1] + shift[layer : layer + 1]).astype(BF16)

    active, slope = gelu_and_slope(raw[...])
    active = active.astype(BF16)
    active_ref[...] = active
    slope_ref[...] = slope.astype(BF16)
    acc[...] = jnp.where(step <= 1, middle[...], acc[...]) + dot_nn(active, down[0])
    raw[...] = dot_nn(normed[...], up[0])

    @pl.when(step == steps)
    def _():
        out[...] = acc[...].astype(out.dtype)


def feed_forward(layer, attended, stream, matrix_out, gain, shift, up, down, kind):
    tokens, width = stream.shape
    hidden = up.shape[2]
    tile = 512
    steps = hidden // tile
    whole = pl.BlockSpec((tokens, width), lambda j: (0, 0))
    row = pl.BlockSpec(gain.shape, lambda j: (0, 0))
    part = pl.BlockSpec((tokens, tile), lambda j: (0, jnp.maximum(j - 1, 0)))
    return pl.pallas_call(
        functools.partial(feed_forward_kernel, layer, steps),
        grid=(steps + 1,),
        in_specs=[
            whole, whole, pl.BlockSpec((1, width, width), lambda j: (layer, 0, 0)), row, row,
            pl.BlockSpec((1, width, tile), lambda j: (layer, 0, jnp.minimum(j, steps - 1))),
            pl.BlockSpec((1, tile, width), lambda j: (layer, jnp.maximum(j - 1, 0), 0)),
        ],
        out_specs=[whole, whole, part, part, whole],
        out_shape=[
            jax.ShapeDtypeStruct((tokens, width), F32),
            jax.ShapeDtypeStruct((tokens, width), BF16),
            jax.ShapeDtypeStruct((tokens, hidden), BF16),
            jax.ShapeDtypeStruct((tokens, hidden), BF16),
            jax.ShapeDtypeStruct((tokens, width), kind),
        ],
        scratch_shapes=[pltpu.VMEM((tokens, tile), F32), pltpu.VMEM((tokens, width), F32)],
        compiler_params=pltpu.CompilerParams(vmem_limit_bytes=VMEM_BYTES),
        cost_estimate=pl.CostEstimate(flops=10_000_000_000, bytes_accessed=20_000_000, transcendentals=3_000_000),
        name="feed_forward",
    )(attended, stream, matrix_out, gain, shift, up, down)


def feed_back_kernel(
    layer, steps, meta, upstream, slope, up, down, middle, gain, matrix_out, sums_in,
    own, send, back_out, back_out_send, back_middle, back_branch, branch_send, back_attended, grads, acc,
):
    step = pl.program_id(0)
    half = back_out_send.shape[1]
    theirs = pl.ds(pl.multiple_of((1 - meta[1]) * half, 128), half)

    @pl.when(step == 0)
    def _():
        back_out[...] = upstream[...].astype(BF16)
        back_out_send[...] = back_out[:, theirs]
        acc[...] = jnp.zeros_like(acc)

    back_up = (dot_nt(back_out[...], down[0]) * slope[...].astype(F32)).astype(BF16)

    @pl.when(step < steps // 2)
    def _():
        send[...] = back_up

    @pl.when(step >= steps // 2)
    def _():
        own[...] = back_up

    acc[...] += dot_nt(back_up, up[0])

    @pl.when(step == steps - 1)
    def _():
        back, sums = norm_back(middle[...], gain[layer : layer + 1], acc[...])
        back = back + upstream[...]
        grads[...] = with_rows(sums_in[...], 4 * layer + 2, sums)
        back_middle[...] = back
        back_branch[...] = back.astype(BF16)
        branch_send[...] = back_branch[:, theirs]
        back_attended[...] = dot_nt(back_branch[...], matrix_out[0]).astype(BF16)


def feed_back(layer, meta, upstream, slope, up, down, middle, gain, matrix_out, sums):
    tokens, width = upstream.shape
    hidden = up.shape[2]
    tile = 512
    steps = hidden // tile
    half = steps // 2

    def place(j, m):
        return jnp.where(j < half, (1 - m[1]) * half + j, m[1] * half + j - half)

    whole = pl.BlockSpec((tokens, width), lambda j, m: (0, 0))
    narrow = pl.BlockSpec((tokens, width // 2), lambda j, m: (0, 0))
    wide = jax.ShapeDtypeStruct((tokens, width), BF16)
    return pl.pallas_call(
        functools.partial(feed_back_kernel, layer, steps),
        grid_spec=pltpu.PrefetchScalarGridSpec(
            num_scalar_prefetch=1,
            grid=(steps,),
            in_specs=[
                whole, pl.BlockSpec((tokens, tile), lambda j, m: (0, place(j, m))),
                pl.BlockSpec((1, width, tile), lambda j, m: (layer, 0, place(j, m))),
                pl.BlockSpec((1, tile, width), lambda j, m: (layer, place(j, m), 0)),
                whole, pl.BlockSpec(gain.shape, lambda j, m: (0, 0)),
                pl.BlockSpec((1, width, width), lambda j, m: (layer, 0, 0)),
                pl.BlockSpec((8, width), lambda j, m: (0, 0)),
            ],
            out_specs=[
                pl.BlockSpec((tokens, tile), lambda j, m: (0, jnp.maximum(j - half, 0))),
                pl.BlockSpec((tokens, tile), lambda j, m: (0, jnp.minimum(j, half - 1))),
                whole, narrow, whole, whole, narrow, whole,
                pl.BlockSpec((8, width), lambda j, m: (0, 0)),
            ],
            scratch_shapes=[pltpu.VMEM((tokens, width), F32)],
        ),
        out_shape=[
            jax.ShapeDtypeStruct((tokens, hidden // 2), BF16),
            jax.ShapeDtypeStruct((tokens, hidden // 2), BF16),
            wide, jax.ShapeDtypeStruct((tokens, width // 2), BF16),
            jax.ShapeDtypeStruct((tokens, width), F32),
            wide, jax.ShapeDtypeStruct((tokens, width // 2), BF16),
            wide, jax.ShapeDtypeStruct((8, width), F32),
        ],
        compiler_params=pltpu.CompilerParams(vmem_limit_bytes=VMEM_BYTES),
        cost_estimate=pl.CostEstimate(flops=10_000_000_000, bytes_accessed=22_000_000, transcendentals=0),
        name="feed_back",
    )(meta, upstream, slope, up, down, middle, gain, matrix_out, sums)


def project_back_kernel(
    layer, meta, back_q, own, got, matrix, stream, gain, back_middle, sums_in,
    mine, theirs, upstream, grads, table, acc,
):
    step = pl.program_id(0)
    width = back_q.shape[1]

    @pl.when(step == 0)
    def _():
        table[0] = back_q[...]
        for which in range(2):
            table[1 + which] = (own[which] + got[which].astype(F32)).astype(BF16)
        half = width // 2

        @pl.when(meta[1] == 0)
        def _():
            mine[:, :width] = table[0]
            mine[:, width:] = table[1, :, :half]
            theirs[:, :half] = table[1, :, half:]
            theirs[:, half:] = table[2]

        @pl.when(meta[1] == 1)
        def _():
            theirs[:, :width] = table[0]
            theirs[:, width:] = table[1, :, :half]
            mine[:, :half] = table[1, :, half:]
            mine[:, half:] = table[2]

        acc[...] = jnp.zeros_like(acc)

    acc[...] += dot_nt(table[step], matrix[0])

    @pl.when(step == 2)
    def _():
        back, sums = norm_back(stream[...].astype(F32), gain[layer : layer + 1], acc[...])
        upstream[...] = (back + back_middle[...]).astype(upstream.dtype)
        grads[...] = with_rows(sums_in[...], 4 * layer, sums)


def project_back(layer, meta, back_q, own, got, matrix, stream, gain, back_middle, sums, kind):
    tokens, width = stream.shape
    whole = pl.BlockSpec((tokens, width), lambda j, m: (0, 0))
    both = pl.BlockSpec((2, tokens, width), lambda j, m: (0, 0, 0))
    side = pl.BlockSpec((tokens, 3 * width // 2), lambda j, m: (0, 0))
    return pl.pallas_call(
        functools.partial(project_back_kernel, layer),
        grid_spec=pltpu.PrefetchScalarGridSpec(
            num_scalar_prefetch=1,
            grid=(3,),
            in_specs=[
                whole, both, both, pl.BlockSpec((1, width, width), lambda j, m: (layer, 0, j)),
                whole, pl.BlockSpec(gain.shape, lambda j, m: (0, 0)), whole,
                pl.BlockSpec((8, width), lambda j, m: (0, 0)),
            ],
            out_specs=[side, side, whole, pl.BlockSpec((8, width), lambda j, m: (0, 0))],
            scratch_shapes=[pltpu.VMEM((3, tokens, width), BF16), pltpu.VMEM((tokens, width), F32)],
        ),
        out_shape=[
            jax.ShapeDtypeStruct((tokens, 3 * width // 2), BF16),
            jax.ShapeDtypeStruct((tokens, 3 * width // 2), BF16),
            jax.ShapeDtypeStruct((tokens, width), kind),
            jax.ShapeDtypeStruct((8, width), F32),
        ],
        compiler_params=pltpu.CompilerParams(vmem_limit_bytes=VMEM_BYTES),
        cost_estimate=pl.CostEstimate(flops=3_000_000_000, bytes_accessed=20_000_000, transcendentals=0),
        name="project_back",
    )(meta, back_q, own, got, matrix, stream, gain, back_middle, sums)


def store_chunks(chips, meta, acc, keep, send):
    rows = acc.shape[0] // chips
    for position in range(chips):
        chunk = acc[pl.ds(pl.multiple_of(meta[2 + position] * rows, 16), rows), :]
        if position < chips // 2:
            keep[position] = chunk
        else:
            send[position - chips // 2] = chunk


def grad_up_kernel(chips, meta, ao, ax, bo, bx, co, cx, do, dx, keep, send, acc):
    step = pl.program_id(0)

    @pl.when(step < 4)
    def _():
        acc[...] = (dot_tn(ao[...], bo[...]) + dot_tn(ax[...], bx[...])).astype(BF16)

    @pl.when(step == 4)
    def _():
        acc[...] = (dot_tn(co[...], do[...]) + dot_tn(cx[...], dx[...])).astype(BF16)

    store_chunks(chips, meta, acc, keep, send)


def grad_down_kernel(chips, meta, ao, ax, bo, bx, keep_in, send_in, keep, send):
    rows = keep.shape[1]
    each = ao.shape[1] // rows
    total = (dot_tn(ao[...], bo[...]) + dot_tn(ax[...], bx[...])).astype(BF16)
    for local in range(each):
        position = meta[2 + chips + pl.program_id(0) * each + local]
        chunk = total[local * rows : (local + 1) * rows]

        @pl.when(position < chips // 2)
        def _():
            keep[position] = chunk

        @pl.when(position >= chips // 2)
        def _():
            send[position - chips // 2] = chunk


def grad_qkv_kernel(chips, meta, ao, ax, bo, bx, sums, keep, send, acc, columns):
    wide = bo.shape[1]
    acc[:, :wide] = (dot_tn(ao[...], bo[...]) + dot_tn(ax[...], bx[...])).astype(BF16)
    columns[...] = jnp.concatenate([sums[...], jnp.zeros((120, sums.shape[1]), F32)], 0).T
    acc[:, wide:] = columns[...].astype(BF16)
    store_chunks(chips, meta, acc, keep, send)


def ordered(total, ids, chips):
    split = total.astype(BF16).reshape(chips, total.shape[0] // chips, total.shape[1])
    return jnp.take(split, ids, axis=0)


def mlp_gradients(
    meta, chips, normed, normed_x, back_up, back_up_x, active, active_x, back_out, back_out_x,
    attended, attended_x, back_branch, branch_x,
):
    tokens, width = normed.shape
    hidden = active.shape[1]
    half = width // 2
    rows = width // chips
    params = pltpu.CompilerParams(vmem_limit_bytes=VMEM_BYTES)
    if rows % 16 != 0:
        ids = meta[2 : 2 + chips]
        up = dot_tn(normed, back_up) + dot_tn(normed_x, back_up_x)
        own = lax.dynamic_slice_in_dim(back_out, meta[1] * half, half, 1)
        down = dot_tn(active, own) + dot_tn(active_x, back_out_x)
        own = lax.dynamic_slice_in_dim(back_branch, meta[1] * half, half, 1)
        out = dot_tn(attended, own) + dot_tn(attended_x, branch_x)
        up = ordered(up, ids, chips).reshape(chips, rows, 4, half)
        up = up.transpose(0, 2, 1, 3).reshape(chips, 4 * rows, half)
        both = jnp.concatenate([up, ordered(down, ids, chips), ordered(out, ids, chips)], 1)
        return both[: chips // 2], both[chips // 2 :]
    shape = jax.ShapeDtypeStruct((chips // 2, 9 * rows, half), BF16)
    whole = pl.BlockSpec((tokens, width), lambda j, m: (0, 0))
    tile = pl.BlockSpec((tokens, half), lambda j, m: (0, jnp.minimum(j, 3)))
    fixed = pl.BlockSpec((tokens, half), lambda j, m: (0, 0))
    mine = pl.BlockSpec((tokens, half), lambda j, m: (0, m[1]))
    out = pl.BlockSpec((chips // 2, rows, half), lambda j, m: (0, jnp.where(j < 4, j, 8), 0))
    keep, send = pl.pallas_call(
        functools.partial(grad_up_kernel, chips),
        grid_spec=pltpu.PrefetchScalarGridSpec(
            num_scalar_prefetch=1,
            grid=(5,),
            in_specs=[whole, whole, tile, tile, whole, whole, mine, fixed],
            out_specs=[out, out],
            scratch_shapes=[pltpu.VMEM((width, half), BF16)],
        ),
        out_shape=[shape, shape],
        compiler_params=params,
        cost_estimate=pl.CostEstimate(flops=6_000_000_000, bytes_accessed=9_000_000, transcendentals=0),
        name="gradient_up",
    )(meta, normed, normed_x, back_up, back_up_x, attended, attended_x, back_branch, branch_x)
    tile = pl.BlockSpec((tokens, width), lambda j, m: (0, j))
    out = pl.BlockSpec((chips // 2, 4 * rows, half), lambda j, m: (0, 1, 0))
    return pl.pallas_call(
        functools.partial(grad_down_kernel, chips),
        grid_spec=pltpu.PrefetchScalarGridSpec(
            num_scalar_prefetch=1,
            grid=(hidden // width,),
            in_specs=[tile, tile, mine, fixed,
                      pl.BlockSpec(memory_space=pl.ANY), pl.BlockSpec(memory_space=pl.ANY)],
            out_specs=[out, out],
        ),
        out_shape=[shape, shape],
        input_output_aliases={5: 0, 6: 1},
        compiler_params=params,
        cost_estimate=pl.CostEstimate(flops=4_800_000_000, bytes_accessed=10_000_000, transcendentals=0),
        name="gradient_down",
    )(meta, active, active_x, back_out, back_out_x, keep, send)


def qkv_gradients(meta, chips, hidden, hidden_x, back_projected, back_projected_x, sums):
    tokens, width = hidden.shape
    wide = back_projected.shape[1]
    rows = width // chips
    if rows % 16 != 0:
        qkv = dot_tn(hidden, back_projected) + dot_tn(hidden_x, back_projected_x)
        table = jnp.pad(sums.T, ((0, 0), (0, 120)))
        both = ordered(jnp.concatenate([qkv, table], -1), meta[2 : 2 + chips], chips)
        return both[: chips // 2], both[chips // 2 :]
    shape = jax.ShapeDtypeStruct((chips // 2, rows, wide + 128), BF16)
    return pl.pallas_call(
        functools.partial(grad_qkv_kernel, chips),
        grid_spec=pltpu.PrefetchScalarGridSpec(
            num_scalar_prefetch=1,
            grid=(1,),
            in_specs=[pl.BlockSpec((tokens, width), lambda j, m: (0, 0))] * 2
            + [pl.BlockSpec((tokens, wide), lambda j, m: (0, 0))] * 2
            + [pl.BlockSpec((8, width), lambda j, m: (0, 0))],
            out_specs=[pl.BlockSpec((chips // 2, rows, wide + 128), lambda j, m: (0, 0, 0))] * 2,
            scratch_shapes=[pltpu.VMEM((width, wide + 128), BF16), pltpu.VMEM((width, 128), F32)],
        ),
        out_shape=[shape, shape],
        compiler_params=pltpu.CompilerParams(vmem_limit_bytes=VMEM_BYTES),
        cost_estimate=pl.CostEstimate(flops=4_800_000_000, bytes_accessed=8_000_000, transcendentals=0),
        name="gradient_qkv",
    )(meta, hidden, hidden_x, back_projected, back_projected_x, sums)


class Exchange:
    def __init__(self, dp):
        self.dp = dp
        self.chips = 2 * dp
        self.bits = int(math.log2(self.chips))
        self.core_pairs = [(s, s ^ 1) for s in range(4)]
        self.mirror_pairs = [(s, 3 - s) for s in range(4)]
        rest = list(range(2, self.bits))
        self.orders = ([1, 0] + rest, [0, 1] + rest)

    def swap_core(self, value):
        return lax.ppermute(value, "seq", self.core_pairs)

    def mirror(self, value):
        return lax.ppermute(value, "seq", self.mirror_pairs)

    def pairs(self, phase):
        result = []
        for device in range(2 * self.chips):
            chip = (device // 4) * 2 + (device % 4) // 2
            core = device % 2
            other = chip ^ (1 << self.orders[core][phase])
            result.append((device, (other // 2) * 4 + (other % 2) * 2 + core))
        return result

    def tables(self, chip, core):
        index = np.arange(self.chips)
        maps, inverses = [], []
        for order in self.orders:
            value = np.zeros_like(index)
            for phase, bit in enumerate(order):
                value |= ((index >> (self.bits - 1 - phase)) & 1) << bit
            inverse = np.zeros_like(index)
            inverse[value] = index
            maps.append(value.astype(np.int32))
            inverses.append(order)
        ids = chip ^ jnp.where(core == 0, jnp.asarray(maps[0]), jnp.asarray(maps[1]))
        relative = jnp.asarray(index.astype(np.int32)) ^ chip
        places = []
        for order in self.orders:
            place = jnp.zeros_like(relative)
            for phase, bit in enumerate(order):
                place = place | (((relative >> bit) & 1) << (self.bits - 1 - phase))
            places.append(place)
        return ids.astype(jnp.int32), jnp.where(core == 0, places[0], places[1]).astype(jnp.int32)


class Reduction:
    def __init__(self, exchange, keep, send):
        self.exchange, self.parts, self.send, self.phase = exchange, [keep], send, 0

    def step(self):
        kind = self.send.dtype
        self.parts.append(lax.ppermute(self.send, AXES, self.exchange.pairs(self.phase)))
        size = self.parts[-1].shape[0]
        self.phase += 1
        if self.phase < self.exchange.bits:
            terms = [part[size // 2 : size].astype(F32) for part in self.parts]
            self.send = functools.reduce(jnp.add, terms).astype(kind)
        else:
            self.send = functools.reduce(jnp.add, [part[0].astype(F32) for part in self.parts])

    def steps(self, count):
        for _ in range(min(count, self.exchange.bits - self.phase)):
            self.step()

    def finish(self):
        self.steps(self.exchange.bits)
        return self.send


def together(value, *reductions):
    tied = lax.optimization_barrier((value,) + tuple(r.send for r in reductions))
    for reduction, message in zip(reductions, tied[1:]):
        reduction.send = message
    return tied[0]


def by_core(core, mine, theirs, axis):
    return jnp.where(
        core == 0,
        jnp.concatenate([mine, theirs], axis),
        jnp.concatenate([theirs, mine], axis),
    )


def order(first, *others):
    return lax.optimization_barrier((first,) + others)


def unpack_mlp(share, core, exchange):
    long, half = share.shape
    rows, each = long // 9, long // 18
    up = share[: 4 * rows].reshape(4, 2, each, half)
    down = share[4 * rows : 8 * rows].reshape(2, 4 * each, half)
    out = share[8 * rows :].reshape(2, each, half)

    def pick(which):
        return jnp.concatenate(
            [lax.dynamic_index_in_dim(up, which, 1, False).reshape(4 * each, half),
             lax.dynamic_index_in_dim(down, which, 0, False),
             lax.dynamic_index_in_dim(out, which, 0, False)], 0)

    mine, theirs = pick(core), exchange.swap_core(pick(1 - core))

    def widen(value):
        return value[: 4 * each].reshape(4, each, half).transpose(1, 0, 2).reshape(each, 4 * half)

    grad_up = by_core(core, widen(mine), widen(theirs), 1)
    grad_down = by_core(core, mine[4 * each : 8 * each], theirs[4 * each : 8 * each], 1)
    grad_out = by_core(core, mine[8 * each :], theirs[8 * each :], 1)
    return grad_up, grad_down, grad_out


def unpack_qkv(share, core, exchange):
    rows, wide = share.shape
    split = share.reshape(2, rows // 2, wide)
    mine = lax.dynamic_index_in_dim(split, core, 0, False)
    theirs = exchange.swap_core(lax.dynamic_index_in_dim(split, 1 - core, 0, False))
    wide -= 128
    table = mine[:, wide : wide + 8] + theirs[:, wide : wide + 8]
    return by_core(core, mine[:, :wide], theirs[:, :wide], 1), table


def per_device(
    inputs, cotangent, task_table, type_counts,
    gain_one, bias_one, proj_qkv, proj_out, gain_two, bias_two, proj_up, proj_down,
):
    slots, rows, width = inputs.shape
    length = rows * lax.axis_size("seq")
    exchange = Exchange(lax.axis_size("dp"))
    place = lax.axis_index("seq")
    side, core = place // 2, place % 2
    chip = lax.axis_index("dp") * 2 + side
    low = jnp.minimum(place, 3 - place)
    own_first = place < 2
    ids, places = exchange.tables(chip, core)
    flag = low.astype(jnp.int32).reshape(1)
    meta = jnp.concatenate([flag, core.astype(jnp.int32).reshape(1), ids, places])

    def gather_slot(value):
        own = lax.dynamic_index_in_dim(value, side, 0, False)
        got = exchange.mirror(lax.dynamic_index_in_dim(value, 1 - side, 0, False))
        return jnp.where(own_first, jnp.concatenate([own, got]), jnp.concatenate([got, own]))

    def return_slot(value):
        first, second = value[:rows], value[rows:]
        own = jnp.where(own_first, first, second)
        got = exchange.mirror(jnp.where(own_first, second, first))
        return jnp.where(side == 0, jnp.stack([own, got]), jnp.stack([got, own]))

    stream = gather_slot(inputs)
    cotangent = gather_slot(cotangent)
    choose = (task_table[:, None] == jnp.arange(TASKS, dtype=jnp.int32)[None, :]).astype(F32)
    targets = (length - type_counts[:, 0]).astype(F32)
    totals = jnp.sum(choose * targets[:, None], 0)
    bits = int(math.log2(exchange.dp))

    def add_totals(totals, bit):
        if bit >= bits:
            return totals
        return totals + lax.ppermute(totals, "dp", [(d, d ^ (1 << bit)) for d in range(exchange.dp)])

    kept = []
    for layer in range(LAYERS):
        kind = BF16 if layer == LAYERS - 1 else F32
        hidden, queries, own = project(layer, stream, gain_one, bias_one, proj_qkv)
        other = exchange.swap_core(own)
        if layer == 0:
            queries, totals = order(queries, totals)
            totals = add_totals(totals, 0)
        else:
            queries, attended_x, normed_x, active_x = order(queries, attended_x, normed_x, active_x)
            kept[0] += (attended_x, normed_x, active_x)
            totals = add_totals(totals, 2)
        attended, logs = attention_forward(flag, queries, own, other)
        hidden_x = exchange.swap_core(hidden)
        attended, hidden_x, totals = order(attended, hidden_x, totals)
        if layer == 0:
            totals = add_totals(totals, 1)
        middle, normed, active, slope, output = feed_forward(
            layer, attended, stream, proj_out, gain_two, bias_two, proj_up, proj_down, kind
        )
        attended_x, normed_x, active_x = (exchange.swap_core(v) for v in (attended, normed, active))
        kept.append((stream, hidden, queries, own, other, logs, attended, middle, normed, active, slope, hidden_x))
        stream, totals = order(output, totals)
    kept[1] += (attended_x, normed_x, active_x)
    for bit in range(3, bits):
        totals = add_totals(totals, bit)
    factor = jnp.sum(totals) / TASKS / totals
    seq_weight = jnp.sum(choose * factor[None, :], 1)
    own_weight = lax.dynamic_index_in_dim(seq_weight, side, 0, False)
    own_start = lax.dynamic_index_in_dim(type_counts[:, 0], side, 0, False)
    steps = jnp.arange(rows, dtype=jnp.int32)
    query_pos = jnp.concatenate([low * rows + steps, (3 - low) * rows + steps])
    scale = jnp.where(query_pos >= own_start, own_weight, 0.0)
    upstream = cotangent.astype(F32) * scale[:, None]

    outputs = return_slot(stream)
    chips = exchange.chips
    sums = jnp.zeros((8, width), F32)
    mlp, branch = [None] * LAYERS, [None] * LAYERS
    for layer in reversed(range(LAYERS)):
        (stream, hidden, queries, own, other, logs, attended, middle, normed, active, slope,
         hidden_x, attended_x, normed_x, active_x) = kept[layer]
        last = layer == LAYERS - 1
        if not last:
            upstream = together(upstream, mlp[layer + 1], branch[layer + 1])
        (back_up, back_up_send, back_out, back_out_send, back_middle, back_branch, branch_send,
         back_attended, sums) = feed_back(
            layer, meta, upstream, slope, proj_up, proj_down, middle, gain_two, proj_out, sums
        )
        back_up_x, back_out_x, branch_x = (
            exchange.swap_core(v) for v in (back_up_send, back_out_send, branch_send)
        )
        if last:
            back_up, attended_x, normed_x, active_x = order(back_up, attended_x, normed_x, active_x)
        else:
            mlp[layer + 1].steps(1)
            branch[layer + 1].steps(1)
            back_up = together(back_up, mlp[layer + 1], branch[layer + 1])
        keep, send = mlp_gradients(
            meta, chips, normed, normed_x, back_up, back_up_x, active, active_x, back_out, back_out_x,
            attended, attended_x, back_branch, branch_x,
        )
        mlp[layer] = Reduction(exchange, keep, send)
        waiting = [mlp[layer]]
        if not last:
            mlp[layer + 1].steps(1)
            branch[layer + 1].steps(1)
            waiting += [mlp[layer + 1], branch[layer + 1]]
        back_attended = together(back_attended, *waiting)
        back_q, back_own, back_other = attention_backward(
            flag, queries, own, other, back_attended, attended, logs
        )
        back_got = exchange.swap_core(back_other)
        mlp[layer].steps(1)
        waiting = [mlp[layer]]
        if not last:
            branch[layer + 1].steps(1)
            waiting += [branch[layer + 1]]
        back_q = together(back_q, *waiting)
        kind = BF16 if layer == 0 else F32
        mine, theirs, upstream, sums = project_back(
            layer, meta, back_q, back_own, back_got, proj_qkv, stream, gain_one, back_middle, sums, kind
        )
        keep, send = qkv_gradients(meta, chips, hidden, hidden_x, mine, exchange.swap_core(theirs), sums)
        branch[layer] = Reduction(exchange, keep, send)
        mlp[layer].steps(1)
    upstream = together(upstream, branch[0], mlp[0])
    branch[0].steps(1)
    upstream = together(upstream, branch[0])
    branch[0].steps(1)
    mlp[0].steps(1)
    upstream = together(upstream, branch[0], mlp[0])
    branch[0].steps(1)
    upstream = together(upstream, branch[0])
    back_inputs = return_slot(upstream).astype(F32)
    mlp = [reduction.finish() for reduction in mlp]
    branch = [reduction.finish() for reduction in branch]
    ups, downs, outs = zip(*(unpack_mlp(share, core, exchange) for share in mlp))
    qkvs, tables = zip(*(unpack_qkv(share, core, exchange) for share in branch))
    table = tables[0].T.reshape(LAYERS, 4, width // chips // 2)
    return (
        outputs, back_inputs, table[:, 0], table[:, 1], jnp.stack(qkvs), jnp.stack(outs),
        table[:, 2], table[:, 3], jnp.stack(ups), jnp.stack(downs),
    )


def solution(mesh):
    tokens = P("dp", "seq", None)
    shared = P(None, AXES)
    in_specs = (tokens, tokens, P("dp"), P("dp", None)) + (P(),) * 8
    out_specs = (
        tokens, tokens, shared, shared, P(None, AXES, None), P(None, AXES, None),
        shared, shared, P(None, AXES, None), P(None, AXES, None),
    )
    return jax.shard_map(
        per_device, mesh=mesh, in_specs=in_specs, out_specs=out_specs, check_vma=False
    )
```

```python
import functools
import math

import jax
import jax.numpy as jnp
import numpy as np
from jax import lax
from jax.experimental import pallas as pl
from jax.experimental.pallas import tpu as pltpu
from jax.sharding import PartitionSpec as P

HEADS = 12
HEAD_DIM = 64
LAYERS = 2
TASKS = 3
AXES = ("dp", "seq")
F32 = jnp.float32
BF16 = jnp.bfloat16
epsilon = 1e-05
VMEM_BYTES = 32 * 1024 * 1024
SMALL_COST = pl.CostEstimate(flops=1000, bytes_accessed=1000, transcendentals=0)


def in_hbm(*values):
    return tuple(pltpu.with_memory_space_constraint(v, pltpu.HBM) for v in values)


def dot_nn(a, b):
    return lax.dot_general(a, b, (((1,), (0,)), ((), ())), preferred_element_type=F32)


def dot_nt(a, b):
    return lax.dot_general(a, b, (((1,), (1,)), ((), ())), preferred_element_type=F32)


def dot_tn(a, b):
    return lax.dot_general(a, b, (((0,), (0,)), ((), ())), preferred_element_type=F32)


def gelu_and_slope(x):
    z = jnp.abs(x) * 0.7071067811865476
    d = 1.0 + 0.3275911 * z
    t = pl.reciprocal(d, approx=True)
    t = t * (2.0 - d * t)
    poly = t * (
        0.254829592
        + t * (-0.284496736 + t * (1.421413741 + t * (-1.453152027 + t * 1.061405429)))
    )
    bell = jnp.exp(-0.5 * x * x)
    tail = 0.5 * poly * bell
    below = jnp.where(x >= 0.0, 1.0 - tail, tail)
    return x * below, below + x * bell * 0.3989422804014327


def pair_lists(variant):
    if variant == 0:
        return [[(0, 0, True)], [(0, 0, False), (1, 0, False), (1, 1, False), (0, 1, True)]]
    return [[(1, 0, False), (0, 0, True)], [(0, 0, False), (1, 0, False), (0, 1, True)]]


def head_masks(scale):
    lane = lax.broadcasted_iota(jnp.int32, (1, 2 * HEAD_DIM), 1)
    first = jnp.where(lane < HEAD_DIM, scale, 0.0)
    return first.astype(BF16), (scale - first).astype(BF16)


def attention_forward_kernel(meta, q_ref, ko_ref, vo_ref, kx_ref, vx_ref, out_ref, lse_ref):
    rows = q_ref.shape[0] // 2
    masks = head_masks(1.0 / math.sqrt(HEAD_DIM))
    keys = (ko_ref, kx_ref)
    values = (vo_ref, vx_ref)

    def run(variant):
        below = lax.broadcasted_iota(jnp.int32, (rows, rows), 1) <= lax.broadcasted_iota(
            jnp.int32, (rows, rows), 0
        )
        lane = lax.broadcasted_iota(jnp.int32, (rows, 2 * HEAD_DIM), 1)
        for block, pairs in enumerate(pair_lists(variant)):
            span = pl.ds(block * rows, rows)
            q = q_ref[span, :]
            results, logs = [], []
            for head in range(2):
                qm = q * masks[head]
                scores = []
                for source, kblock, diagonal in pairs:
                    part = dot_nt(qm, keys[source][pl.ds(kblock * rows, rows), :])
                    scores.append(jnp.where(below, part, -1e30) if diagonal else part)
                peak = functools.reduce(jnp.maximum, scores)
                peak = jnp.max(peak, -1, keepdims=True)
                total, acc = None, None
                for part, (source, kblock, diagonal) in zip(scores, pairs):
                    raised = jnp.exp(part - peak)
                    total = raised if total is None else total + raised
                    term = dot_nn(raised.astype(BF16), values[source][pl.ds(kblock * rows, rows), :])
                    acc = term if acc is None else acc + term
                total = jnp.sum(total, -1, keepdims=True)
                results.append(acc / total)
                logs.append(peak + jnp.log(total))
            out_ref[span, :] = jnp.where(lane < HEAD_DIM, results[0], results[1]).astype(BF16)
            packed = jnp.where(lane == 0, logs[0], logs[1])
            lse_ref[0, :, span] = packed.T[:8, :]

    @pl.when(meta[0] == 0)
    def _():
        run(0)

    @pl.when(meta[0] == 1)
    def _():
        run(1)


def attention_forward(meta, queries, own, other):
    tokens = queries.shape[0]
    pairs = HEADS // 2
    wide = 2 * HEAD_DIM

    def at(offset):
        return pl.BlockSpec((tokens, wide), lambda g, m: (0, offset + g))

    return pl.pallas_call(
        attention_forward_kernel,
        grid_spec=pltpu.PrefetchScalarGridSpec(
            num_scalar_prefetch=1,
            grid=(pairs,),
            in_specs=[at(0), at(0), at(pairs), at(0), at(pairs)],
            out_specs=[at(0), pl.BlockSpec((1, 8, tokens), lambda g, m: (g, 0, 0))],
        ),
        out_shape=[
            pltpu.HBM((tokens, HEADS * HEAD_DIM), BF16),
            pltpu.HBM((pairs, 8, tokens), F32),
        ],
        compiler_params=pltpu.CompilerParams(vmem_limit_bytes=VMEM_BYTES),
        cost_estimate=SMALL_COST,
        name="attention_forward",
    )(meta, *in_hbm(queries, own, own, other, other))


def attention_backward_kernel(
    meta, q_ref, ko_ref, vo_ref, kx_ref, vx_ref, do_ref, o_ref, lse_ref,
    dq_ref, own_ref, other_ref,
):
    rows = q_ref.shape[0] // 2
    scale = 1.0 / math.sqrt(HEAD_DIM)
    scaled = head_masks(scale)
    plain = head_masks(1.0)
    keys = (ko_ref, kx_ref)
    values = (vo_ref, vx_ref)
    grads = (own_ref, other_ref)
    product = (do_ref[...].astype(F32) * o_ref[...].astype(F32)).T
    dots = (
        jnp.sum(product[:HEAD_DIM], 0, keepdims=True),
        jnp.sum(product[HEAD_DIM:], 0, keepdims=True),
    )
    logs = lse_ref[0]

    def run(variant):
        below = lax.broadcasted_iota(jnp.int32, (rows, rows), 0) <= lax.broadcasted_iota(
            jnp.int32, (rows, rows), 1
        )
        dk_acc, dv_acc = {}, {}
        for block, pairs in enumerate(pair_lists(variant)):
            span = slice(block * rows, (block + 1) * rows)
            q, do = q_ref[span, :], do_ref[span, :]
            dq = None
            for head in range(2):
                qm, dom = q * scaled[head], do * plain[head]
                log_row = logs[head : head + 1, span]
                dot_row = dots[head][:, span]
                for source, kblock, diagonal in pairs:
                    where = pl.ds(kblock * rows, rows)
                    k, v = keys[source][where, :], values[source][where, :]
                    raised = jnp.exp(dot_nt(k, qm) - log_row)
                    if diagonal:
                        raised = jnp.where(below, raised, 0.0)
                    slope = (raised * (dot_nt(v, dom) - dot_row)).astype(BF16)
                    term_v = dot_nn(raised.astype(BF16), dom)
                    term_k = dot_nn(slope, qm)
                    term_q = dot_tn(slope, k * scaled[head])
                    slot = (source, kblock)
                    dv_acc[slot] = dv_acc[slot] + term_v if slot in dv_acc else term_v
                    dk_acc[slot] = dk_acc[slot] + term_k if slot in dk_acc else term_k
                    dq = term_q if dq is None else dq + term_q
            dq_ref[span, :] = dq.astype(BF16)
        for source in range(2):
            for kblock in range(2):
                span = slice(kblock * rows, (kblock + 1) * rows)
                slot = (source, kblock)
                for which, acc in enumerate((dk_acc, dv_acc)):
                    value = acc[slot] if slot in acc else jnp.zeros((rows, 2 * HEAD_DIM), F32)
                    grads[source][which, span, :] = value.astype(grads[source].dtype)

    @pl.when(meta[0] == 0)
    def _():
        run(0)

    @pl.when(meta[0] == 1)
    def _():
        run(1)


def attention_backward(meta, queries, own, other, back_attended, attended, logs):
    tokens = queries.shape[0]
    pairs = HEADS // 2
    wide = 2 * HEAD_DIM
    width = HEADS * HEAD_DIM

    def at(offset):
        return pl.BlockSpec((tokens, wide), lambda g, m: (0, offset + g))

    return pl.pallas_call(
        attention_backward_kernel,
        grid_spec=pltpu.PrefetchScalarGridSpec(
            num_scalar_prefetch=1,
            grid=(pairs,),
            in_specs=[at(0), at(0), at(pairs), at(0), at(pairs), at(0), at(0),
                      pl.BlockSpec((1, 8, tokens), lambda g, m: (g, 0, 0))],
            out_specs=[at(0)] + [pl.BlockSpec((2, tokens, wide), lambda g, m: (0, 0, g))] * 2,
        ),
        out_shape=[
            jax.ShapeDtypeStruct((tokens, width), BF16),
            pltpu.HBM((2, tokens, width), F32),
            jax.ShapeDtypeStruct((2, tokens, width), BF16),
        ],
        compiler_params=pltpu.CompilerParams(vmem_limit_bytes=VMEM_BYTES),
        cost_estimate=SMALL_COST,
        name="attention_backward",
    )(meta, *in_hbm(queries, own, own, other, other, back_attended, attended, logs))


def normalised(rows_in):
    average = jnp.mean(rows_in, -1, keepdims=True)
    centred = rows_in - average
    inverse = lax.rsqrt(jnp.mean(centred * centred, -1, keepdims=True) + epsilon)
    return centred * inverse, inverse


def norm_back(rows_in, gain_row, back):
    unit, inverse = normalised(rows_in)
    slope = back * gain_row
    first = jnp.mean(slope, -1, keepdims=True)
    second = jnp.mean(slope * unit, -1, keepdims=True)
    return inverse * (slope - first - unit * second), (
        jnp.sum(back * unit, 0, keepdims=True), jnp.sum(back, 0, keepdims=True))


def with_rows(table, row, sums):
    index = lax.broadcasted_iota(jnp.int32, table.shape, 0)
    return jnp.where(index == row, sums[0], jnp.where(index == row + 1, sums[1], table))


def project_kernel(layer, stream, gain, shift, matrix, hidden, queries, pairs):
    step = pl.program_id(0)

    @pl.when(step == 0)
    def _():
        unit, unused = normalised(stream[...].astype(F32))
        hidden[...] = (unit * gain[layer : layer + 1] + shift[layer : layer + 1]).astype(BF16)

    out = dot_nn(hidden[...], matrix[0]).astype(BF16)

    @pl.when(step < 2)
    def _():
        pairs[...] = out

    @pl.when(step == 2)
    def _():
        queries[...] = out


def project(layer, stream, gain, shift, matrix):
    tokens, width = stream.shape
    whole = pl.BlockSpec((tokens, width), lambda j: (0, 0))
    row = pl.BlockSpec(gain.shape, lambda j: (0, 0))
    return pl.pallas_call(
        functools.partial(project_kernel, layer),
        grid=(3,),
        in_specs=[whole, row, row, pl.BlockSpec((1, width, width), lambda j: (layer, 0, (j + 1) % 3))],
        out_specs=[whole, whole, pl.BlockSpec((tokens, width), lambda j: (0, jnp.minimum(j, 1)))],
        out_shape=[
            pltpu.HBM((tokens, width), BF16),
            pltpu.HBM((tokens, width), BF16),
            pltpu.HBM((tokens, 2 * width), BF16),
        ],
        compiler_params=pltpu.CompilerParams(vmem_limit_bytes=VMEM_BYTES),
        cost_estimate=SMALL_COST,
        name="project",
    )(*in_hbm(stream), gain, shift, *in_hbm(matrix))


def feed_forward_kernel(
    layer, steps, attended, stream, matrix_out, gain, shift, up, down,
    middle, normed, active_ref, slope_ref, out, acc,
):
    step = pl.program_id(0)

    @pl.when(step == 0)
    def _():
        middle[...] = stream[...].astype(F32) + dot_nn(attended[...], matrix_out[0])
        acc[...] = middle[...]
        unit, unused = normalised(middle[...])
        normed[...] = (unit * gain[layer : layer + 1] + shift[layer : layer + 1]).astype(BF16)

    groups = 4
    rows = normed.shape[0] // groups
    raw = {}
    for group in range(groups + 1):
        if group < groups:
            raw[group] = dot_nn(normed[group * rows : (group + 1) * rows, :], up[0])
        if group > 0:
            span = slice((group - 1) * rows, group * rows)
            active, slope = gelu_and_slope(raw.pop(group - 1))
            active = active.astype(BF16)
            active_ref[span, :] = active
            slope_ref[span, :] = slope.astype(BF16)
            acc[span, :] += dot_nn(active, down[0])

    @pl.when(step == steps - 1)
    def _():
        out[...] = acc[...].astype(out.dtype)


def feed_forward(layer, attended, stream, matrix_out, gain, shift, up, down, kind):
    tokens, width = stream.shape
    hidden = up.shape[2]
    tile = 1024
    steps = hidden // tile
    whole = pl.BlockSpec((tokens, width), lambda j: (0, 0))
    row = pl.BlockSpec(gain.shape, lambda j: (0, 0))
    part = pl.BlockSpec((tokens, tile), lambda j: (0, j))
    return pl.pallas_call(
        functools.partial(feed_forward_kernel, layer, steps),
        grid=(steps,),
        in_specs=[
            whole, whole, pl.BlockSpec((1, width, width), lambda j: (layer, 0, 0)), row, row,
            pl.BlockSpec((1, width, tile), lambda j: (layer, 0, j)),
            pl.BlockSpec((1, tile, width), lambda j: (layer, j, 0)),
        ],
        out_specs=[whole, whole, part, part, whole],
        out_shape=[
            pltpu.HBM((tokens, width), F32),
            pltpu.HBM((tokens, width), BF16),
            pltpu.HBM((tokens, hidden), BF16),
            pltpu.HBM((tokens, hidden), BF16),
            pltpu.HBM((tokens, width), kind),
        ],
        scratch_shapes=[pltpu.VMEM((tokens, width), F32)],
        compiler_params=pltpu.CompilerParams(vmem_limit_bytes=VMEM_BYTES),
        cost_estimate=SMALL_COST,
        name="feed_forward",
    )(*in_hbm(attended, stream, matrix_out), gain, shift, *in_hbm(up, down))


def feed_back_kernel(
    layer, steps, meta, upstream, back_out, slope, up, down, middle, gain, matrix_out, sums_in,
    own, send, back_middle, back_branch, branch_send, back_attended, grads, acc,
):
    step = pl.program_id(0)
    half = branch_send.shape[1]
    theirs = pl.ds(pl.multiple_of((1 - meta[1]) * half, 128), half)

    @pl.when(step == 0)
    def _():
        acc[...] = jnp.zeros_like(acc)

    back_up = (dot_nt(back_out[...], down[0]) * slope[...].astype(F32)).astype(BF16)

    @pl.when(step < steps // 2)
    def _():
        send[...] = back_up

    @pl.when(step >= steps // 2)
    def _():
        own[...] = back_up

    acc[...] += dot_nt(back_up, up[0])

    @pl.when(step == steps - 1)
    def _():
        back, sums = norm_back(middle[...], gain[layer : layer + 1], acc[...])
        back = back + upstream[...]
        grads[...] = with_rows(sums_in[...], 4 * layer + 2, sums)
        back_middle[...] = back
        back_branch[...] = back.astype(BF16)
        branch_send[...] = back_branch[:, theirs]
        back_attended[...] = dot_nt(back_branch[...], matrix_out[0]).astype(BF16)


def feed_back(layer, meta, upstream, back_out, slope, up, down, middle, gain, matrix_out, sums):
    tokens, width = upstream.shape
    hidden = up.shape[2]
    tile = 512
    steps = hidden // tile
    half = steps // 2

    def place(j, m):
        return jnp.where(j < half, (1 - m[1]) * half + j, m[1] * half + j - half)

    whole = pl.BlockSpec((tokens, width), lambda j, m: (0, 0))
    narrow = pl.BlockSpec((tokens, width // 2), lambda j, m: (0, 0))
    wide = jax.ShapeDtypeStruct((tokens, width), BF16)
    return pl.pallas_call(
        functools.partial(feed_back_kernel, layer, steps),
        grid_spec=pltpu.PrefetchScalarGridSpec(
            num_scalar_prefetch=1,
            grid=(steps,),
            in_specs=[
                whole, whole, pl.BlockSpec((tokens, tile), lambda j, m: (0, place(j, m))),
                pl.BlockSpec((1, width, tile), lambda j, m: (layer, 0, place(j, m))),
                pl.BlockSpec((1, tile, width), lambda j, m: (layer, place(j, m), 0)),
                whole, pl.BlockSpec(gain.shape, lambda j, m: (0, 0)),
                pl.BlockSpec((1, width, width), lambda j, m: (layer, 0, 0)),
                pl.BlockSpec((8, width), lambda j, m: (0, 0)),
            ],
            out_specs=[
                pl.BlockSpec((tokens, tile), lambda j, m: (0, jnp.maximum(j - half, 0))),
                pl.BlockSpec((tokens, tile), lambda j, m: (0, jnp.minimum(j, half - 1))),
                whole, whole, narrow, whole,
                pl.BlockSpec((8, width), lambda j, m: (0, 0)),
            ],
            scratch_shapes=[pltpu.VMEM((tokens, width), F32)],
        ),
        out_shape=[
            jax.ShapeDtypeStruct((tokens, hidden // 2), BF16),
            jax.ShapeDtypeStruct((tokens, hidden // 2), BF16),
            pltpu.HBM((tokens, width), F32),
            wide, jax.ShapeDtypeStruct((tokens, width // 2), BF16),
            wide, jax.ShapeDtypeStruct((8, width), F32),
        ],
        compiler_params=pltpu.CompilerParams(vmem_limit_bytes=VMEM_BYTES),
        cost_estimate=SMALL_COST,
        name="feed_back",
    )(meta, *in_hbm(upstream), back_out, *in_hbm(slope, up, down, middle), gain, *in_hbm(matrix_out), sums)


def project_back_kernel(
    layer, meta, back_q, own, got, matrix, stream, gain, back_middle, sums_in,
    mine, theirs, upstream, back_out, back_out_send, grads, table, acc,
):
    step = pl.program_id(0)
    width = back_q.shape[1]

    @pl.when(step == 0)
    def _():
        table[0] = back_q[...]
        for which in range(2):
            table[1 + which] = (own[which] + got[which].astype(F32)).astype(BF16)
        half = width // 2

        @pl.when(meta[1] == 0)
        def _():
            mine[:, :width] = table[0]
            mine[:, width:] = table[1, :, :half]
            theirs[:, :half] = table[1, :, half:]
            theirs[:, half:] = table[2]

        @pl.when(meta[1] == 1)
        def _():
            theirs[:, :width] = table[0]
            theirs[:, width:] = table[1, :, :half]
            mine[:, :half] = table[1, :, half:]
            mine[:, half:] = table[2]

        acc[...] = jnp.zeros_like(acc)

    acc[...] += dot_nt(table[step], matrix[0])

    @pl.when(step == 2)
    def _():
        back, sums = norm_back(stream[...].astype(F32), gain[layer : layer + 1], acc[...])
        back = back + back_middle[...]
        upstream[...] = back.astype(upstream.dtype)
        back_out[...] = back.astype(BF16)
        half = width // 2
        back_out_send[...] = back_out[:, pl.ds(pl.multiple_of((1 - meta[1]) * half, 128), half)]
        grads[...] = with_rows(sums_in[...], 4 * layer, sums)


def project_back(layer, meta, back_q, own, got, matrix, stream, gain, back_middle, sums, kind):
    tokens, width = stream.shape
    whole = pl.BlockSpec((tokens, width), lambda j, m: (0, 0))
    both = pl.BlockSpec((2, tokens, width), lambda j, m: (0, 0, 0))
    side = pl.BlockSpec((tokens, 3 * width // 2), lambda j, m: (0, 0))
    return pl.pallas_call(
        functools.partial(project_back_kernel, layer),
        grid_spec=pltpu.PrefetchScalarGridSpec(
            num_scalar_prefetch=1,
            grid=(3,),
            in_specs=[
                whole, both, both, pl.BlockSpec((1, width, width), lambda j, m: (layer, 0, j)),
                whole, pl.BlockSpec(gain.shape, lambda j, m: (0, 0)), whole,
                pl.BlockSpec((8, width), lambda j, m: (0, 0)),
            ],
            out_specs=[side, side, whole, whole, pl.BlockSpec((tokens, width // 2), lambda j, m: (0, 0)),
                       pl.BlockSpec((8, width), lambda j, m: (0, 0))],
            scratch_shapes=[pltpu.VMEM((3, tokens, width), BF16), pltpu.VMEM((tokens, width), F32)],
        ),
        out_shape=[
            jax.ShapeDtypeStruct((tokens, 3 * width // 2), BF16),
            jax.ShapeDtypeStruct((tokens, 3 * width // 2), BF16),
            pltpu.HBM((tokens, width), kind),
            jax.ShapeDtypeStruct((tokens, width), BF16),
            jax.ShapeDtypeStruct((tokens, width // 2), BF16),
            jax.ShapeDtypeStruct((8, width), F32),
        ],
        compiler_params=pltpu.CompilerParams(vmem_limit_bytes=VMEM_BYTES),
        cost_estimate=SMALL_COST,
        name="project_back",
    )(meta, *in_hbm(back_q, own), got, matrix, *in_hbm(stream), gain, *in_hbm(back_middle), sums)


def store_chunks(chips, meta, acc, keep, send):
    rows = acc.shape[0] // chips
    for position in range(chips):
        chunk = acc[pl.ds(pl.multiple_of(meta[2 + position] * rows, 16), rows), :]
        if position < chips // 2:
            keep[position] = chunk
        else:
            send[position - chips // 2] = chunk


def grad_up_kernel(chips, meta, ao, ax, bo, bx, co, cx, do, dx, *refs):
    keep, send, acc = refs[-3:]
    step = pl.program_id(0)

    @pl.when(step < 4)
    def _():
        acc[...] = (dot_tn(ao[...], bo[...]) + dot_tn(ax[...], bx[...])).astype(BF16)

    @pl.when(step == 4)
    def _():
        acc[...] = (dot_tn(co[...], do[...]) + dot_tn(cx[...], dx[...])).astype(BF16)

    store_chunks(chips, meta, acc, keep, send)


def grad_down_kernel(chips, meta, ao, ax, bo, bx, *refs):
    keep, send = refs[-2:]
    rows = keep.shape[1]
    each = ao.shape[1] // rows
    total = (dot_tn(ao[...], bo[...]) + dot_tn(ax[...], bx[...])).astype(BF16)
    for local in range(each):
        position = meta[2 + chips + pl.program_id(0) * each + local]
        chunk = total[local * rows : (local + 1) * rows]

        @pl.when(position < chips // 2)
        def _():
            keep[position] = chunk

        @pl.when(position >= chips // 2)
        def _():
            send[position - chips // 2] = chunk


def grad_qkv_kernel(chips, meta, ao, ax, bo, bx, sums, keep, send, acc, columns):
    wide = bo.shape[1]
    acc[:, :wide] = (dot_tn(ao[...], bo[...]) + dot_tn(ax[...], bx[...])).astype(BF16)
    columns[...] = jnp.concatenate([sums[...], jnp.zeros((120, sums.shape[1]), F32)], 0).T
    acc[:, wide:] = columns[...].astype(BF16)
    store_chunks(chips, meta, acc, keep, send)


def ordered(total, ids, chips):
    split = total.astype(BF16).reshape(chips, total.shape[0] // chips, total.shape[1])
    return jnp.take(split, ids, axis=0)


def gradient_call(kernel, name, chips, grid, in_specs, out_spec, shape, scratch):
    return pl.pallas_call(
        functools.partial(kernel, chips),
        grid_spec=pltpu.PrefetchScalarGridSpec(
            num_scalar_prefetch=1, grid=(grid,), in_specs=in_specs, out_specs=[out_spec] * 2,
            scratch_shapes=scratch,
        ),
        out_shape=[pltpu.HBM(shape, BF16)] * 2,
        compiler_params=pltpu.CompilerParams(vmem_limit_bytes=VMEM_BYTES),
        cost_estimate=SMALL_COST,
        name=name,
    )


def up_gradients(
    meta, chips, normed, normed_x, back_up, back_up_x, attended, attended_x, back_branch, branch_x
):
    tokens, width = normed.shape
    half = width // 2
    rows = width // chips
    if rows % 16 != 0:
        ids = meta[2 : 2 + chips]
        up = dot_tn(normed, back_up) + dot_tn(normed_x, back_up_x)
        own = lax.dynamic_slice_in_dim(back_branch, meta[1] * half, half, 1)
        out = dot_tn(attended, own) + dot_tn(attended_x, branch_x)
        up = ordered(up, ids, chips).reshape(chips, rows, 4, half)
        up = up.transpose(0, 2, 1, 3).reshape(chips, 4 * rows, half)
        both = jnp.concatenate([up, ordered(out, ids, chips)], 1)
        return both[: chips // 2], both[chips // 2 :]
    whole = pl.BlockSpec((tokens, width), lambda j, m: (0, 0))
    fixed = pl.BlockSpec((tokens, half), lambda j, m: (0, 0))
    mine = pl.BlockSpec((tokens, half), lambda j, m: (0, m[1]))
    tile = pl.BlockSpec((tokens, half), lambda j, m: (0, jnp.minimum(j, 3)))
    return gradient_call(
        grad_up_kernel, "gradient_up", chips, 5, [whole, whole, tile, tile, whole, whole, mine, fixed],
        pl.BlockSpec((chips // 2, rows, half), lambda j, m: (0, j, 0)),
        (chips // 2, 5 * rows, half), [pltpu.VMEM((width, half), BF16)],
    )(meta, *in_hbm(normed, normed_x), back_up, back_up_x, *in_hbm(attended, attended_x), back_branch, branch_x)


def down_gradients(meta, chips, active, active_x, back_out, back_out_x):
    tokens, hidden = active.shape
    width = back_out.shape[1]
    half = width // 2
    rows = hidden // chips
    if rows % 64 != 0:
        own = lax.dynamic_slice_in_dim(back_out, meta[1] * half, half, 1)
        down = dot_tn(active, own) + dot_tn(active_x, back_out_x)
        down = ordered(down, meta[2 : 2 + chips], chips)
        return down[: chips // 2], down[chips // 2 :]
    fixed = pl.BlockSpec((tokens, half), lambda j, m: (0, 0))
    mine = pl.BlockSpec((tokens, half), lambda j, m: (0, m[1]))
    tile = pl.BlockSpec((tokens, width), lambda j, m: (0, j))
    return gradient_call(
        grad_down_kernel, "gradient_down", chips, hidden // width, [tile, tile, mine, fixed],
        pl.BlockSpec((chips // 2, rows, half), lambda j, m: (0, 0, 0)), (chips // 2, rows, half), [],
    )(meta, *in_hbm(active, active_x), back_out, back_out_x)


def qkv_gradients(meta, chips, hidden, hidden_x, back_projected, back_projected_x, sums):
    tokens, width = hidden.shape
    wide = back_projected.shape[1]
    rows = width // chips
    if rows % 16 != 0:
        qkv = dot_tn(hidden, back_projected) + dot_tn(hidden_x, back_projected_x)
        table = jnp.pad(sums.T, ((0, 0), (0, 120)))
        both = ordered(jnp.concatenate([qkv, table], -1), meta[2 : 2 + chips], chips)
        return both[: chips // 2], both[chips // 2 :]
    specs = [pl.BlockSpec((tokens, width), lambda j, m: (0, 0))] * 2
    specs += [pl.BlockSpec((tokens, wide), lambda j, m: (0, 0))] * 2
    specs += [pl.BlockSpec((8, width), lambda j, m: (0, 0))]
    return gradient_call(
        grad_qkv_kernel, "gradient_qkv", chips, 1, specs,
        pl.BlockSpec((chips // 2, rows, wide + 128), lambda j, m: (0, 0, 0)),
        (chips // 2, rows, wide + 128),
        [pltpu.VMEM((width, wide + 128), BF16), pltpu.VMEM((width, 128), F32)],
    )(meta, *in_hbm(hidden, hidden_x), back_projected, back_projected_x, sums)


class Exchange:
    def __init__(self, dp):
        self.dp = dp
        self.chips = 2 * dp
        self.bits = int(math.log2(self.chips))
        self.core_pairs = [(s, s ^ 1) for s in range(4)]
        self.mirror_pairs = [(s, 3 - s) for s in range(4)]
        rest = list(range(2, self.bits))
        self.orders = ([1, 0] + rest, [0, 1] + rest[::-1])

    def swap_core(self, value):
        return lax.ppermute(value, "seq", self.core_pairs)

    def mirror(self, value):
        return lax.ppermute(value, "seq", self.mirror_pairs)

    def pairs(self, phase):
        result = []
        for device in range(2 * self.chips):
            chip = (device // 4) * 2 + (device % 4) // 2
            core = device % 2
            other = chip ^ (1 << self.orders[core][phase])
            result.append((device, (other // 2) * 4 + (other % 2) * 2 + core))
        return result

    def tables(self, chip, core):
        index = np.arange(self.chips)
        maps, inverses = [], []
        for order in self.orders:
            value = np.zeros_like(index)
            for phase, bit in enumerate(order):
                value |= ((index >> (self.bits - 1 - phase)) & 1) << bit
            inverse = np.zeros_like(index)
            inverse[value] = index
            maps.append(value.astype(np.int32))
            inverses.append(order)
        ids = chip ^ jnp.where(core == 0, jnp.asarray(maps[0]), jnp.asarray(maps[1]))
        relative = jnp.asarray(index.astype(np.int32)) ^ chip
        places = []
        for order in self.orders:
            place = jnp.zeros_like(relative)
            for phase, bit in enumerate(order):
                place = place | (((relative >> bit) & 1) << (self.bits - 1 - phase))
            places.append(place)
        return ids.astype(jnp.int32), jnp.where(core == 0, places[0], places[1]).astype(jnp.int32)


class Reduction:
    def __init__(self, exchange, keep, send):
        self.exchange, self.parts, self.send, self.phase = exchange, [keep], send, 0

    def step(self):
        kind = self.send.dtype
        self.parts.append(lax.ppermute(self.send, AXES, self.exchange.pairs(self.phase)))
        size = self.parts[-1].shape[0]
        self.phase += 1
        if self.phase < self.exchange.bits:
            terms = [part[size // 2 : size].astype(F32) for part in self.parts]
            self.send = functools.reduce(jnp.add, terms).astype(kind)
        else:
            self.send = functools.reduce(jnp.add, [part[0].astype(F32) for part in self.parts])

    def finish(self):
        while self.phase < self.exchange.bits:
            self.step()
        return self.send


class Move:
    def __init__(self, transfer, value):
        self.transfer, self.send = transfer, value

    def step(self):
        self.send = self.transfer(self.send)


def order(first, *others):
    return lax.optimization_barrier((first,) + others)


def host(run, inputs, *moves):
    tied = lax.optimization_barrier(tuple(inputs) + tuple(move.send for move in moves))
    for move, message in zip(moves, tied[len(inputs) :]):
        move.send = message
    results = tuple(run(*tied[: len(inputs)]))
    for move in moves:
        move.step()
    tied = lax.optimization_barrier(results + tuple(move.send for move in moves))
    for move, message in zip(moves, tied[len(results) :]):
        move.send = message
    return tied[: len(results)]


def by_core(core, mine, theirs, axis):
    return jnp.where(
        core == 0,
        jnp.concatenate([mine, theirs], axis),
        jnp.concatenate([theirs, mine], axis),
    )


def unpack_mlp(share, rows, core, exchange):
    half, each = share.shape[1], rows // 2
    down = share[: 4 * rows].reshape(2, 4 * each, half)
    rest = share[4 * rows :].reshape(share.shape[0] // rows - 4, 2, each, half)

    def pick(which):
        return jnp.concatenate(
            [lax.dynamic_index_in_dim(down, which, 0, False),
             lax.dynamic_index_in_dim(rest, which, 1, False).reshape(-1, half)], 0)

    mine, theirs = pick(core), exchange.swap_core(pick(1 - core))

    def widen(value, start, count):
        value = value[start * each : (start + count) * each].reshape(count, each, half)
        return value.transpose(1, 0, 2).reshape(each, count * half)

    def join(start, count):
        return by_core(core, widen(mine, start, count), widen(theirs, start, count), 1)

    grad_down = by_core(core, mine[: 4 * each], theirs[: 4 * each], 1)
    return grad_down, join(4, 4), join(8, 1)


def unpack_qkv(share, core, exchange):
    rows, wide = share.shape
    split = share.reshape(2, rows // 2, wide)
    mine = lax.dynamic_index_in_dim(split, core, 0, False)
    theirs = exchange.swap_core(lax.dynamic_index_in_dim(split, 1 - core, 0, False))
    wide -= 128
    table = mine[:, wide : wide + 8] + theirs[:, wide : wide + 8]
    return by_core(core, mine[:, :wide], theirs[:, :wide], 1), table


def per_device(
    inputs, cotangent, task_table, type_counts,
    gain_one, bias_one, proj_qkv, proj_out, gain_two, bias_two, proj_up, proj_down,
):
    slots, rows, width = inputs.shape
    length = rows * lax.axis_size("seq")
    exchange = Exchange(lax.axis_size("dp"))
    place = lax.axis_index("seq")
    side, core = place // 2, place % 2
    chip = lax.axis_index("dp") * 2 + side
    low = jnp.minimum(place, 3 - place)
    own_first = place < 2
    ids, places = exchange.tables(chip, core)
    flag = low.astype(jnp.int32).reshape(1)
    meta = jnp.concatenate([flag, core.astype(jnp.int32).reshape(1), ids, places])

    def gather_slot(value, got):
        own = lax.dynamic_index_in_dim(value, side, 0, False)
        return jnp.where(own_first, jnp.concatenate([own, got]), jnp.concatenate([got, own]))

    choose = (task_table[:, None] == jnp.arange(TASKS, dtype=jnp.int32)[None, :]).astype(F32)
    targets = (length - type_counts[:, 0]).astype(F32)
    totals = jnp.sum(choose * targets[:, None], 0)
    bits = int(math.log2(exchange.dp))

    for bit in range(bits):
        pairs = [(d, d ^ (1 << bit)) for d in range(exchange.dp)]
        totals = totals + lax.ppermute(totals, "dp", pairs)
    got = exchange.mirror(lax.dynamic_index_in_dim(inputs, 1 - side, 0, False))
    got, totals = order(got, totals)
    stream = gather_slot(inputs, got)
    factor = jnp.sum(totals) / TASKS / totals
    seq_weight = jnp.sum(choose * factor[None, :], 1)
    own_weight = lax.dynamic_index_in_dim(seq_weight, side, 0, False)
    own_start = lax.dynamic_index_in_dim(type_counts[:, 0], side, 0, False)
    steps = jnp.arange(rows, dtype=jnp.int32)
    query_pos = jnp.concatenate([low * rows + steps, (3 - low) * rows + steps])
    scale = jnp.where(query_pos >= own_start, own_weight, 0.0)
    chips = exchange.chips
    half = width // 2
    swap, mirror = exchange.swap_core, exchange.mirror

    def forward(layer, stream, moves_project, moves_attention, kind):
        hidden, queries, own = host(
            lambda v: project(layer, v, gain_one, bias_one, proj_qkv), (stream,), *moves_project
        )
        other = swap(own)
        hidden_x = Move(swap, hidden)
        attended, logs = host(
            lambda q, k, kx: attention_forward(flag, q, k, kx), (queries, own, other),
            hidden_x, *moves_attention
        )
        attended_x = Move(swap, attended)
        middle, normed, active, slope, output = host(
            lambda a, v: feed_forward(layer, a, v, proj_out, gain_two, bias_two, proj_up, proj_down, kind),
            (attended, stream), attended_x,
        )
        moves = Move(swap, normed), Move(swap, active)
        return output, moves, (stream, hidden, hidden_x, queries, own, other, logs, attended, attended_x, middle, normed, active, slope)

    def attention_step(layer, back_attended, moves):
        unused, unused, unused, queries, own, other, logs, attended, unused, unused, unused, unused, unused = kept[layer]
        back_q, back_own, back_other = host(
            lambda b: attention_backward(flag, queries, own, other, b, attended, logs), (back_attended,), *moves
        )
        return back_q, back_own, swap(back_other)

    def project_step(layer, back_q, back_own, back_got, back_middle, sums, moves):
        kind = BF16 if layer == 0 else F32
        return host(
            lambda q, k, kx: project_back(
                layer, meta, q, k, kx, proj_qkv, kept[layer][0], gain_one, back_middle, sums, kind
            ),
            (back_q, back_own, back_got), *moves
        )

    def feed_step(layer, upstream, back_out, sums, moves):
        middle, slope = kept[layer][9], kept[layer][12]
        return host(
            lambda u, b: feed_back(
                layer, meta, u, b, slope, proj_up, proj_down, middle, gain_two, proj_out, sums
            ),
            (upstream, back_out), *moves
        )

    def down_step(layer, back_out, back_out_x, active_x, moves):
        active = kept[layer][11]
        return Reduction(exchange, *host(
            lambda b, bx: down_gradients(meta, chips, active, active_x, b, bx), (back_out, back_out_x), *moves
        ))

    def up_step(layer, back_up, back_up_x, back_branch, branch_x, normed_x, moves):
        normed, attended, attended_x = kept[layer][10], kept[layer][7], kept[layer][8].send
        return Reduction(exchange, *host(
            lambda b, bx: up_gradients(
                meta, chips, normed, normed_x, b, bx, attended, attended_x, back_branch, branch_x
            ),
            (back_up, back_up_x), *moves
        ))

    def qkv_step(layer, mine, theirs_x, sums, moves):
        hidden, hidden_x = kept[layer][1], kept[layer][2].send
        return Reduction(exchange, *host(
            lambda b, bx: qkv_gradients(meta, chips, hidden, hidden_x, b, bx, sums), (mine, theirs_x), *moves
        ))

    got_cotangent = Move(mirror, lax.dynamic_index_in_dim(cotangent, 1 - side, 0, False))
    stream, moves, saved = forward(0, stream, (), (got_cotangent,), F32)
    kept = [saved]
    upstream = gather_slot(cotangent, got_cotangent.send).astype(F32) * scale[:, None]
    back_out = upstream.astype(BF16)
    back_out_x = Move(swap, lax.dynamic_slice_in_dim(back_out, (1 - core) * half, half, 1))
    stream, last_moves, saved = forward(1, stream, moves, (back_out_x,), BF16)
    normed_x, active_x = (move.send for move in moves)
    kept.append(saved)
    outputs_move = Move(mirror, jnp.where(own_first, stream[rows:], stream[:rows]))

    sums = jnp.zeros((8, width), F32)
    back_up, back_up_send, back_middle, back_branch, branch_send, back_attended, sums = feed_step(
        1, upstream, back_out, sums, last_moves + (outputs_move,)
    )
    last_normed_x, last_active_x = (move.send for move in last_moves)
    back_up_x, branch_x = Move(swap, back_up_send), Move(swap, branch_send)
    down1 = down_step(1, back_out, back_out_x.send, last_active_x, (back_up_x, branch_x))
    up1 = up_step(1, back_up, back_up_x.send, back_branch, branch_x.send, last_normed_x, (down1,))
    back_q, back_own, back_got = attention_step(1, back_attended, (up1, down1))
    mine, theirs, upstream, back_out, back_out_send, sums = project_step(
        1, back_q, back_own, back_got, back_middle, sums, (up1, down1)
    )
    theirs_x = Move(swap, theirs)
    down0 = down_step(0, back_out, swap(back_out_send), active_x, (theirs_x, up1, down1))
    back_up, back_up_send, back_middle, back_branch, branch_send, back_attended, sums0 = feed_step(
        0, upstream, back_out, sums, (down0, up1)
    )
    back_up_x, branch_x = Move(swap, back_up_send), Move(swap, branch_send)
    qkv1 = qkv_step(1, mine, theirs_x.send, sums, (back_up_x, branch_x, down0))
    up0 = up_step(0, back_up, back_up_x.send, back_branch, branch_x.send, normed_x, (qkv1,))
    back_q, back_own, back_got = attention_step(0, back_attended, (up0, qkv1, down0))
    mine, theirs, upstream, back_out, back_out_send, sums = project_step(
        0, back_q, back_own, back_got, back_middle, sums0, (up0, qkv1, down0)
    )
    back_move = Move(mirror, jnp.where(own_first, upstream[rows:], upstream[:rows]))
    qkv0 = qkv_step(0, mine, swap(theirs), sums, (up0, qkv1))
    down, up, qkv = (down0, down1), (up0, up1), (qkv0, qkv1)
    message = back_move.send
    for _ in range(2):
        qkv0.step()
        message, qkv0.send = order(message, qkv0.send)
    back_move.send = message
    back_move.step()

    def return_slot(value, got):
        own = jnp.where(own_first, value[:rows], value[rows:])
        return jnp.where(side == 0, jnp.stack([own, got]), jnp.stack([got, own]))

    outputs = return_slot(stream, outputs_move.send)
    back_inputs = return_slot(upstream, back_move.send).astype(F32)
    unit = width // chips
    shares = [jnp.concatenate([down[l].finish(), up[l].finish()], 0) for l in range(LAYERS)]
    downs, ups, outs = zip(*(unpack_mlp(share, unit, core, exchange) for share in shares))
    qkvs, tables = zip(*(unpack_qkv(one.finish(), core, exchange) for one in qkv))
    table = tables[0].T.reshape(LAYERS, 4, unit // 2)
    return (
        outputs, back_inputs, table[:, 0], table[:, 1], jnp.stack(qkvs), jnp.stack(outs),
        table[:, 2], table[:, 3], jnp.stack(ups), jnp.stack(downs),
    )


def solution(mesh):
    tokens = P("dp", "seq", None)
    shared = P(None, AXES)
    in_specs = (tokens, tokens, P("dp"), P("dp", None)) + (P(),) * 8
    out_specs = (
        tokens, tokens, shared, shared, P(None, AXES, None), P(None, AXES, None),
        shared, shared, P(None, AXES, None), P(None, AXES, None),
    )
    return jax.shard_map(
        per_device, mesh=mesh, in_specs=in_specs, out_specs=out_specs, check_vma=False
    )
```

```python
import functools
import math

import jax
import jax.numpy as jnp
import numpy as np
from jax import lax
from jax.experimental import pallas as pl
from jax.experimental.pallas import tpu as pltpu
from jax.sharding import PartitionSpec as P

HEADS = 12
HEAD_DIM = 64
LAYERS = 2
TASKS = 3
AXES = ("dp", "seq")
F32 = jnp.float32
BF16 = jnp.bfloat16
epsilon = 1e-05
PAIRS = 2
VMEM_BYTES = 32 * 1024 * 1024
SMALL_COST = pl.CostEstimate(flops=1000, bytes_accessed=1000, transcendentals=0)


def in_hbm(*values):
    return tuple(pltpu.with_memory_space_constraint(v, pltpu.HBM) for v in values)


def dot_nn(a, b):
    return lax.dot_general(a, b, (((1,), (0,)), ((), ())), preferred_element_type=F32)


def dot_nt(a, b):
    return lax.dot_general(a, b, (((1,), (1,)), ((), ())), preferred_element_type=F32)


def dot_tn(a, b):
    return lax.dot_general(a, b, (((0,), (0,)), ((), ())), preferred_element_type=F32)


def gelu_and_slope(x):
    z = jnp.abs(x) * 0.7071067811865476
    d = 1.0 + 0.3275911 * z
    t = pl.reciprocal(d, approx=True)
    t = t * (2.0 - d * t)
    poly = t * (
        0.254829592
        + t * (-0.284496736 + t * (1.421413741 + t * (-1.453152027 + t * 1.061405429)))
    )
    bell = jnp.exp(-0.5 * x * x)
    tail = 0.5 * poly * bell
    below = jnp.where(x >= 0.0, 1.0 - tail, tail)
    return x * below, below + x * bell * 0.3989422804014327


def head_masks(scale):
    lane = lax.broadcasted_iota(jnp.int32, (1, 2 * HEAD_DIM), 1)
    first = jnp.where(lane < HEAD_DIM, scale, 0.0)
    return first.astype(BF16), (scale - first).astype(BF16)


def stacked(value, masks):
    return jnp.concatenate([value * masks[0], value * masks[1]], 0)


def merged(value):
    rows = value.shape[0] // 2
    lane = lax.broadcasted_iota(jnp.int32, (rows, 2 * HEAD_DIM), 1)
    return jnp.where(lane < HEAD_DIM, value[:rows], value[rows:])


def by_variant(meta, run):
    @pl.when(meta[0] == 0)
    def _():
        run(0)

    @pl.when(meta[0] == 1)
    def _():
        run(1)


def attention_forward_kernel(meta, q_ref, ko_ref, vo_ref, kx_ref, vx_ref, out_ref, lse_ref):
    def run_all(variant):
        for pair in range(PAIRS):
            lanes = (slice(None), slice(pair * 2 * HEAD_DIM, (pair + 1) * 2 * HEAD_DIM))
            refs = [ref.at[lanes] for ref in (q_ref, ko_ref, vo_ref, kx_ref, vx_ref, out_ref)]
            attention_forward_pair(variant, *refs, lse_ref.at[pair])

    by_variant(meta, run_all)


def attention_forward_pair(variant, q_ref, ko_ref, vo_ref, kx_ref, vx_ref, out_ref, lse_ref):
    rows = q_ref.shape[0] // 2
    masks = head_masks(1.0 / math.sqrt(HEAD_DIM))

    def run(variant):
        position = lax.broadcasted_iota(jnp.int32, (2 * rows, rows), 0) % rows
        below = lax.broadcasted_iota(jnp.int32, (2 * rows, rows), 1) <= position
        low, high = slice(0, rows), slice(rows, 2 * rows)
        if variant == 0:
            plan = [
                (low, [(ko_ref, vo_ref, low)]),
                (high, [(ko_ref, vo_ref, low), (kx_ref, vx_ref, low), (kx_ref, vx_ref, high), (ko_ref, vo_ref, high)]),
            ]
        else:
            plan = [
                (low, [(kx_ref, vx_ref, low), (ko_ref, vo_ref, low)]),
                (high, [(ko_ref, vo_ref, low), (kx_ref, vx_ref, low), (ko_ref, vo_ref, high)]),
            ]
        all_scores = []
        for span, parts in plan:
            q2 = stacked(q_ref[span, :], masks)
            all_scores.append([dot_nt(q2, keys[place, :]) for keys, unused, place in parts])
        for (span, parts), scores in zip(plan, all_scores):
            scores[-1] = jnp.where(below, scores[-1], -1e30)
            peak = jnp.max(functools.reduce(jnp.maximum, scores), -1, keepdims=True)
            total, acc = None, None
            for part, (unused, values, place) in zip(scores, parts):
                raised = jnp.exp(part - peak)
                total = raised if total is None else total + raised
                term = dot_nn(raised.astype(BF16), values[place, :])
                acc = term if acc is None else acc + term
            total = jnp.sum(total, -1, keepdims=True)
            out_ref[span, :] = merged(acc / total).astype(BF16)
            log = peak + jnp.log(total)
            lane = lax.broadcasted_iota(jnp.int32, (rows, 2 * HEAD_DIM), 1)
            lse_ref[:, span] = jnp.where(lane == 0, log[:rows], log[rows:]).T[:8, :]

    run(variant)


def attention_forward(meta, queries, own, other):
    tokens = queries.shape[0]
    pairs = HEADS // 2
    wide = 2 * HEAD_DIM * PAIRS

    def at(offset):
        return pl.BlockSpec((tokens, wide), lambda g, m: (0, offset // PAIRS + g))

    return pl.pallas_call(
        attention_forward_kernel,
        grid_spec=pltpu.PrefetchScalarGridSpec(
            num_scalar_prefetch=1,
            grid=(pairs // PAIRS,),
            in_specs=[at(0), at(0), at(pairs), at(0), at(pairs)],
            out_specs=[at(0), pl.BlockSpec((PAIRS, 8, tokens), lambda g, m: (g, 0, 0))],
        ),
        out_shape=[
            pltpu.HBM((tokens, HEADS * HEAD_DIM), BF16),
            pltpu.HBM((pairs, 8, tokens), F32),
        ],
        compiler_params=pltpu.CompilerParams(vmem_limit_bytes=VMEM_BYTES),
        cost_estimate=SMALL_COST,
        name="attention_forward",
    )(meta, *in_hbm(queries, own, own, other, other))


def attention_backward_kernel(
    meta, q_ref, ko_ref, vo_ref, kx_ref, vx_ref, do_ref, o_ref, lse_ref,
    dq_ref, own_ref, other_ref, q4, do4,
):
    def run_all(variant):
        for pair in range(PAIRS):
            lanes = (slice(None), slice(pair * 2 * HEAD_DIM, (pair + 1) * 2 * HEAD_DIM))
            refs = [ref.at[lanes] for ref in (q_ref, ko_ref, vo_ref, kx_ref, vx_ref, do_ref, o_ref)]
            grads = [ref.at[(slice(None),) + lanes] for ref in (own_ref, other_ref)]
            attention_backward_pair(
                variant, *refs, lse_ref.at[pair], dq_ref.at[lanes], *grads, q4.at[pair], do4.at[pair]
            )

    by_variant(meta, run_all)


def attention_backward_pair(
    variant, q_ref, ko_ref, vo_ref, kx_ref, vx_ref, do_ref, o_ref, lse_ref,
    dq_ref, own_ref, other_ref, q4, do4,
):
    rows = q_ref.shape[0] // 2
    scale = 1.0 / math.sqrt(HEAD_DIM)
    scaled, plain = head_masks(scale), head_masks(1.0)
    product = (do_ref[...].astype(F32) * o_ref[...].astype(F32)).T
    first = jnp.sum(product[:HEAD_DIM], 0, keepdims=True)
    second = jnp.sum(product[HEAD_DIM:], 0, keepdims=True)
    logs = lse_ref[...]
    dot_row = jnp.concatenate([first[:, :rows], second[:, :rows], first[:, rows:], second[:, rows:]], 1)
    log_row = jnp.concatenate(
        [logs[0:1, :rows], logs[1:2, :rows], logs[0:1, rows:], logs[1:2, rows:]], 1
    )
    for block in range(2):
        span = slice(block * rows, (block + 1) * rows)
        q4[2 * block * rows : 2 * (block + 1) * rows, :] = stacked(q_ref[span, :], scaled)
        do4[2 * block * rows : 2 * (block + 1) * rows, :] = stacked(do_ref[span, :], plain)

    def run(variant):
        column = lax.broadcasted_iota(jnp.int32, (rows, 2 * rows), 1) % rows
        below = lax.broadcasted_iota(jnp.int32, (rows, 2 * rows), 0) <= column
        low, high = slice(0, rows), slice(rows, 2 * rows)
        both, upper, lower = slice(0, 4 * rows), slice(2 * rows, 4 * rows), slice(0, 2 * rows)
        plan = [(0, low, lower, True), (0, low, upper, False), (1, low, upper, False), (0, high, upper, True)]
        plan.insert(3, (1, high, upper, False) if variant == 0 else (1, low, lower, False))
        keys, values, grads = (ko_ref, kx_ref), (vo_ref, vx_ref), (own_ref, other_ref)
        dq_parts = {}
        sums = {}
        ahead = {}

        def products(index):
            source, place, cols, unused = plan[index]
            ahead[index] = dot_nt(keys[source][place, :], q4[cols, :]), dot_nt(values[source][place, :], do4[cols, :])

        products(0)
        products(1)
        for index, (source, place, cols, diagonal) in enumerate(plan):
            if index + 2 < len(plan):
                products(index + 2)
            scores, back = ahead.pop(index)
            raised = jnp.exp(scores - log_row[:, cols])
            if diagonal:
                raised = jnp.where(below, raised, 0.0)
            slope = (raised * (back - dot_row[:, cols])).astype(BF16)
            slot = (source, place.start)
            terms = dot_nn(slope, q4[cols, :]), dot_nn(raised.astype(BF16), do4[cols, :])
            sums[slot] = tuple(a + b for a, b in zip(sums[slot], terms)) if slot in sums else terms
            term = dot_tn(slope, keys[source][place, :])
            dq_parts[cols.start] = dq_parts[cols.start] + term if cols.start in dq_parts else term
        for block in range(2):
            dq_ref[block * rows : (block + 1) * rows, :] = (
                merged(dq_parts[2 * block * rows]) * scale
            ).astype(BF16)
        for source in range(2):
            for place in (low, high):
                zero = jnp.zeros((rows, 2 * HEAD_DIM), F32)
                for which, value in enumerate(sums.get((source, place.start), (zero, zero))):
                    grads[source][which, place, :] = value.astype(grads[source].dtype)

    run(variant)


def attention_backward(meta, queries, own, other, back_attended, attended, logs):
    tokens = queries.shape[0]
    pairs = HEADS // 2
    wide = 2 * HEAD_DIM * PAIRS
    width = HEADS * HEAD_DIM

    def at(offset):
        return pl.BlockSpec((tokens, wide), lambda g, m: (0, offset // PAIRS + g))

    return pl.pallas_call(
        attention_backward_kernel,
        grid_spec=pltpu.PrefetchScalarGridSpec(
            num_scalar_prefetch=1,
            grid=(pairs // PAIRS,),
            in_specs=[at(0), at(0), at(pairs), at(0), at(pairs), at(0), at(0),
                      pl.BlockSpec((PAIRS, 8, tokens), lambda g, m: (g, 0, 0))],
            out_specs=[at(0)] + [pl.BlockSpec((2, tokens, wide), lambda g, m: (0, 0, g))] * 2,
            scratch_shapes=[pltpu.VMEM((PAIRS, 2 * tokens, 2 * HEAD_DIM), BF16)] * 2,
        ),
        out_shape=[
            jax.ShapeDtypeStruct((tokens, width), BF16),
            pltpu.HBM((2, tokens, width), F32),
            jax.ShapeDtypeStruct((2, tokens, width), BF16),
        ],
        compiler_params=pltpu.CompilerParams(vmem_limit_bytes=VMEM_BYTES),
        cost_estimate=SMALL_COST,
        name="attention_backward",
    )(meta, *in_hbm(queries, own, own, other, other, back_attended, attended, logs))


def normalised(rows_in):
    average = jnp.mean(rows_in, -1, keepdims=True)
    centred = rows_in - average
    inverse = lax.rsqrt(jnp.mean(centred * centred, -1, keepdims=True) + epsilon)
    return centred * inverse, inverse


def norm_back(rows_in, gain_row, back):
    unit, inverse = normalised(rows_in)
    slope = back * gain_row
    first = jnp.mean(slope, -1, keepdims=True)
    second = jnp.mean(slope * unit, -1, keepdims=True)
    return inverse * (slope - first - unit * second), (
        jnp.sum(back * unit, 0, keepdims=True), jnp.sum(back, 0, keepdims=True))


def with_rows(table, row, sums):
    index = lax.broadcasted_iota(jnp.int32, table.shape, 0)
    return jnp.where(index == row, sums[0], jnp.where(index == row + 1, sums[1], table))


def project_kernel(layer, stream, gain, shift, matrix, hidden, queries, pairs):
    step = pl.program_id(0)

    @pl.when(step == 0)
    def _():
        unit, unused = normalised(stream[...].astype(F32))
        hidden[...] = (unit * gain[layer : layer + 1] + shift[layer : layer + 1]).astype(BF16)

    out = dot_nn(hidden[...], matrix[0]).astype(BF16)

    @pl.when(step < 2)
    def _():
        pairs[...] = out

    @pl.when(step == 2)
    def _():
        queries[...] = out


def project(layer, stream, gain, shift, matrix):
    tokens, width = stream.shape
    whole = pl.BlockSpec((tokens, width), lambda j: (0, 0))
    row = pl.BlockSpec(gain.shape, lambda j: (0, 0))
    return pl.pallas_call(
        functools.partial(project_kernel, layer),
        grid=(3,),
        in_specs=[whole, row, row, pl.BlockSpec((1, width, width), lambda j: (layer, 0, (j + 1) % 3))],
        out_specs=[whole, whole, pl.BlockSpec((tokens, width), lambda j: (0, jnp.minimum(j, 1)))],
        out_shape=[
            pltpu.HBM((tokens, width), BF16),
            pltpu.HBM((tokens, width), BF16),
            pltpu.HBM((tokens, 2 * width), BF16),
        ],
        compiler_params=pltpu.CompilerParams(vmem_limit_bytes=VMEM_BYTES),
        cost_estimate=SMALL_COST,
        name="project",
    )(*in_hbm(stream), gain, shift, *in_hbm(matrix))


def feed_forward_kernel(
    layer, steps, attended, stream, matrix_out, gain, shift, up, down,
    middle, normed, active_ref, slope_ref, out, acc,
):
    step = pl.program_id(0)

    @pl.when(step == 0)
    def _():
        middle[...] = stream[...].astype(F32) + dot_nn(attended[...], matrix_out[0])
        acc[...] = middle[...]
        unit, unused = normalised(middle[...])
        normed[...] = (unit * gain[layer : layer + 1] + shift[layer : layer + 1]).astype(BF16)

    groups = 4
    rows = normed.shape[0] // groups
    raw = {}
    for group in range(groups + 1):
        if group < groups:
            raw[group] = dot_nn(normed[group * rows : (group + 1) * rows, :], up[0])
        if group > 0:
            span = slice((group - 1) * rows, group * rows)
            active, slope = gelu_and_slope(raw.pop(group - 1))
            active = active.astype(BF16)
            active_ref[span, :] = active
            slope_ref[span, :] = slope.astype(BF16)
            acc[span, :] += dot_nn(active, down[0])

    @pl.when(step == steps - 1)
    def _():
        out[...] = acc[...].astype(out.dtype)


def feed_forward(layer, attended, stream, matrix_out, gain, shift, up, down, kind):
    tokens, width = stream.shape
    hidden = up.shape[2]
    tile = 1024
    steps = hidden // tile
    whole = pl.BlockSpec((tokens, width), lambda j: (0, 0))
    row = pl.BlockSpec(gain.shape, lambda j: (0, 0))
    part = pl.BlockSpec((tokens, tile), lambda j: (0, j))
    return pl.pallas_call(
        functools.partial(feed_forward_kernel, layer, steps),
        grid=(steps,),
        in_specs=[
            whole, whole, pl.BlockSpec((1, width, width), lambda j: (layer, 0, 0)), row, row,
            pl.BlockSpec((1, width, tile), lambda j: (layer, 0, j)),
            pl.BlockSpec((1, tile, width), lambda j: (layer, j, 0)),
        ],
        out_specs=[whole, whole, part, part, whole],
        out_shape=[
            pltpu.HBM((tokens, width), F32),
            pltpu.HBM((tokens, width), BF16),
            pltpu.HBM((tokens, hidden), BF16),
            pltpu.HBM((tokens, hidden), BF16),
            pltpu.HBM((tokens, width), kind),
        ],
        scratch_shapes=[pltpu.VMEM((tokens, width), F32)],
        compiler_params=pltpu.CompilerParams(vmem_limit_bytes=VMEM_BYTES),
        cost_estimate=SMALL_COST,
        name="feed_forward",
    )(*in_hbm(attended, stream, matrix_out), gain, shift, *in_hbm(up, down))


def feed_back_kernel(
    layer, steps, meta, upstream, back_out, slope, up, down, middle, gain, matrix_out, sums_in,
    own, send, back_middle, back_branch, branch_send, back_attended, grads, acc,
):
    step = pl.program_id(0)
    half = branch_send.shape[1]
    theirs = pl.ds(pl.multiple_of((1 - meta[1]) * half, 128), half)

    @pl.when(step == 0)
    def _():
        acc[...] = jnp.zeros_like(acc)

    back_up = (dot_nt(back_out[...], down[0]) * slope[...].astype(F32)).astype(BF16)

    @pl.when(step < steps // 2)
    def _():
        send[...] = back_up

    @pl.when(step >= steps // 2)
    def _():
        own[...] = back_up

    acc[...] += dot_nt(back_up, up[0])

    @pl.when(step == steps - 1)
    def _():
        back, sums = norm_back(middle[...], gain[layer : layer + 1], acc[...])
        back = back + upstream[...]
        grads[...] = with_rows(sums_in[...], 4 * layer + 2, sums)
        back_middle[...] = back
        back_branch[...] = back.astype(BF16)
        branch_send[...] = back_branch[:, theirs]
        back_attended[...] = dot_nt(back_branch[...], matrix_out[0]).astype(BF16)


def feed_back(layer, meta, upstream, back_out, slope, up, down, middle, gain, matrix_out, sums):
    tokens, width = upstream.shape
    hidden = up.shape[2]
    tile = 512
    steps = hidden // tile
    half = steps // 2

    def place(j, m):
        return jnp.where(j < half, (1 - m[1]) * half + j, m[1] * half + j - half)

    whole = pl.BlockSpec((tokens, width), lambda j, m: (0, 0))
    narrow = pl.BlockSpec((tokens, width // 2), lambda j, m: (0, 0))
    wide = jax.ShapeDtypeStruct((tokens, width), BF16)
    return pl.pallas_call(
        functools.partial(feed_back_kernel, layer, steps),
        grid_spec=pltpu.PrefetchScalarGridSpec(
            num_scalar_prefetch=1,
            grid=(steps,),
            in_specs=[
                whole, whole, pl.BlockSpec((tokens, tile), lambda j, m: (0, place(j, m))),
                pl.BlockSpec((1, width, tile), lambda j, m: (layer, 0, place(j, m))),
                pl.BlockSpec((1, tile, width), lambda j, m: (layer, place(j, m), 0)),
                whole, pl.BlockSpec(gain.shape, lambda j, m: (0, 0)),
                pl.BlockSpec((1, width, width), lambda j, m: (layer, 0, 0)),
                pl.BlockSpec((8, width), lambda j, m: (0, 0)),
            ],
            out_specs=[
                pl.BlockSpec((tokens, tile), lambda j, m: (0, jnp.maximum(j - half, 0))),
                pl.BlockSpec((tokens, tile), lambda j, m: (0, jnp.minimum(j, half - 1))),
                whole, whole, narrow, whole,
                pl.BlockSpec((8, width), lambda j, m: (0, 0)),
            ],
            scratch_shapes=[pltpu.VMEM((tokens, width), F32)],
        ),
        out_shape=[
            jax.ShapeDtypeStruct((tokens, hidden // 2), BF16),
            jax.ShapeDtypeStruct((tokens, hidden // 2), BF16),
            pltpu.HBM((tokens, width), F32),
            wide, jax.ShapeDtypeStruct((tokens, width // 2), BF16),
            wide, jax.ShapeDtypeStruct((8, width), F32),
        ],
        compiler_params=pltpu.CompilerParams(vmem_limit_bytes=VMEM_BYTES),
        cost_estimate=SMALL_COST,
        name="feed_back",
    )(meta, *in_hbm(upstream), back_out, *in_hbm(slope, up, down, middle), gain, *in_hbm(matrix_out), sums)


def project_back_kernel(
    layer, meta, back_q, own, got, matrix, stream, gain, back_middle, sums_in,
    mine, theirs, upstream, back_out, back_out_send, grads, table, acc,
):
    step = pl.program_id(0)
    width = back_q.shape[1]

    @pl.when(step == 0)
    def _():
        table[0] = back_q[...]
        for which in range(2):
            table[1 + which] = (own[which] + got[which].astype(F32)).astype(BF16)
        half = width // 2

        @pl.when(meta[1] == 0)
        def _():
            mine[:, :width] = table[0]
            mine[:, width:] = table[1, :, :half]
            theirs[:, :half] = table[1, :, half:]
            theirs[:, half:] = table[2]

        @pl.when(meta[1] == 1)
        def _():
            theirs[:, :width] = table[0]
            theirs[:, width:] = table[1, :, :half]
            mine[:, :half] = table[1, :, half:]
            mine[:, half:] = table[2]

        acc[...] = jnp.zeros_like(acc)

    acc[...] += dot_nt(table[step], matrix[0])

    @pl.when(step == 2)
    def _():
        back, sums = norm_back(stream[...].astype(F32), gain[layer : layer + 1], acc[...])
        back = back + back_middle[...]
        upstream[...] = back.astype(upstream.dtype)
        back_out[...] = back.astype(BF16)
        half = width // 2
        back_out_send[...] = back_out[:, pl.ds(pl.multiple_of((1 - meta[1]) * half, 128), half)]
        grads[...] = with_rows(sums_in[...], 4 * layer, sums)


def project_back(layer, meta, back_q, own, got, matrix, stream, gain, back_middle, sums, kind):
    tokens, width = stream.shape
    whole = pl.BlockSpec((tokens, width), lambda j, m: (0, 0))
    both = pl.BlockSpec((2, tokens, width), lambda j, m: (0, 0, 0))
    side = pl.BlockSpec((tokens, 3 * width // 2), lambda j, m: (0, 0))
    return pl.pallas_call(
        functools.partial(project_back_kernel, layer),
        grid_spec=pltpu.PrefetchScalarGridSpec(
            num_scalar_prefetch=1,
            grid=(3,),
            in_specs=[
                whole, both, both, pl.BlockSpec((1, width, width), lambda j, m: (layer, 0, j)),
                whole, pl.BlockSpec(gain.shape, lambda j, m: (0, 0)), whole,
                pl.BlockSpec((8, width), lambda j, m: (0, 0)),
            ],
            out_specs=[side, side, whole, whole, pl.BlockSpec((tokens, width // 2), lambda j, m: (0, 0)),
                       pl.BlockSpec((8, width), lambda j, m: (0, 0))],
            scratch_shapes=[pltpu.VMEM((3, tokens, width), BF16), pltpu.VMEM((tokens, width), F32)],
        ),
        out_shape=[
            jax.ShapeDtypeStruct((tokens, 3 * width // 2), BF16),
            jax.ShapeDtypeStruct((tokens, 3 * width // 2), BF16),
            pltpu.HBM((tokens, width), kind),
            jax.ShapeDtypeStruct((tokens, width), BF16),
            jax.ShapeDtypeStruct((tokens, width // 2), BF16),
            jax.ShapeDtypeStruct((8, width), F32),
        ],
        compiler_params=pltpu.CompilerParams(vmem_limit_bytes=VMEM_BYTES),
        cost_estimate=SMALL_COST,
        name="project_back",
    )(meta, *in_hbm(back_q, own), got, *in_hbm(matrix, stream), gain, *in_hbm(back_middle), sums)


def store_chunks(chips, meta, acc, keep, send):
    rows = acc.shape[0] // chips
    for position in range(chips):
        chunk = acc[pl.ds(pl.multiple_of(meta[2 + position] * rows, 16), rows), :]
        if position < chips // 2:
            keep[position] = chunk
        else:
            send[position - chips // 2] = chunk


def grad_up_kernel(chips, meta, ao, ax, bo, bx, co, cx, do, dx, *refs):
    keep, send, acc = refs[-3:]
    step = pl.program_id(0)

    @pl.when(step < 4)
    def _():
        acc[...] = (dot_tn(ao[...], bo[...]) + dot_tn(ax[...], bx[...])).astype(BF16)

    @pl.when(step == 4)
    def _():
        acc[...] = (dot_tn(co[...], do[...]) + dot_tn(cx[...], dx[...])).astype(BF16)

    store_chunks(chips, meta, acc, keep, send)


def grad_down_kernel(chips, meta, ao, ax, bo, bx, *refs):
    keep, send = refs[-2:]
    rows = keep.shape[1]
    each = ao.shape[1] // rows
    total = (dot_tn(ao[...], bo[...]) + dot_tn(ax[...], bx[...])).astype(BF16)
    for local in range(each):
        position = meta[2 + chips + pl.program_id(0) * each + local]
        chunk = total[local * rows : (local + 1) * rows]

        @pl.when(position < chips // 2)
        def _():
            keep[position] = chunk

        @pl.when(position >= chips // 2)
        def _():
            send[position - chips // 2] = chunk


def grad_qkv_kernel(chips, meta, ao, ax, bo, bx, sums, keep, send, acc, columns):
    wide = bo.shape[1]
    acc[:, :wide] = (dot_tn(ao[...], bo[...]) + dot_tn(ax[...], bx[...])).astype(BF16)
    columns[...] = jnp.concatenate([sums[...], jnp.zeros((120, sums.shape[1]), F32)], 0).T
    acc[:, wide:] = columns[...].astype(BF16)
    store_chunks(chips, meta, acc, keep, send)


def ordered(total, ids, chips):
    split = total.astype(BF16).reshape(chips, total.shape[0] // chips, total.shape[1])
    return jnp.take(split, ids, axis=0)


def gradient_call(kernel, name, chips, grid, in_specs, out_spec, shape, scratch):
    return pl.pallas_call(
        functools.partial(kernel, chips),
        grid_spec=pltpu.PrefetchScalarGridSpec(
            num_scalar_prefetch=1, grid=(grid,), in_specs=in_specs, out_specs=[out_spec] * 2,
            scratch_shapes=scratch,
        ),
        out_shape=[pltpu.HBM(shape, BF16)] * 2,
        compiler_params=pltpu.CompilerParams(vmem_limit_bytes=VMEM_BYTES),
        cost_estimate=SMALL_COST,
        name=name,
    )


def up_gradients(
    meta, chips, normed, normed_x, back_up, back_up_x, attended, attended_x, back_branch, branch_x
):
    tokens, width = normed.shape
    half = width // 2
    rows = width // chips
    if rows % 16 != 0:
        ids = meta[2 : 2 + chips]
        up = dot_tn(normed, back_up) + dot_tn(normed_x, back_up_x)
        own = lax.dynamic_slice_in_dim(back_branch, meta[1] * half, half, 1)
        out = dot_tn(attended, own) + dot_tn(attended_x, branch_x)
        up = ordered(up, ids, chips).reshape(chips, rows, 4, half)
        up = up.transpose(0, 2, 1, 3).reshape(chips, 4 * rows, half)
        both = jnp.concatenate([up, ordered(out, ids, chips)], 1)
        return both[: chips // 2], both[chips // 2 :]
    whole = pl.BlockSpec((tokens, width), lambda j, m: (0, 0))
    fixed = pl.BlockSpec((tokens, half), lambda j, m: (0, 0))
    mine = pl.BlockSpec((tokens, half), lambda j, m: (0, m[1]))
    tile = pl.BlockSpec((tokens, half), lambda j, m: (0, jnp.minimum(j, 3)))
    return gradient_call(
        grad_up_kernel, "gradient_up", chips, 5, [whole, whole, tile, tile, whole, whole, mine, fixed],
        pl.BlockSpec((chips // 2, rows, half), lambda j, m: (0, j, 0)),
        (chips // 2, 5 * rows, half), [pltpu.VMEM((width, half), BF16)],
    )(meta, *in_hbm(normed, normed_x), back_up, back_up_x, *in_hbm(attended, attended_x), back_branch, branch_x)


def down_gradients(meta, chips, active, active_x, back_out, back_out_x):
    tokens, hidden = active.shape
    width = back_out.shape[1]
    half = width // 2
    rows = hidden // chips
    if rows % 64 != 0:
        own = lax.dynamic_slice_in_dim(back_out, meta[1] * half, half, 1)
        down = dot_tn(active, own) + dot_tn(active_x, back_out_x)
        down = ordered(down, meta[2 : 2 + chips], chips)
        return down[: chips // 2], down[chips // 2 :]
    fixed = pl.BlockSpec((tokens, half), lambda j, m: (0, 0))
    mine = pl.BlockSpec((tokens, half), lambda j, m: (0, m[1]))
    tile = pl.BlockSpec((tokens, width), lambda j, m: (0, j))
    return gradient_call(
        grad_down_kernel, "gradient_down", chips, hidden // width, [tile, tile, mine, fixed],
        pl.BlockSpec((chips // 2, rows, half), lambda j, m: (0, 0, 0)), (chips // 2, rows, half), [],
    )(meta, *in_hbm(active, active_x), back_out, back_out_x)


def qkv_gradients(meta, chips, hidden, hidden_x, back_projected, back_projected_x, sums):
    tokens, width = hidden.shape
    wide = back_projected.shape[1]
    rows = width // chips
    if rows % 16 != 0:
        qkv = dot_tn(hidden, back_projected) + dot_tn(hidden_x, back_projected_x)
        table = jnp.pad(sums.T, ((0, 0), (0, 120)))
        both = ordered(jnp.concatenate([qkv, table], -1), meta[2 : 2 + chips], chips)
        return both[: chips // 2], both[chips // 2 :]
    specs = [pl.BlockSpec((tokens, width), lambda j, m: (0, 0))] * 2
    specs += [pl.BlockSpec((tokens, wide), lambda j, m: (0, 0))] * 2
    specs += [pl.BlockSpec((8, width), lambda j, m: (0, 0))]
    return gradient_call(
        grad_qkv_kernel, "gradient_qkv", chips, 1, specs,
        pl.BlockSpec((chips // 2, rows, wide + 128), lambda j, m: (0, 0, 0)),
        (chips // 2, rows, wide + 128),
        [pltpu.VMEM((width, wide + 128), BF16), pltpu.VMEM((width, 128), F32)],
    )(meta, *in_hbm(hidden, hidden_x), back_projected, back_projected_x, sums)


class Exchange:
    def __init__(self, dp):
        self.dp = dp
        self.chips = 2 * dp
        self.bits = int(math.log2(self.chips))
        self.core_pairs = [(s, s ^ 1) for s in range(4)]
        self.mirror_pairs = [(s, 3 - s) for s in range(4)]
        rest = list(range(2, self.bits))
        self.orders = ([1, 0] + rest, [0, 1] + rest[::-1])

    def swap_core(self, value):
        return lax.ppermute(value, "seq", self.core_pairs)

    def mirror(self, value):
        return lax.ppermute(value, "seq", self.mirror_pairs)

    def pairs(self, phase):
        result = []
        for device in range(2 * self.chips):
            chip = (device // 4) * 2 + (device % 4) // 2
            core = device % 2
            other = chip ^ (1 << self.orders[core][phase])
            result.append((device, (other // 2) * 4 + (other % 2) * 2 + core))
        return result

    def tables(self, chip, core):
        index = np.arange(self.chips)
        maps = []
        for order in self.orders:
            value = np.zeros_like(index)
            for phase, bit in enumerate(order):
                value |= ((index >> (self.bits - 1 - phase)) & 1) << bit
            maps.append(value.astype(np.int32))
        ids = chip ^ jnp.where(core == 0, jnp.asarray(maps[0]), jnp.asarray(maps[1]))
        relative = jnp.asarray(index.astype(np.int32)) ^ chip
        places = []
        for order in self.orders:
            place = jnp.zeros_like(relative)
            for phase, bit in enumerate(order):
                place = place | (((relative >> bit) & 1) << (self.bits - 1 - phase))
            places.append(place)
        return ids.astype(jnp.int32), jnp.where(core == 0, places[0], places[1]).astype(jnp.int32)


class Reduction:
    def __init__(self, exchange, keep, send):
        self.exchange, self.parts, self.phase = exchange, [keep], 0
        self.first, self.kind = send, send.dtype

    def message(self):
        if self.phase == 0:
            return self.first
        size = self.parts[-1].shape[0]
        terms = [part[size // 2 : size].astype(F32) for part in self.parts]
        return functools.reduce(jnp.add, terms).astype(self.kind)

    def transfer(self, message):
        self.phase += 1
        return lax.ppermute(message, AXES, self.exchange.pairs(self.phase - 1))

    def arrived(self, value):
        self.parts.append(value)

    def result(self):
        while self.phase < self.exchange.bits:
            self.arrived(self.transfer(self.message()))
        return functools.reduce(jnp.add, [part[0].astype(F32) for part in self.parts])


class Move:
    def __init__(self, transfer, value):
        self.transfer, self.value = transfer, value

    def message(self):
        return self.value

    def arrived(self, value):
        self.value = value


def host(run, inputs, *moves):
    count = len(inputs)
    tied = lax.optimization_barrier(tuple(inputs) + tuple(move.message() for move in moves))
    results = tuple(run(*tied[:count]))
    got = tuple(move.transfer(message) for move, message in zip(moves, tied[count:]))
    tied = lax.optimization_barrier(results + got)
    for move, value in zip(moves, tied[len(results) :]):
        move.arrived(value)
    return tied[: len(results)]


def by_core(core, mine, theirs, axis):
    return jnp.where(
        core == 0,
        jnp.concatenate([mine, theirs], axis),
        jnp.concatenate([theirs, mine], axis),
    )


def unpack_mlp(share, rows, core, exchange):
    half, each = share.shape[1], rows // 2
    down = share[: 4 * rows].reshape(2, 4 * each, half)
    rest = share[4 * rows :].reshape(share.shape[0] // rows - 4, 2, each, half)

    def pick(which):
        return jnp.concatenate(
            [lax.dynamic_index_in_dim(down, which, 0, False),
             lax.dynamic_index_in_dim(rest, which, 1, False).reshape(-1, half)], 0)

    mine, theirs = pick(core), exchange.swap_core(pick(1 - core))

    def widen(value, start, count):
        value = value[start * each : (start + count) * each].reshape(count, each, half)
        return value.transpose(1, 0, 2).reshape(each, count * half)

    def join(start, count):
        return by_core(core, widen(mine, start, count), widen(theirs, start, count), 1)

    grad_down = by_core(core, mine[: 4 * each], theirs[: 4 * each], 1)
    return grad_down, join(4, 4), join(8, 1)


def unpack_qkv(share, core, exchange):
    rows, wide = share.shape
    split = share.reshape(2, rows // 2, wide)
    mine = lax.dynamic_index_in_dim(split, core, 0, False)
    theirs = exchange.swap_core(lax.dynamic_index_in_dim(split, 1 - core, 0, False))
    wide -= 128
    table = mine[:, wide : wide + 8] + theirs[:, wide : wide + 8]
    return by_core(core, mine[:, :wide], theirs[:, :wide], 1), table


def per_device(
    inputs, cotangent, task_table, type_counts,
    gain_one, bias_one, proj_qkv, proj_out, gain_two, bias_two, proj_up, proj_down,
):
    slots, rows, width = inputs.shape
    length = rows * lax.axis_size("seq")
    exchange = Exchange(lax.axis_size("dp"))
    place = lax.axis_index("seq")
    side, core = place // 2, place % 2
    chip = lax.axis_index("dp") * 2 + side
    low = jnp.minimum(place, 3 - place)
    own_first = place < 2
    flag = low.astype(jnp.int32).reshape(1)

    meta = jnp.concatenate([flag, core.astype(jnp.int32).reshape(1), *exchange.tables(chip, core)])

    def gather_slot(value, got):
        own = lax.dynamic_index_in_dim(value, side, 0, False)
        return jnp.where(own_first, jnp.concatenate([own, got]), jnp.concatenate([got, own]))

    choose = (task_table[:, None] == jnp.arange(TASKS, dtype=jnp.int32)[None, :]).astype(F32)
    targets = (length - type_counts[:, 0]).astype(F32)
    totals = jnp.sum(choose * targets[:, None], 0)
    bits = int(math.log2(exchange.dp))

    for bit in range(bits):
        pairs = [(d, d ^ (1 << bit)) for d in range(exchange.dp)]
        totals = totals + lax.ppermute(totals, "dp", pairs)
    got = exchange.mirror(lax.dynamic_index_in_dim(inputs, 1 - side, 0, False))
    got, totals = lax.optimization_barrier((got, totals))
    stream = gather_slot(inputs, got)
    factor = jnp.sum(totals) / TASKS / totals
    seq_weight = jnp.sum(choose * factor[None, :], 1)
    own_weight = lax.dynamic_index_in_dim(seq_weight, side, 0, False)
    own_start = lax.dynamic_index_in_dim(type_counts[:, 0], side, 0, False)
    steps = jnp.arange(rows, dtype=jnp.int32)
    query_pos = jnp.concatenate([low * rows + steps, (3 - low) * rows + steps])
    scale = jnp.where(query_pos >= own_start, own_weight, 0.0)
    chips = exchange.chips
    half = width // 2
    swap, mirror = exchange.swap_core, exchange.mirror

    def forward(layer, stream, moves_project, moves_attention, kind):
        hidden, queries, own = host(
            lambda v: project(layer, v, gain_one, bias_one, proj_qkv), (stream,), *moves_project
        )
        other = swap(own)
        hidden_x = Move(swap, hidden)
        attended, logs = host(
            lambda q, k, kx: attention_forward(flag, q, k, kx), (queries, own, other),
            hidden_x, *moves_attention
        )
        attended_x = Move(swap, attended)
        middle, normed, active, slope, output = host(
            lambda a, v: feed_forward(layer, a, v, proj_out, gain_two, bias_two, proj_up, proj_down, kind),
            (attended, stream), attended_x,
        )
        moves = Move(swap, normed), Move(swap, active)
        return output, moves, (stream, hidden, hidden_x, queries, own, other, logs, attended, attended_x, middle, normed, active, slope)

    def attention_step(layer, back_attended, moves):
        unused, unused, unused, queries, own, other, logs, attended, unused, unused, unused, unused, unused = kept[layer]
        back_q, back_own, back_other = host(
            lambda b: attention_backward(flag, queries, own, other, b, attended, logs), (back_attended,), *moves
        )
        return back_q, back_own, swap(back_other)

    def project_step(layer, back_q, back_own, back_got, back_middle, sums, moves):
        kind = BF16 if layer == 0 else F32
        return host(
            lambda q, k, kx: project_back(
                layer, meta, q, k, kx, proj_qkv, kept[layer][0], gain_one, back_middle, sums, kind
            ),
            (back_q, back_own, back_got), *moves
        )

    def feed_step(layer, upstream, back_out, sums, moves):
        middle, slope = kept[layer][9], kept[layer][12]
        return host(
            lambda u, b: feed_back(
                layer, meta, u, b, slope, proj_up, proj_down, middle, gain_two, proj_out, sums
            ),
            (upstream, back_out), *moves
        )

    def down_step(layer, back_out, back_out_x, active_x, moves):
        active = kept[layer][11]
        return Reduction(exchange, *host(
            lambda b, bx: down_gradients(meta, chips, active, active_x, b, bx), (back_out, back_out_x), *moves
        ))

    def up_step(layer, back_up, back_up_x, back_branch, branch_x, normed_x, moves):
        normed, attended, attended_x = kept[layer][10], kept[layer][7], kept[layer][8].value
        return Reduction(exchange, *host(
            lambda b, bx: up_gradients(
                meta, chips, normed, normed_x, b, bx, attended, attended_x, back_branch, branch_x
            ),
            (back_up, back_up_x), *moves
        ))

    def qkv_step(layer, mine, theirs_x, sums, moves):
        hidden, hidden_x = kept[layer][1], kept[layer][2].value
        return Reduction(exchange, *host(
            lambda b, bx: qkv_gradients(meta, chips, hidden, hidden_x, b, bx, sums), (mine, theirs_x), *moves
        ))

    got_cotangent = Move(mirror, lax.dynamic_index_in_dim(cotangent, 1 - side, 0, False))
    stream, moves, saved = forward(0, stream, (), (got_cotangent,), F32)
    kept = [saved]
    upstream = gather_slot(cotangent, got_cotangent.value).astype(F32) * scale[:, None]
    back_out = upstream.astype(BF16)
    back_out_x = Move(swap, lax.dynamic_slice_in_dim(back_out, (1 - core) * half, half, 1))
    stream, last_moves, saved = forward(1, stream, moves, (back_out_x,), BF16)
    normed_x, active_x = (move.value for move in moves)
    kept.append(saved)
    outputs_move = Move(mirror, jnp.where(own_first, stream[rows:], stream[:rows]))

    sums = jnp.zeros((8, width), F32)
    back_up, back_up_send, back_middle, back_branch, branch_send, back_attended, sums = feed_step(
        1, upstream, back_out, sums, last_moves + (outputs_move,)
    )
    last_normed_x, last_active_x = (move.value for move in last_moves)
    back_up_x, branch_x = Move(swap, back_up_send), Move(swap, branch_send)
    down1 = down_step(1, back_out, back_out_x.value, last_active_x, (back_up_x, branch_x))
    up1 = up_step(1, back_up, back_up_x.value, back_branch, branch_x.value, last_normed_x, (down1,))
    back_q, back_own, back_got = attention_step(1, back_attended, (up1,))
    mine, theirs, upstream, back_out, back_out_send, sums = project_step(
        1, back_q, back_own, back_got, back_middle, sums, (down1,)
    )
    theirs_x = Move(swap, theirs)
    down0 = down_step(0, back_out, swap(back_out_send), active_x, (theirs_x, up1, down1))
    back_up, back_up_send, back_middle, back_branch, branch_send, back_attended, sums0 = feed_step(
        0, upstream, back_out, sums, (down0, up1)
    )
    back_up_x, branch_x = Move(swap, back_up_send), Move(swap, branch_send)
    qkv1 = qkv_step(1, mine, theirs_x.value, sums, (back_up_x, branch_x, down0, down1))
    up0 = up_step(0, back_up, back_up_x.value, back_branch, branch_x.value, normed_x, (qkv1, up1))
    back_q, back_own, back_got = attention_step(0, back_attended, (up0, down0))
    mine, theirs, upstream, back_out, back_out_send, sums = project_step(
        0, back_q, back_own, back_got, back_middle, sums0, (up0, qkv1, down0)
    )
    back_move = Move(mirror, jnp.where(own_first, upstream[rows:], upstream[:rows]))
    qkv0 = qkv_step(0, mine, swap(theirs), sums, (up0, qkv1))
    unit = width // chips

    def return_slot(value, got):
        own = jnp.where(own_first, value[:rows], value[rows:])
        return jnp.where(side == 0, jnp.stack([own, got]), jnp.stack([got, own]))

    def finish_second(*unused):
        share = jnp.concatenate([down1.result(), up1.result()], 0)
        return unpack_mlp(share, unit, core, exchange)

    def finish_first(*unused):
        share = jnp.concatenate([down0.result(), up0.result()], 0)
        return unpack_mlp(share, unit, core, exchange) + unpack_qkv(qkv1.result(), core, exchange)[:1]

    down_b, up_b, out_b = host(finish_second, (down1.parts[-1],), qkv0, up0, qkv1)
    down_a, up_a, out_a, qkv_b = host(finish_first, (down0.parts[-1],), qkv0, back_move)
    outputs, grad_up, grad_down, grad_out = host(
        lambda got: (
            return_slot(stream, got), jnp.stack([up_a, up_b]), jnp.stack([down_a, down_b]), jnp.stack([out_a, out_b])
        ),
        (outputs_move.value,), qkv0,
    )
    (back_inputs,) = host(lambda got: (return_slot(upstream, got).astype(F32),), (back_move.value,), qkv0)
    qkv_a, table = unpack_qkv(qkv0.result(), core, exchange)
    table = table.T.reshape(LAYERS, 4, unit // 2)
    return (
        outputs, back_inputs, table[:, 0], table[:, 1], jnp.stack([qkv_a, qkv_b]), grad_out,
        table[:, 2], table[:, 3], grad_up, grad_down,
    )


def solution(mesh):
    tokens = P("dp", "seq", None)
    shared = P(None, AXES)
    in_specs = (tokens, tokens, P("dp"), P("dp", None)) + (P(),) * 8
    out_specs = (
        tokens, tokens, shared, shared, P(None, AXES, None), P(None, AXES, None),
        shared, shared, P(None, AXES, None), P(None, AXES, None),
    )
    return jax.shard_map(
        per_device, mesh=mesh, in_specs=in_specs, out_specs=out_specs, check_vma=False
    )
```

```python
import functools
import math

import jax
import jax.numpy as jnp
import numpy as np
from jax import lax
from jax.experimental import pallas as pl
from jax.experimental.pallas import tpu as pltpu
from jax.sharding import PartitionSpec as P

HEADS = 12
HEAD_DIM = 64
LAYERS = 2
TASKS = 3
AXES = ("dp", "seq")
F32 = jnp.float32
BF16 = jnp.bfloat16
epsilon = 1e-05
PAIRS = 2
VMEM_BYTES = 32 * 1024 * 1024
SMALL_COST = pl.CostEstimate(flops=1000, bytes_accessed=1000, transcendentals=0)


def in_hbm(*values):
    return tuple(pltpu.with_memory_space_constraint(v, pltpu.HBM) for v in values)


def dot_nn(a, b):
    return lax.dot_general(a, b, (((1,), (0,)), ((), ())), preferred_element_type=F32)


def dot_nt(a, b):
    return lax.dot_general(a, b, (((1,), (1,)), ((), ())), preferred_element_type=F32)


def dot_tn(a, b):
    return lax.dot_general(a, b, (((0,), (0,)), ((), ())), preferred_element_type=F32)


def gelu_and_slope(x):
    z = jnp.abs(x) * 0.7071067811865476
    d = 1.0 + 0.3275911 * z
    t = pl.reciprocal(d, approx=True)
    t = t * (2.0 - d * t)
    poly = t * (
        0.254829592
        + t * (-0.284496736 + t * (1.421413741 + t * (-1.453152027 + t * 1.061405429)))
    )
    bell = jnp.exp(-0.5 * x * x)
    tail = 0.5 * poly * bell
    below = jnp.where(x >= 0.0, 1.0 - tail, tail)
    return x * below, below + x * bell * 0.3989422804014327


def hosted_call(name, number, body, grid, in_specs, out_specs, out_shape, scratch_shapes, operands, moves):
    plans = [move.plan() for move in moves]
    count_in, count_out = len(in_specs), len(out_specs)
    count_scratch = len(scratch_shapes)
    anywhere = pl.BlockSpec(memory_space=pl.ANY)
    sources = [array for plan in plans for array in plan["arrays"]]
    extra = []
    for plan in plans:
        if plan["half"]:
            extra.append(pltpu.VMEM((len(plan["arrays"]),) + plan["shape"], plan["dtype"]))
            extra.append(pltpu.VMEM(plan["shape"], plan["dtype"]))
            extra.append(pltpu.SemaphoreType.DMA((len(plan["arrays"]),)))
        extra += [pltpu.SemaphoreType.DMA] * 2

    def kernel(*refs):
        refs = list(refs)

        def take(count):
            taken = refs[:count]
            del refs[:count]
            return taken

        ins = take(count_in)
        given = [take(len(plan["arrays"])) for plan in plans]
        outs = take(count_out)
        landing = take(len(plans))
        scratch = take(count_scratch)
        buffers = [take(5 if plan["half"] else 2) for plan in plans]
        step = pl.program_id(0)
        partners = [plan["partner"]() for plan in plans]

        def remote(index):
            source = buffers[index][1] if plans[index]["half"] else given[index][0]
            return pltpu.make_async_remote_copy(
                src_ref=source, dst_ref=landing[index], send_sem=buffers[index][-2],
                recv_sem=buffers[index][-1], device_id=partners[index],
                device_id_type=pl.DeviceIdType.MESH,
            )

        def loads(index):
            half = plans[index]["half"]
            return [
                pltpu.make_async_copy(
                    ref.at[pl.ds(half, half)], buffers[index][0].at[which], buffers[index][2].at[which]
                )
                for which, ref in enumerate(given[index])
            ]

        @pl.when(step == 0)
        def _():
            barrier = pltpu.get_barrier_semaphore()
            for partner in partners:
                pl.semaphore_signal(barrier, inc=1, device_id=partner, device_id_type=pl.DeviceIdType.MESH)
            for index, plan in enumerate(plans):
                if plan["half"]:
                    for load in loads(index):
                        load.start()

        body(*ins, *outs, *scratch)

        @pl.when(step == 0)
        def _():
            pl.semaphore_wait(pltpu.get_barrier_semaphore(), len(plans))
            for index, plan in enumerate(plans):
                if plan["half"]:
                    for load in loads(index):
                        load.wait()
                    terms = [buffers[index][0][which].astype(F32) for which in range(len(plan["arrays"]))]
                    buffers[index][1][...] = functools.reduce(jnp.add, terms).astype(plan["dtype"])
                remote(index).start()

        @pl.when(step == grid - 1)
        def _():
            for index in range(len(plans)):
                remote(index).wait()

    results = pl.pallas_call(
        kernel,
        grid=(grid,),
        in_specs=in_specs + [anywhere] * len(sources),
        out_specs=out_specs + [anywhere] * len(plans),
        out_shape=list(out_shape) + [pltpu.HBM(plan["shape"], plan["dtype"]) for plan in plans],
        scratch_shapes=list(scratch_shapes) + extra,
        compiler_params=pltpu.CompilerParams(
            vmem_limit_bytes=VMEM_BYTES, collective_id=number, has_side_effects=True
        ),
        cost_estimate=SMALL_COST,
        name=name,
    )(*operands, *in_hbm(*sources))
    for move, value in zip(moves, results[count_out:]):
        move.arrived(value)
    return results[:count_out]


def low_block():
    return ((lax.axis_index("seq") + 1) // 2) % 2


def head_masks(scale):
    lane = lax.broadcasted_iota(jnp.int32, (1, 2 * HEAD_DIM), 1)
    first = jnp.where(lane < HEAD_DIM, scale, 0.0)
    return first.astype(BF16), (scale - first).astype(BF16)


def stacked(value, masks):
    return jnp.concatenate([value * masks[0], value * masks[1]], 0)


def merged(value):
    rows = value.shape[0] // 2
    lane = lax.broadcasted_iota(jnp.int32, (rows, 2 * HEAD_DIM), 1)
    return jnp.where(lane < HEAD_DIM, value[:rows], value[rows:])


def by_variant(run):
    low = low_block()

    @pl.when(low == 0)
    def _():
        run(0)

    @pl.when(low == 1)
    def _():
        run(1)


def attention_forward_kernel(q_ref, ko_ref, vo_ref, kx_ref, vx_ref, out_ref, lse_ref):
    def run_all(variant):
        for pair in range(PAIRS):
            lanes = (slice(None), slice(pair * 2 * HEAD_DIM, (pair + 1) * 2 * HEAD_DIM))
            refs = [ref.at[lanes] for ref in (q_ref, ko_ref, vo_ref, kx_ref, vx_ref, out_ref)]
            attention_forward_pair(variant, *refs, lse_ref.at[pair])

    by_variant(run_all)


def attention_forward_pair(variant, q_ref, ko_ref, vo_ref, kx_ref, vx_ref, out_ref, lse_ref):
    rows = q_ref.shape[0] // 2
    masks = head_masks(1.0 / math.sqrt(HEAD_DIM))

    def run(variant):
        position = lax.broadcasted_iota(jnp.int32, (2 * rows, rows), 0) % rows
        below = lax.broadcasted_iota(jnp.int32, (2 * rows, rows), 1) <= position
        low, high = slice(0, rows), slice(rows, 2 * rows)
        if variant == 0:
            plan = [
                (low, [(ko_ref, vo_ref, low)]),
                (high, [(ko_ref, vo_ref, low), (kx_ref, vx_ref, low), (kx_ref, vx_ref, high), (ko_ref, vo_ref, high)]),
            ]
        else:
            plan = [
                (low, [(kx_ref, vx_ref, low), (ko_ref, vo_ref, low)]),
                (high, [(ko_ref, vo_ref, low), (kx_ref, vx_ref, low), (ko_ref, vo_ref, high)]),
            ]
        all_scores = []
        for span, parts in plan:
            q2 = stacked(q_ref[span, :], masks)
            all_scores.append([dot_nt(q2, keys[place, :]) for keys, unused, place in parts])
        for (span, parts), scores in zip(plan, all_scores):
            scores[-1] = jnp.where(below, scores[-1], -1e30)
            peak = jnp.max(functools.reduce(jnp.maximum, scores), -1, keepdims=True)
            total, acc = None, None
            for part, (unused, values, place) in zip(scores, parts):
                raised = jnp.exp(part - peak)
                total = raised if total is None else total + raised
                term = dot_nn(raised.astype(BF16), values[place, :])
                acc = term if acc is None else acc + term
            total = jnp.sum(total, -1, keepdims=True)
            out_ref[span, :] = merged(acc / total).astype(BF16)
            log = peak + jnp.log(total)
            lane = lax.broadcasted_iota(jnp.int32, (rows, 2 * HEAD_DIM), 1)
            lse_ref[:, span] = jnp.where(lane == 0, log[:rows], log[rows:]).T[:8, :]

    run(variant)


def attention_forward(queries, own, other):
    tokens = queries.shape[0]
    pairs = HEADS // 2
    wide = 2 * HEAD_DIM * PAIRS

    def at(offset):
        return pl.BlockSpec((tokens, wide), lambda g: (0, offset // PAIRS + g))

    return pl.pallas_call(
        attention_forward_kernel,
        grid=(pairs // PAIRS,),
        in_specs=[at(0), at(0), at(pairs), at(0), at(pairs)],
        out_specs=[at(0), pl.BlockSpec((PAIRS, 8, tokens), lambda g: (g, 0, 0))],
        out_shape=[
            pltpu.HBM((tokens, HEADS * HEAD_DIM), BF16),
            pltpu.HBM((pairs, 8, tokens), F32),
        ],
        compiler_params=pltpu.CompilerParams(vmem_limit_bytes=VMEM_BYTES),
        cost_estimate=SMALL_COST,
        name="attention_forward",
    )(*in_hbm(queries, own, own, other, other))


def attention_backward_kernel(
    q_ref, ko_ref, vo_ref, kx_ref, vx_ref, do_ref, o_ref, lse_ref,
    dq_ref, own_ref, other_ref, q4, do4,
):
    def run_all(variant):
        for pair in range(PAIRS):
            lanes = (slice(None), slice(pair * 2 * HEAD_DIM, (pair + 1) * 2 * HEAD_DIM))
            refs = [ref.at[lanes] for ref in (q_ref, ko_ref, vo_ref, kx_ref, vx_ref, do_ref, o_ref)]
            grads = [ref.at[(slice(None),) + lanes] for ref in (own_ref, other_ref)]
            attention_backward_pair(
                variant, *refs, lse_ref.at[pair], dq_ref.at[lanes], *grads, q4.at[pair], do4.at[pair]
            )

    by_variant(run_all)


def attention_backward_pair(
    variant, q_ref, ko_ref, vo_ref, kx_ref, vx_ref, do_ref, o_ref, lse_ref,
    dq_ref, own_ref, other_ref, q4, do4,
):
    rows = q_ref.shape[0] // 2
    scale = 1.0 / math.sqrt(HEAD_DIM)
    scaled, plain = head_masks(scale), head_masks(1.0)
    product = (do_ref[...].astype(F32) * o_ref[...].astype(F32)).T
    first = jnp.sum(product[:HEAD_DIM], 0, keepdims=True)
    second = jnp.sum(product[HEAD_DIM:], 0, keepdims=True)
    logs = lse_ref[...]
    dot_row = jnp.concatenate([first[:, :rows], second[:, :rows], first[:, rows:], second[:, rows:]], 1)
    log_row = jnp.concatenate(
        [logs[0:1, :rows], logs[1:2, :rows], logs[0:1, rows:], logs[1:2, rows:]], 1
    )
    for block in range(2):
        span = slice(block * rows, (block + 1) * rows)
        q4[2 * block * rows : 2 * (block + 1) * rows, :] = stacked(q_ref[span, :], scaled)
        do4[2 * block * rows : 2 * (block + 1) * rows, :] = stacked(do_ref[span, :], plain)

    def run(variant):
        column = lax.broadcasted_iota(jnp.int32, (rows, 2 * rows), 1) % rows
        below = lax.broadcasted_iota(jnp.int32, (rows, 2 * rows), 0) <= column
        low, high = slice(0, rows), slice(rows, 2 * rows)
        both, upper, lower = slice(0, 4 * rows), slice(2 * rows, 4 * rows), slice(0, 2 * rows)
        plan = [(0, low, lower, True), (0, low, upper, False), (1, low, upper, False), (0, high, upper, True)]
        plan.insert(3, (1, high, upper, False) if variant == 0 else (1, low, lower, False))
        keys, values, grads = (ko_ref, kx_ref), (vo_ref, vx_ref), (own_ref, other_ref)
        dq_parts = {}
        sums = {}
        ahead = {}

        def products(index):
            source, place, cols, unused = plan[index]
            ahead[index] = dot_nt(keys[source][place, :], q4[cols, :]), dot_nt(values[source][place, :], do4[cols, :])

        products(0)
        products(1)
        for index, (source, place, cols, diagonal) in enumerate(plan):
            if index + 2 < len(plan):
                products(index + 2)
            scores, back = ahead.pop(index)
            raised = jnp.exp(scores - log_row[:, cols])
            if diagonal:
                raised = jnp.where(below, raised, 0.0)
            slope = (raised * (back - dot_row[:, cols])).astype(BF16)
            slot = (source, place.start)
            terms = dot_nn(slope, q4[cols, :]), dot_nn(raised.astype(BF16), do4[cols, :])
            sums[slot] = tuple(a + b for a, b in zip(sums[slot], terms)) if slot in sums else terms
            term = dot_tn(slope, keys[source][place, :])
            dq_parts[cols.start] = dq_parts[cols.start] + term if cols.start in dq_parts else term
        for block in range(2):
            dq_ref[block * rows : (block + 1) * rows, :] = (
                merged(dq_parts[2 * block * rows]) * scale
            ).astype(BF16)
        for source in range(2):
            for place in (low, high):
                zero = jnp.zeros((rows, 2 * HEAD_DIM), F32)
                for which, value in enumerate(sums.get((source, place.start), (zero, zero))):
                    grads[source][which, place, :] = value.astype(grads[source].dtype)

    run(variant)


def attention_backward(number, queries, own, other, back_attended, attended, logs, moves):
    tokens = queries.shape[0]
    pairs = HEADS // 2
    wide = 2 * HEAD_DIM * PAIRS
    width = HEADS * HEAD_DIM

    def at(offset):
        return pl.BlockSpec((tokens, wide), lambda g: (0, offset // PAIRS + g))

    return hosted_call(
        "attention_backward", number, attention_backward_kernel, pairs // PAIRS,
        [at(0), at(0), at(pairs), at(0), at(pairs), at(0), at(0),
         pl.BlockSpec((PAIRS, 8, tokens), lambda g: (g, 0, 0))],
        [at(0)] + [pl.BlockSpec((2, tokens, wide), lambda g: (0, 0, g))] * 2,
        [jax.ShapeDtypeStruct((tokens, width), BF16), pltpu.HBM((2, tokens, width), F32),
         jax.ShapeDtypeStruct((2, tokens, width), BF16)],
        [pltpu.VMEM((PAIRS, 2 * tokens, 2 * HEAD_DIM), BF16)] * 2,
        in_hbm(queries, own, own, other, other, back_attended, attended, logs),
        moves,
    )


def normalised(rows_in):
    average = jnp.mean(rows_in, -1, keepdims=True)
    centred = rows_in - average
    inverse = lax.rsqrt(jnp.mean(centred * centred, -1, keepdims=True) + epsilon)
    return centred * inverse, inverse


def norm_back(rows_in, gain_row, back):
    unit, inverse = normalised(rows_in)
    slope = back * gain_row
    first = jnp.mean(slope, -1, keepdims=True)
    second = jnp.mean(slope * unit, -1, keepdims=True)
    return inverse * (slope - first - unit * second), (
        jnp.sum(back * unit, 0, keepdims=True), jnp.sum(back, 0, keepdims=True))


def with_rows(table, row, sums):
    index = lax.broadcasted_iota(jnp.int32, table.shape, 0)
    return jnp.where(index == row, sums[0], jnp.where(index == row + 1, sums[1], table))


def project_kernel(layer, stream, gain, shift, matrix, hidden, queries, pairs):
    step = pl.program_id(0)

    @pl.when(step == 0)
    def _():
        unit, unused = normalised(stream[...].astype(F32))
        hidden[...] = (unit * gain[layer : layer + 1] + shift[layer : layer + 1]).astype(BF16)

    out = dot_nn(hidden[...], matrix[0]).astype(BF16)

    @pl.when(step < 2)
    def _():
        pairs[...] = out

    @pl.when(step == 2)
    def _():
        queries[...] = out


def project(layer, stream, gain, shift, matrix):
    tokens, width = stream.shape
    whole = pl.BlockSpec((tokens, width), lambda j: (0, 0))
    row = pl.BlockSpec(gain.shape, lambda j: (0, 0))
    return pl.pallas_call(
        functools.partial(project_kernel, layer),
        grid=(3,),
        in_specs=[whole, row, row, pl.BlockSpec((1, width, width), lambda j: (layer, 0, (j + 1) % 3))],
        out_specs=[whole, whole, pl.BlockSpec((tokens, width), lambda j: (0, jnp.minimum(j, 1)))],
        out_shape=[
            pltpu.HBM((tokens, width), BF16),
            pltpu.HBM((tokens, width), BF16),
            pltpu.HBM((tokens, 2 * width), BF16),
        ],
        compiler_params=pltpu.CompilerParams(vmem_limit_bytes=VMEM_BYTES),
        cost_estimate=SMALL_COST,
        name="project",
    )(*in_hbm(stream), gain, shift, *in_hbm(matrix))


def feed_forward_kernel(
    layer, steps, attended, stream, matrix_out, gain, shift, up, down,
    middle, normed, active_ref, slope_ref, out, acc,
):
    step = pl.program_id(0)

    @pl.when(step == 0)
    def _():
        middle[...] = stream[...].astype(F32) + dot_nn(attended[...], matrix_out[0])
        acc[...] = middle[...]
        unit, unused = normalised(middle[...])
        normed[...] = (unit * gain[layer : layer + 1] + shift[layer : layer + 1]).astype(BF16)

    groups = 4
    rows = normed.shape[0] // groups
    raw = {}
    for group in range(groups + 1):
        if group < groups:
            raw[group] = dot_nn(normed[group * rows : (group + 1) * rows, :], up[0])
        if group > 0:
            span = slice((group - 1) * rows, group * rows)
            active, slope = gelu_and_slope(raw.pop(group - 1))
            active = active.astype(BF16)
            active_ref[span, :] = active
            slope_ref[span, :] = slope.astype(BF16)
            acc[span, :] += dot_nn(active, down[0])

    @pl.when(step == steps - 1)
    def _():
        out[...] = acc[...].astype(out.dtype)


def feed_forward(layer, attended, stream, matrix_out, gain, shift, up, down, kind):
    tokens, width = stream.shape
    hidden = up.shape[2]
    tile = 1024
    steps = hidden // tile
    whole = pl.BlockSpec((tokens, width), lambda j: (0, 0))
    row = pl.BlockSpec(gain.shape, lambda j: (0, 0))
    part = pl.BlockSpec((tokens, tile), lambda j: (0, j))
    return pl.pallas_call(
        functools.partial(feed_forward_kernel, layer, steps),
        grid=(steps,),
        in_specs=[
            whole, whole, pl.BlockSpec((1, width, width), lambda j: (layer, 0, 0)), row, row,
            pl.BlockSpec((1, width, tile), lambda j: (layer, 0, j)),
            pl.BlockSpec((1, tile, width), lambda j: (layer, j, 0)),
        ],
        out_specs=[whole, whole, part, part, whole],
        out_shape=[
            pltpu.HBM((tokens, width), F32),
            pltpu.HBM((tokens, width), BF16),
            pltpu.HBM((tokens, hidden), BF16),
            pltpu.HBM((tokens, hidden), BF16),
            pltpu.HBM((tokens, width), kind),
        ],
        scratch_shapes=[pltpu.VMEM((tokens, width), F32)],
        compiler_params=pltpu.CompilerParams(vmem_limit_bytes=VMEM_BYTES),
        cost_estimate=SMALL_COST,
        name="feed_forward",
    )(*in_hbm(attended, stream, matrix_out), gain, shift, *in_hbm(up, down))


def feed_back_kernel(
    layer, steps, meta, upstream, back_out, slope, up, down, middle, gain, matrix_out, sums_in,
    own, send, back_middle, back_branch, branch_send, back_attended, grads, acc,
):
    step = pl.program_id(0)
    half = branch_send.shape[1]
    theirs = pl.ds(pl.multiple_of((1 - meta[1]) * half, 128), half)

    @pl.when(step == 0)
    def _():
        acc[...] = jnp.zeros_like(acc)

    back_up = (dot_nt(back_out[...], down[0]) * slope[...].astype(F32)).astype(BF16)

    @pl.when(step < steps // 2)
    def _():
        send[...] = back_up

    @pl.when(step >= steps // 2)
    def _():
        own[...] = back_up

    acc[...] += dot_nt(back_up, up[0])

    @pl.when(step == steps - 1)
    def _():
        back, sums = norm_back(middle[...], gain[layer : layer + 1], acc[...])
        back = back + upstream[...]
        grads[...] = with_rows(sums_in[...], 4 * layer + 2, sums)
        back_middle[...] = back
        back_branch[...] = back.astype(BF16)
        branch_send[...] = back_branch[:, theirs]
        back_attended[...] = dot_nt(back_branch[...], matrix_out[0]).astype(BF16)


def feed_back(layer, meta, upstream, back_out, slope, up, down, middle, gain, matrix_out, sums):
    tokens, width = upstream.shape
    hidden = up.shape[2]
    tile = 512
    steps = hidden // tile
    half = steps // 2

    def place(j, m):
        return jnp.where(j < half, (1 - m[1]) * half + j, m[1] * half + j - half)

    whole = pl.BlockSpec((tokens, width), lambda j, m: (0, 0))
    narrow = pl.BlockSpec((tokens, width // 2), lambda j, m: (0, 0))
    wide = jax.ShapeDtypeStruct((tokens, width), BF16)
    return pl.pallas_call(
        functools.partial(feed_back_kernel, layer, steps),
        grid_spec=pltpu.PrefetchScalarGridSpec(
            num_scalar_prefetch=1,
            grid=(steps,),
            in_specs=[
                whole, whole, pl.BlockSpec((tokens, tile), lambda j, m: (0, place(j, m))),
                pl.BlockSpec((1, width, tile), lambda j, m: (layer, 0, place(j, m))),
                pl.BlockSpec((1, tile, width), lambda j, m: (layer, place(j, m), 0)),
                whole, pl.BlockSpec(gain.shape, lambda j, m: (0, 0)),
                pl.BlockSpec((1, width, width), lambda j, m: (layer, 0, 0)),
                pl.BlockSpec((8, width), lambda j, m: (0, 0)),
            ],
            out_specs=[
                pl.BlockSpec((tokens, tile), lambda j, m: (0, jnp.maximum(j - half, 0))),
                pl.BlockSpec((tokens, tile), lambda j, m: (0, jnp.minimum(j, half - 1))),
                whole, whole, narrow, whole,
                pl.BlockSpec((8, width), lambda j, m: (0, 0)),
            ],
            scratch_shapes=[pltpu.VMEM((tokens, width), F32)],
        ),
        out_shape=[
            jax.ShapeDtypeStruct((tokens, hidden // 2), BF16),
            jax.ShapeDtypeStruct((tokens, hidden // 2), BF16),
            pltpu.HBM((tokens, width), F32),
            wide, jax.ShapeDtypeStruct((tokens, width // 2), BF16),
            wide, jax.ShapeDtypeStruct((8, width), F32),
        ],
        compiler_params=pltpu.CompilerParams(vmem_limit_bytes=VMEM_BYTES),
        cost_estimate=SMALL_COST,
        name="feed_back",
    )(meta, *in_hbm(upstream), back_out, *in_hbm(slope, up, down, middle), gain, *in_hbm(matrix_out), sums)


def project_back_kernel(
    layer, meta, back_q, own, got, matrix, stream, gain, back_middle, sums_in,
    mine, theirs, upstream, back_out, back_out_send, grads, table, acc,
):
    step = pl.program_id(0)
    width = back_q.shape[1]

    @pl.when(step == 0)
    def _():
        table[0] = back_q[...]
        for which in range(2):
            table[1 + which] = (own[which] + got[which].astype(F32)).astype(BF16)
        half = width // 2

        @pl.when(meta[1] == 0)
        def _():
            mine[:, :width] = table[0]
            mine[:, width:] = table[1, :, :half]
            theirs[:, :half] = table[1, :, half:]
            theirs[:, half:] = table[2]

        @pl.when(meta[1] == 1)
        def _():
            theirs[:, :width] = table[0]
            theirs[:, width:] = table[1, :, :half]
            mine[:, :half] = table[1, :, half:]
            mine[:, half:] = table[2]

        acc[...] = jnp.zeros_like(acc)

    acc[...] += dot_nt(table[step], matrix[0])

    @pl.when(step == 2)
    def _():
        back, sums = norm_back(stream[...].astype(F32), gain[layer : layer + 1], acc[...])
        back = back + back_middle[...]
        upstream[...] = back.astype(upstream.dtype)
        back_out[...] = back.astype(BF16)
        half = width // 2
        back_out_send[...] = back_out[:, pl.ds(pl.multiple_of((1 - meta[1]) * half, 128), half)]
        grads[...] = with_rows(sums_in[...], 4 * layer, sums)


def project_back(layer, meta, back_q, own, got, matrix, stream, gain, back_middle, sums, kind):
    tokens, width = stream.shape
    whole = pl.BlockSpec((tokens, width), lambda j, m: (0, 0))
    both = pl.BlockSpec((2, tokens, width), lambda j, m: (0, 0, 0))
    side = pl.BlockSpec((tokens, 3 * width // 2), lambda j, m: (0, 0))
    return pl.pallas_call(
        functools.partial(project_back_kernel, layer),
        grid_spec=pltpu.PrefetchScalarGridSpec(
            num_scalar_prefetch=1,
            grid=(3,),
            in_specs=[
                whole, both, both, pl.BlockSpec((1, width, width), lambda j, m: (layer, 0, j)),
                whole, pl.BlockSpec(gain.shape, lambda j, m: (0, 0)), whole,
                pl.BlockSpec((8, width), lambda j, m: (0, 0)),
            ],
            out_specs=[side, side, whole, whole, pl.BlockSpec((tokens, width // 2), lambda j, m: (0, 0)),
                       pl.BlockSpec((8, width), lambda j, m: (0, 0))],
            scratch_shapes=[pltpu.VMEM((3, tokens, width), BF16), pltpu.VMEM((tokens, width), F32)],
        ),
        out_shape=[
            jax.ShapeDtypeStruct((tokens, 3 * width // 2), BF16),
            jax.ShapeDtypeStruct((tokens, 3 * width // 2), BF16),
            pltpu.HBM((tokens, width), kind),
            jax.ShapeDtypeStruct((tokens, width), BF16),
            jax.ShapeDtypeStruct((tokens, width // 2), BF16),
            jax.ShapeDtypeStruct((8, width), F32),
        ],
        compiler_params=pltpu.CompilerParams(vmem_limit_bytes=VMEM_BYTES),
        cost_estimate=SMALL_COST,
        name="project_back",
    )(meta, *in_hbm(back_q, own), got, *in_hbm(matrix, stream), gain, *in_hbm(back_middle), sums)


def store_chunks(chips, meta, acc, keep, send):
    rows = acc.shape[0] // chips
    for position in range(chips):
        chunk = acc[pl.ds(pl.multiple_of(meta[2 + position] * rows, 16), rows), :]
        if position < chips // 2:
            keep[position] = chunk
        else:
            send[position - chips // 2] = chunk


def grad_up_kernel(chips, meta, ao, ax, bo, bx, co, cx, do, dx, *refs):
    keep, send, acc = refs[-3:]
    step = pl.program_id(0)

    @pl.when(step < 4)
    def _():
        acc[...] = (dot_tn(ao[...], bo[...]) + dot_tn(ax[...], bx[...])).astype(BF16)

    @pl.when(step == 4)
    def _():
        acc[...] = (dot_tn(co[...], do[...]) + dot_tn(cx[...], dx[...])).astype(BF16)

    store_chunks(chips, meta, acc, keep, send)


def grad_down_kernel(chips, meta, ao, ax, bo, bx, *refs):
    keep, send = refs[-2:]
    rows = keep.shape[1]
    each = ao.shape[1] // rows
    total = (dot_tn(ao[...], bo[...]) + dot_tn(ax[...], bx[...])).astype(BF16)
    for local in range(each):
        position = meta[2 + chips + pl.program_id(0) * each + local]
        chunk = total[local * rows : (local + 1) * rows]

        @pl.when(position < chips // 2)
        def _():
            keep[position] = chunk

        @pl.when(position >= chips // 2)
        def _():
            send[position - chips // 2] = chunk


def grad_qkv_kernel(chips, meta, ao, ax, bo, bx, sums, keep, send, acc, columns):
    wide = bo.shape[1]
    acc[:, :wide] = (dot_tn(ao[...], bo[...]) + dot_tn(ax[...], bx[...])).astype(BF16)
    columns[...] = jnp.concatenate([sums[...], jnp.zeros((120, sums.shape[1]), F32)], 0).T
    acc[:, wide:] = columns[...].astype(BF16)
    store_chunks(chips, meta, acc, keep, send)


def ordered(total, ids, chips):
    split = total.astype(BF16).reshape(chips, total.shape[0] // chips, total.shape[1])
    return jnp.take(split, ids, axis=0)


def gradient_call(kernel, name, chips, grid, in_specs, out_spec, shape, scratch):
    return pl.pallas_call(
        functools.partial(kernel, chips),
        grid_spec=pltpu.PrefetchScalarGridSpec(
            num_scalar_prefetch=1, grid=(grid,), in_specs=in_specs, out_specs=[out_spec] * 2,
            scratch_shapes=scratch,
        ),
        out_shape=[pltpu.HBM(shape, BF16)] * 2,
        compiler_params=pltpu.CompilerParams(vmem_limit_bytes=VMEM_BYTES),
        cost_estimate=SMALL_COST,
        name=name,
    )


def up_gradients(
    meta, chips, normed, normed_x, back_up, back_up_x, attended, attended_x, back_branch, branch_x
):
    tokens, width = normed.shape
    half = width // 2
    rows = width // chips
    if rows % 16 != 0:
        ids = meta[2 : 2 + chips]
        up = dot_tn(normed, back_up) + dot_tn(normed_x, back_up_x)
        own = lax.dynamic_slice_in_dim(back_branch, meta[1] * half, half, 1)
        out = dot_tn(attended, own) + dot_tn(attended_x, branch_x)
        up = ordered(up, ids, chips).reshape(chips, rows, 4, half)
        up = up.transpose(0, 2, 1, 3).reshape(chips, 4 * rows, half)
        both = jnp.concatenate([up, ordered(out, ids, chips)], 1)
        return both[: chips // 2], both[chips // 2 :]
    whole = pl.BlockSpec((tokens, width), lambda j, m: (0, 0))
    fixed = pl.BlockSpec((tokens, half), lambda j, m: (0, 0))
    mine = pl.BlockSpec((tokens, half), lambda j, m: (0, m[1]))
    tile = pl.BlockSpec((tokens, half), lambda j, m: (0, jnp.minimum(j, 3)))
    return gradient_call(
        grad_up_kernel, "gradient_up", chips, 5, [whole, whole, tile, tile, whole, whole, mine, fixed],
        pl.BlockSpec((chips // 2, rows, half), lambda j, m: (0, j, 0)),
        (chips // 2, 5 * rows, half), [pltpu.VMEM((width, half), BF16)],
    )(meta, *in_hbm(normed, normed_x), back_up, back_up_x, *in_hbm(attended, attended_x), back_branch, branch_x)


def down_gradients(meta, chips, active, active_x, back_out, back_out_x):
    tokens, hidden = active.shape
    width = back_out.shape[1]
    half = width // 2
    rows = hidden // chips
    if rows % 64 != 0:
        own = lax.dynamic_slice_in_dim(back_out, meta[1] * half, half, 1)
        down = dot_tn(active, own) + dot_tn(active_x, back_out_x)
        down = ordered(down, meta[2 : 2 + chips], chips)
        return down[: chips // 2], down[chips // 2 :]
    fixed = pl.BlockSpec((tokens, half), lambda j, m: (0, 0))
    mine = pl.BlockSpec((tokens, half), lambda j, m: (0, m[1]))
    tile = pl.BlockSpec((tokens, width), lambda j, m: (0, j))
    return gradient_call(
        grad_down_kernel, "gradient_down", chips, hidden // width, [tile, tile, mine, fixed],
        pl.BlockSpec((chips // 2, rows, half), lambda j, m: (0, 0, 0)), (chips // 2, rows, half), [],
    )(meta, *in_hbm(active, active_x), back_out, back_out_x)


def qkv_gradients(meta, chips, hidden, hidden_x, back_projected, back_projected_x, sums):
    tokens, width = hidden.shape
    wide = back_projected.shape[1]
    rows = width // chips
    if rows % 16 != 0:
        qkv = dot_tn(hidden, back_projected) + dot_tn(hidden_x, back_projected_x)
        table = jnp.pad(sums.T, ((0, 0), (0, 120)))
        both = ordered(jnp.concatenate([qkv, table], -1), meta[2 : 2 + chips], chips)
        return both[: chips // 2], both[chips // 2 :]
    specs = [pl.BlockSpec((tokens, width), lambda j, m: (0, 0))] * 2
    specs += [pl.BlockSpec((tokens, wide), lambda j, m: (0, 0))] * 2
    specs += [pl.BlockSpec((8, width), lambda j, m: (0, 0))]
    return gradient_call(
        grad_qkv_kernel, "gradient_qkv", chips, 1, specs,
        pl.BlockSpec((chips // 2, rows, wide + 128), lambda j, m: (0, 0, 0)),
        (chips // 2, rows, wide + 128),
        [pltpu.VMEM((width, wide + 128), BF16), pltpu.VMEM((width, 128), F32)],
    )(meta, *in_hbm(hidden, hidden_x), back_projected, back_projected_x, sums)


class Exchange:
    def __init__(self, dp):
        self.dp = dp
        self.chips = 2 * dp
        self.bits = int(math.log2(self.chips))
        self.core_pairs = [(s, s ^ 1) for s in range(4)]
        self.mirror_pairs = [(s, 3 - s) for s in range(4)]
        rest = list(range(2, self.bits))
        self.orders = ([1, 0] + rest, [0, 1] + rest[::-1])

    def swap_core(self, value):
        return lax.ppermute(value, "seq", self.core_pairs)

    def mirror(self, value):
        return lax.ppermute(value, "seq", self.mirror_pairs)

    def pairs(self, phase):
        result = []
        for device in range(2 * self.chips):
            chip = (device // 4) * 2 + (device % 4) // 2
            core = device % 2
            other = chip ^ (1 << self.orders[core][phase])
            result.append((device, (other // 2) * 4 + (other % 2) * 2 + core))
        return result

    def tables(self, chip, core):
        index = np.arange(self.chips)
        maps = []
        for order in self.orders:
            value = np.zeros_like(index)
            for phase, bit in enumerate(order):
                value |= ((index >> (self.bits - 1 - phase)) & 1) << bit
            maps.append(value.astype(np.int32))
        ids = chip ^ jnp.where(core == 0, jnp.asarray(maps[0]), jnp.asarray(maps[1]))
        relative = jnp.asarray(index.astype(np.int32)) ^ chip
        places = []
        for order in self.orders:
            place = jnp.zeros_like(relative)
            for phase, bit in enumerate(order):
                place = place | (((relative >> bit) & 1) << (self.bits - 1 - phase))
            places.append(place)
        return ids.astype(jnp.int32), jnp.where(core == 0, places[0], places[1]).astype(jnp.int32)


class Reduction:
    def __init__(self, exchange, keep, send):
        self.exchange, self.parts, self.phase = exchange, [keep], 0
        self.first, self.kind = send, send.dtype

    def message(self):
        if self.phase == 0:
            return self.first
        size = self.parts[-1].shape[0]
        terms = [part[size // 2 : size].astype(F32) for part in self.parts]
        return functools.reduce(jnp.add, terms).astype(self.kind)

    def partner(self, phase):
        dp, seq = lax.axis_index("dp"), lax.axis_index("seq")
        core = seq % 2
        where = []
        for order in self.exchange.orders:
            bit = order[phase]
            if bit == 0:
                where.append((dp, (seq + 2) % 4))
            else:
                size = 1 << (bit - 1)
                where.append((dp + size - 2 * size * ((dp // size) % 2), seq))
        (dp0, seq0), (dp1, seq1) = where
        return dp0 + core * (dp1 - dp0), seq0 + core * (seq1 - seq0)

    def plan(self):
        phase = self.phase
        self.phase += 1
        if phase == 0:
            arrays, half, shape = [self.first], 0, self.first.shape
        else:
            half = self.parts[-1].shape[0] // 2
            arrays, shape = list(self.parts), (half,) + self.parts[-1].shape[1:]
        return dict(
            arrays=arrays, half=half, shape=shape, dtype=self.kind, partner=lambda: self.partner(phase)
        )

    def transfer(self, message):
        self.phase += 1
        return lax.ppermute(message, AXES, self.exchange.pairs(self.phase - 1))

    def arrived(self, value):
        self.parts.append(value)

    def result(self):
        while self.phase < self.exchange.bits:
            self.arrived(self.transfer(self.message()))
        return functools.reduce(jnp.add, [part[0].astype(F32) for part in self.parts])


class Move:
    def __init__(self, transfer, value):
        self.transfer, self.value = transfer, value

    def message(self):
        return self.value

    def arrived(self, value):
        self.value = value


def host(run, inputs, *moves):
    count = len(inputs)
    tied = lax.optimization_barrier(tuple(inputs) + tuple(move.message() for move in moves))
    results = tuple(run(*tied[:count]))
    got = tuple(move.transfer(message) for move, message in zip(moves, tied[count:]))
    tied = lax.optimization_barrier(results + got)
    for move, value in zip(moves, tied[len(results) :]):
        move.arrived(value)
    return tied[: len(results)]


def by_core(core, mine, theirs, axis):
    return jnp.where(
        core == 0,
        jnp.concatenate([mine, theirs], axis),
        jnp.concatenate([theirs, mine], axis),
    )


def unpack_mlp(share, rows, core, exchange):
    half, each = share.shape[1], rows // 2
    down = share[: 4 * rows].reshape(2, 4 * each, half)
    rest = share[4 * rows :].reshape(share.shape[0] // rows - 4, 2, each, half)

    def pick(which):
        return jnp.concatenate(
            [lax.dynamic_index_in_dim(down, which, 0, False),
             lax.dynamic_index_in_dim(rest, which, 1, False).reshape(-1, half)], 0)

    mine, theirs = pick(core), exchange.swap_core(pick(1 - core))

    def widen(value, start, count):
        value = value[start * each : (start + count) * each].reshape(count, each, half)
        return value.transpose(1, 0, 2).reshape(each, count * half)

    def join(start, count):
        return by_core(core, widen(mine, start, count), widen(theirs, start, count), 1)

    grad_down = by_core(core, mine[: 4 * each], theirs[: 4 * each], 1)
    return grad_down, join(4, 4), join(8, 1)


def unpack_qkv(share, core, exchange):
    rows, wide = share.shape
    split = share.reshape(2, rows // 2, wide)
    mine = lax.dynamic_index_in_dim(split, core, 0, False)
    theirs = exchange.swap_core(lax.dynamic_index_in_dim(split, 1 - core, 0, False))
    wide -= 128
    table = mine[:, wide : wide + 8] + theirs[:, wide : wide + 8]
    return by_core(core, mine[:, :wide], theirs[:, :wide], 1), table


def per_device(
    inputs, cotangent, task_table, type_counts,
    gain_one, bias_one, proj_qkv, proj_out, gain_two, bias_two, proj_up, proj_down,
):
    slots, rows, width = inputs.shape
    length = rows * lax.axis_size("seq")
    exchange = Exchange(lax.axis_size("dp"))
    place = lax.axis_index("seq")
    side, core = place // 2, place % 2
    chip = lax.axis_index("dp") * 2 + side
    low = jnp.minimum(place, 3 - place)
    own_first = place < 2
    flag = low.astype(jnp.int32).reshape(1)

    meta = jnp.concatenate([flag, core.astype(jnp.int32).reshape(1), *exchange.tables(chip, core)])

    def gather_slot(value, got):
        own = lax.dynamic_index_in_dim(value, side, 0, False)
        return jnp.where(own_first, jnp.concatenate([own, got]), jnp.concatenate([got, own]))

    choose = (task_table[:, None] == jnp.arange(TASKS, dtype=jnp.int32)[None, :]).astype(F32)
    targets = (length - type_counts[:, 0]).astype(F32)
    totals = jnp.sum(choose * targets[:, None], 0)
    bits = int(math.log2(exchange.dp))

    for bit in range(bits):
        pairs = [(d, d ^ (1 << bit)) for d in range(exchange.dp)]
        totals = totals + lax.ppermute(totals, "dp", pairs)
    got = exchange.mirror(lax.dynamic_index_in_dim(inputs, 1 - side, 0, False))
    got, totals = lax.optimization_barrier((got, totals))
    stream = gather_slot(inputs, got)
    factor = jnp.sum(totals) / TASKS / totals
    seq_weight = jnp.sum(choose * factor[None, :], 1)
    own_weight = lax.dynamic_index_in_dim(seq_weight, side, 0, False)
    own_start = lax.dynamic_index_in_dim(type_counts[:, 0], side, 0, False)
    steps = jnp.arange(rows, dtype=jnp.int32)
    query_pos = jnp.concatenate([low * rows + steps, (3 - low) * rows + steps])
    scale = jnp.where(query_pos >= own_start, own_weight, 0.0)
    chips = exchange.chips
    half = width // 2
    swap, mirror = exchange.swap_core, exchange.mirror

    def forward(layer, stream, moves_project, moves_attention, kind):
        hidden, queries, own = host(
            lambda v: project(layer, v, gain_one, bias_one, proj_qkv), (stream,), *moves_project
        )
        other = swap(own)
        hidden_x = Move(swap, hidden)
        attended, logs = host(
            attention_forward, (queries, own, other),
            hidden_x, *moves_attention
        )
        attended_x = Move(swap, attended)
        middle, normed, active, slope, output = host(
            lambda a, v: feed_forward(layer, a, v, proj_out, gain_two, bias_two, proj_up, proj_down, kind),
            (attended, stream), attended_x,
        )
        moves = Move(swap, normed), Move(swap, active)
        return output, moves, (stream, hidden, hidden_x, queries, own, other, logs, attended, attended_x, middle, normed, active, slope)

    def attention_step(layer, back_attended, moves):
        unused, unused, unused, queries, own, other, logs, attended, unused, unused, unused, unused, unused = kept[layer]
        back_q, back_own, back_other = attention_backward(
            layer, queries, own, other, back_attended, attended, logs, moves
        )
        return back_q, back_own, swap(back_other)

    def project_step(layer, back_q, back_own, back_got, back_middle, sums, moves):
        kind = BF16 if layer == 0 else F32
        return host(
            lambda q, k, kx: project_back(
                layer, meta, q, k, kx, proj_qkv, kept[layer][0], gain_one, back_middle, sums, kind
            ),
            (back_q, back_own, back_got), *moves
        )

    def feed_step(layer, upstream, back_out, sums, moves):
        middle, slope = kept[layer][9], kept[layer][12]
        return host(
            lambda u, b: feed_back(
                layer, meta, u, b, slope, proj_up, proj_down, middle, gain_two, proj_out, sums
            ),
            (upstream, back_out), *moves
        )

    def down_step(layer, back_out, back_out_x, active_x, moves):
        active = kept[layer][11]
        return Reduction(exchange, *host(
            lambda b, bx: down_gradients(meta, chips, active, active_x, b, bx), (back_out, back_out_x), *moves
        ))

    def up_step(layer, back_up, back_up_x, back_branch, branch_x, normed_x, moves):
        normed, attended, attended_x = kept[layer][10], kept[layer][7], kept[layer][8].value
        return Reduction(exchange, *host(
            lambda b, bx: up_gradients(
                meta, chips, normed, normed_x, b, bx, attended, attended_x, back_branch, branch_x
            ),
            (back_up, back_up_x), *moves
        ))

    def qkv_step(layer, mine, theirs_x, sums, moves):
        hidden, hidden_x = kept[layer][1], kept[layer][2].value
        return Reduction(exchange, *host(
            lambda b, bx: qkv_gradients(meta, chips, hidden, hidden_x, b, bx, sums), (mine, theirs_x), *moves
        ))

    got_cotangent = Move(mirror, lax.dynamic_index_in_dim(cotangent, 1 - side, 0, False))
    stream, moves, saved = forward(0, stream, (), (got_cotangent,), F32)
    kept = [saved]
    upstream = gather_slot(cotangent, got_cotangent.value).astype(F32) * scale[:, None]
    back_out = upstream.astype(BF16)
    back_out_x = Move(swap, lax.dynamic_slice_in_dim(back_out, (1 - core) * half, half, 1))
    stream, last_moves, saved = forward(1, stream, moves, (back_out_x,), BF16)
    normed_x, active_x = (move.value for move in moves)
    kept.append(saved)
    outputs_move = Move(mirror, jnp.where(own_first, stream[rows:], stream[:rows]))

    sums = jnp.zeros((8, width), F32)
    back_up, back_up_send, back_middle, back_branch, branch_send, back_attended, sums = feed_step(
        1, upstream, back_out, sums, last_moves + (outputs_move,)
    )
    last_normed_x, last_active_x = (move.value for move in last_moves)
    back_up_x, branch_x = Move(swap, back_up_send), Move(swap, branch_send)
    down1 = down_step(1, back_out, back_out_x.value, last_active_x, (back_up_x, branch_x))
    up1 = up_step(1, back_up, back_up_x.value, back_branch, branch_x.value, last_normed_x, (down1,))
    back_q, back_own, back_got = attention_step(1, back_attended, (up1,))
    mine, theirs, upstream, back_out, back_out_send, sums = project_step(
        1, back_q, back_own, back_got, back_middle, sums, (down1,)
    )
    theirs_x = Move(swap, theirs)
    down0 = down_step(0, back_out, swap(back_out_send), active_x, (theirs_x, up1, down1))
    back_up, back_up_send, back_middle, back_branch, branch_send, back_attended, sums0 = feed_step(
        0, upstream, back_out, sums, (down0, up1)
    )
    back_up_x, branch_x = Move(swap, back_up_send), Move(swap, branch_send)
    qkv1 = qkv_step(1, mine, theirs_x.value, sums, (back_up_x, branch_x, down0, down1))
    up0 = up_step(0, back_up, back_up_x.value, back_branch, branch_x.value, normed_x, (qkv1, up1))
    back_q, back_own, back_got = attention_step(0, back_attended, (up0, down0))
    mine, theirs, upstream, back_out, back_out_send, sums = project_step(
        0, back_q, back_own, back_got, back_middle, sums0, (up0, qkv1, down0)
    )
    back_move = Move(mirror, jnp.where(own_first, upstream[rows:], upstream[:rows]))
    qkv0 = qkv_step(0, mine, swap(theirs), sums, (up0, qkv1))
    unit = width // chips

    def return_slot(value, got):
        own = jnp.where(own_first, value[:rows], value[rows:])
        return jnp.where(side == 0, jnp.stack([own, got]), jnp.stack([got, own]))

    def finish_second(*unused):
        share = jnp.concatenate([down1.result(), up1.result()], 0)
        return unpack_mlp(share, unit, core, exchange)

    def finish_first(*unused):
        share = jnp.concatenate([down0.result(), up0.result()], 0)
        return unpack_mlp(share, unit, core, exchange) + unpack_qkv(qkv1.result(), core, exchange)[:1]

    down_b, up_b, out_b = host(finish_second, (down1.parts[-1],), qkv0, up0, qkv1)
    down_a, up_a, out_a, qkv_b = host(finish_first, (down0.parts[-1],), qkv0, back_move)
    outputs, grad_up, grad_down, grad_out = host(
        lambda got: (
            return_slot(stream, got), jnp.stack([up_a, up_b]), jnp.stack([down_a, down_b]), jnp.stack([out_a, out_b])
        ),
        (outputs_move.value,), qkv0,
    )
    (back_inputs,) = host(lambda got: (return_slot(upstream, got).astype(F32),), (back_move.value,), qkv0)
    qkv_a, table = unpack_qkv(qkv0.result(), core, exchange)
    table = table.T.reshape(LAYERS, 4, unit // 2)
    return (
        outputs, back_inputs, table[:, 0], table[:, 1], jnp.stack([qkv_a, qkv_b]), grad_out,
        table[:, 2], table[:, 3], grad_up, grad_down,
    )


def solution(mesh):
    tokens = P("dp", "seq", None)
    shared = P(None, AXES)
    in_specs = (tokens, tokens, P("dp"), P("dp", None)) + (P(),) * 8
    out_specs = (
        tokens, tokens, shared, shared, P(None, AXES, None), P(None, AXES, None),
        shared, shared, P(None, AXES, None), P(None, AXES, None),
    )
    return jax.shard_map(
        per_device, mesh=mesh, in_specs=in_specs, out_specs=out_specs, check_vma=False
    )
```

```python
import functools
import math

import jax
import jax.numpy as jnp
import numpy as np
from jax import lax
from jax.experimental import pallas as pl
from jax.experimental.pallas import tpu as pltpu
from jax.sharding import PartitionSpec as P

HEADS = 12
HEAD_DIM = 64
LAYERS = 2
TASKS = 3
AXES = ("dp", "seq")
F32 = jnp.float32
BF16 = jnp.bfloat16
epsilon = 1e-05
PAIRS = 2
VMEM_BYTES = 32 * 1024 * 1024
SMALL_COST = pl.CostEstimate(flops=1000, bytes_accessed=1000, transcendentals=0)


def in_hbm(*values):
    return tuple(pltpu.with_memory_space_constraint(v, pltpu.HBM) for v in values)


def dot_nn(a, b):
    return lax.dot_general(a, b, (((1,), (0,)), ((), ())), preferred_element_type=F32)


def dot_nt(a, b):
    return lax.dot_general(a, b, (((1,), (1,)), ((), ())), preferred_element_type=F32)


def dot_tn(a, b):
    return lax.dot_general(a, b, (((0,), (0,)), ((), ())), preferred_element_type=F32)


def gelu_and_slope(x):
    z = jnp.abs(x) * 0.7071067811865476
    d = 1.0 + 0.3275911 * z
    t = pl.reciprocal(d, approx=True)
    t = t * (2.0 - d * t)
    poly = t * (
        0.254829592
        + t * (-0.284496736 + t * (1.421413741 + t * (-1.453152027 + t * 1.061405429)))
    )
    bell = jnp.exp(-0.5 * x * x)
    tail = 0.5 * poly * bell
    below = jnp.where(x >= 0.0, 1.0 - tail, tail)
    return x * below, below + x * bell * 0.3989422804014327


def head_masks(scale):
    lane = lax.broadcasted_iota(jnp.int32, (1, 2 * HEAD_DIM), 1)
    first = jnp.where(lane < HEAD_DIM, scale, 0.0)
    return first.astype(BF16), (scale - first).astype(BF16)


def stacked(value, masks):
    return jnp.concatenate([value * masks[0], value * masks[1]], 0)


def merged(value):
    rows = value.shape[0] // 2
    lane = lax.broadcasted_iota(jnp.int32, (rows, 2 * HEAD_DIM), 1)
    return jnp.where(lane < HEAD_DIM, value[:rows], value[rows:])


def by_variant(meta, run):
    @pl.when(meta[0] == 0)
    def _():
        run(0)

    @pl.when(meta[0] == 1)
    def _():
        run(1)


def attention_forward_kernel(meta, q_ref, ko_ref, vo_ref, kx_ref, vx_ref, out_ref, lse_ref):
    def run_all(variant):
        for pair in range(PAIRS):
            lanes = (slice(None), slice(pair * 2 * HEAD_DIM, (pair + 1) * 2 * HEAD_DIM))
            refs = [ref.at[lanes] for ref in (q_ref, ko_ref, vo_ref, kx_ref, vx_ref, out_ref)]
            attention_forward_pair(variant, *refs, lse_ref.at[pair])

    by_variant(meta, run_all)


def attention_forward_pair(variant, q_ref, ko_ref, vo_ref, kx_ref, vx_ref, out_ref, lse_ref):
    rows = q_ref.shape[0] // 2
    masks = head_masks(1.0 / math.sqrt(HEAD_DIM))

    def run(variant):
        position = lax.broadcasted_iota(jnp.int32, (2 * rows, rows), 0) % rows
        below = lax.broadcasted_iota(jnp.int32, (2 * rows, rows), 1) <= position
        low, high = slice(0, rows), slice(rows, 2 * rows)
        if variant == 0:
            plan = [
                (low, [(ko_ref, vo_ref, low)]),
                (high, [(ko_ref, vo_ref, low), (kx_ref, vx_ref, low), (kx_ref, vx_ref, high), (ko_ref, vo_ref, high)]),
            ]
        else:
            plan = [
                (low, [(kx_ref, vx_ref, low), (ko_ref, vo_ref, low)]),
                (high, [(ko_ref, vo_ref, low), (kx_ref, vx_ref, low), (ko_ref, vo_ref, high)]),
            ]
        all_scores = []
        for span, parts in plan:
            q2 = stacked(q_ref[span, :], masks)
            all_scores.append([dot_nt(q2, keys[place, :]) for keys, unused, place in parts])
        for (span, parts), scores in zip(plan, all_scores):
            scores[-1] = jnp.where(below, scores[-1], -1e30)
            peak = jnp.max(functools.reduce(jnp.maximum, scores), -1, keepdims=True)
            total, acc = None, None
            for part, (unused, values, place) in zip(scores, parts):
                raised = jnp.exp(part - peak)
                total = raised if total is None else total + raised
                term = dot_nn(raised.astype(BF16), values[place, :])
                acc = term if acc is None else acc + term
            total = jnp.sum(total, -1, keepdims=True)
            out_ref[span, :] = merged(acc / total).astype(BF16)
            log = peak + jnp.log(total)
            lane = lax.broadcasted_iota(jnp.int32, (rows, 2 * HEAD_DIM), 1)
            lse_ref[:, span] = jnp.where(lane == 0, log[:rows], log[rows:]).T[:8, :]

    run(variant)


def attention_forward(meta, queries, own, other):
    tokens = queries.shape[0]
    pairs = HEADS // 2
    wide = 2 * HEAD_DIM * PAIRS

    def at(offset):
        return pl.BlockSpec((tokens, wide), lambda g, m: (0, offset // PAIRS + g))

    return pl.pallas_call(
        attention_forward_kernel,
        grid_spec=pltpu.PrefetchScalarGridSpec(
            num_scalar_prefetch=1,
            grid=(pairs // PAIRS,),
            in_specs=[at(0), at(0), at(pairs), at(0), at(pairs)],
            out_specs=[at(0), pl.BlockSpec((PAIRS, 8, tokens), lambda g, m: (g, 0, 0))],
        ),
        out_shape=[
            pltpu.HBM((tokens, HEADS * HEAD_DIM), BF16),
            pltpu.HBM((pairs, 8, tokens), F32),
        ],
        compiler_params=pltpu.CompilerParams(vmem_limit_bytes=VMEM_BYTES),
        cost_estimate=SMALL_COST,
        name="attention_forward",
    )(meta, *in_hbm(queries, own, own, other, other))


def attention_backward_kernel(
    meta, q_ref, ko_ref, vo_ref, kx_ref, vx_ref, do_ref, o_ref, lse_ref,
    dq_ref, own_ref, other_ref, q4, do4,
):
    def run_all(variant):
        for pair in range(PAIRS):
            lanes = (slice(None), slice(pair * 2 * HEAD_DIM, (pair + 1) * 2 * HEAD_DIM))
            refs = [ref.at[lanes] for ref in (q_ref, ko_ref, vo_ref, kx_ref, vx_ref, do_ref, o_ref)]
            grads = [ref.at[(slice(None),) + lanes] for ref in (own_ref, other_ref)]
            attention_backward_pair(
                variant, *refs, lse_ref.at[pair], dq_ref.at[lanes], *grads, q4.at[pair], do4.at[pair]
            )

    by_variant(meta, run_all)


def attention_backward_pair(
    variant, q_ref, ko_ref, vo_ref, kx_ref, vx_ref, do_ref, o_ref, lse_ref,
    dq_ref, own_ref, other_ref, q4, do4,
):
    rows = q_ref.shape[0] // 2
    scale = 1.0 / math.sqrt(HEAD_DIM)
    scaled, plain = head_masks(scale), head_masks(1.0)
    product = (do_ref[...].astype(F32) * o_ref[...].astype(F32)).T
    first = jnp.sum(product[:HEAD_DIM], 0, keepdims=True)
    second = jnp.sum(product[HEAD_DIM:], 0, keepdims=True)
    logs = lse_ref[...]
    dot_row = jnp.concatenate([first[:, :rows], second[:, :rows], first[:, rows:], second[:, rows:]], 1)
    log_row = jnp.concatenate(
        [logs[0:1, :rows], logs[1:2, :rows], logs[0:1, rows:], logs[1:2, rows:]], 1
    )
    for block in range(2):
        span = slice(block * rows, (block + 1) * rows)
        q4[2 * block * rows : 2 * (block + 1) * rows, :] = stacked(q_ref[span, :], scaled)
        do4[2 * block * rows : 2 * (block + 1) * rows, :] = stacked(do_ref[span, :], plain)

    def run(variant):
        column = lax.broadcasted_iota(jnp.int32, (rows, 2 * rows), 1) % rows
        below = lax.broadcasted_iota(jnp.int32, (rows, 2 * rows), 0) <= column
        low, high = slice(0, rows), slice(rows, 2 * rows)
        both, upper, lower = slice(0, 4 * rows), slice(2 * rows, 4 * rows), slice(0, 2 * rows)
        plan = [(0, low, lower, True), (0, low, upper, False), (1, low, upper, False), (0, high, upper, True)]
        plan.insert(3, (1, high, upper, False) if variant == 0 else (1, low, lower, False))
        keys, values, grads = (ko_ref, kx_ref), (vo_ref, vx_ref), (own_ref, other_ref)
        dq_parts = {}
        sums = {}
        ahead = {}

        def products(index):
            source, place, cols, unused = plan[index]
            ahead[index] = dot_nt(keys[source][place, :], q4[cols, :]), dot_nt(values[source][place, :], do4[cols, :])

        products(0)
        products(1)
        for index, (source, place, cols, diagonal) in enumerate(plan):
            if index + 2 < len(plan):
                products(index + 2)
            scores, back = ahead.pop(index)
            raised = jnp.exp(scores - log_row[:, cols])
            if diagonal:
                raised = jnp.where(below, raised, 0.0)
            slope = (raised * (back - dot_row[:, cols])).astype(BF16)
            slot = (source, place.start)
            terms = dot_nn(slope, q4[cols, :]), dot_nn(raised.astype(BF16), do4[cols, :])
            sums[slot] = tuple(a + b for a, b in zip(sums[slot], terms)) if slot in sums else terms
            term = dot_tn(slope, keys[source][place, :])
            dq_parts[cols.start] = dq_parts[cols.start] + term if cols.start in dq_parts else term
        for block in range(2):
            dq_ref[block * rows : (block + 1) * rows, :] = (
                merged(dq_parts[2 * block * rows]) * scale
            ).astype(BF16)
        for source in range(2):
            for place in (low, high):
                zero = jnp.zeros((rows, 2 * HEAD_DIM), F32)
                for which, value in enumerate(sums.get((source, place.start), (zero, zero))):
                    grads[source][which, place, :] = value.astype(grads[source].dtype)

    run(variant)


def attention_backward(meta, queries, own, other, back_attended, attended, logs):
    tokens = queries.shape[0]
    pairs = HEADS // 2
    wide = 2 * HEAD_DIM * PAIRS
    width = HEADS * HEAD_DIM

    def at(offset):
        return pl.BlockSpec((tokens, wide), lambda g, m: (0, offset // PAIRS + g))

    return pl.pallas_call(
        attention_backward_kernel,
        grid_spec=pltpu.PrefetchScalarGridSpec(
            num_scalar_prefetch=1,
            grid=(pairs // PAIRS,),
            in_specs=[at(0), at(0), at(pairs), at(0), at(pairs), at(0), at(0),
                      pl.BlockSpec((PAIRS, 8, tokens), lambda g, m: (g, 0, 0))],
            out_specs=[at(0)] + [pl.BlockSpec((2, tokens, wide), lambda g, m: (0, 0, g))] * 2,
            scratch_shapes=[pltpu.VMEM((PAIRS, 2 * tokens, 2 * HEAD_DIM), BF16)] * 2,
        ),
        out_shape=[
            jax.ShapeDtypeStruct((tokens, width), BF16),
            pltpu.HBM((2, tokens, width), F32),
            jax.ShapeDtypeStruct((2, tokens, width), BF16),
        ],
        compiler_params=pltpu.CompilerParams(vmem_limit_bytes=VMEM_BYTES),
        cost_estimate=SMALL_COST,
        name="attention_backward",
    )(meta, *in_hbm(queries, own, own, other, other, back_attended, attended, logs))


def normalised(rows_in):
    average = jnp.mean(rows_in, -1, keepdims=True)
    centred = rows_in - average
    inverse = lax.rsqrt(jnp.mean(centred * centred, -1, keepdims=True) + epsilon)
    return centred * inverse, inverse


def norm_back(rows_in, gain_row, back):
    unit, inverse = normalised(rows_in)
    slope = back * gain_row
    first = jnp.mean(slope, -1, keepdims=True)
    second = jnp.mean(slope * unit, -1, keepdims=True)
    return inverse * (slope - first - unit * second), (
        jnp.sum(back * unit, 0, keepdims=True), jnp.sum(back, 0, keepdims=True))


def with_rows(table, row, sums):
    index = lax.broadcasted_iota(jnp.int32, table.shape, 0)
    return jnp.where(index == row, sums[0], jnp.where(index == row + 1, sums[1], table))


def project_kernel(layer, stream, gain, shift, matrix, hidden, queries, pairs):
    step = pl.program_id(0)

    @pl.when(step == 0)
    def _():
        unit, unused = normalised(stream[...].astype(F32))
        hidden[...] = (unit * gain[layer : layer + 1] + shift[layer : layer + 1]).astype(BF16)

    out = dot_nn(hidden[...], matrix[0]).astype(BF16)

    @pl.when(step < 2)
    def _():
        pairs[...] = out

    @pl.when(step == 2)
    def _():
        queries[...] = out


def project(layer, stream, gain, shift, matrix):
    tokens, width = stream.shape
    whole = pl.BlockSpec((tokens, width), lambda j: (0, 0))
    row = pl.BlockSpec(gain.shape, lambda j: (0, 0))
    return pl.pallas_call(
        functools.partial(project_kernel, layer),
        grid=(3,),
        in_specs=[whole, row, row, pl.BlockSpec((1, width, width), lambda j: (layer, 0, (j + 1) % 3))],
        out_specs=[whole, whole, pl.BlockSpec((tokens, width), lambda j: (0, jnp.minimum(j, 1)))],
        out_shape=[
            pltpu.HBM((tokens, width), BF16),
            pltpu.HBM((tokens, width), BF16),
            pltpu.HBM((tokens, 2 * width), BF16),
        ],
        compiler_params=pltpu.CompilerParams(vmem_limit_bytes=VMEM_BYTES),
        cost_estimate=SMALL_COST,
        name="project",
    )(*in_hbm(stream), gain, shift, *in_hbm(matrix))


def feed_forward_kernel(
    layer, steps, attended, stream, matrix_out, gain, shift, up, down,
    middle, normed, active_ref, slope_ref, out, *rest,
):
    acc = rest[-1]
    step = pl.program_id(0)

    @pl.when(step == 0)
    def _():
        middle[...] = stream[...].astype(F32) + dot_nn(attended[...], matrix_out[0])
        acc[...] = middle[...]
        unit, unused = normalised(middle[...])
        normed[...] = (unit * gain[layer : layer + 1] + shift[layer : layer + 1]).astype(BF16)

    groups = 4
    rows = normed.shape[0] // groups
    raw = {}
    for group in range(groups + 1):
        if group < groups:
            raw[group] = dot_nn(normed[group * rows : (group + 1) * rows, :], up[0])
        if group > 0:
            span = slice((group - 1) * rows, group * rows)
            active, slope = gelu_and_slope(raw.pop(group - 1))
            active = active.astype(BF16)
            active_ref[span, :] = active
            slope_ref[span, :] = slope.astype(BF16)
            acc[span, :] += dot_nn(active, down[0])

    @pl.when(step == steps - 1)
    def _():
        out[...] = acc[...].astype(out.dtype)
        if len(rest) == 2:
            rest[0][...] = acc[other_block(acc.shape[0] // 2), :].astype(out.dtype)


def other_block(rows):
    return pl.ds(pl.multiple_of((1 - lax.axis_index("seq") // 2) * rows, rows), rows)


def feed_forward(layer, attended, stream, matrix_out, gain, shift, up, down, kind):
    tokens, width = stream.shape
    last = layer == LAYERS - 1
    block = pl.BlockSpec((tokens // 2, width), lambda j: (0, 0))
    hidden = up.shape[2]
    tile = 1024
    steps = hidden // tile
    whole = pl.BlockSpec((tokens, width), lambda j: (0, 0))
    row = pl.BlockSpec(gain.shape, lambda j: (0, 0))
    part = pl.BlockSpec((tokens, tile), lambda j: (0, j))
    return pl.pallas_call(
        functools.partial(feed_forward_kernel, layer, steps),
        grid=(steps,),
        in_specs=[
            whole, whole, pl.BlockSpec((1, width, width), lambda j: (layer, 0, 0)), row, row,
            pl.BlockSpec((1, width, tile), lambda j: (layer, 0, j)),
            pl.BlockSpec((1, tile, width), lambda j: (layer, j, 0)),
        ],
        out_specs=[whole, whole, part, part, whole] + [block] * last,
        out_shape=[
            pltpu.HBM((tokens, width), F32),
            pltpu.HBM((tokens, width), BF16),
            pltpu.HBM((tokens, hidden), BF16),
            pltpu.HBM((tokens, hidden), BF16),
            pltpu.HBM((tokens, width), kind),
        ] + [jax.ShapeDtypeStruct((tokens // 2, width), kind)] * last,
        scratch_shapes=[pltpu.VMEM((tokens, width), F32)],
        compiler_params=pltpu.CompilerParams(vmem_limit_bytes=VMEM_BYTES),
        cost_estimate=SMALL_COST,
        name="feed_forward",
    )(*in_hbm(attended, stream, matrix_out), gain, shift, *in_hbm(up, down))


def feed_back_kernel(
    layer, steps, meta, upstream, back_out, slope, up, down, middle, gain, matrix_out, sums_in,
    own, send, back_middle, back_branch, branch_send, back_attended, grads, acc,
):
    step = pl.program_id(0)
    half = branch_send.shape[1]
    theirs = pl.ds(pl.multiple_of((1 - meta[1]) * half, 128), half)

    @pl.when(step == 0)
    def _():
        acc[...] = jnp.zeros_like(acc)

    back_up = (dot_nt(back_out[...], down[0]) * slope[...].astype(F32)).astype(BF16)

    @pl.when(step < steps // 2)
    def _():
        send[...] = back_up

    @pl.when(step >= steps // 2)
    def _():
        own[...] = back_up

    acc[...] += dot_nt(back_up, up[0])

    @pl.when(step == steps - 1)
    def _():
        back, sums = norm_back(middle[...], gain[layer : layer + 1], acc[...])
        back = back + upstream[...]
        grads[...] = with_rows(sums_in[...], 4 * layer + 2, sums)
        back_middle[...] = back
        back_branch[...] = back.astype(BF16)
        branch_send[...] = back_branch[:, theirs]
        back_attended[...] = dot_nt(back_branch[...], matrix_out[0]).astype(BF16)


def feed_back(layer, meta, upstream, back_out, slope, up, down, middle, gain, matrix_out, sums):
    tokens, width = upstream.shape
    hidden = up.shape[2]
    tile = 512
    steps = hidden // tile
    half = steps // 2

    def place(j, m):
        return jnp.where(j < half, (1 - m[1]) * half + j, m[1] * half + j - half)

    whole = pl.BlockSpec((tokens, width), lambda j, m: (0, 0))
    narrow = pl.BlockSpec((tokens, width // 2), lambda j, m: (0, 0))
    wide = jax.ShapeDtypeStruct((tokens, width), BF16)
    return pl.pallas_call(
        functools.partial(feed_back_kernel, layer, steps),
        grid_spec=pltpu.PrefetchScalarGridSpec(
            num_scalar_prefetch=1,
            grid=(steps,),
            in_specs=[
                whole, whole, pl.BlockSpec((tokens, tile), lambda j, m: (0, place(j, m))),
                pl.BlockSpec((1, width, tile), lambda j, m: (layer, 0, place(j, m))),
                pl.BlockSpec((1, tile, width), lambda j, m: (layer, place(j, m), 0)),
                whole, pl.BlockSpec(gain.shape, lambda j, m: (0, 0)),
                pl.BlockSpec((1, width, width), lambda j, m: (layer, 0, 0)),
                pl.BlockSpec((8, width), lambda j, m: (0, 0)),
            ],
            out_specs=[
                pl.BlockSpec((tokens, tile), lambda j, m: (0, jnp.maximum(j - half, 0))),
                pl.BlockSpec((tokens, tile), lambda j, m: (0, jnp.minimum(j, half - 1))),
                whole, whole, narrow, whole,
                pl.BlockSpec((8, width), lambda j, m: (0, 0)),
            ],
            scratch_shapes=[pltpu.VMEM((tokens, width), F32)],
        ),
        out_shape=[
            jax.ShapeDtypeStruct((tokens, hidden // 2), BF16),
            jax.ShapeDtypeStruct((tokens, hidden // 2), BF16),
            pltpu.HBM((tokens, width), F32),
            wide, jax.ShapeDtypeStruct((tokens, width // 2), BF16),
            wide, jax.ShapeDtypeStruct((8, width), F32),
        ],
        compiler_params=pltpu.CompilerParams(vmem_limit_bytes=VMEM_BYTES),
        cost_estimate=SMALL_COST,
        name="feed_back",
    )(meta, *in_hbm(upstream), back_out, *in_hbm(slope, up, down, middle), gain, *in_hbm(matrix_out), sums)


def project_back_kernel(
    layer, meta, back_q, own, got, matrix, stream, gain, back_middle, sums_in,
    mine, theirs, upstream, back_out, back_out_send, grads, *rest,
):
    step = pl.program_id(0)
    width = back_q.shape[1]
    table, acc = rest[-2:]

    @pl.when(step == 0)
    def _():
        table[0] = back_q[...]
        for which in range(2):
            table[1 + which] = (own[which] + got[which].astype(F32)).astype(BF16)
        half = width // 2

        @pl.when(meta[1] == 0)
        def _():
            mine[:, :width] = table[0]
            mine[:, width:] = table[1, :, :half]
            theirs[:, :half] = table[1, :, half:]
            theirs[:, half:] = table[2]

        @pl.when(meta[1] == 1)
        def _():
            theirs[:, :width] = table[0]
            theirs[:, width:] = table[1, :, :half]
            mine[:, :half] = table[1, :, half:]
            mine[:, half:] = table[2]

        acc[...] = jnp.zeros_like(acc)

    acc[...] += dot_nt(table[step], matrix[0])

    @pl.when(step == 2)
    def _():
        back, sums = norm_back(stream[...].astype(F32), gain[layer : layer + 1], acc[...])
        back = back + back_middle[...]
        upstream[...] = back.astype(upstream.dtype)
        back_out[...] = back.astype(BF16)
        half = width // 2
        back_out_send[...] = back_out[:, pl.ds(pl.multiple_of((1 - meta[1]) * half, 128), half)]
        grads[...] = with_rows(sums_in[...], 4 * layer, sums)
        if len(rest) == 3:
            rest[0][...] = back_out[other_block(back_out.shape[0] // 2), :]


def project_back(layer, meta, back_q, own, got, matrix, stream, gain, back_middle, sums, kind):
    tokens, width = stream.shape
    whole = pl.BlockSpec((tokens, width), lambda j, m: (0, 0))
    both = pl.BlockSpec((2, tokens, width), lambda j, m: (0, 0, 0))
    side = pl.BlockSpec((tokens, 3 * width // 2), lambda j, m: (0, 0))
    return pl.pallas_call(
        functools.partial(project_back_kernel, layer),
        grid_spec=pltpu.PrefetchScalarGridSpec(
            num_scalar_prefetch=1,
            grid=(3,),
            in_specs=[
                whole, both, both, pl.BlockSpec((1, width, width), lambda j, m: (layer, 0, j)),
                whole, pl.BlockSpec(gain.shape, lambda j, m: (0, 0)), whole,
                pl.BlockSpec((8, width), lambda j, m: (0, 0)),
            ],
            out_specs=[side, side, whole, whole, pl.BlockSpec((tokens, width // 2), lambda j, m: (0, 0)),
                       pl.BlockSpec((8, width), lambda j, m: (0, 0))]
            + [pl.BlockSpec((tokens // 2, width), lambda j, m: (0, 0))] * (layer == 0),
            scratch_shapes=[pltpu.VMEM((3, tokens, width), BF16), pltpu.VMEM((tokens, width), F32)],
        ),
        out_shape=[
            jax.ShapeDtypeStruct((tokens, 3 * width // 2), BF16),
            jax.ShapeDtypeStruct((tokens, 3 * width // 2), BF16),
            pltpu.HBM((tokens, width), kind),
            jax.ShapeDtypeStruct((tokens, width), BF16),
            jax.ShapeDtypeStruct((tokens, width // 2), BF16),
            jax.ShapeDtypeStruct((8, width), F32),
        ] + [jax.ShapeDtypeStruct((tokens // 2, width), BF16)] * (layer == 0),
        compiler_params=pltpu.CompilerParams(vmem_limit_bytes=VMEM_BYTES),
        cost_estimate=SMALL_COST,
        name="project_back",
    )(meta, *in_hbm(back_q, own), got, *in_hbm(matrix, stream), gain, *in_hbm(back_middle), sums)


def weigh_kernel(weight, start, own, got, upstream, back_out, back_out_send):
    rows, half = own.shape[0], back_out_send.shape[1]
    place = lax.axis_index("seq")
    core, low = place % 2, ((place + 1) // 2) % 2
    step = lax.broadcasted_iota(jnp.int32, (rows, 1), 0)
    first = place < 2
    for which, block in enumerate((low, 3 - low)):
        span = slice(which * rows, (which + 1) * rows)
        scale = jnp.where(block * rows + step >= start[0], weight[0], 0.0)
        mine = own[...].astype(F32) if which == 0 else got[...].astype(F32)
        other = got[...].astype(F32) if which == 0 else own[...].astype(F32)
        value = jnp.where(first, mine, other) * scale
        upstream[span, :] = value
        back_out[span, :] = value.astype(BF16)
    back_out_send[...] = back_out[:, pl.ds(pl.multiple_of((1 - core) * half, 128), half)]


def weigh(weight, start, own, got):
    rows, width = own.shape
    scalar = pl.BlockSpec(memory_space=pltpu.SMEM)
    return pl.pallas_call(
        weigh_kernel,
        in_specs=[scalar, scalar, pl.BlockSpec(memory_space=pltpu.VMEM), pl.BlockSpec(memory_space=pltpu.VMEM)],
        out_specs=[pl.BlockSpec(memory_space=pltpu.VMEM)] * 3,
        out_shape=[
            jax.ShapeDtypeStruct((2 * rows, width), F32), jax.ShapeDtypeStruct((2 * rows, width), BF16),
            jax.ShapeDtypeStruct((2 * rows, width // 2), BF16),
        ],
        compiler_params=pltpu.CompilerParams(vmem_limit_bytes=VMEM_BYTES),
        cost_estimate=SMALL_COST,
        name="weigh",
    )(weight, start, own, got)


def store_chunks(chips, meta, acc, keep, send):
    rows = acc.shape[0] // chips
    for position in range(chips):
        chunk = acc[pl.ds(pl.multiple_of(meta[2 + position] * rows, 16), rows), :]
        if position < chips // 2:
            keep[position] = chunk
        else:
            send[position - chips // 2] = chunk


def grad_up_kernel(chips, meta, ao, ax, bo, bx, co, cx, do, dx, *refs):
    keep, send, acc = refs[-3:]
    step = pl.program_id(0)

    @pl.when(step < 4)
    def _():
        acc[...] = (dot_tn(ao[...], bo[...]) + dot_tn(ax[...], bx[...])).astype(BF16)

    @pl.when(step == 4)
    def _():
        acc[...] = (dot_tn(co[...], do[...]) + dot_tn(cx[...], dx[...])).astype(BF16)

    store_chunks(chips, meta, acc, keep, send)


def grad_down_kernel(chips, meta, ao, ax, bo, bx, *refs):
    keep, send = refs[-2:]
    rows = keep.shape[1]
    each = ao.shape[1] // rows
    total = (dot_tn(ao[...], bo[...]) + dot_tn(ax[...], bx[...])).astype(BF16)
    for local in range(each):
        position = meta[2 + chips + pl.program_id(0) * each + local]
        chunk = total[local * rows : (local + 1) * rows]

        @pl.when(position < chips // 2)
        def _():
            keep[position] = chunk

        @pl.when(position >= chips // 2)
        def _():
            send[position - chips // 2] = chunk


def grad_qkv_kernel(chips, meta, ao, ax, bo, bx, sums, keep, send, acc, columns):
    wide = bo.shape[1]
    acc[:, :wide] = (dot_tn(ao[...], bo[...]) + dot_tn(ax[...], bx[...])).astype(BF16)
    columns[...] = jnp.concatenate([sums[...], jnp.zeros((120, sums.shape[1]), F32)], 0).T
    acc[:, wide:] = columns[...].astype(BF16)
    store_chunks(chips, meta, acc, keep, send)


def ordered(total, ids, chips):
    split = total.astype(BF16).reshape(chips, total.shape[0] // chips, total.shape[1])
    return jnp.take(split, ids, axis=0)


def gradient_call(kernel, name, chips, grid, in_specs, out_spec, shape, scratch):
    return pl.pallas_call(
        functools.partial(kernel, chips),
        grid_spec=pltpu.PrefetchScalarGridSpec(
            num_scalar_prefetch=1, grid=(grid,), in_specs=in_specs, out_specs=[out_spec] * 2,
            scratch_shapes=scratch,
        ),
        out_shape=[pltpu.HBM(shape, BF16)] * 2,
        compiler_params=pltpu.CompilerParams(vmem_limit_bytes=VMEM_BYTES),
        cost_estimate=SMALL_COST,
        name=name,
    )


def up_gradients(
    meta, chips, normed, normed_x, back_up, back_up_x, attended, attended_x, back_branch, branch_x
):
    tokens, width = normed.shape
    half = width // 2
    rows = width // chips
    if rows % 16 != 0:
        ids = meta[2 : 2 + chips]
        up = dot_tn(normed, back_up) + dot_tn(normed_x, back_up_x)
        own = lax.dynamic_slice_in_dim(back_branch, meta[1] * half, half, 1)
        out = dot_tn(attended, own) + dot_tn(attended_x, branch_x)
        up = ordered(up, ids, chips).reshape(chips, rows, 4, half)
        up = up.transpose(0, 2, 1, 3).reshape(chips, 4 * rows, half)
        both = jnp.concatenate([up, ordered(out, ids, chips)], 1)
        return both[: chips // 2], both[chips // 2 :]
    whole = pl.BlockSpec((tokens, width), lambda j, m: (0, 0))
    fixed = pl.BlockSpec((tokens, half), lambda j, m: (0, 0))
    mine = pl.BlockSpec((tokens, half), lambda j, m: (0, m[1]))
    tile = pl.BlockSpec((tokens, half), lambda j, m: (0, jnp.minimum(j, 3)))
    return gradient_call(
        grad_up_kernel, "gradient_up", chips, 5, [whole, whole, tile, tile, whole, whole, mine, fixed],
        pl.BlockSpec((chips // 2, rows, half), lambda j, m: (0, j, 0)),
        (chips // 2, 5 * rows, half), [pltpu.VMEM((width, half), BF16)],
    )(meta, *in_hbm(normed, normed_x), back_up, back_up_x, *in_hbm(attended, attended_x), back_branch, branch_x)


def down_gradients(meta, chips, active, active_x, back_out, back_out_x):
    tokens, hidden = active.shape
    width = back_out.shape[1]
    half = width // 2
    rows = hidden // chips
    if rows % 64 != 0:
        own = lax.dynamic_slice_in_dim(back_out, meta[1] * half, half, 1)
        down = dot_tn(active, own) + dot_tn(active_x, back_out_x)
        down = ordered(down, meta[2 : 2 + chips], chips)
        return down[: chips // 2], down[chips // 2 :]
    fixed = pl.BlockSpec((tokens, half), lambda j, m: (0, 0))
    mine = pl.BlockSpec((tokens, half), lambda j, m: (0, m[1]))
    tile = pl.BlockSpec((tokens, width), lambda j, m: (0, j))
    return gradient_call(
        grad_down_kernel, "gradient_down", chips, hidden // width, [tile, tile, mine, fixed],
        pl.BlockSpec((chips // 2, rows, half), lambda j, m: (0, 0, 0)), (chips // 2, rows, half), [],
    )(meta, *in_hbm(active, active_x), back_out, back_out_x)


def qkv_gradients(meta, chips, hidden, hidden_x, back_projected, back_projected_x, sums):
    tokens, width = hidden.shape
    wide = back_projected.shape[1]
    rows = width // chips
    if rows % 16 != 0:
        qkv = dot_tn(hidden, back_projected) + dot_tn(hidden_x, back_projected_x)
        table = jnp.pad(sums.T, ((0, 0), (0, 120)))
        both = ordered(jnp.concatenate([qkv, table], -1), meta[2 : 2 + chips], chips)
        return both[: chips // 2], both[chips // 2 :]
    specs = [pl.BlockSpec((tokens, width), lambda j, m: (0, 0))] * 2
    specs += [pl.BlockSpec((tokens, wide), lambda j, m: (0, 0))] * 2
    specs += [pl.BlockSpec((8, width), lambda j, m: (0, 0))]
    return gradient_call(
        grad_qkv_kernel, "gradient_qkv", chips, 1, specs,
        pl.BlockSpec((chips // 2, rows, wide + 128), lambda j, m: (0, 0, 0)),
        (chips // 2, rows, wide + 128),
        [pltpu.VMEM((width, wide + 128), BF16), pltpu.VMEM((width, 128), F32)],
    )(meta, *in_hbm(hidden, hidden_x), back_projected, back_projected_x, sums)


class Exchange:
    def __init__(self, dp):
        self.dp = dp
        self.chips = 2 * dp
        self.bits = int(math.log2(self.chips))
        self.core_pairs = [(s, s ^ 1) for s in range(4)]
        self.mirror_pairs = [(s, 3 - s) for s in range(4)]
        rest = list(range(2, self.bits))
        self.orders = ([1, 0] + rest, [0, 1] + rest[::-1])

    def swap_core(self, value):
        return lax.ppermute(value, "seq", self.core_pairs)

    def mirror(self, value):
        return lax.ppermute(value, "seq", self.mirror_pairs)

    def pairs(self, phase):
        result = []
        for device in range(2 * self.chips):
            chip = (device // 4) * 2 + (device % 4) // 2
            core = device % 2
            other = chip ^ (1 << self.orders[core][phase])
            result.append((device, (other // 2) * 4 + (other % 2) * 2 + core))
        return result

    def tables(self, chip, core):
        index = np.arange(self.chips)
        maps = []
        for order in self.orders:
            value = np.zeros_like(index)
            for phase, bit in enumerate(order):
                value |= ((index >> (self.bits - 1 - phase)) & 1) << bit
            maps.append(value.astype(np.int32))
        ids = chip ^ jnp.where(core == 0, jnp.asarray(maps[0]), jnp.asarray(maps[1]))
        relative = jnp.asarray(index.astype(np.int32)) ^ chip
        places = []
        for order in self.orders:
            place = jnp.zeros_like(relative)
            for phase, bit in enumerate(order):
                place = place | (((relative >> bit) & 1) << (self.bits - 1 - phase))
            places.append(place)
        return ids.astype(jnp.int32), jnp.where(core == 0, places[0], places[1]).astype(jnp.int32)


class Reduction:
    def __init__(self, exchange, keep, send):
        self.exchange, self.parts, self.phase = exchange, [keep], 0
        self.first, self.kind = send, send.dtype

    def message(self):
        if self.phase == 0:
            return self.first
        size = self.parts[-1].shape[0]
        terms = [part[size // 2 : size].astype(F32) for part in self.parts]
        return functools.reduce(jnp.add, terms).astype(self.kind)

    def transfer(self, message):
        self.phase += 1
        return lax.ppermute(message, AXES, self.exchange.pairs(self.phase - 1))

    def arrived(self, value):
        self.parts.append(value)

    def result(self):
        while self.phase < self.exchange.bits:
            self.arrived(self.transfer(self.message()))
        return functools.reduce(jnp.add, [part[0].astype(F32) for part in self.parts])


class Move:
    def __init__(self, transfer, value):
        self.transfer, self.value = transfer, value

    def message(self):
        return self.value

    def arrived(self, value):
        self.value = value


def host(run, inputs, *moves):
    count = len(inputs)
    tied = lax.optimization_barrier(tuple(inputs) + tuple(move.message() for move in moves))
    results = tuple(run(*tied[:count]))
    got = tuple(move.transfer(message) for move, message in zip(moves, tied[count:]))
    tied = lax.optimization_barrier(results + got)
    for move, value in zip(moves, tied[len(results) :]):
        move.arrived(value)
    return tied[: len(results)]


def by_core(core, mine, theirs, axis):
    return jnp.where(
        core == 0,
        jnp.concatenate([mine, theirs], axis),
        jnp.concatenate([theirs, mine], axis),
    )


def unpack_mlp(share, rows, core, exchange):
    half, each = share.shape[1], rows // 2
    down = share[: 4 * rows].reshape(2, 4 * each, half)
    rest = share[4 * rows :].reshape(share.shape[0] // rows - 4, 2, each, half)

    def pick(which):
        return jnp.concatenate(
            [lax.dynamic_index_in_dim(down, which, 0, False),
             lax.dynamic_index_in_dim(rest, which, 1, False).reshape(-1, half)], 0)

    mine, theirs = pick(core), exchange.swap_core(pick(1 - core))

    def widen(value, start, count):
        value = value[start * each : (start + count) * each].reshape(count, each, half)
        return value.transpose(1, 0, 2).reshape(each, count * half)

    def join(start, count):
        return by_core(core, widen(mine, start, count), widen(theirs, start, count), 1)

    grad_down = by_core(core, mine[: 4 * each], theirs[: 4 * each], 1)
    return grad_down, join(4, 4), join(8, 1)


def unpack_qkv(share, core, exchange):
    rows, wide = share.shape
    split = share.reshape(2, rows // 2, wide)
    mine = lax.dynamic_index_in_dim(split, core, 0, False)
    theirs = exchange.swap_core(lax.dynamic_index_in_dim(split, 1 - core, 0, False))
    wide -= 128
    table = mine[:, wide : wide + 8] + theirs[:, wide : wide + 8]
    return by_core(core, mine[:, :wide], theirs[:, :wide], 1), table


def per_device(
    inputs, cotangent, task_table, type_counts,
    gain_one, bias_one, proj_qkv, proj_out, gain_two, bias_two, proj_up, proj_down,
):
    slots, rows, width = inputs.shape
    length = rows * lax.axis_size("seq")
    exchange = Exchange(lax.axis_size("dp"))
    place = lax.axis_index("seq")
    side, core = place // 2, place % 2
    chip = lax.axis_index("dp") * 2 + side
    low = jnp.minimum(place, 3 - place)
    own_first = place < 2
    flag = low.astype(jnp.int32).reshape(1)

    meta = jnp.concatenate([flag, core.astype(jnp.int32).reshape(1), *exchange.tables(chip, core)])

    def gather_slot(value, got):
        own = lax.dynamic_index_in_dim(value, side, 0, False)
        return jnp.where(own_first, jnp.concatenate([own, got]), jnp.concatenate([got, own]))

    choose = (task_table[:, None] == jnp.arange(TASKS, dtype=jnp.int32)[None, :]).astype(F32)
    targets = (length - type_counts[:, 0]).astype(F32)
    totals = jnp.sum(choose * targets[:, None], 0)
    bits = int(math.log2(exchange.dp))

    for bit in range(bits):
        pairs = [(d, d ^ (1 << bit)) for d in range(exchange.dp)]
        totals = totals + lax.ppermute(totals, "dp", pairs)
    cotangent_own, cotangent_send = (lax.dynamic_index_in_dim(cotangent, s, 0, False) for s in (side, 1 - side))
    got = exchange.mirror(lax.dynamic_index_in_dim(inputs, 1 - side, 0, False))
    got, totals, cotangent_own, cotangent_send = lax.optimization_barrier(
        (got, totals, cotangent_own, cotangent_send)
    )
    stream = gather_slot(inputs, got)
    factor = jnp.sum(totals) / TASKS / totals
    seq_weight = jnp.sum(choose * factor[None, :], 1)
    own_weight = lax.dynamic_index_in_dim(seq_weight, side, 0, False)
    own_start = lax.dynamic_index_in_dim(type_counts[:, 0], side, 0, False)
    chips = exchange.chips
    half = width // 2
    swap, mirror = exchange.swap_core, exchange.mirror

    def forward(layer, stream, moves_project, moves_attention, kind):
        hidden, queries, own = host(
            lambda v: project(layer, v, gain_one, bias_one, proj_qkv), (stream,), *moves_project
        )
        other = swap(own)
        hidden_x = Move(swap, hidden)
        attended, logs = host(
            lambda q, k, kx: attention_forward(flag, q, k, kx), (queries, own, other),
            hidden_x, *moves_attention
        )
        attended_x = Move(swap, attended)
        middle, normed, active, slope, *output = host(
            lambda a, v: feed_forward(layer, a, v, proj_out, gain_two, bias_two, proj_up, proj_down, kind),
            (attended, stream), attended_x,
        )
        moves = Move(swap, normed), Move(swap, active)
        return output, moves, (stream, hidden, hidden_x, queries, own, other, logs, attended, attended_x, middle, normed, active, slope)

    def attention_step(layer, back_attended, moves):
        unused, unused, unused, queries, own, other, logs, attended, unused, unused, unused, unused, unused = kept[layer]
        back_q, back_own, back_other = host(
            lambda b: attention_backward(flag, queries, own, other, b, attended, logs), (back_attended,), *moves
        )
        return back_q, back_own, swap(back_other)

    def project_step(layer, back_q, back_own, back_got, back_middle, sums, moves):
        kind = BF16 if layer == 0 else F32
        return host(
            lambda q, k, kx: project_back(
                layer, meta, q, k, kx, proj_qkv, kept[layer][0], gain_one, back_middle, sums, kind
            ),
            (back_q, back_own, back_got), *moves
        )

    def feed_step(layer, upstream, back_out, sums, moves):
        middle, slope = kept[layer][9], kept[layer][12]
        return host(
            lambda u, b: feed_back(
                layer, meta, u, b, slope, proj_up, proj_down, middle, gain_two, proj_out, sums
            ),
            (upstream, back_out), *moves
        )

    def down_step(layer, back_out, back_out_x, active_x, moves):
        active = kept[layer][11]
        return Reduction(exchange, *host(
            lambda b, bx: down_gradients(meta, chips, active, active_x, b, bx), (back_out, back_out_x), *moves
        ))

    def up_step(layer, back_up, back_up_x, back_branch, branch_x, normed_x, moves):
        normed, attended, attended_x = kept[layer][10], kept[layer][7], kept[layer][8].value
        return Reduction(exchange, *host(
            lambda b, bx: up_gradients(
                meta, chips, normed, normed_x, b, bx, attended, attended_x, back_branch, branch_x
            ),
            (back_up, back_up_x), *moves
        ))

    def qkv_step(layer, mine, theirs_x, sums, moves):
        hidden, hidden_x = kept[layer][1], kept[layer][2].value
        return Reduction(exchange, *host(
            lambda b, bx: qkv_gradients(meta, chips, hidden, hidden_x, b, bx, sums), (mine, theirs_x), *moves
        ))

    got_cotangent = Move(mirror, cotangent_send)
    (stream,), moves, saved = forward(0, stream, (), (got_cotangent,), F32)
    kept = [saved]
    upstream, back_out, back_out_send = weigh(
        own_weight.reshape(1), own_start.reshape(1), cotangent_own, got_cotangent.value
    )
    back_out_x = Move(swap, back_out_send)
    (stream, stream_send), last_moves, saved = forward(1, stream, moves, (back_out_x,), BF16)
    normed_x, active_x = (move.value for move in moves)
    kept.append(saved)
    outputs_move = Move(mirror, stream_send)

    sums = jnp.zeros((8, width), F32)
    back_up, back_up_send, back_middle, back_branch, branch_send, back_attended, sums = feed_step(
        1, upstream, back_out, sums, last_moves + (outputs_move,)
    )
    last_normed_x, last_active_x = (move.value for move in last_moves)
    back_up_x, branch_x = Move(swap, back_up_send), Move(swap, branch_send)
    down1 = down_step(1, back_out, back_out_x.value, last_active_x, (back_up_x, branch_x))
    up1 = up_step(1, back_up, back_up_x.value, back_branch, branch_x.value, last_normed_x, (down1,))
    back_q, back_own, back_got = attention_step(1, back_attended, (up1,))
    mine, theirs, upstream, back_out, back_out_send, sums = project_step(
        1, back_q, back_own, back_got, back_middle, sums, (down1,)
    )
    theirs_x = Move(swap, theirs)
    down0 = down_step(0, back_out, swap(back_out_send), active_x, (theirs_x, up1, down1))
    back_up, back_up_send, back_middle, back_branch, branch_send, back_attended, sums0 = feed_step(
        0, upstream, back_out, sums, (down0, up1)
    )
    back_up_x, branch_x = Move(swap, back_up_send), Move(swap, branch_send)
    qkv1 = qkv_step(1, mine, theirs_x.value, sums, (back_up_x, branch_x, down0, down1))
    up0 = up_step(0, back_up, back_up_x.value, back_branch, branch_x.value, normed_x, (qkv1, up1))
    back_q, back_own, back_got = attention_step(0, back_attended, (up0, down0))
    mine, theirs, upstream, back_out, back_out_send, sums, upstream_send = project_step(
        0, back_q, back_own, back_got, back_middle, sums0, (up0, qkv1, down0)
    )
    back_move = Move(mirror, upstream_send)
    qkv0 = qkv_step(0, mine, swap(theirs), sums, (up0, back_move))
    unit = width // chips

    def return_slot(value, got):
        own = jnp.where(own_first, value[:rows], value[rows:])
        return jnp.where(side == 0, jnp.stack([own, got]), jnp.stack([got, own]))

    def finish_second(*unused):
        share = jnp.concatenate([down1.result(), up1.result()], 0)
        return unpack_mlp(share, unit, core, exchange)

    def finish_first(*unused):
        share = jnp.concatenate([down0.result(), up0.result()], 0)
        return unpack_mlp(share, unit, core, exchange)

    down_b, up_b, out_b = host(finish_second, (down1.parts[-1],), qkv0, up0, qkv1)
    down_a, up_a, out_a = host(finish_first, (down0.parts[-1],), qkv0, qkv1)
    outputs, back_inputs, qkv_b = host(
        lambda got, back_got: (
            return_slot(stream, got), return_slot(upstream, back_got).astype(F32),
            unpack_qkv(qkv1.result(), core, exchange)[0],
        ),
        (outputs_move.value, back_move.value), qkv0,
    )
    grad_up, grad_down, grad_out = host(
        lambda *parts: tuple(jnp.stack(parts[which : which + 2]) for which in (0, 2, 4)),
        (up_a, up_b, down_a, down_b, out_a, out_b), qkv0,
    )
    qkv_a, table = unpack_qkv(qkv0.result(), core, exchange)
    table = table.T.reshape(LAYERS, 4, unit // 2)
    return (
        outputs, back_inputs, table[:, 0], table[:, 1], jnp.stack([qkv_a, qkv_b]), grad_out,
        table[:, 2], table[:, 3], grad_up, grad_down,
    )


def solution(mesh):
    tokens = P("dp", "seq", None)
    shared = P(None, AXES)
    in_specs = (tokens, tokens, P("dp"), P("dp", None)) + (P(),) * 8
    out_specs = (
        tokens, tokens, shared, shared, P(None, AXES, None), P(None, AXES, None),
        shared, shared, P(None, AXES, None), P(None, AXES, None),
    )
    return jax.shard_map(
        per_device, mesh=mesh, in_specs=in_specs, out_specs=out_specs, check_vma=False
    )
```

```python
import functools
import math

import jax
import jax.numpy as jnp
import numpy as np
from jax import lax
from jax.experimental import pallas as pl
from jax.experimental.pallas import tpu as pltpu
from jax.sharding import PartitionSpec as P

HEADS = 12
HEAD_DIM = 64
LAYERS = 2
TASKS = 3
AXES = ("dp", "seq")
F32 = jnp.float32
BF16 = jnp.bfloat16
epsilon = 1e-05
PAIRS = 2
VMEM_BYTES = 32 * 1024 * 1024
SMALL_COST = pl.CostEstimate(flops=1000, bytes_accessed=1000, transcendentals=0)


def in_hbm(*values):
    return tuple(pltpu.with_memory_space_constraint(v, pltpu.HBM) for v in values)


def dot_nn(a, b):
    return lax.dot_general(a, b, (((1,), (0,)), ((), ())), preferred_element_type=F32)


def dot_nt(a, b):
    return lax.dot_general(a, b, (((1,), (1,)), ((), ())), preferred_element_type=F32)


def dot_tn(a, b):
    return lax.dot_general(a, b, (((0,), (0,)), ((), ())), preferred_element_type=F32)


def gelu_and_slope(x):
    z = jnp.abs(x) * 0.7071067811865476
    d = 1.0 + 0.3275911 * z
    t = pl.reciprocal(d, approx=True)
    t = t * (2.0 - d * t)
    poly = t * (
        0.254829592
        + t * (-0.284496736 + t * (1.421413741 + t * (-1.453152027 + t * 1.061405429)))
    )
    bell = jnp.exp(-0.5 * x * x)
    tail = 0.5 * poly * bell
    below = jnp.where(x >= 0.0, 1.0 - tail, tail)
    return x * below, below + x * bell * 0.3989422804014327


def head_masks(scale):
    lane = lax.broadcasted_iota(jnp.int32, (1, 2 * HEAD_DIM), 1)
    first = jnp.where(lane < HEAD_DIM, scale, 0.0)
    return first.astype(BF16), (scale - first).astype(BF16)


def stacked(value, masks):
    return jnp.concatenate([value * masks[0], value * masks[1]], 0)


def merged(value):
    rows = value.shape[0] // 2
    lane = lax.broadcasted_iota(jnp.int32, (rows, 2 * HEAD_DIM), 1)
    return jnp.where(lane < HEAD_DIM, value[:rows], value[rows:])


def by_variant(meta, run):
    @pl.when(meta[0] == 0)
    def _():
        run(0)

    @pl.when(meta[0] == 1)
    def _():
        run(1)


def attention_forward_kernel(meta, q_ref, ko_ref, vo_ref, kx_ref, vx_ref, out_ref, lse_ref):
    def run_all(variant):
        for pair in range(PAIRS):
            lanes = (slice(None), slice(pair * 2 * HEAD_DIM, (pair + 1) * 2 * HEAD_DIM))
            refs = [ref.at[lanes] for ref in (q_ref, ko_ref, vo_ref, kx_ref, vx_ref, out_ref)]
            attention_forward_pair(variant, *refs, lse_ref.at[pair])

    by_variant(meta, run_all)


def attention_forward_pair(variant, q_ref, ko_ref, vo_ref, kx_ref, vx_ref, out_ref, lse_ref):
    rows = q_ref.shape[0] // 2
    masks = head_masks(1.0 / math.sqrt(HEAD_DIM))

    def run(variant):
        position = lax.broadcasted_iota(jnp.int32, (2 * rows, rows), 0) % rows
        below = lax.broadcasted_iota(jnp.int32, (2 * rows, rows), 1) <= position
        low, high = slice(0, rows), slice(rows, 2 * rows)
        if variant == 0:
            plan = [
                (low, [(ko_ref, vo_ref, low)]),
                (high, [(ko_ref, vo_ref, low), (kx_ref, vx_ref, low), (kx_ref, vx_ref, high), (ko_ref, vo_ref, high)]),
            ]
        else:
            plan = [
                (low, [(kx_ref, vx_ref, low), (ko_ref, vo_ref, low)]),
                (high, [(ko_ref, vo_ref, low), (kx_ref, vx_ref, low), (ko_ref, vo_ref, high)]),
            ]
        all_scores = []
        for span, parts in plan:
            q2 = stacked(q_ref[span, :], masks)
            all_scores.append([dot_nt(q2, keys[place, :]) for keys, unused, place in parts])
        for (span, parts), scores in zip(plan, all_scores):
            scores[-1] = jnp.where(below, scores[-1], -1e30)
            peak = jnp.max(functools.reduce(jnp.maximum, scores), -1, keepdims=True)
            total, acc = None, None
            for part, (unused, values, place) in zip(scores, parts):
                raised = jnp.exp(part - peak)
                total = raised if total is None else total + raised
                term = dot_nn(raised.astype(BF16), values[place, :])
                acc = term if acc is None else acc + term
            total = jnp.sum(total, -1, keepdims=True)
            out_ref[span, :] = merged(acc / total).astype(BF16)
            log = peak + jnp.log(total)
            lane = lax.broadcasted_iota(jnp.int32, (rows, 2 * HEAD_DIM), 1)
            lse_ref[:, span] = jnp.where(lane == 0, log[:rows], log[rows:]).T[:8, :]

    run(variant)


def attention_forward(meta, queries, own, other):
    tokens = queries.shape[0]
    pairs = HEADS // 2
    wide = 2 * HEAD_DIM * PAIRS

    def at(offset):
        return pl.BlockSpec((tokens, wide), lambda g, m: (0, offset // PAIRS + g))

    return pl.pallas_call(
        attention_forward_kernel,
        grid_spec=pltpu.PrefetchScalarGridSpec(
            num_scalar_prefetch=1,
            grid=(pairs // PAIRS,),
            in_specs=[at(0), at(0), at(pairs), at(0), at(pairs)],
            out_specs=[at(0), pl.BlockSpec((PAIRS, 8, tokens), lambda g, m: (g, 0, 0))],
        ),
        out_shape=[
            pltpu.HBM((tokens, HEADS * HEAD_DIM), BF16),
            pltpu.HBM((pairs, 8, tokens), F32),
        ],
        compiler_params=pltpu.CompilerParams(vmem_limit_bytes=VMEM_BYTES),
        cost_estimate=SMALL_COST,
        name="attention_forward",
    )(meta, *in_hbm(queries, own, own, other, other))


def attention_backward_kernel(
    meta, q_ref, ko_ref, vo_ref, kx_ref, vx_ref, do_ref, o_ref, lse_ref,
    dq_ref, own_ref, other_ref, q4, do4,
):
    def run_all(variant):
        for pair in range(PAIRS):
            lanes = (slice(None), slice(pair * 2 * HEAD_DIM, (pair + 1) * 2 * HEAD_DIM))
            refs = [ref.at[lanes] for ref in (q_ref, ko_ref, vo_ref, kx_ref, vx_ref, do_ref, o_ref)]
            grads = [ref.at[(slice(None),) + lanes] for ref in (own_ref, other_ref)]
            attention_backward_pair(
                variant, *refs, lse_ref.at[pair], dq_ref.at[lanes], *grads, q4.at[pair], do4.at[pair]
            )

    by_variant(meta, run_all)


def attention_backward_pair(
    variant, q_ref, ko_ref, vo_ref, kx_ref, vx_ref, do_ref, o_ref, lse_ref,
    dq_ref, own_ref, other_ref, q4, do4,
):
    rows = q_ref.shape[0] // 2
    scale = 1.0 / math.sqrt(HEAD_DIM)
    scaled, plain = head_masks(scale), head_masks(1.0)
    product = (do_ref[...].astype(F32) * o_ref[...].astype(F32)).T
    first = jnp.sum(product[:HEAD_DIM], 0, keepdims=True)
    second = jnp.sum(product[HEAD_DIM:], 0, keepdims=True)
    logs = lse_ref[...]
    dot_row = jnp.concatenate([first[:, :rows], second[:, :rows], first[:, rows:], second[:, rows:]], 1)
    log_row = jnp.concatenate(
        [logs[0:1, :rows], logs[1:2, :rows], logs[0:1, rows:], logs[1:2, rows:]], 1
    )
    for block in range(2):
        span = slice(block * rows, (block + 1) * rows)
        q4[2 * block * rows : 2 * (block + 1) * rows, :] = stacked(q_ref[span, :], scaled)
        do4[2 * block * rows : 2 * (block + 1) * rows, :] = stacked(do_ref[span, :], plain)

    def run(variant):
        column = lax.broadcasted_iota(jnp.int32, (rows, 2 * rows), 1) % rows
        below = lax.broadcasted_iota(jnp.int32, (rows, 2 * rows), 0) <= column
        low, high = slice(0, rows), slice(rows, 2 * rows)
        both, upper, lower = slice(0, 4 * rows), slice(2 * rows, 4 * rows), slice(0, 2 * rows)
        plan = [(0, low, lower, True), (0, low, upper, False), (1, low, upper, False), (0, high, upper, True)]
        plan.insert(3, (1, high, upper, False) if variant == 0 else (1, low, lower, False))
        keys, values, grads = (ko_ref, kx_ref), (vo_ref, vx_ref), (own_ref, other_ref)
        dq_parts = {}
        sums = {}
        ahead = {}

        def products(index):
            source, place, cols, unused = plan[index]
            ahead[index] = dot_nt(keys[source][place, :], q4[cols, :]), dot_nt(values[source][place, :], do4[cols, :])

        products(0)
        products(1)
        for index, (source, place, cols, diagonal) in enumerate(plan):
            if index + 2 < len(plan):
                products(index + 2)
            scores, back = ahead.pop(index)
            raised = jnp.exp(scores - log_row[:, cols])
            if diagonal:
                raised = jnp.where(below, raised, 0.0)
            slope = (raised * (back - dot_row[:, cols])).astype(BF16)
            slot = (source, place.start)
            terms = dot_nn(slope, q4[cols, :]), dot_nn(raised.astype(BF16), do4[cols, :])
            sums[slot] = tuple(a + b for a, b in zip(sums[slot], terms)) if slot in sums else terms
            term = dot_tn(slope, keys[source][place, :])
            dq_parts[cols.start] = dq_parts[cols.start] + term if cols.start in dq_parts else term
        for block in range(2):
            dq_ref[block * rows : (block + 1) * rows, :] = (
                merged(dq_parts[2 * block * rows]) * scale
            ).astype(BF16)
        for source in range(2):
            for place in (low, high):
                zero = jnp.zeros((rows, 2 * HEAD_DIM), F32)
                for which, value in enumerate(sums.get((source, place.start), (zero, zero))):
                    grads[source][which, place, :] = value.astype(grads[source].dtype)

    run(variant)


def attention_backward(meta, queries, own, other, back_attended, attended, logs):
    tokens = queries.shape[0]
    pairs = HEADS // 2
    wide = 2 * HEAD_DIM * PAIRS
    width = HEADS * HEAD_DIM

    def at(offset):
        return pl.BlockSpec((tokens, wide), lambda g, m: (0, offset // PAIRS + g))

    return pl.pallas_call(
        attention_backward_kernel,
        grid_spec=pltpu.PrefetchScalarGridSpec(
            num_scalar_prefetch=1,
            grid=(pairs // PAIRS,),
            in_specs=[at(0), at(0), at(pairs), at(0), at(pairs), at(0), at(0),
                      pl.BlockSpec((PAIRS, 8, tokens), lambda g, m: (g, 0, 0))],
            out_specs=[at(0)] + [pl.BlockSpec((2, tokens, wide), lambda g, m: (0, 0, g))] * 2,
            scratch_shapes=[pltpu.VMEM((PAIRS, 2 * tokens, 2 * HEAD_DIM), BF16)] * 2,
        ),
        out_shape=[
            jax.ShapeDtypeStruct((tokens, width), BF16),
            pltpu.HBM((2, tokens, width), BF16),
            jax.ShapeDtypeStruct((2, tokens, width), BF16),
        ],
        compiler_params=pltpu.CompilerParams(vmem_limit_bytes=VMEM_BYTES),
        cost_estimate=SMALL_COST,
        name="attention_backward",
    )(meta, *in_hbm(queries, own, own, other, other, back_attended, attended, logs))


def normalised(rows_in):
    average = jnp.mean(rows_in, -1, keepdims=True)
    centred = rows_in - average
    inverse = lax.rsqrt(jnp.mean(centred * centred, -1, keepdims=True) + epsilon)
    return centred * inverse, inverse


def norm_back(rows_in, gain_row, back):
    unit, inverse = normalised(rows_in)
    slope = back * gain_row
    first = jnp.mean(slope, -1, keepdims=True)
    second = jnp.mean(slope * unit, -1, keepdims=True)
    return inverse * (slope - first - unit * second), (
        jnp.sum(back * unit, 0, keepdims=True), jnp.sum(back, 0, keepdims=True))


def with_rows(table, row, sums):
    index = lax.broadcasted_iota(jnp.int32, table.shape, 0)
    return jnp.where(index == row, sums[0], jnp.where(index == row + 1, sums[1], table))


def project_kernel(layer, stream, gain, shift, matrix, hidden, queries, pairs):
    step = pl.program_id(0)

    @pl.when(step == 0)
    def _():
        unit, unused = normalised(stream[...].astype(F32))
        hidden[...] = (unit * gain[layer : layer + 1] + shift[layer : layer + 1]).astype(BF16)

    out = dot_nn(hidden[...], matrix[0]).astype(BF16)

    @pl.when(step < 2)
    def _():
        pairs[...] = out

    @pl.when(step == 2)
    def _():
        queries[...] = out


def project(layer, stream, gain, shift, matrix):
    tokens, width = stream.shape
    whole = pl.BlockSpec((tokens, width), lambda j: (0, 0))
    row = pl.BlockSpec(gain.shape, lambda j: (0, 0))
    return pl.pallas_call(
        functools.partial(project_kernel, layer),
        grid=(3,),
        in_specs=[whole, row, row, pl.BlockSpec((1, width, width), lambda j: (layer, 0, (j + 1) % 3))],
        out_specs=[whole, whole, pl.BlockSpec((tokens, width), lambda j: (0, jnp.minimum(j, 1)))],
        out_shape=[
            pltpu.HBM((tokens, width), BF16),
            pltpu.HBM((tokens, width), BF16),
            pltpu.HBM((tokens, 2 * width), BF16),
        ],
        compiler_params=pltpu.CompilerParams(vmem_limit_bytes=VMEM_BYTES),
        cost_estimate=SMALL_COST,
        name="project",
    )(*in_hbm(stream), gain, shift, *in_hbm(matrix))


def feed_forward_kernel(
    layer, steps, attended, stream, matrix_out, gain, shift, up, down,
    middle, normed, active_ref, slope_ref, out, *rest,
):
    acc = rest[-1]
    step = pl.program_id(0)

    @pl.when(step == 0)
    def _():
        acc[...] = stream[...].astype(F32) + dot_nn(attended[...], matrix_out[0])
        middle[...] = acc[...].astype(BF16)
        unit, unused = normalised(acc[...])
        normed[...] = (unit * gain[layer : layer + 1] + shift[layer : layer + 1]).astype(BF16)

    groups = 4
    rows = normed.shape[0] // groups
    raw = {}
    for group in range(groups + 1):
        if group < groups:
            raw[group] = dot_nn(normed[group * rows : (group + 1) * rows, :], up[0])
        if group > 0:
            span = slice((group - 1) * rows, group * rows)
            active, slope = gelu_and_slope(raw.pop(group - 1))
            active = active.astype(BF16)
            active_ref[span, :] = active
            slope_ref[span, :] = slope.astype(BF16)
            acc[span, :] += dot_nn(active, down[0])

    @pl.when(step == steps - 1)
    def _():
        out[...] = acc[...].astype(out.dtype)
        if len(rest) == 2:
            rest[0][...] = acc[other_block(acc.shape[0] // 2), :].astype(out.dtype)


def other_block(rows):
    return pl.ds(pl.multiple_of((1 - lax.axis_index("seq") // 2) * rows, rows), rows)


def feed_forward(layer, attended, stream, matrix_out, gain, shift, up, down):
    tokens, width = stream.shape
    last = layer == LAYERS - 1
    block = pl.BlockSpec((tokens // 2, width), lambda j: (0, 0))
    hidden = up.shape[2]
    tile = 1024
    steps = hidden // tile
    whole = pl.BlockSpec((tokens, width), lambda j: (0, 0))
    row = pl.BlockSpec(gain.shape, lambda j: (0, 0))
    part = pl.BlockSpec((tokens, tile), lambda j: (0, j))
    return pl.pallas_call(
        functools.partial(feed_forward_kernel, layer, steps),
        grid=(steps,),
        in_specs=[
            whole, whole, pl.BlockSpec((1, width, width), lambda j: (layer, 0, 0)), row, row,
            pl.BlockSpec((1, width, tile), lambda j: (layer, 0, j)),
            pl.BlockSpec((1, tile, width), lambda j: (layer, j, 0)),
        ],
        out_specs=[whole, whole, part, part, whole] + [block] * last,
        out_shape=[
            pltpu.HBM((tokens, width), BF16),
            pltpu.HBM((tokens, width), BF16),
            pltpu.HBM((tokens, hidden), BF16),
            pltpu.HBM((tokens, hidden), BF16),
            pltpu.HBM((tokens, width), BF16),
        ] + [jax.ShapeDtypeStruct((tokens // 2, width), BF16)] * last,
        scratch_shapes=[pltpu.VMEM((tokens, width), F32)],
        compiler_params=pltpu.CompilerParams(vmem_limit_bytes=VMEM_BYTES),
        cost_estimate=SMALL_COST,
        name="feed_forward",
    )(*in_hbm(attended, stream, matrix_out), gain, shift, *in_hbm(up, down))


def feed_back_kernel(
    layer, steps, meta, back_out, slope, up, down, middle, gain, matrix_out, sums_in,
    own, send, back_branch, branch_send, back_attended, grads, acc,
):
    step = pl.program_id(0)
    half = branch_send.shape[1]
    theirs = pl.ds(pl.multiple_of((1 - meta[1]) * half, 128), half)

    @pl.when(step == 0)
    def _():
        acc[...] = jnp.zeros_like(acc)

    back_up = (dot_nt(back_out[...], down[0]) * slope[...].astype(F32)).astype(BF16)

    @pl.when(step < steps // 2)
    def _():
        send[...] = back_up

    @pl.when(step >= steps // 2)
    def _():
        own[...] = back_up

    acc[...] += dot_nt(back_up, up[0])

    @pl.when(step == steps - 1)
    def _():
        back, sums = norm_back(middle[...].astype(F32), gain[layer : layer + 1], acc[...])
        back = back + back_out[...].astype(F32)
        grads[...] = with_rows(sums_in[...], 4 * layer + 2, sums)
        back_branch[...] = back.astype(BF16)
        branch_send[...] = back_branch[:, theirs]
        back_attended[...] = dot_nt(back_branch[...], matrix_out[0]).astype(BF16)


def feed_back(layer, meta, back_out, slope, up, down, middle, gain, matrix_out, sums):
    tokens, width = back_out.shape
    hidden = up.shape[2]
    tile = 512
    steps = hidden // tile
    half = steps // 2

    def place(j, m):
        return jnp.where(j < half, (1 - m[1]) * half + j, m[1] * half + j - half)

    whole = pl.BlockSpec((tokens, width), lambda j, m: (0, 0))
    narrow = pl.BlockSpec((tokens, width // 2), lambda j, m: (0, 0))
    wide = jax.ShapeDtypeStruct((tokens, width), BF16)
    return pl.pallas_call(
        functools.partial(feed_back_kernel, layer, steps),
        grid_spec=pltpu.PrefetchScalarGridSpec(
            num_scalar_prefetch=1,
            grid=(steps,),
            in_specs=[
                whole, pl.BlockSpec((tokens, tile), lambda j, m: (0, place(j, m))),
                pl.BlockSpec((1, width, tile), lambda j, m: (layer, 0, place(j, m))),
                pl.BlockSpec((1, tile, width), lambda j, m: (layer, place(j, m), 0)),
                whole, pl.BlockSpec(gain.shape, lambda j, m: (0, 0)),
                pl.BlockSpec((1, width, width), lambda j, m: (layer, 0, 0)),
                pl.BlockSpec((8, width), lambda j, m: (0, 0)),
            ],
            out_specs=[
                pl.BlockSpec((tokens, tile), lambda j, m: (0, jnp.maximum(j - half, 0))),
                pl.BlockSpec((tokens, tile), lambda j, m: (0, jnp.minimum(j, half - 1))),
                whole, narrow, whole,
                pl.BlockSpec((8, width), lambda j, m: (0, 0)),
            ],
            scratch_shapes=[pltpu.VMEM((tokens, width), F32)],
        ),
        out_shape=[
            jax.ShapeDtypeStruct((tokens, hidden // 2), BF16),
            jax.ShapeDtypeStruct((tokens, hidden // 2), BF16),
            wide, jax.ShapeDtypeStruct((tokens, width // 2), BF16),
            wide, jax.ShapeDtypeStruct((8, width), F32),
        ],
        compiler_params=pltpu.CompilerParams(vmem_limit_bytes=VMEM_BYTES),
        cost_estimate=SMALL_COST,
        name="feed_back",
    )(meta, back_out, *in_hbm(slope, up, down, middle), gain, *in_hbm(matrix_out), sums)


def project_back_kernel(
    layer, meta, back_q, own, got, matrix, stream, gain, back_middle, sums_in,
    mine, theirs, back_out, back_out_send, grads, *rest,
):
    step = pl.program_id(0)
    width = back_q.shape[1]
    table, acc = rest[-2:]

    @pl.when(step == 0)
    def _():
        table[0] = back_q[...]
        for which in range(2):
            table[1 + which] = (own[which].astype(F32) + got[which].astype(F32)).astype(BF16)
        half = width // 2

        @pl.when(meta[1] == 0)
        def _():
            mine[:, :width] = table[0]
            mine[:, width:] = table[1, :, :half]
            theirs[:, :half] = table[1, :, half:]
            theirs[:, half:] = table[2]

        @pl.when(meta[1] == 1)
        def _():
            theirs[:, :width] = table[0]
            theirs[:, width:] = table[1, :, :half]
            mine[:, :half] = table[1, :, half:]
            mine[:, half:] = table[2]

        acc[...] = jnp.zeros_like(acc)

    acc[...] += dot_nt(table[step], matrix[0])

    @pl.when(step == 2)
    def _():
        back, sums = norm_back(stream[...].astype(F32), gain[layer : layer + 1], acc[...])
        back = back + back_middle[...].astype(F32)
        back_out[...] = back.astype(BF16)
        half = width // 2
        back_out_send[...] = back_out[:, pl.ds(pl.multiple_of((1 - meta[1]) * half, 128), half)]
        grads[...] = with_rows(sums_in[...], 4 * layer, sums)
        if len(rest) == 3:
            rest[0][...] = back_out[other_block(back_out.shape[0] // 2), :]


def project_back(layer, meta, back_q, own, got, matrix, stream, gain, back_middle, sums):
    tokens, width = stream.shape
    whole = pl.BlockSpec((tokens, width), lambda j, m: (0, 0))
    both = pl.BlockSpec((2, tokens, width), lambda j, m: (0, 0, 0))
    side = pl.BlockSpec((tokens, 3 * width // 2), lambda j, m: (0, 0))
    return pl.pallas_call(
        functools.partial(project_back_kernel, layer),
        grid_spec=pltpu.PrefetchScalarGridSpec(
            num_scalar_prefetch=1,
            grid=(3,),
            in_specs=[
                whole, both, both, pl.BlockSpec((1, width, width), lambda j, m: (layer, 0, j)),
                whole, pl.BlockSpec(gain.shape, lambda j, m: (0, 0)), whole,
                pl.BlockSpec((8, width), lambda j, m: (0, 0)),
            ],
            out_specs=[side, side, whole, pl.BlockSpec((tokens, width // 2), lambda j, m: (0, 0)),
                       pl.BlockSpec((8, width), lambda j, m: (0, 0))]
            + [pl.BlockSpec((tokens // 2, width), lambda j, m: (0, 0))] * (layer == 0),
            scratch_shapes=[pltpu.VMEM((3, tokens, width), BF16), pltpu.VMEM((tokens, width), F32)],
        ),
        out_shape=[
            jax.ShapeDtypeStruct((tokens, 3 * width // 2), BF16),
            jax.ShapeDtypeStruct((tokens, 3 * width // 2), BF16),
            jax.ShapeDtypeStruct((tokens, width), BF16),
            jax.ShapeDtypeStruct((tokens, width // 2), BF16),
            jax.ShapeDtypeStruct((8, width), F32),
        ] + [jax.ShapeDtypeStruct((tokens // 2, width), BF16)] * (layer == 0),
        compiler_params=pltpu.CompilerParams(vmem_limit_bytes=VMEM_BYTES),
        cost_estimate=SMALL_COST,
        name="project_back",
    )(meta, *in_hbm(back_q, own), got, *in_hbm(matrix, stream), gain, *in_hbm(back_middle), sums)


def weigh_kernel(weight, start, own, got, back_out, back_out_send):
    rows, half = own.shape[0], back_out_send.shape[1]
    place = lax.axis_index("seq")
    core, low = place % 2, ((place + 1) // 2) % 2
    step = lax.broadcasted_iota(jnp.int32, (rows, 1), 0)
    first = place < 2
    for which, block in enumerate((low, 3 - low)):
        span = slice(which * rows, (which + 1) * rows)
        scale = jnp.where(block * rows + step >= start[0], weight[0], 0.0)
        mine = own[...].astype(F32) if which == 0 else got[...].astype(F32)
        other = got[...].astype(F32) if which == 0 else own[...].astype(F32)
        back_out[span, :] = (jnp.where(first, mine, other) * scale).astype(BF16)
    back_out_send[...] = back_out[:, pl.ds(pl.multiple_of((1 - core) * half, 128), half)]


def weigh(weight, start, own, got):
    rows, width = own.shape
    scalar = pl.BlockSpec(memory_space=pltpu.SMEM)
    return pl.pallas_call(
        weigh_kernel,
        in_specs=[scalar, scalar, pl.BlockSpec(memory_space=pltpu.VMEM), pl.BlockSpec(memory_space=pltpu.VMEM)],
        out_specs=[pl.BlockSpec(memory_space=pltpu.VMEM)] * 2,
        out_shape=[
            jax.ShapeDtypeStruct((2 * rows, width), BF16),
            jax.ShapeDtypeStruct((2 * rows, width // 2), BF16),
        ],
        compiler_params=pltpu.CompilerParams(vmem_limit_bytes=VMEM_BYTES),
        cost_estimate=SMALL_COST,
        name="weigh",
    )(weight, start, own, got)


def store_chunks(chips, meta, acc, keep, send):
    rows = acc.shape[0] // chips
    for position in range(chips):
        chunk = acc[pl.ds(pl.multiple_of(meta[2 + position] * rows, 16), rows), :]
        if position < chips // 2:
            keep[position] = chunk
        else:
            send[position - chips // 2] = chunk


def grad_up_kernel(chips, meta, ao, ax, bo, bx, co, cx, do, dx, *refs):
    keep, send, acc = refs[-3:]
    step = pl.program_id(0)

    @pl.when(step < 4)
    def _():
        acc[...] = (dot_tn(ao[...], bo[...]) + dot_tn(ax[...], bx[...])).astype(BF16)

    @pl.when(step == 4)
    def _():
        acc[...] = (dot_tn(co[...], do[...]) + dot_tn(cx[...], dx[...])).astype(BF16)

    store_chunks(chips, meta, acc, keep, send)


def grad_down_kernel(chips, meta, ao, ax, bo, bx, *refs):
    keep, send = refs[-2:]
    rows = keep.shape[1]
    each = ao.shape[1] // rows
    total = (dot_tn(ao[...], bo[...]) + dot_tn(ax[...], bx[...])).astype(BF16)
    for local in range(each):
        position = meta[2 + chips + pl.program_id(0) * each + local]
        chunk = total[local * rows : (local + 1) * rows]

        @pl.when(position < chips // 2)
        def _():
            keep[position] = chunk

        @pl.when(position >= chips // 2)
        def _():
            send[position - chips // 2] = chunk


def grad_qkv_kernel(chips, meta, ao, ax, bo, bx, sums, keep, send, acc, columns):
    wide = bo.shape[1]
    acc[:, :wide] = (dot_tn(ao[...], bo[...]) + dot_tn(ax[...], bx[...])).astype(BF16)
    columns[...] = jnp.concatenate([sums[...], jnp.zeros((120, sums.shape[1]), F32)], 0).T
    acc[:, wide:] = columns[...].astype(BF16)
    store_chunks(chips, meta, acc, keep, send)


def ordered(total, ids, chips):
    split = total.astype(BF16).reshape(chips, total.shape[0] // chips, total.shape[1])
    return jnp.take(split, ids, axis=0)


def gradient_call(kernel, name, chips, grid, in_specs, out_spec, shape, scratch):
    return pl.pallas_call(
        functools.partial(kernel, chips),
        grid_spec=pltpu.PrefetchScalarGridSpec(
            num_scalar_prefetch=1, grid=(grid,), in_specs=in_specs, out_specs=[out_spec] * 2,
            scratch_shapes=scratch,
        ),
        out_shape=[pltpu.HBM(shape, BF16)] * 2,
        compiler_params=pltpu.CompilerParams(vmem_limit_bytes=VMEM_BYTES),
        cost_estimate=SMALL_COST,
        name=name,
    )


def up_gradients(
    meta, chips, normed, normed_x, back_up, back_up_x, attended, attended_x, back_branch, branch_x
):
    tokens, width = normed.shape
    half = width // 2
    rows = width // chips
    if rows % 16 != 0:
        ids = meta[2 : 2 + chips]
        up = dot_tn(normed, back_up) + dot_tn(normed_x, back_up_x)
        own = lax.dynamic_slice_in_dim(back_branch, meta[1] * half, half, 1)
        out = dot_tn(attended, own) + dot_tn(attended_x, branch_x)
        up = ordered(up, ids, chips).reshape(chips, rows, 4, half)
        up = up.transpose(0, 2, 1, 3).reshape(chips, 4 * rows, half)
        both = jnp.concatenate([up, ordered(out, ids, chips)], 1)
        return both[: chips // 2], both[chips // 2 :]
    whole = pl.BlockSpec((tokens, width), lambda j, m: (0, 0))
    fixed = pl.BlockSpec((tokens, half), lambda j, m: (0, 0))
    mine = pl.BlockSpec((tokens, half), lambda j, m: (0, m[1]))
    tile = pl.BlockSpec((tokens, half), lambda j, m: (0, jnp.minimum(j, 3)))
    return gradient_call(
        grad_up_kernel, "gradient_up", chips, 5, [whole, whole, tile, tile, whole, whole, mine, fixed],
        pl.BlockSpec((chips // 2, rows, half), lambda j, m: (0, j, 0)),
        (chips // 2, 5 * rows, half), [pltpu.VMEM((width, half), BF16)],
    )(meta, *in_hbm(normed, normed_x), back_up, back_up_x, *in_hbm(attended, attended_x), back_branch, branch_x)


def down_gradients(meta, chips, active, active_x, back_out, back_out_x):
    tokens, hidden = active.shape
    width = back_out.shape[1]
    half = width // 2
    rows = hidden // chips
    if rows % 64 != 0:
        own = lax.dynamic_slice_in_dim(back_out, meta[1] * half, half, 1)
        down = dot_tn(active, own) + dot_tn(active_x, back_out_x)
        down = ordered(down, meta[2 : 2 + chips], chips)
        return down[: chips // 2], down[chips // 2 :]
    fixed = pl.BlockSpec((tokens, half), lambda j, m: (0, 0))
    mine = pl.BlockSpec((tokens, half), lambda j, m: (0, m[1]))
    tile = pl.BlockSpec((tokens, width), lambda j, m: (0, j))
    return gradient_call(
        grad_down_kernel, "gradient_down", chips, hidden // width, [tile, tile, mine, fixed],
        pl.BlockSpec((chips // 2, rows, half), lambda j, m: (0, 0, 0)), (chips // 2, rows, half), [],
    )(meta, *in_hbm(active, active_x), back_out, back_out_x)


def qkv_gradients(meta, chips, hidden, hidden_x, back_projected, back_projected_x, sums):
    tokens, width = hidden.shape
    wide = back_projected.shape[1]
    rows = width // chips
    if rows % 16 != 0:
        qkv = dot_tn(hidden, back_projected) + dot_tn(hidden_x, back_projected_x)
        table = jnp.pad(sums.T, ((0, 0), (0, 120)))
        both = ordered(jnp.concatenate([qkv, table], -1), meta[2 : 2 + chips], chips)
        return both[: chips // 2], both[chips // 2 :]
    specs = [pl.BlockSpec((tokens, width), lambda j, m: (0, 0))] * 2
    specs += [pl.BlockSpec((tokens, wide), lambda j, m: (0, 0))] * 2
    specs += [pl.BlockSpec((8, width), lambda j, m: (0, 0))]
    return gradient_call(
        grad_qkv_kernel, "gradient_qkv", chips, 1, specs,
        pl.BlockSpec((chips // 2, rows, wide + 128), lambda j, m: (0, 0, 0)),
        (chips // 2, rows, wide + 128),
        [pltpu.VMEM((width, wide + 128), BF16), pltpu.VMEM((width, 128), F32)],
    )(meta, *in_hbm(hidden, hidden_x), back_projected, back_projected_x, sums)


class Exchange:
    def __init__(self, dp):
        self.dp = dp
        self.chips = 2 * dp
        self.bits = int(math.log2(self.chips))
        self.core_pairs = [(s, s ^ 1) for s in range(4)]
        self.mirror_pairs = [(s, 3 - s) for s in range(4)]
        rest = list(range(2, self.bits))
        self.orders = ([1, 0] + rest, [0, 1] + rest[::-1])

    def swap_core(self, value):
        return lax.ppermute(value, "seq", self.core_pairs)

    def mirror(self, value):
        return lax.ppermute(value, "seq", self.mirror_pairs)

    def pairs(self, phase):
        result = []
        for device in range(2 * self.chips):
            chip = (device // 4) * 2 + (device % 4) // 2
            core = device % 2
            other = chip ^ (1 << self.orders[core][phase])
            result.append((device, (other // 2) * 4 + (other % 2) * 2 + core))
        return result

    def tables(self, chip, core):
        index = np.arange(self.chips)
        maps = []
        for order in self.orders:
            value = np.zeros_like(index)
            for phase, bit in enumerate(order):
                value |= ((index >> (self.bits - 1 - phase)) & 1) << bit
            maps.append(value.astype(np.int32))
        ids = chip ^ jnp.where(core == 0, jnp.asarray(maps[0]), jnp.asarray(maps[1]))
        relative = jnp.asarray(index.astype(np.int32)) ^ chip
        places = []
        for order in self.orders:
            place = jnp.zeros_like(relative)
            for phase, bit in enumerate(order):
                place = place | (((relative >> bit) & 1) << (self.bits - 1 - phase))
            places.append(place)
        return ids.astype(jnp.int32), jnp.where(core == 0, places[0], places[1]).astype(jnp.int32)


class Reduction:
    def __init__(self, exchange, keep, send):
        self.exchange, self.parts, self.phase = exchange, [keep], 0
        self.first, self.kind = send, send.dtype

    def message(self):
        if self.phase == 0:
            return self.first
        size = self.parts[-1].shape[0]
        terms = [part[size // 2 : size].astype(F32) for part in self.parts]
        return functools.reduce(jnp.add, terms).astype(self.kind)

    def transfer(self, message):
        self.phase += 1
        return lax.ppermute(message, AXES, self.exchange.pairs(self.phase - 1))

    def arrived(self, value):
        self.parts.append(value)

    def complete(self):
        while self.phase < self.exchange.bits:
            self.arrived(self.transfer(self.message()))


def total(parts):
    return functools.reduce(jnp.add, [part[0].astype(F32) for part in parts])


class Move:
    def __init__(self, transfer, value):
        self.transfer, self.value = transfer, value

    def message(self):
        return self.value

    def arrived(self, value):
        self.value = value


def host(run, inputs, *moves):
    count = len(inputs)
    tied = lax.optimization_barrier(tuple(inputs) + tuple(move.message() for move in moves))
    results = tuple(run(*tied[:count]))
    got = tuple(move.transfer(message) for move, message in zip(moves, tied[count:]))
    tied = lax.optimization_barrier(results + got)
    for move, value in zip(moves, tied[len(results) :]):
        move.arrived(value)
    return tied[: len(results)]


def by_core(core, mine, theirs, axis):
    return jnp.where(
        core == 0,
        jnp.concatenate([mine, theirs], axis),
        jnp.concatenate([theirs, mine], axis),
    )


def small_call(kernel, name, shapes, operands, scratch=()):
    def spec(value):
        if value.ndim == 3 and value.dtype == BF16:
            return pl.BlockSpec((1,) + value.shape[1:], lambda i: (0, 0, 0))
        return pl.BlockSpec(value.shape, lambda i: (0,) * value.ndim)

    return pl.pallas_call(
        kernel,
        grid=(1,),
        in_specs=[spec(value) for value in operands],
        out_specs=[spec(shape) for shape in shapes],
        out_shape=shapes,
        scratch_shapes=list(scratch),
        compiler_params=pltpu.CompilerParams(vmem_limit_bytes=VMEM_BYTES),
        cost_estimate=SMALL_COST,
        name=name,
    )(*operands)


def collect(groups):
    counts = [len(parts) for parts, unused in groups]
    units = [unit for unused, unit in groups]
    totals = [parts[0].shape[1:] for parts, unused in groups]
    wide = totals[0][1]
    half = sum(rows for rows, unused in totals) // 2

    def kernel(*refs):
        refs = list(refs)
        core = lax.axis_index("seq") % 2
        mine, theirs = refs[sum(counts) : sum(counts) + 2]
        sums = refs[sum(counts) + 2 :]
        at = 0
        for count, unit, scratch in zip(counts, units, sums):
            parts, refs = refs[:count], refs[count:]
            scratch[...] = functools.reduce(jnp.add, [part[0].astype(F32) for part in parts])
            each = unit // 2
            for start in range(0, scratch.shape[0], unit):
                span = slice(at, at + each)
                mine[span, :] = scratch[pl.ds(pl.multiple_of(start + core * each, 8), each), :]
                theirs[span, :] = scratch[pl.ds(pl.multiple_of(start + (1 - core) * each, 8), each), :]
                at += each

    shape = jax.ShapeDtypeStruct((half, wide), F32)
    operands = in_hbm(*[part for parts, unused in groups for part in parts])
    return small_call(kernel, "collect", [shape, shape], operands, [pltpu.VMEM(t, F32) for t in totals])


def place_mlp(each, mine_a, theirs_a, mine_b, theirs_b):
    half = mine_a.shape[1]

    def kernel(*refs):
        ups, downs, outs = refs[4:]
        core = lax.axis_index("seq") % 2
        for layer in range(2):
            for side, value in ((core, refs[2 * layer]), (1 - core, refs[2 * layer + 1])):
                narrow = pl.ds(pl.multiple_of(side * half, 128), half)
                downs[layer, :, narrow] = value[: 4 * each, :]
                for unit in range(4):
                    lanes = pl.ds(pl.multiple_of(side * 4 * half + unit * half, 128), half)
                    ups[layer, :, lanes] = value[(4 + unit) * each : (5 + unit) * each, :]
                outs[layer, :, narrow] = value[8 * each :, :]

    shapes = [
        jax.ShapeDtypeStruct((2, each, 8 * half), F32), jax.ShapeDtypeStruct((2, 4 * each, 2 * half), F32),
        jax.ShapeDtypeStruct((2, each, 2 * half), F32),
    ]
    return small_call(kernel, "place", shapes, (mine_a, theirs_a, mine_b, theirs_b))


def place_qkv(mine_a, theirs_a, mine_b, theirs_b):
    each, wide = mine_a.shape
    wide -= 128

    def kernel(*refs):
        out, table = refs[4:]
        core = lax.axis_index("seq") % 2
        for layer in range(2):
            for side, value in ((core, refs[2 * layer]), (1 - core, refs[2 * layer + 1])):
                out[layer, :, pl.ds(pl.multiple_of(side * wide, 128), wide)] = value[:, :wide]
        table[...] = refs[0][:, wide:] + refs[1][:, wide:]

    shapes = [jax.ShapeDtypeStruct((2, each, 2 * wide), F32), jax.ShapeDtypeStruct((each, 128), F32)]
    return small_call(kernel, "place_qkv", shapes, (mine_a, theirs_a, mine_b, theirs_b))


def unpack_mlp(share, rows, core, exchange):
    half, each = share.shape[1], rows // 2
    down = share[: 4 * rows].reshape(2, 4 * each, half)
    rest = share[4 * rows :].reshape(share.shape[0] // rows - 4, 2, each, half)

    def pick(which):
        return jnp.concatenate(
            [lax.dynamic_index_in_dim(down, which, 0, False),
             lax.dynamic_index_in_dim(rest, which, 1, False).reshape(-1, half)], 0)

    mine, theirs = pick(core), exchange.swap_core(pick(1 - core))

    def widen(value, start, count):
        value = value[start * each : (start + count) * each].reshape(count, each, half)
        return value.transpose(1, 0, 2).reshape(each, count * half)

    def join(start, count):
        return by_core(core, widen(mine, start, count), widen(theirs, start, count), 1)

    grad_down = by_core(core, mine[: 4 * each], theirs[: 4 * each], 1)
    return grad_down, join(4, 4), join(8, 1)


def unpack_qkv(share, core, exchange):
    rows, wide = share.shape
    split = share.reshape(2, rows // 2, wide)
    mine = lax.dynamic_index_in_dim(split, core, 0, False)
    theirs = exchange.swap_core(lax.dynamic_index_in_dim(split, 1 - core, 0, False))
    wide -= 128
    table = mine[:, wide : wide + 8] + theirs[:, wide : wide + 8]
    return by_core(core, mine[:, :wide], theirs[:, :wide], 1), table


def per_device(
    inputs, cotangent, task_table, type_counts,
    gain_one, bias_one, proj_qkv, proj_out, gain_two, bias_two, proj_up, proj_down,
):
    slots, rows, width = inputs.shape
    length = rows * lax.axis_size("seq")
    exchange = Exchange(lax.axis_size("dp"))
    place = lax.axis_index("seq")
    side, core = place // 2, place % 2
    chip = lax.axis_index("dp") * 2 + side
    low = jnp.minimum(place, 3 - place)
    own_first = place < 2
    flag = low.astype(jnp.int32).reshape(1)

    meta = jnp.concatenate([flag, core.astype(jnp.int32).reshape(1), *exchange.tables(chip, core)])

    def gather_slot(value, got):
        own = lax.dynamic_index_in_dim(value, side, 0, False)
        return jnp.where(own_first, jnp.concatenate([own, got]), jnp.concatenate([got, own]))

    choose = (task_table[:, None] == jnp.arange(TASKS, dtype=jnp.int32)[None, :]).astype(F32)
    targets = (length - type_counts[:, 0]).astype(F32)
    totals = jnp.sum(choose * targets[:, None], 0)
    bits = int(math.log2(exchange.dp))

    for bit in range(bits):
        pairs = [(d, d ^ (1 << bit)) for d in range(exchange.dp)]
        totals = totals + lax.ppermute(totals, "dp", pairs)
    cotangent_own, cotangent_send = (lax.dynamic_index_in_dim(cotangent, s, 0, False) for s in (side, 1 - side))
    got = exchange.mirror(lax.dynamic_index_in_dim(inputs, 1 - side, 0, False))
    got, totals, cotangent_own, cotangent_send = lax.optimization_barrier(
        (got, totals, cotangent_own, cotangent_send)
    )
    stream = gather_slot(inputs, got)
    factor = jnp.sum(totals) / TASKS / totals
    seq_weight = jnp.sum(choose * factor[None, :], 1)
    own_weight = lax.dynamic_index_in_dim(seq_weight, side, 0, False)
    own_start = lax.dynamic_index_in_dim(type_counts[:, 0], side, 0, False)
    chips = exchange.chips
    half = width // 2
    swap, mirror = exchange.swap_core, exchange.mirror

    def forward(layer, stream, moves_project, moves_attention):
        hidden, queries, own = host(
            lambda v: project(layer, v, gain_one, bias_one, proj_qkv), (stream,), *moves_project
        )
        other = swap(own)
        hidden_x = Move(swap, hidden)
        attended, logs = host(
            lambda q, k, kx: attention_forward(flag, q, k, kx), (queries, own, other),
            hidden_x, *moves_attention
        )
        attended_x = Move(swap, attended)
        middle, normed, active, slope, *output = host(
            lambda a, v: feed_forward(layer, a, v, proj_out, gain_two, bias_two, proj_up, proj_down),
            (attended, stream), attended_x,
        )
        moves = Move(swap, normed), Move(swap, active)
        return output, moves, (stream, hidden, hidden_x, queries, own, other, logs, attended, attended_x, middle, normed, active, slope)

    def attention_step(layer, back_attended, moves):
        unused, unused, unused, queries, own, other, logs, attended, unused, unused, unused, unused, unused = kept[layer]
        back_q, back_own, back_other = host(
            lambda b: attention_backward(flag, queries, own, other, b, attended, logs), (back_attended,), *moves
        )
        return back_q, back_own, swap(back_other)

    def project_step(layer, back_q, back_own, back_got, back_branch, sums, moves):
        return host(
            lambda q, k, kx: project_back(
                layer, meta, q, k, kx, proj_qkv, kept[layer][0], gain_one, back_branch, sums
            ),
            (back_q, back_own, back_got), *moves
        )

    def feed_step(layer, back_out, sums, moves):
        middle, slope = kept[layer][9], kept[layer][12]
        return host(
            lambda b: feed_back(layer, meta, b, slope, proj_up, proj_down, middle, gain_two, proj_out, sums),
            (back_out,), *moves
        )

    def down_step(layer, back_out, back_out_x, active_x, moves):
        active = kept[layer][11]
        return Reduction(exchange, *host(
            lambda b, bx: down_gradients(meta, chips, active, active_x, b, bx), (back_out, back_out_x), *moves
        ))

    def up_step(layer, back_up, back_up_x, back_branch, branch_x, normed_x, moves):
        normed, attended, attended_x = kept[layer][10], kept[layer][7], kept[layer][8].value
        return Reduction(exchange, *host(
            lambda b, bx: up_gradients(
                meta, chips, normed, normed_x, b, bx, attended, attended_x, back_branch, branch_x
            ),
            (back_up, back_up_x), *moves
        ))

    def qkv_step(layer, mine, theirs_x, sums, moves):
        hidden, hidden_x = kept[layer][1], kept[layer][2].value
        return Reduction(exchange, *host(
            lambda b, bx: qkv_gradients(meta, chips, hidden, hidden_x, b, bx, sums), (mine, theirs_x), *moves
        ))

    got_cotangent = Move(mirror, cotangent_send)
    (stream,), moves, saved = forward(0, stream, (), (got_cotangent,))
    kept = [saved]
    back_out, back_out_send = weigh(
        own_weight.reshape(1), own_start.reshape(1), cotangent_own, got_cotangent.value
    )
    back_out_x = Move(swap, back_out_send)
    (stream, stream_send), last_moves, saved = forward(1, stream, moves, (back_out_x,))
    normed_x, active_x = (move.value for move in moves)
    kept.append(saved)
    outputs_move = Move(mirror, stream_send)

    sums = jnp.zeros((8, width), F32)
    back_up, back_up_send, back_branch, branch_send, back_attended, sums = feed_step(
        1, back_out, sums, last_moves + (outputs_move,)
    )
    last_normed_x, last_active_x = (move.value for move in last_moves)
    back_up_x, branch_x = Move(swap, back_up_send), Move(swap, branch_send)
    down1 = down_step(1, back_out, back_out_x.value, last_active_x, (back_up_x, branch_x))
    up1 = up_step(1, back_up, back_up_x.value, back_branch, branch_x.value, last_normed_x, (down1,))
    back_q, back_own, back_got = attention_step(1, back_attended, (up1,))
    mine, theirs, back_out, back_out_send, sums = project_step(
        1, back_q, back_own, back_got, back_branch, sums, (down1,)
    )
    theirs_x = Move(swap, theirs)
    down0 = down_step(0, back_out, swap(back_out_send), active_x, (theirs_x, up1, down1))
    back_up, back_up_send, back_branch, branch_send, back_attended, sums0 = feed_step(
        0, back_out, sums, (down0, up1)
    )
    back_up_x, branch_x = Move(swap, back_up_send), Move(swap, branch_send)
    qkv1 = qkv_step(1, mine, theirs_x.value, sums, (back_up_x, branch_x, down0, down1))
    up0 = up_step(0, back_up, back_up_x.value, back_branch, branch_x.value, normed_x, (qkv1, up1))
    back_q, back_own, back_got = attention_step(0, back_attended, (up0, down0))
    mine, theirs, back_out, back_out_send, sums, back_send = project_step(
        0, back_q, back_own, back_got, back_branch, sums0, (up0, qkv1, down0)
    )
    back_move = Move(mirror, back_send)
    qkv0 = qkv_step(0, mine, swap(theirs), sums, (up0, back_move))
    unit = width // chips

    def return_slot(value, got):
        own = jnp.where(own_first, value[:rows], value[rows:])
        return jnp.where(side == 0, jnp.stack([own, got]), jnp.stack([got, own]))

    each = unit // 2
    if each % 8 != 0:
        for one in (down0, down1, up0, up1, qkv0, qkv1):
            one.complete()
        shares = [jnp.concatenate([total(d.parts), total(u.parts)], 0) for d, u in ((down0, up0), (down1, up1))]
        down, up, out = (
            jnp.stack(value) for value in zip(*(unpack_mlp(share, unit, core, exchange) for share in shares))
        )
        (qkv_a, table), (qkv_b, unused) = (unpack_qkv(total(one.parts), core, exchange) for one in (qkv0, qkv1))
        qkv = jnp.stack([qkv_a, qkv_b])
        outputs = return_slot(stream, outputs_move.value)
        back_inputs = return_slot(back_out, back_move.value).astype(F32)
    else:
        count = len(down1.parts)
        mine_b, theirs_b = host(
            lambda *parts: collect([(parts[:count], 8 * each), (parts[count:], unit)]),
            tuple(down1.parts) + tuple(up1.parts), qkv0, up0, qkv1,
        )
        theirs_b = Move(swap, theirs_b)
        mine_a, theirs_a = host(
            lambda *parts: collect([(parts[:count], 8 * each), (parts[count:], unit)]),
            tuple(down0.parts) + tuple(up0.parts), qkv0, qkv1, theirs_b,
        )
        theirs_a = Move(swap, theirs_a)
        mine_q, theirs_q, outputs, back_inputs = host(
            lambda got, back_got, *parts: (
                *collect([(parts, unit)]), return_slot(stream, got), return_slot(back_out, back_got).astype(F32)
            ),
            (outputs_move.value, back_move.value) + tuple(qkv1.parts), qkv0, theirs_a,
        )
        theirs_q = Move(swap, theirs_q)
        up, down, out = host(
            lambda *values: place_mlp(each, *values), (mine_a, theirs_a.value, mine_b, theirs_b.value), qkv0, theirs_q
        )
        last_q, last_theirs = collect([(qkv0.parts, unit)])
        qkv, table = place_qkv(last_q, swap(last_theirs), mine_q, theirs_q.value)
        table = table[:, :8]
    table = table.T.reshape(LAYERS, 4, each)
    return outputs, back_inputs, table[:, 0], table[:, 1], qkv, out, table[:, 2], table[:, 3], up, down


def solution(mesh):
    tokens = P("dp", "seq", None)
    shared = P(None, AXES)
    in_specs = (tokens, tokens, P("dp"), P("dp", None)) + (P(),) * 8
    out_specs = (
        tokens, tokens, shared, shared, P(None, AXES, None), P(None, AXES, None),
        shared, shared, P(None, AXES, None), P(None, AXES, None),
    )
    return jax.shard_map(
        per_device, mesh=mesh, in_specs=in_specs, out_specs=out_specs, check_vma=False
    )
```

```python
import functools
import math

import jax
import jax.numpy as jnp
import numpy as np
from jax import lax
from jax.experimental import pallas as pl
from jax.experimental.pallas import tpu as pltpu
from jax.sharding import PartitionSpec as P

HEADS = 12
HEAD_DIM = 64
LAYERS = 2
TASKS = 3
AXES = ("dp", "seq")
F32 = jnp.float32
BF16 = jnp.bfloat16
epsilon = 1e-05
PAIRS = 2
VMEM_BYTES = 32 * 1024 * 1024
SMALL_COST = pl.CostEstimate(flops=1000, bytes_accessed=1000, transcendentals=0)


def in_hbm(*values):
    return tuple(pltpu.with_memory_space_constraint(v, pltpu.HBM) for v in values)


def dot_nn(a, b):
    return lax.dot_general(a, b, (((1,), (0,)), ((), ())), preferred_element_type=F32)


def dot_nt(a, b):
    return lax.dot_general(a, b, (((1,), (1,)), ((), ())), preferred_element_type=F32)


def dot_tn(a, b):
    return lax.dot_general(a, b, (((0,), (0,)), ((), ())), preferred_element_type=F32)


def gelu_and_slope(x):
    z = jnp.abs(x) * 0.7071067811865476
    d = 1.0 + 0.3275911 * z
    t = pl.reciprocal(d, approx=True)
    t = t * (2.0 - d * t)
    poly = t * (
        0.254829592
        + t * (-0.284496736 + t * (1.421413741 + t * (-1.453152027 + t * 1.061405429)))
    )
    bell = jnp.exp(-0.5 * x * x)
    tail = 0.5 * poly * bell
    below = jnp.where(x >= 0.0, 1.0 - tail, tail)
    return x * below, below + x * bell * 0.3989422804014327


def head_masks(scale):
    lane = lax.broadcasted_iota(jnp.int32, (1, 2 * HEAD_DIM), 1)
    first = jnp.where(lane < HEAD_DIM, scale, 0.0)
    return first.astype(BF16), (scale - first).astype(BF16)


def stacked(value, masks):
    return jnp.concatenate([value * masks[0], value * masks[1]], 0)


def merged(value):
    rows = value.shape[0] // 2
    lane = lax.broadcasted_iota(jnp.int32, (rows, 2 * HEAD_DIM), 1)
    return jnp.where(lane < HEAD_DIM, value[:rows], value[rows:])


def by_variant(meta, run):
    @pl.when(meta[0] == 0)
    def _():
        run(0)

    @pl.when(meta[0] == 1)
    def _():
        run(1)


def attention_forward_kernel(meta, q_ref, ko_ref, vo_ref, kx_ref, vx_ref, out_ref, lse_ref):
    def run_all(variant):
        for pair in range(PAIRS):
            lanes = (slice(None), slice(pair * 2 * HEAD_DIM, (pair + 1) * 2 * HEAD_DIM))
            refs = [ref.at[lanes] for ref in (q_ref, ko_ref, vo_ref, kx_ref, vx_ref, out_ref)]
            attention_forward_pair(variant, *refs, lse_ref.at[pair])

    by_variant(meta, run_all)


def attention_forward_pair(variant, q_ref, ko_ref, vo_ref, kx_ref, vx_ref, out_ref, lse_ref):
    rows = q_ref.shape[0] // 2
    masks = head_masks(1.0 / math.sqrt(HEAD_DIM))

    def run(variant):
        position = lax.broadcasted_iota(jnp.int32, (2 * rows, rows), 0) % rows
        below = lax.broadcasted_iota(jnp.int32, (2 * rows, rows), 1) <= position
        low, high = slice(0, rows), slice(rows, 2 * rows)
        if variant == 0:
            plan = [
                (low, [(ko_ref, vo_ref, low)]),
                (high, [(ko_ref, vo_ref, low), (kx_ref, vx_ref, low), (kx_ref, vx_ref, high), (ko_ref, vo_ref, high)]),
            ]
        else:
            plan = [
                (low, [(kx_ref, vx_ref, low), (ko_ref, vo_ref, low)]),
                (high, [(ko_ref, vo_ref, low), (kx_ref, vx_ref, low), (ko_ref, vo_ref, high)]),
            ]
        all_scores = []
        for span, parts in plan:
            q2 = stacked(q_ref[span, :], masks)
            all_scores.append([dot_nt(q2, keys[place, :]) for keys, unused, place in parts])
        for (span, parts), scores in zip(plan, all_scores):
            scores[-1] = jnp.where(below, scores[-1], -1e30)
            peak = jnp.max(functools.reduce(jnp.maximum, scores), -1, keepdims=True)
            total, acc = None, None
            for part, (unused, values, place) in zip(scores, parts):
                raised = jnp.exp(part - peak)
                total = raised if total is None else total + raised
                term = dot_nn(raised.astype(BF16), values[place, :])
                acc = term if acc is None else acc + term
            total = jnp.sum(total, -1, keepdims=True)
            out_ref[span, :] = merged(acc / total).astype(BF16)
            log = peak + jnp.log(total)
            lane = lax.broadcasted_iota(jnp.int32, (rows, 2 * HEAD_DIM), 1)
            lse_ref[:, span] = jnp.where(lane == 0, log[:rows], log[rows:]).T[:8, :]

    run(variant)


def attention_forward(meta, queries, own, other):
    tokens = queries.shape[0]
    pairs = HEADS // 2
    wide = 2 * HEAD_DIM * PAIRS

    def at(offset):
        return pl.BlockSpec((tokens, wide), lambda g, m: (0, offset // PAIRS + g))

    return pl.pallas_call(
        attention_forward_kernel,
        grid_spec=pltpu.PrefetchScalarGridSpec(
            num_scalar_prefetch=1,
            grid=(pairs // PAIRS,),
            in_specs=[at(0), at(0), at(pairs), at(0), at(pairs)],
            out_specs=[at(0), pl.BlockSpec((PAIRS, 8, tokens), lambda g, m: (g, 0, 0))],
        ),
        out_shape=[
            pltpu.HBM((tokens, HEADS * HEAD_DIM), BF16),
            pltpu.HBM((pairs, 8, tokens), F32),
        ],
        compiler_params=pltpu.CompilerParams(vmem_limit_bytes=VMEM_BYTES),
        cost_estimate=SMALL_COST,
        name="attention_forward",
    )(meta, *in_hbm(queries, own, own, other, other))


def attention_backward_kernel(
    meta, q_ref, ko_ref, vo_ref, kx_ref, vx_ref, do_ref, o_ref, lse_ref,
    dq_ref, own_ref, other_ref, q4, do4,
):
    def run_all(variant):
        for pair in range(PAIRS):
            lanes = (slice(None), slice(pair * 2 * HEAD_DIM, (pair + 1) * 2 * HEAD_DIM))
            refs = [ref.at[lanes] for ref in (q_ref, ko_ref, vo_ref, kx_ref, vx_ref, do_ref, o_ref)]
            grads = [ref.at[(slice(None),) + lanes] for ref in (own_ref, other_ref)]
            attention_backward_pair(
                variant, *refs, lse_ref.at[pair], dq_ref.at[lanes], *grads, q4.at[pair], do4.at[pair]
            )

    by_variant(meta, run_all)


def attention_backward_pair(
    variant, q_ref, ko_ref, vo_ref, kx_ref, vx_ref, do_ref, o_ref, lse_ref,
    dq_ref, own_ref, other_ref, q4, do4,
):
    rows = q_ref.shape[0] // 2
    scale = 1.0 / math.sqrt(HEAD_DIM)
    scaled, plain = head_masks(scale), head_masks(1.0)
    product = (do_ref[...].astype(F32) * o_ref[...].astype(F32)).T
    first = jnp.sum(product[:HEAD_DIM], 0, keepdims=True)
    second = jnp.sum(product[HEAD_DIM:], 0, keepdims=True)
    logs = lse_ref[...]
    dot_row = jnp.concatenate([first[:, :rows], second[:, :rows], first[:, rows:], second[:, rows:]], 1)
    log_row = jnp.concatenate(
        [logs[0:1, :rows], logs[1:2, :rows], logs[0:1, rows:], logs[1:2, rows:]], 1
    )
    for block in range(2):
        span = slice(block * rows, (block + 1) * rows)
        q4[2 * block * rows : 2 * (block + 1) * rows, :] = stacked(q_ref[span, :], scaled)
        do4[2 * block * rows : 2 * (block + 1) * rows, :] = stacked(do_ref[span, :], plain)

    def run(variant):
        column = lax.broadcasted_iota(jnp.int32, (rows, 2 * rows), 1) % rows
        below = lax.broadcasted_iota(jnp.int32, (rows, 2 * rows), 0) <= column
        low, high = slice(0, rows), slice(rows, 2 * rows)
        both, upper, lower = slice(0, 4 * rows), slice(2 * rows, 4 * rows), slice(0, 2 * rows)
        plan = [(0, low, lower, True), (0, low, upper, False), (1, low, upper, False), (0, high, upper, True)]
        plan.insert(3, (1, high, upper, False) if variant == 0 else (1, low, lower, False))
        keys, values, grads = (ko_ref, kx_ref), (vo_ref, vx_ref), (own_ref, other_ref)
        dq_parts = {}
        sums = {}
        ahead = {}

        def products(index):
            source, place, cols, unused = plan[index]
            ahead[index] = dot_nt(keys[source][place, :], q4[cols, :]), dot_nt(values[source][place, :], do4[cols, :])

        products(0)
        products(1)
        for index, (source, place, cols, diagonal) in enumerate(plan):
            if index + 2 < len(plan):
                products(index + 2)
            scores, back = ahead.pop(index)
            raised = jnp.exp(scores - log_row[:, cols])
            if diagonal:
                raised = jnp.where(below, raised, 0.0)
            slope = (raised * (back - dot_row[:, cols])).astype(BF16)
            slot = (source, place.start)
            terms = dot_nn(slope, q4[cols, :]), dot_nn(raised.astype(BF16), do4[cols, :])
            sums[slot] = tuple(a + b for a, b in zip(sums[slot], terms)) if slot in sums else terms
            term = dot_tn(slope, keys[source][place, :])
            dq_parts[cols.start] = dq_parts[cols.start] + term if cols.start in dq_parts else term
        for block in range(2):
            dq_ref[block * rows : (block + 1) * rows, :] = (
                merged(dq_parts[2 * block * rows]) * scale
            ).astype(BF16)
        for source in range(2):
            for place in (low, high):
                zero = jnp.zeros((rows, 2 * HEAD_DIM), F32)
                for which, value in enumerate(sums.get((source, place.start), (zero, zero))):
                    grads[source][which, place, :] = value.astype(grads[source].dtype)

    run(variant)


def attention_backward(meta, queries, own, other, back_attended, attended, logs):
    tokens = queries.shape[0]
    pairs = HEADS // 2
    wide = 2 * HEAD_DIM * PAIRS
    width = HEADS * HEAD_DIM

    def at(offset):
        return pl.BlockSpec((tokens, wide), lambda g, m: (0, offset // PAIRS + g))

    return pl.pallas_call(
        attention_backward_kernel,
        grid_spec=pltpu.PrefetchScalarGridSpec(
            num_scalar_prefetch=1,
            grid=(pairs // PAIRS,),
            in_specs=[at(0), at(0), at(pairs), at(0), at(pairs), at(0), at(0),
                      pl.BlockSpec((PAIRS, 8, tokens), lambda g, m: (g, 0, 0))],
            out_specs=[at(0)] + [pl.BlockSpec((2, tokens, wide), lambda g, m: (0, 0, g))] * 2,
            scratch_shapes=[pltpu.VMEM((PAIRS, 2 * tokens, 2 * HEAD_DIM), BF16)] * 2,
        ),
        out_shape=[
            jax.ShapeDtypeStruct((tokens, width), BF16),
            pltpu.HBM((2, tokens, width), BF16),
            jax.ShapeDtypeStruct((2, tokens, width), BF16),
        ],
        compiler_params=pltpu.CompilerParams(vmem_limit_bytes=VMEM_BYTES),
        cost_estimate=SMALL_COST,
        name="attention_backward",
    )(meta, *in_hbm(queries, own, own, other, other, back_attended, attended, logs))


def normalised(rows_in):
    average = jnp.mean(rows_in, -1, keepdims=True)
    centred = rows_in - average
    inverse = lax.rsqrt(jnp.mean(centred * centred, -1, keepdims=True) + epsilon)
    return centred * inverse, inverse


def norm_back(rows_in, gain_row, back):
    unit, inverse = normalised(rows_in)
    slope = back * gain_row
    first = jnp.mean(slope, -1, keepdims=True)
    second = jnp.mean(slope * unit, -1, keepdims=True)
    return inverse * (slope - first - unit * second), (
        jnp.sum(back * unit, 0, keepdims=True), jnp.sum(back, 0, keepdims=True))


def with_rows(table, row, sums):
    index = lax.broadcasted_iota(jnp.int32, table.shape, 0)
    return jnp.where(index == row, sums[0], jnp.where(index == row + 1, sums[1], table))


def project_kernel(layer, stream, gain, shift, matrix, hidden, queries, pairs):
    step = pl.program_id(0)

    @pl.when(step == 0)
    def _():
        unit, unused = normalised(stream[...].astype(F32))
        hidden[...] = (unit * gain[layer : layer + 1] + shift[layer : layer + 1]).astype(BF16)

    out = dot_nn(hidden[...], matrix[0]).astype(BF16)

    @pl.when(step < 2)
    def _():
        pairs[...] = out

    @pl.when(step == 2)
    def _():
        queries[...] = out


def project(layer, stream, gain, shift, matrix):
    tokens, width = stream.shape
    whole = pl.BlockSpec((tokens, width), lambda j: (0, 0))
    row = pl.BlockSpec(gain.shape, lambda j: (0, 0))
    return pl.pallas_call(
        functools.partial(project_kernel, layer),
        grid=(3,),
        in_specs=[whole, row, row, pl.BlockSpec((1, width, width), lambda j: (layer, 0, (j + 1) % 3))],
        out_specs=[whole, whole, pl.BlockSpec((tokens, width), lambda j: (0, jnp.minimum(j, 1)))],
        out_shape=[
            pltpu.HBM((tokens, width), BF16),
            pltpu.HBM((tokens, width), BF16),
            pltpu.HBM((tokens, 2 * width), BF16),
        ],
        compiler_params=pltpu.CompilerParams(vmem_limit_bytes=VMEM_BYTES),
        cost_estimate=SMALL_COST,
        name="project",
    )(*in_hbm(stream), gain, shift, *in_hbm(matrix))


def feed_forward_kernel(
    layer, steps, attended, stream, matrix_out, gain, shift, up, down,
    middle, normed, active_ref, slope_ref, out, *rest,
):
    acc = rest[-1]
    step = pl.program_id(0)

    @pl.when(step == 0)
    def _():
        acc[...] = stream[...].astype(F32) + dot_nn(attended[...], matrix_out[0])
        middle[...] = acc[...].astype(BF16)
        unit, unused = normalised(acc[...])
        normed[...] = (unit * gain[layer : layer + 1] + shift[layer : layer + 1]).astype(BF16)

    groups = 4
    rows = normed.shape[0] // groups
    raw = {}
    for group in range(groups + 1):
        if group < groups:
            raw[group] = dot_nn(normed[group * rows : (group + 1) * rows, :], up[0])
        if group > 0:
            span = slice((group - 1) * rows, group * rows)
            active, slope = gelu_and_slope(raw.pop(group - 1))
            active = active.astype(BF16)
            active_ref[span, :] = active
            slope_ref[span, :] = slope.astype(BF16)
            acc[span, :] += dot_nn(active, down[0])

    @pl.when(step == steps - 1)
    def _():
        out[...] = acc[...].astype(out.dtype)
        if len(rest) == 2:
            rest[0][...] = acc[other_block(acc.shape[0] // 2), :].astype(out.dtype)


def other_block(rows):
    return pl.ds(pl.multiple_of((1 - lax.axis_index("seq") // 2) * rows, rows), rows)


def feed_forward(layer, attended, stream, matrix_out, gain, shift, up, down):
    tokens, width = stream.shape
    last = layer == LAYERS - 1
    block = pl.BlockSpec((tokens // 2, width), lambda j: (0, 0))
    hidden = up.shape[2]
    tile = 1024
    steps = hidden // tile
    whole = pl.BlockSpec((tokens, width), lambda j: (0, 0))
    row = pl.BlockSpec(gain.shape, lambda j: (0, 0))
    part = pl.BlockSpec((tokens, tile), lambda j: (0, j))
    return pl.pallas_call(
        functools.partial(feed_forward_kernel, layer, steps),
        grid=(steps,),
        in_specs=[
            whole, whole, pl.BlockSpec((1, width, width), lambda j: (layer, 0, 0)), row, row,
            pl.BlockSpec((1, width, tile), lambda j: (layer, 0, j)),
            pl.BlockSpec((1, tile, width), lambda j: (layer, j, 0)),
        ],
        out_specs=[whole, whole, part, part, whole] + [block] * last,
        out_shape=[
            pltpu.HBM((tokens, width), BF16),
            pltpu.HBM((tokens, width), BF16),
            pltpu.HBM((tokens, hidden), BF16),
            pltpu.HBM((tokens, hidden), BF16),
            pltpu.HBM((tokens, width), BF16),
        ] + [jax.ShapeDtypeStruct((tokens // 2, width), BF16)] * last,
        scratch_shapes=[pltpu.VMEM((tokens, width), F32)],
        compiler_params=pltpu.CompilerParams(vmem_limit_bytes=VMEM_BYTES),
        cost_estimate=SMALL_COST,
        name="feed_forward",
    )(*in_hbm(attended, stream, matrix_out), gain, shift, *in_hbm(up, down))


def feed_back_kernel(
    layer, steps, meta, back_out, slope, up, down, middle, gain, matrix_out, sums_in,
    own, send, back_branch, branch_send, back_attended, grads, acc,
):
    step = pl.program_id(0)
    half = branch_send.shape[1]
    theirs = pl.ds(pl.multiple_of((1 - meta[1]) * half, 128), half)

    @pl.when(step == 0)
    def _():
        acc[...] = jnp.zeros_like(acc)

    back_up = (dot_nt(back_out[...], down[0]) * slope[...].astype(F32)).astype(BF16)

    @pl.when(step < steps // 2)
    def _():
        send[...] = back_up

    @pl.when(step >= steps // 2)
    def _():
        own[...] = back_up

    acc[...] += dot_nt(back_up, up[0])

    @pl.when(step == steps - 1)
    def _():
        back, sums = norm_back(middle[...].astype(F32), gain[layer : layer + 1], acc[...])
        back = back + back_out[...].astype(F32)
        grads[...] = with_rows(sums_in[...], 4 * layer + 2, sums)
        back_branch[...] = back.astype(BF16)
        branch_send[...] = back_branch[:, theirs]
        back_attended[...] = dot_nt(back_branch[...], matrix_out[0]).astype(BF16)


def feed_back(layer, meta, back_out, slope, up, down, middle, gain, matrix_out, sums):
    tokens, width = back_out.shape
    hidden = up.shape[2]
    tile = 512
    steps = hidden // tile
    half = steps // 2

    def place(j, m):
        return jnp.where(j < half, (1 - m[1]) * half + j, m[1] * half + j - half)

    whole = pl.BlockSpec((tokens, width), lambda j, m: (0, 0))
    narrow = pl.BlockSpec((tokens, width // 2), lambda j, m: (0, 0))
    wide = jax.ShapeDtypeStruct((tokens, width), BF16)
    return pl.pallas_call(
        functools.partial(feed_back_kernel, layer, steps),
        grid_spec=pltpu.PrefetchScalarGridSpec(
            num_scalar_prefetch=1,
            grid=(steps,),
            in_specs=[
                whole, pl.BlockSpec((tokens, tile), lambda j, m: (0, place(j, m))),
                pl.BlockSpec((1, width, tile), lambda j, m: (layer, 0, place(j, m))),
                pl.BlockSpec((1, tile, width), lambda j, m: (layer, place(j, m), 0)),
                whole, pl.BlockSpec(gain.shape, lambda j, m: (0, 0)),
                pl.BlockSpec((1, width, width), lambda j, m: (layer, 0, 0)),
                pl.BlockSpec((8, width), lambda j, m: (0, 0)),
            ],
            out_specs=[
                pl.BlockSpec((tokens, tile), lambda j, m: (0, jnp.maximum(j - half, 0))),
                pl.BlockSpec((tokens, tile), lambda j, m: (0, jnp.minimum(j, half - 1))),
                whole, narrow, whole,
                pl.BlockSpec((8, width), lambda j, m: (0, 0)),
            ],
            scratch_shapes=[pltpu.VMEM((tokens, width), F32)],
        ),
        out_shape=[
            jax.ShapeDtypeStruct((tokens, hidden // 2), BF16),
            jax.ShapeDtypeStruct((tokens, hidden // 2), BF16),
            wide, jax.ShapeDtypeStruct((tokens, width // 2), BF16),
            wide, jax.ShapeDtypeStruct((8, width), F32),
        ],
        compiler_params=pltpu.CompilerParams(vmem_limit_bytes=VMEM_BYTES),
        cost_estimate=SMALL_COST,
        name="feed_back",
    )(meta, back_out, *in_hbm(slope, up, down, middle), gain, *in_hbm(matrix_out), sums)


def project_back_kernel(
    layer, meta, back_q, own, got, matrix, stream, gain, back_middle, sums_in,
    mine, theirs, back_out, back_out_send, grads, *rest,
):
    step = pl.program_id(0)
    width = back_q.shape[1]
    table, acc = rest[-2:]

    @pl.when(step == 0)
    def _():
        table[0] = back_q[...]
        for which in range(2):
            table[1 + which] = (own[which].astype(F32) + got[which].astype(F32)).astype(BF16)
        half = width // 2

        @pl.when(meta[1] == 0)
        def _():
            mine[:, :width] = table[0]
            mine[:, width:] = table[1, :, :half]
            theirs[:, :half] = table[1, :, half:]
            theirs[:, half:] = table[2]

        @pl.when(meta[1] == 1)
        def _():
            theirs[:, :width] = table[0]
            theirs[:, width:] = table[1, :, :half]
            mine[:, :half] = table[1, :, half:]
            mine[:, half:] = table[2]

        acc[...] = jnp.zeros_like(acc)

    acc[...] += dot_nt(table[step], matrix[0])

    @pl.when(step == 2)
    def _():
        back, sums = norm_back(stream[...].astype(F32), gain[layer : layer + 1], acc[...])
        back = back + back_middle[...].astype(F32)
        back_out[...] = back.astype(BF16)
        half = width // 2
        back_out_send[...] = back_out[:, pl.ds(pl.multiple_of((1 - meta[1]) * half, 128), half)]
        grads[...] = with_rows(sums_in[...], 4 * layer, sums)
        if len(rest) == 3:
            rest[0][...] = back_out[other_block(back_out.shape[0] // 2), :]


def project_back(layer, meta, back_q, own, got, matrix, stream, gain, back_middle, sums):
    tokens, width = stream.shape
    whole = pl.BlockSpec((tokens, width), lambda j, m: (0, 0))
    both = pl.BlockSpec((2, tokens, width), lambda j, m: (0, 0, 0))
    side = pl.BlockSpec((tokens, 3 * width // 2), lambda j, m: (0, 0))
    return pl.pallas_call(
        functools.partial(project_back_kernel, layer),
        grid_spec=pltpu.PrefetchScalarGridSpec(
            num_scalar_prefetch=1,
            grid=(3,),
            in_specs=[
                whole, both, both, pl.BlockSpec((1, width, width), lambda j, m: (layer, 0, j)),
                whole, pl.BlockSpec(gain.shape, lambda j, m: (0, 0)), whole,
                pl.BlockSpec((8, width), lambda j, m: (0, 0)),
            ],
            out_specs=[side, side, whole, pl.BlockSpec((tokens, width // 2), lambda j, m: (0, 0)),
                       pl.BlockSpec((8, width), lambda j, m: (0, 0))]
            + [pl.BlockSpec((tokens // 2, width), lambda j, m: (0, 0))] * (layer == 0),
            scratch_shapes=[pltpu.VMEM((3, tokens, width), BF16), pltpu.VMEM((tokens, width), F32)],
        ),
        out_shape=[
            jax.ShapeDtypeStruct((tokens, 3 * width // 2), BF16),
            jax.ShapeDtypeStruct((tokens, 3 * width // 2), BF16),
            jax.ShapeDtypeStruct((tokens, width), BF16),
            jax.ShapeDtypeStruct((tokens, width // 2), BF16),
            jax.ShapeDtypeStruct((8, width), F32),
        ] + [jax.ShapeDtypeStruct((tokens // 2, width), BF16)] * (layer == 0),
        compiler_params=pltpu.CompilerParams(vmem_limit_bytes=VMEM_BYTES),
        cost_estimate=SMALL_COST,
        name="project_back",
    )(meta, *in_hbm(back_q, own), got, *in_hbm(matrix, stream), gain, *in_hbm(back_middle), sums)


def weigh_kernel(weight, start, own, got, back_out, back_out_send):
    rows, half = own.shape[0], back_out_send.shape[1]
    place = lax.axis_index("seq")
    core, low = place % 2, ((place + 1) // 2) % 2
    step = lax.broadcasted_iota(jnp.int32, (rows, 1), 0)
    first = place < 2
    for which, block in enumerate((low, 3 - low)):
        span = slice(which * rows, (which + 1) * rows)
        scale = jnp.where(block * rows + step >= start[0], weight[0], 0.0)
        mine = own[...].astype(F32) if which == 0 else got[...].astype(F32)
        other = got[...].astype(F32) if which == 0 else own[...].astype(F32)
        back_out[span, :] = (jnp.where(first, mine, other) * scale).astype(BF16)
    back_out_send[...] = back_out[:, pl.ds(pl.multiple_of((1 - core) * half, 128), half)]


def weigh(weight, start, own, got):
    rows, width = own.shape
    scalar = pl.BlockSpec(memory_space=pltpu.SMEM)
    return pl.pallas_call(
        weigh_kernel,
        in_specs=[scalar, scalar, pl.BlockSpec(memory_space=pltpu.VMEM), pl.BlockSpec(memory_space=pltpu.VMEM)],
        out_specs=[pl.BlockSpec(memory_space=pltpu.VMEM)] * 2,
        out_shape=[
            jax.ShapeDtypeStruct((2 * rows, width), BF16),
            jax.ShapeDtypeStruct((2 * rows, width // 2), BF16),
        ],
        compiler_params=pltpu.CompilerParams(vmem_limit_bytes=VMEM_BYTES),
        cost_estimate=SMALL_COST,
        name="weigh",
    )(weight, start, own, got)


def store_chunks(chips, meta, acc, keep, send):
    rows = acc.shape[0] // chips
    for position in range(chips):
        chunk = acc[pl.ds(pl.multiple_of(meta[2 + position] * rows, 16), rows), :]
        if position < chips // 2:
            keep[position] = chunk
        else:
            send[position - chips // 2] = chunk


def grad_up_kernel(chips, meta, ao, ax, bo, bx, co, cx, do, dx, *refs):
    keep, send, acc = refs[-3:]
    step = pl.program_id(0)

    @pl.when(step < 4)
    def _():
        acc[...] = (dot_tn(ao[...], bo[...]) + dot_tn(ax[...], bx[...])).astype(BF16)

    @pl.when(step == 4)
    def _():
        acc[...] = (dot_tn(co[...], do[...]) + dot_tn(cx[...], dx[...])).astype(BF16)

    store_chunks(chips, meta, acc, keep, send)


def grad_down_kernel(chips, meta, ao, ax, bo, bx, *refs):
    keep, send = refs[-2:]
    rows = keep.shape[1]
    each = ao.shape[1] // rows
    total = (dot_tn(ao[...], bo[...]) + dot_tn(ax[...], bx[...])).astype(BF16)
    for local in range(each):
        position = meta[2 + chips + pl.program_id(0) * each + local]
        chunk = total[local * rows : (local + 1) * rows]

        @pl.when(position < chips // 2)
        def _():
            keep[position] = chunk

        @pl.when(position >= chips // 2)
        def _():
            send[position - chips // 2] = chunk


def grad_qkv_kernel(chips, meta, ao, ax, bo, bx, sums, keep, send, acc, columns):
    wide = bo.shape[1]
    acc[:, :wide] = (dot_tn(ao[...], bo[...]) + dot_tn(ax[...], bx[...])).astype(BF16)
    columns[...] = jnp.concatenate([sums[...], jnp.zeros((120, sums.shape[1]), F32)], 0).T
    acc[:, wide:] = columns[...].astype(BF16)
    store_chunks(chips, meta, acc, keep, send)


def ordered(total, ids, chips):
    split = total.astype(BF16).reshape(chips, total.shape[0] // chips, total.shape[1])
    return jnp.take(split, ids, axis=0)


def gradient_call(kernel, name, chips, grid, in_specs, out_spec, shape, scratch):
    return pl.pallas_call(
        functools.partial(kernel, chips),
        grid_spec=pltpu.PrefetchScalarGridSpec(
            num_scalar_prefetch=1, grid=(grid,), in_specs=in_specs, out_specs=[out_spec] * 2,
            scratch_shapes=scratch,
        ),
        out_shape=[pltpu.HBM(shape, BF16)] * 2,
        compiler_params=pltpu.CompilerParams(vmem_limit_bytes=VMEM_BYTES),
        cost_estimate=SMALL_COST,
        name=name,
    )


def up_gradients(
    meta, chips, normed, normed_x, back_up, back_up_x, attended, attended_x, back_branch, branch_x
):
    tokens, width = normed.shape
    half = width // 2
    rows = width // chips
    if rows % 16 != 0:
        ids = meta[2 : 2 + chips]
        up = dot_tn(normed, back_up) + dot_tn(normed_x, back_up_x)
        own = lax.dynamic_slice_in_dim(back_branch, meta[1] * half, half, 1)
        out = dot_tn(attended, own) + dot_tn(attended_x, branch_x)
        up = ordered(up, ids, chips).reshape(chips, rows, 4, half)
        up = up.transpose(0, 2, 1, 3).reshape(chips, 4 * rows, half)
        both = jnp.concatenate([up, ordered(out, ids, chips)], 1)
        return both[: chips // 2], both[chips // 2 :]
    whole = pl.BlockSpec((tokens, width), lambda j, m: (0, 0))
    fixed = pl.BlockSpec((tokens, half), lambda j, m: (0, 0))
    mine = pl.BlockSpec((tokens, half), lambda j, m: (0, m[1]))
    tile = pl.BlockSpec((tokens, half), lambda j, m: (0, jnp.minimum(j, 3)))
    return gradient_call(
        grad_up_kernel, "gradient_up", chips, 5, [whole, whole, tile, tile, whole, whole, mine, fixed],
        pl.BlockSpec((chips // 2, rows, half), lambda j, m: (0, j, 0)),
        (chips // 2, 5 * rows, half), [pltpu.VMEM((width, half), BF16)],
    )(meta, *in_hbm(normed, normed_x), back_up, back_up_x, *in_hbm(attended, attended_x), back_branch, branch_x)


def down_gradients(meta, chips, active, active_x, back_out, back_out_x):
    tokens, hidden = active.shape
    width = back_out.shape[1]
    half = width // 2
    rows = hidden // chips
    if rows % 64 != 0:
        own = lax.dynamic_slice_in_dim(back_out, meta[1] * half, half, 1)
        down = dot_tn(active, own) + dot_tn(active_x, back_out_x)
        down = ordered(down, meta[2 : 2 + chips], chips)
        return down[: chips // 2], down[chips // 2 :]
    fixed = pl.BlockSpec((tokens, half), lambda j, m: (0, 0))
    mine = pl.BlockSpec((tokens, half), lambda j, m: (0, m[1]))
    tile = pl.BlockSpec((tokens, width), lambda j, m: (0, j))
    return gradient_call(
        grad_down_kernel, "gradient_down", chips, hidden // width, [tile, tile, mine, fixed],
        pl.BlockSpec((chips // 2, rows, half), lambda j, m: (0, 0, 0)), (chips // 2, rows, half), [],
    )(meta, *in_hbm(active, active_x), back_out, back_out_x)


def qkv_gradients(meta, chips, hidden, hidden_x, back_projected, back_projected_x, sums):
    tokens, width = hidden.shape
    wide = back_projected.shape[1]
    rows = width // chips
    if rows % 16 != 0:
        qkv = dot_tn(hidden, back_projected) + dot_tn(hidden_x, back_projected_x)
        table = jnp.pad(sums.T, ((0, 0), (0, 120)))
        both = ordered(jnp.concatenate([qkv, table], -1), meta[2 : 2 + chips], chips)
        return both[: chips // 2], both[chips // 2 :]
    specs = [pl.BlockSpec((tokens, width), lambda j, m: (0, 0))] * 2
    specs += [pl.BlockSpec((tokens, wide), lambda j, m: (0, 0))] * 2
    specs += [pl.BlockSpec((8, width), lambda j, m: (0, 0))]
    return gradient_call(
        grad_qkv_kernel, "gradient_qkv", chips, 1, specs,
        pl.BlockSpec((chips // 2, rows, wide + 128), lambda j, m: (0, 0, 0)),
        (chips // 2, rows, wide + 128),
        [pltpu.VMEM((width, wide + 128), BF16), pltpu.VMEM((width, 128), F32)],
    )(meta, *in_hbm(hidden, hidden_x), back_projected, back_projected_x, sums)


class Exchange:
    def __init__(self, dp):
        self.dp = dp
        self.chips = 2 * dp
        self.bits = int(math.log2(self.chips))
        self.core_pairs = [(s, s ^ 1) for s in range(4)]
        self.mirror_pairs = [(s, 3 - s) for s in range(4)]
        rest = list(range(2, self.bits))
        self.orders = ([1, 0] + rest, [0, 1] + rest[::-1])

    def swap_core(self, value):
        return lax.ppermute(value, "seq", self.core_pairs)

    def mirror(self, value):
        return lax.ppermute(value, "seq", self.mirror_pairs)

    def pairs(self, phase):
        result = []
        for device in range(2 * self.chips):
            chip = (device // 4) * 2 + (device % 4) // 2
            core = device % 2
            other = chip ^ (1 << self.orders[core][phase])
            result.append((device, (other // 2) * 4 + (other % 2) * 2 + core))
        return result

    def tables(self, chip, core):
        index = np.arange(self.chips)
        maps = []
        for order in self.orders:
            value = np.zeros_like(index)
            for phase, bit in enumerate(order):
                value |= ((index >> (self.bits - 1 - phase)) & 1) << bit
            maps.append(value.astype(np.int32))
        ids = chip ^ jnp.where(core == 0, jnp.asarray(maps[0]), jnp.asarray(maps[1]))
        relative = jnp.asarray(index.astype(np.int32)) ^ chip
        places = []
        for order in self.orders:
            place = jnp.zeros_like(relative)
            for phase, bit in enumerate(order):
                place = place | (((relative >> bit) & 1) << (self.bits - 1 - phase))
            places.append(place)
        return ids.astype(jnp.int32), jnp.where(core == 0, places[0], places[1]).astype(jnp.int32)


class Reduction:
    def __init__(self, exchange, keep, send):
        self.exchange, self.parts, self.phase = exchange, [keep], 0
        self.first, self.kind = send, send.dtype

    def message(self):
        if self.phase == 0:
            return self.first
        size = self.parts[-1].shape[0]
        terms = [part[size // 2 : size].astype(F32) for part in self.parts]
        return functools.reduce(jnp.add, terms).astype(self.kind)

    def partner(self, phase):
        dp, seq = lax.axis_index("dp"), lax.axis_index("seq")
        where = []
        for order in self.exchange.orders:
            bit = order[phase]
            if bit == 0:
                where.append((dp, (seq + 2) % 4))
            else:
                size = 1 << (bit - 1)
                where.append((dp + size - 2 * size * ((dp // size) % 2), seq))
        (dp0, seq0), (dp1, seq1) = where
        return dp0 + (seq % 2) * (dp1 - dp0), seq0 + (seq % 2) * (seq1 - seq0)

    def transfer(self, message):
        self.phase += 1
        return lax.ppermute(message, AXES, self.exchange.pairs(self.phase - 1))

    def arrived(self, value):
        self.parts.append(value)

    def complete(self):
        while self.phase < self.exchange.bits:
            self.arrived(self.transfer(self.message()))


def total(parts):
    return functools.reduce(jnp.add, [part[0].astype(F32) for part in parts])


class Move:
    def __init__(self, transfer, value):
        self.transfer, self.value = transfer, value

    def message(self):
        return self.value

    def arrived(self, value):
        self.value = value


def host(run, inputs, *moves):
    count = len(inputs)
    tied = lax.optimization_barrier(tuple(inputs) + tuple(move.message() for move in moves))
    results = tuple(run(*tied[:count]))
    got = tuple(move.transfer(message) for move, message in zip(moves, tied[count:]))
    tied = lax.optimization_barrier(results + got)
    for move, value in zip(moves, tied[len(results) :]):
        move.arrived(value)
    return tied[: len(results)]


def by_core(core, mine, theirs, axis):
    return jnp.where(
        core == 0,
        jnp.concatenate([mine, theirs], axis),
        jnp.concatenate([theirs, mine], axis),
    )


def small_call(kernel, name, shapes, operands, scratch=()):
    def spec(value):
        if value.ndim == 3 and value.dtype == BF16:
            return pl.BlockSpec((1,) + value.shape[1:], lambda i: (0, 0, 0))
        return pl.BlockSpec(value.shape, lambda i: (0,) * value.ndim)

    return pl.pallas_call(
        kernel,
        grid=(1,),
        in_specs=[spec(value) for value in operands],
        out_specs=[spec(shape) for shape in shapes],
        out_shape=shapes,
        scratch_shapes=list(scratch),
        compiler_params=pltpu.CompilerParams(vmem_limit_bytes=VMEM_BYTES),
        cost_estimate=SMALL_COST,
        name=name,
    )(*operands)


def collect(groups):
    counts = [len(parts) for parts, unused in groups]
    units = [unit for unused, unit in groups]
    totals = [parts[0].shape[1:] for parts, unused in groups]
    wide = totals[0][1]
    half = sum(rows for rows, unused in totals) // 2

    def kernel(*refs):
        refs = list(refs)
        core = lax.axis_index("seq") % 2
        mine, theirs = refs[sum(counts) : sum(counts) + 2]
        sums = refs[sum(counts) + 2 :]
        at = 0
        for count, unit, scratch in zip(counts, units, sums):
            parts, refs = refs[:count], refs[count:]
            scratch[...] = functools.reduce(jnp.add, [part[0].astype(F32) for part in parts])
            each = unit // 2
            for start in range(0, scratch.shape[0], unit):
                span = slice(at, at + each)
                mine[span, :] = scratch[pl.ds(pl.multiple_of(start + core * each, 8), each), :]
                theirs[span, :] = scratch[pl.ds(pl.multiple_of(start + (1 - core) * each, 8), each), :]
                at += each

    shape = jax.ShapeDtypeStruct((half, wide), F32)
    operands = in_hbm(*[part for parts, unused in groups for part in parts])
    return small_call(kernel, "collect", [shape, shape], operands, [pltpu.VMEM(t, F32) for t in totals])


def place_mlp(each, mine_a, theirs_a, mine_b, theirs_b):
    half = mine_a.shape[1]

    def kernel(*refs):
        ups, downs, outs = refs[4:]
        core = lax.axis_index("seq") % 2
        for layer in range(2):
            for side, value in ((core, refs[2 * layer]), (1 - core, refs[2 * layer + 1])):
                narrow = pl.ds(pl.multiple_of(side * half, 128), half)
                downs[layer, :, narrow] = value[: 4 * each, :]
                for unit in range(4):
                    lanes = pl.ds(pl.multiple_of(side * 4 * half + unit * half, 128), half)
                    ups[layer, :, lanes] = value[(4 + unit) * each : (5 + unit) * each, :]
                outs[layer, :, narrow] = value[8 * each :, :]

    shapes = [
        jax.ShapeDtypeStruct((2, each, 8 * half), F32), jax.ShapeDtypeStruct((2, 4 * each, 2 * half), F32),
        jax.ShapeDtypeStruct((2, each, 2 * half), F32),
    ]
    return small_call(kernel, "place", shapes, (mine_a, theirs_a, mine_b, theirs_b))


def place_qkv(mine_a, theirs_a, mine_b, theirs_b):
    each, wide = mine_a.shape
    wide -= 128

    def kernel(*refs):
        out, table = refs[4:]
        core = lax.axis_index("seq") % 2
        for layer in range(2):
            for side, value in ((core, refs[2 * layer]), (1 - core, refs[2 * layer + 1])):
                out[layer, :, pl.ds(pl.multiple_of(side * wide, 128), wide)] = value[:, :wide]
        table[...] = refs[0][:, wide:] + refs[1][:, wide:]

    shapes = [jax.ShapeDtypeStruct((2, each, 2 * wide), F32), jax.ShapeDtypeStruct((each, 128), F32)]
    return small_call(kernel, "place_qkv", shapes, (mine_a, theirs_a, mine_b, theirs_b))


def last_exchanges(last, before, up, down, theirs_b):
    keep, message = last.parts[0], last.first
    chunk = keep.shape[1:]
    each, wide = chunk[0] // 2, chunk[1]
    up_rows, down_rows, half = up.parts[0].shape[1], down.parts[0].shape[1], up.parts[0].shape[2]
    mesh = pl.DeviceIdType.MESH

    def kernel(keep, message, *refs):
        refs = list(refs)

        def take(count):
            taken = refs[:count]
            del refs[:count]
            return taken

        before_parts, up_parts, down_parts, (theirs_b,) = take(3), take(4), take(5), take(1)
        mine_a, got_a, got_b, mine_l, got_l, mine_q, got_q = take(7)
        land1, land2, land3, land4, q_land3, q_land4, up_land = take(7)
        send2, send3, send4, q_send3, q_send4, up_send = take(6)
        sums, up_sum, down_sum, swap_q, swap_q_land, swap_a, swap_a_land = take(7)
        send_sem, recv_sem = take(2)
        seq = lax.axis_index("seq")
        core = seq % 2
        other = lax.axis_index("dp"), seq + 1 - 2 * core
        partners = [last.partner(phase) for phase in range(4)]
        barrier = pltpu.get_barrier_semaphore()
        for partner in partners + [other]:
            pl.semaphore_signal(barrier, inc=1, device_id=partner, device_id_type=mesh)
        pl.semaphore_wait(barrier, 5)

        def remote(index, source, target, partner):
            return pltpu.make_async_remote_copy(
                src_ref=source, dst_ref=target, send_sem=send_sem.at[index], recv_sem=recv_sem.at[index],
                device_id=partner, device_id_type=mesh,
            )

        def added(values, kind=BF16):
            return functools.reduce(jnp.add, [value.astype(F32) for value in values]).astype(kind)

        def rows_of(ref, start, count, side):
            return ref[pl.ds(pl.multiple_of(start + side * count, 8), count), :]

        first = [remote(0, message.at[4:8], land1.at[4:8], partners[0]), remote(1, message.at[0:4], land1.at[0:4], partners[0])]
        second = [remote(2, send2.at[2:4], land2.at[2:4], partners[1]), remote(3, send2.at[0:2], land2.at[0:2], partners[1])]
        third, fourth = remote(4, send3, land3, partners[2]), remote(5, send4, land4, partners[3])
        q_third, q_fourth = remote(6, q_send3, q_land3, partners[2]), remote(7, q_send4, q_land4, partners[3])
        up_fourth = remote(8, up_send, up_land, partners[3])
        swap_b, swap_own = (remote(9 + k, swap_a.at[k], swap_a_land.at[k], other) for k in range(2))
        swap_qs = [remote(11 + k, swap_q.at[k], swap_q_land.at[k], other) for k in range(2)]

        for copy in first:
            copy.start()
        up_send[...] = added([part[1:2] for part in up_parts])
        up_fourth.start()
        q_send3[...] = added([part[2:4] for part in before_parts])
        q_third.start()
        swap_a[0] = theirs_b[...]
        swap_b.start()
        down_sum[...] = added([part[0] for part in down_parts], F32)
        up_sum[...] = added([part[0] for part in up_parts], F32)
        sums[1] = added([part[0] for part in before_parts], F32)

        first[0].wait()
        send2[...] = added([keep[4:8], land1[4:8]])
        for copy in second:
            copy.start()

        q_third.wait()
        q_send4[...] = added([part[1:2] for part in before_parts] + [q_land3[1:2]])
        q_fourth.start()
        sums[1] = sums[1] + q_land3[0].astype(F32)

        up_fourth.wait()
        up_sum[...] = up_sum[...] + up_land[0].astype(F32)
        at = 0
        for scratch, unit in ((down_sum, 8 * each), (up_sum, 2 * each)):
            count = unit // 2
            for start in range(0, scratch.shape[0], unit):
                mine_a[at : at + count, :] = rows_of(scratch, start, count, core)
                swap_a[1, at : at + count, :] = rows_of(scratch, start, count, 1 - core)
                at += count
        swap_own.start()
        swap_b.wait()
        got_b[...] = swap_a_land[0]

        first[1].wait()
        second[0].wait()
        send3[...] = added([keep[2:4], land1[2:4], land2[2:4]])
        third.start()

        q_fourth.wait()
        sums[1] = sums[1] + q_land4[0].astype(F32)
        mine_q[...] = rows_of(sums.at[1], 0, each, core)
        swap_q[1] = rows_of(sums.at[1], 0, each, 1 - core)
        swap_qs[1].start()
        swap_own.wait()
        got_a[...] = swap_a_land[1]

        second[1].wait()
        sums[0] = added([keep[0], land1[0], land2[0]], F32)
        third.wait()
        send4[...] = added([keep[1:2], land1[1:2], land2[1:2], land3[1:2]])
        fourth.start()
        swap_qs[1].wait()
        got_q[...] = swap_q_land[1]
        sums[0] = sums[0] + land3[0].astype(F32)
        fourth.wait()
        sums[0] = sums[0] + land4[0].astype(F32)
        mine_l[...] = rows_of(sums.at[0], 0, each, core)
        swap_q[0] = rows_of(sums.at[0], 0, each, 1 - core)
        swap_qs[0].start()
        swap_qs[0].wait()
        got_l[...] = swap_q_land[0]

    def leading(count, value):
        return pl.BlockSpec((count,) + value.shape[1:], lambda i: (0, 0, 0))

    long = theirs_b.shape
    flat, out = pl.BlockSpec(long, lambda i: (0, 0)), pl.BlockSpec((each, wide), lambda i: (0, 0))
    up_chunk = (1, up_rows, half)
    return pl.pallas_call(
        kernel,
        grid=(1,),
        in_specs=[leading(8, keep), pl.BlockSpec(memory_space=pl.ANY)]
        + [leading(4, part) for part in before.parts] + [leading(2, part) for part in up.parts]
        + [leading(1, part) for part in down.parts] + [flat],
        out_specs=[flat] * 3 + [out] * 4,
        out_shape=[jax.ShapeDtypeStruct(long, F32)] * 3 + [jax.ShapeDtypeStruct((each, wide), F32)] * 4,
        scratch_shapes=[pltpu.VMEM((size,) + chunk, BF16) for size in (8, 4, 2, 1, 2, 1)]
        + [pltpu.VMEM(up_chunk, BF16)]
        + [pltpu.VMEM((size,) + chunk, BF16) for size in (4, 2, 1, 2, 1)]
        + [
            pltpu.VMEM(up_chunk, BF16),
            pltpu.VMEM((2,) + chunk, F32), pltpu.VMEM(up_chunk[1:], F32), pltpu.VMEM((down_rows, half), F32),
            pltpu.VMEM((2, each, wide), F32), pltpu.VMEM((2, each, wide), F32),
            pltpu.VMEM((2,) + long, F32), pltpu.VMEM((2,) + long, F32),
            pltpu.SemaphoreType.DMA((13,)), pltpu.SemaphoreType.DMA((13,)),
        ],
        compiler_params=pltpu.CompilerParams(
            vmem_limit_bytes=VMEM_BYTES, collective_id=0, has_side_effects=True
        ),
        cost_estimate=SMALL_COST,
        name="last_exchanges",
    )(*in_hbm(keep, message, *before.parts, *up.parts, *down.parts), theirs_b)


def unpack_mlp(share, rows, core, exchange):
    half, each = share.shape[1], rows // 2
    down = share[: 4 * rows].reshape(2, 4 * each, half)
    rest = share[4 * rows :].reshape(share.shape[0] // rows - 4, 2, each, half)

    def pick(which):
        return jnp.concatenate(
            [lax.dynamic_index_in_dim(down, which, 0, False),
             lax.dynamic_index_in_dim(rest, which, 1, False).reshape(-1, half)], 0)

    mine, theirs = pick(core), exchange.swap_core(pick(1 - core))

    def widen(value, start, count):
        value = value[start * each : (start + count) * each].reshape(count, each, half)
        return value.transpose(1, 0, 2).reshape(each, count * half)

    def join(start, count):
        return by_core(core, widen(mine, start, count), widen(theirs, start, count), 1)

    grad_down = by_core(core, mine[: 4 * each], theirs[: 4 * each], 1)
    return grad_down, join(4, 4), join(8, 1)


def unpack_qkv(share, core, exchange):
    rows, wide = share.shape
    split = share.reshape(2, rows // 2, wide)
    mine = lax.dynamic_index_in_dim(split, core, 0, False)
    theirs = exchange.swap_core(lax.dynamic_index_in_dim(split, 1 - core, 0, False))
    wide -= 128
    table = mine[:, wide : wide + 8] + theirs[:, wide : wide + 8]
    return by_core(core, mine[:, :wide], theirs[:, :wide], 1), table


def per_device(
    inputs, cotangent, task_table, type_counts,
    gain_one, bias_one, proj_qkv, proj_out, gain_two, bias_two, proj_up, proj_down,
):
    slots, rows, width = inputs.shape
    length = rows * lax.axis_size("seq")
    exchange = Exchange(lax.axis_size("dp"))
    place = lax.axis_index("seq")
    side, core = place // 2, place % 2
    chip = lax.axis_index("dp") * 2 + side
    low = jnp.minimum(place, 3 - place)
    own_first = place < 2
    flag = low.astype(jnp.int32).reshape(1)

    meta = jnp.concatenate([flag, core.astype(jnp.int32).reshape(1), *exchange.tables(chip, core)])

    def gather_slot(value, got):
        own = lax.dynamic_index_in_dim(value, side, 0, False)
        return jnp.where(own_first, jnp.concatenate([own, got]), jnp.concatenate([got, own]))

    choose = (task_table[:, None] == jnp.arange(TASKS, dtype=jnp.int32)[None, :]).astype(F32)
    targets = (length - type_counts[:, 0]).astype(F32)
    totals = jnp.sum(choose * targets[:, None], 0)
    bits = int(math.log2(exchange.dp))

    for bit in range(bits):
        pairs = [(d, d ^ (1 << bit)) for d in range(exchange.dp)]
        totals = totals + lax.ppermute(totals, "dp", pairs)
    cotangent_own, cotangent_send = (lax.dynamic_index_in_dim(cotangent, s, 0, False) for s in (side, 1 - side))
    got = exchange.mirror(lax.dynamic_index_in_dim(inputs, 1 - side, 0, False))
    got, totals, cotangent_own, cotangent_send = lax.optimization_barrier(
        (got, totals, cotangent_own, cotangent_send)
    )
    stream = gather_slot(inputs, got)
    factor = jnp.sum(totals) / TASKS / totals
    seq_weight = jnp.sum(choose * factor[None, :], 1)
    own_weight = lax.dynamic_index_in_dim(seq_weight, side, 0, False)
    own_start = lax.dynamic_index_in_dim(type_counts[:, 0], side, 0, False)
    chips = exchange.chips
    half = width // 2
    swap, mirror = exchange.swap_core, exchange.mirror

    def forward(layer, stream, moves_project, moves_attention):
        hidden, queries, own = host(
            lambda v: project(layer, v, gain_one, bias_one, proj_qkv), (stream,), *moves_project
        )
        other = swap(own)
        hidden_x = Move(swap, hidden)
        attended, logs = host(
            lambda q, k, kx: attention_forward(flag, q, k, kx), (queries, own, other),
            hidden_x, *moves_attention
        )
        attended_x = Move(swap, attended)
        middle, normed, active, slope, *output = host(
            lambda a, v: feed_forward(layer, a, v, proj_out, gain_two, bias_two, proj_up, proj_down),
            (attended, stream), attended_x,
        )
        moves = Move(swap, normed), Move(swap, active)
        return output, moves, (stream, hidden, hidden_x, queries, own, other, logs, attended, attended_x, middle, normed, active, slope)

    def attention_step(layer, back_attended, moves):
        unused, unused, unused, queries, own, other, logs, attended, unused, unused, unused, unused, unused = kept[layer]
        back_q, back_own, back_other = host(
            lambda b: attention_backward(flag, queries, own, other, b, attended, logs), (back_attended,), *moves
        )
        return back_q, back_own, swap(back_other)

    def project_step(layer, back_q, back_own, back_got, back_branch, sums, moves, beside=lambda: (), ready=()):
        return host(
            lambda q, k, kx, *more: (
                *project_back(layer, meta, q, k, kx, proj_qkv, kept[layer][0], gain_one, back_branch, sums),
                *beside(*more),
            ),
            (back_q, back_own, back_got) + tuple(ready), *moves
        )

    def feed_step(layer, back_out, sums, moves):
        middle, slope = kept[layer][9], kept[layer][12]
        return host(
            lambda b: feed_back(layer, meta, b, slope, proj_up, proj_down, middle, gain_two, proj_out, sums),
            (back_out,), *moves
        )

    def down_step(layer, back_out, back_out_x, active_x, moves):
        active = kept[layer][11]
        return Reduction(exchange, *host(
            lambda b, bx: down_gradients(meta, chips, active, active_x, b, bx), (back_out, back_out_x), *moves
        ))

    def up_step(layer, back_up, back_up_x, back_branch, branch_x, normed_x, moves):
        normed, attended, attended_x = kept[layer][10], kept[layer][7], kept[layer][8].value
        return Reduction(exchange, *host(
            lambda b, bx: up_gradients(
                meta, chips, normed, normed_x, b, bx, attended, attended_x, back_branch, branch_x
            ),
            (back_up, back_up_x), *moves
        ))

    def qkv_step(layer, mine, theirs_x, sums, moves):
        hidden, hidden_x = kept[layer][1], kept[layer][2].value
        return Reduction(exchange, *host(
            lambda b, bx: qkv_gradients(meta, chips, hidden, hidden_x, b, bx, sums), (mine, theirs_x), *moves
        ))

    got_cotangent = Move(mirror, cotangent_send)
    (stream,), moves, saved = forward(0, stream, (), (got_cotangent,))
    kept = [saved]
    back_out, back_out_send = weigh(
        own_weight.reshape(1), own_start.reshape(1), cotangent_own, got_cotangent.value
    )
    back_out_x = Move(swap, back_out_send)
    (stream, stream_send), last_moves, saved = forward(1, stream, moves, (back_out_x,))
    normed_x, active_x = (move.value for move in moves)
    kept.append(saved)
    outputs_move = Move(mirror, stream_send)

    sums = jnp.zeros((8, width), F32)
    back_up, back_up_send, back_branch, branch_send, back_attended, sums = feed_step(
        1, back_out, sums, last_moves + (outputs_move,)
    )
    last_normed_x, last_active_x = (move.value for move in last_moves)
    back_up_x, branch_x = Move(swap, back_up_send), Move(swap, branch_send)
    down1 = down_step(1, back_out, back_out_x.value, last_active_x, (back_up_x, branch_x))
    up1 = up_step(1, back_up, back_up_x.value, back_branch, branch_x.value, last_normed_x, (down1,))
    back_q, back_own, back_got = attention_step(1, back_attended, (up1,))
    mine, theirs, back_out, back_out_send, sums = project_step(
        1, back_q, back_own, back_got, back_branch, sums, (down1,)
    )
    theirs_x = Move(swap, theirs)
    down0 = down_step(0, back_out, swap(back_out_send), active_x, (theirs_x, up1, down1))
    back_up, back_up_send, back_branch, branch_send, back_attended, sums0 = feed_step(
        0, back_out, sums, (down0, up1)
    )
    back_up_x, branch_x = Move(swap, back_up_send), Move(swap, branch_send)
    qkv1 = qkv_step(1, mine, theirs_x.value, sums, (back_up_x, branch_x, down0, down1))
    up0 = up_step(0, back_up, back_up_x.value, back_branch, branch_x.value, normed_x, (qkv1, up1))
    back_q, back_own, back_got = attention_step(0, back_attended, (up0, down0))
    unit = width // chips

    def return_slot(value, got):
        own = jnp.where(own_first, value[:rows], value[rows:])
        return jnp.where(side == 0, jnp.stack([own, got]), jnp.stack([got, own]))

    each = unit // 2
    whole_tiles = each % 8 == 0 and exchange.bits == 4
    ready = (outputs_move.value,) + tuple(down1.parts) + tuple(up1.parts)

    def beside(got, *parts):
        count = len(down1.parts)
        return (return_slot(stream, got), *collect([(parts[:count], 8 * each), (parts[count:], unit)]))

    mine, theirs, back_out, back_out_send, sums, back_send, *finished = project_step(
        0, back_q, back_own, back_got, back_branch, sums0, (up0, qkv1, down0),
        *((beside, ready) if whole_tiles else ()),
    )
    back_move = Move(mirror, back_send)
    qkv0 = qkv_step(0, mine, swap(theirs), sums, (up0, back_move))
    back_inputs = return_slot(back_out, back_move.value).astype(F32)
    if not whole_tiles:
        for one in (down0, down1, up0, up1, qkv0, qkv1):
            one.complete()
        shares = [jnp.concatenate([total(d.parts), total(u.parts)], 0) for d, u in ((down0, up0), (down1, up1))]
        down, up, out = (
            jnp.stack(value) for value in zip(*(unpack_mlp(share, unit, core, exchange) for share in shares))
        )
        (qkv_a, table), (qkv_b, unused) = (unpack_qkv(total(one.parts), core, exchange) for one in (qkv0, qkv1))
        qkv = jnp.stack([qkv_a, qkv_b])
        outputs = return_slot(stream, outputs_move.value)
    else:
        outputs, mine_b, theirs_b = finished
        mine_a, got_a, got_b, last_q, last_got, mine_q, got_q = last_exchanges(qkv0, qkv1, up0, down0, theirs_b)
        up, down, out = place_mlp(each, mine_a, got_a, mine_b, got_b)
        qkv, table = place_qkv(last_q, last_got, mine_q, got_q)
        table = table[:, :8]
    table = table.T.reshape(LAYERS, 4, each)
    return outputs, back_inputs, table[:, 0], table[:, 1], qkv, out, table[:, 2], table[:, 3], up, down


def solution(mesh):
    tokens = P("dp", "seq", None)
    shared = P(None, AXES)
    in_specs = (tokens, tokens, P("dp"), P("dp", None)) + (P(),) * 8
    out_specs = (
        tokens, tokens, shared, shared, P(None, AXES, None), P(None, AXES, None),
        shared, shared, P(None, AXES, None), P(None, AXES, None),
    )
    return jax.shard_map(
        per_device, mesh=mesh, in_specs=in_specs, out_specs=out_specs, check_vma=False
    )
```

```python
import functools
import math

import jax
import jax.numpy as jnp
import numpy as np
from jax import lax
from jax.experimental import pallas as pl
from jax.experimental.pallas import tpu as pltpu
from jax.sharding import PartitionSpec as P

HEADS = 12
HEAD_DIM = 64
LAYERS = 2
TASKS = 3
AXES = ("dp", "seq")
F32 = jnp.float32
BF16 = jnp.bfloat16
epsilon = 1e-05
PAIRS = 2
VMEM_BYTES = 32 * 1024 * 1024
SMALL_COST = pl.CostEstimate(flops=1000, bytes_accessed=1000, transcendentals=0)


def in_hbm(*values):
    return tuple(pltpu.with_memory_space_constraint(v, pltpu.HBM) for v in values)


def dot_nn(a, b):
    return lax.dot_general(a, b, (((1,), (0,)), ((), ())), preferred_element_type=F32)


def dot_nt(a, b):
    return lax.dot_general(a, b, (((1,), (1,)), ((), ())), preferred_element_type=F32)


def dot_tn(a, b):
    return lax.dot_general(a, b, (((0,), (0,)), ((), ())), preferred_element_type=F32)


def gelu_and_slope(x):
    z = jnp.abs(x) * 0.7071067811865476
    d = 1.0 + 0.3275911 * z
    t = pl.reciprocal(d, approx=True)
    t = t * (2.0 - d * t)
    poly = t * (
        0.254829592
        + t * (-0.284496736 + t * (1.421413741 + t * (-1.453152027 + t * 1.061405429)))
    )
    bell = jnp.exp(-0.5 * x * x)
    tail = 0.5 * poly * bell
    below = jnp.where(x >= 0.0, 1.0 - tail, tail)
    return x * below, below + x * bell * 0.3989422804014327


def head_masks(scale):
    lane = lax.broadcasted_iota(jnp.int32, (1, 2 * HEAD_DIM), 1)
    first = jnp.where(lane < HEAD_DIM, scale, 0.0)
    return first.astype(BF16), (scale - first).astype(BF16)


def stacked(value, masks):
    return jnp.concatenate([value * masks[0], value * masks[1]], 0)


def merged(value):
    rows = value.shape[0] // 2
    lane = lax.broadcasted_iota(jnp.int32, (rows, 2 * HEAD_DIM), 1)
    return jnp.where(lane < HEAD_DIM, value[:rows], value[rows:])


def by_variant(meta, run):
    @pl.when(meta[0] == 0)
    def _():
        run(0)

    @pl.when(meta[0] == 1)
    def _():
        run(1)


def attention_forward_kernel(meta, q_ref, ko_ref, vo_ref, kx_ref, vx_ref, out_ref, lse_ref):
    def run_all(variant):
        for pair in range(PAIRS):
            lanes = (slice(None), slice(pair * 2 * HEAD_DIM, (pair + 1) * 2 * HEAD_DIM))
            refs = [ref.at[lanes] for ref in (q_ref, ko_ref, vo_ref, kx_ref, vx_ref, out_ref)]
            attention_forward_pair(variant, *refs, lse_ref.at[pair])

    by_variant(meta, run_all)


def attention_forward_pair(variant, q_ref, ko_ref, vo_ref, kx_ref, vx_ref, out_ref, lse_ref):
    rows = q_ref.shape[0] // 2
    masks = head_masks(1.0 / math.sqrt(HEAD_DIM))

    def run(variant):
        position = lax.broadcasted_iota(jnp.int32, (2 * rows, rows), 0) % rows
        below = lax.broadcasted_iota(jnp.int32, (2 * rows, rows), 1) <= position
        low, high = slice(0, rows), slice(rows, 2 * rows)
        if variant == 0:
            plan = [
                (low, [(ko_ref, vo_ref, low)]),
                (high, [(ko_ref, vo_ref, low), (kx_ref, vx_ref, low), (kx_ref, vx_ref, high), (ko_ref, vo_ref, high)]),
            ]
        else:
            plan = [
                (low, [(kx_ref, vx_ref, low), (ko_ref, vo_ref, low)]),
                (high, [(ko_ref, vo_ref, low), (kx_ref, vx_ref, low), (ko_ref, vo_ref, high)]),
            ]
        all_scores = []
        for span, parts in plan:
            q2 = stacked(q_ref[span, :], masks)
            all_scores.append([dot_nt(q2, keys[place, :]) for keys, unused, place in parts])
        for (span, parts), scores in zip(plan, all_scores):
            scores[-1] = jnp.where(below, scores[-1], -1e30)
            peak = jnp.max(functools.reduce(jnp.maximum, scores), -1, keepdims=True)
            total, acc = None, None
            for part, (unused, values, place) in zip(scores, parts):
                raised = jnp.exp(part - peak)
                total = raised if total is None else total + raised
                term = dot_nn(raised.astype(BF16), values[place, :])
                acc = term if acc is None else acc + term
            total = jnp.sum(total, -1, keepdims=True)
            out_ref[span, :] = merged(acc / total).astype(BF16)
            log = peak + jnp.log(total)
            lane = lax.broadcasted_iota(jnp.int32, (rows, 2 * HEAD_DIM), 1)
            lse_ref[:, span] = jnp.where(lane == 0, log[:rows], log[rows:]).T[:8, :]

    run(variant)


def attention_forward(meta, queries, own, other):
    tokens = queries.shape[0]
    pairs = HEADS // 2
    wide = 2 * HEAD_DIM * PAIRS

    def at(offset):
        return pl.BlockSpec((tokens, wide), lambda g, m: (0, offset // PAIRS + g))

    return pl.pallas_call(
        attention_forward_kernel,
        grid_spec=pltpu.PrefetchScalarGridSpec(
            num_scalar_prefetch=1,
            grid=(pairs // PAIRS,),
            in_specs=[at(0), at(0), at(pairs), at(0), at(pairs)],
            out_specs=[at(0), pl.BlockSpec((PAIRS, 8, tokens), lambda g, m: (g, 0, 0))],
        ),
        out_shape=[
            pltpu.HBM((tokens, HEADS * HEAD_DIM), BF16),
            pltpu.HBM((pairs, 8, tokens), F32),
        ],
        compiler_params=pltpu.CompilerParams(vmem_limit_bytes=VMEM_BYTES),
        cost_estimate=SMALL_COST,
        name="attention_forward",
    )(meta, *in_hbm(queries, own, own, other, other))


def attention_backward_kernel(
    meta, q_ref, ko_ref, vo_ref, kx_ref, vx_ref, do_ref, o_ref, lse_ref,
    dq_ref, own_ref, other_ref, q4, do4,
):
    def run_all(variant):
        for pair in range(PAIRS):
            lanes = (slice(None), slice(pair * 2 * HEAD_DIM, (pair + 1) * 2 * HEAD_DIM))
            refs = [ref.at[lanes] for ref in (q_ref, ko_ref, vo_ref, kx_ref, vx_ref, do_ref, o_ref)]
            grads = [ref.at[(slice(None),) + lanes] for ref in (own_ref, other_ref)]
            attention_backward_pair(
                variant, *refs, lse_ref.at[pair], dq_ref.at[lanes], *grads, q4.at[pair], do4.at[pair]
            )

    by_variant(meta, run_all)


def attention_backward_pair(
    variant, q_ref, ko_ref, vo_ref, kx_ref, vx_ref, do_ref, o_ref, lse_ref,
    dq_ref, own_ref, other_ref, q4, do4,
):
    rows = q_ref.shape[0] // 2
    scale = 1.0 / math.sqrt(HEAD_DIM)
    scaled, plain = head_masks(scale), head_masks(1.0)
    product = (do_ref[...].astype(F32) * o_ref[...].astype(F32)).T
    first = jnp.sum(product[:HEAD_DIM], 0, keepdims=True)
    second = jnp.sum(product[HEAD_DIM:], 0, keepdims=True)
    logs = lse_ref[...]
    dot_row = jnp.concatenate([first[:, :rows], second[:, :rows], first[:, rows:], second[:, rows:]], 1)
    log_row = jnp.concatenate(
        [logs[0:1, :rows], logs[1:2, :rows], logs[0:1, rows:], logs[1:2, rows:]], 1
    )
    for block in range(2):
        span = slice(block * rows, (block + 1) * rows)
        q4[2 * block * rows : 2 * (block + 1) * rows, :] = stacked(q_ref[span, :], scaled)
        do4[2 * block * rows : 2 * (block + 1) * rows, :] = stacked(do_ref[span, :], plain)

    def run(variant):
        column = lax.broadcasted_iota(jnp.int32, (rows, 2 * rows), 1) % rows
        below = lax.broadcasted_iota(jnp.int32, (rows, 2 * rows), 0) <= column
        low, high = slice(0, rows), slice(rows, 2 * rows)
        both, upper, lower = slice(0, 4 * rows), slice(2 * rows, 4 * rows), slice(0, 2 * rows)
        plan = [(0, low, lower, True), (0, low, upper, False), (1, low, upper, False), (0, high, upper, True)]
        plan.insert(3, (1, high, upper, False) if variant == 0 else (1, low, lower, False))
        keys, values, grads = (ko_ref, kx_ref), (vo_ref, vx_ref), (own_ref, other_ref)
        dq_parts = {}
        sums = {}
        ahead = {}

        def products(index):
            source, place, cols, unused = plan[index]
            ahead[index] = dot_nt(keys[source][place, :], q4[cols, :]), dot_nt(values[source][place, :], do4[cols, :])

        products(0)
        products(1)
        for index, (source, place, cols, diagonal) in enumerate(plan):
            if index + 2 < len(plan):
                products(index + 2)
            scores, back = ahead.pop(index)
            raised = jnp.exp(scores - log_row[:, cols])
            if diagonal:
                raised = jnp.where(below, raised, 0.0)
            slope = (raised * (back - dot_row[:, cols])).astype(BF16)
            slot = (source, place.start)
            terms = dot_nn(slope, q4[cols, :]), dot_nn(raised.astype(BF16), do4[cols, :])
            sums[slot] = tuple(a + b for a, b in zip(sums[slot], terms)) if slot in sums else terms
            term = dot_tn(slope, keys[source][place, :])
            dq_parts[cols.start] = dq_parts[cols.start] + term if cols.start in dq_parts else term
        for block in range(2):
            dq_ref[block * rows : (block + 1) * rows, :] = (
                merged(dq_parts[2 * block * rows]) * scale
            ).astype(BF16)
        for source in range(2):
            for place in (low, high):
                zero = jnp.zeros((rows, 2 * HEAD_DIM), F32)
                for which, value in enumerate(sums.get((source, place.start), (zero, zero))):
                    grads[source][which, place, :] = value.astype(grads[source].dtype)

    run(variant)


def attention_backward(meta, queries, own, other, back_attended, attended, logs):
    tokens = queries.shape[0]
    pairs = HEADS // 2
    wide = 2 * HEAD_DIM * PAIRS
    width = HEADS * HEAD_DIM

    def at(offset):
        return pl.BlockSpec((tokens, wide), lambda g, m: (0, offset // PAIRS + g))

    return pl.pallas_call(
        attention_backward_kernel,
        grid_spec=pltpu.PrefetchScalarGridSpec(
            num_scalar_prefetch=1,
            grid=(pairs // PAIRS,),
            in_specs=[at(0), at(0), at(pairs), at(0), at(pairs), at(0), at(0),
                      pl.BlockSpec((PAIRS, 8, tokens), lambda g, m: (g, 0, 0))],
            out_specs=[at(0)] + [pl.BlockSpec((2, tokens, wide), lambda g, m: (0, 0, g))] * 2,
            scratch_shapes=[pltpu.VMEM((PAIRS, 2 * tokens, 2 * HEAD_DIM), BF16)] * 2,
        ),
        out_shape=[
            jax.ShapeDtypeStruct((tokens, width), BF16),
            pltpu.HBM((2, tokens, width), BF16),
            jax.ShapeDtypeStruct((2, tokens, width), BF16),
        ],
        compiler_params=pltpu.CompilerParams(vmem_limit_bytes=VMEM_BYTES),
        cost_estimate=SMALL_COST,
        name="attention_backward",
    )(meta, *in_hbm(queries, own, own, other, other, back_attended, attended, logs))


def normalised(rows_in):
    average = jnp.mean(rows_in, -1, keepdims=True)
    centred = rows_in - average
    inverse = lax.rsqrt(jnp.mean(centred * centred, -1, keepdims=True) + epsilon)
    return centred * inverse, inverse


def norm_back(rows_in, gain_row, back):
    unit, inverse = normalised(rows_in)
    slope = back * gain_row
    first = jnp.mean(slope, -1, keepdims=True)
    second = jnp.mean(slope * unit, -1, keepdims=True)
    return inverse * (slope - first - unit * second), (
        jnp.sum(back * unit, 0, keepdims=True), jnp.sum(back, 0, keepdims=True))


def with_rows(table, row, sums):
    index = lax.broadcasted_iota(jnp.int32, table.shape, 0)
    return jnp.where(index == row, sums[0], jnp.where(index == row + 1, sums[1], table))


def project_kernel(layer, stream, gain, shift, matrix, hidden, queries, pairs):
    step = pl.program_id(0)

    @pl.when(step == 0)
    def _():
        unit, unused = normalised(stream[...].astype(F32))
        hidden[...] = (unit * gain[layer : layer + 1] + shift[layer : layer + 1]).astype(BF16)

    out = dot_nn(hidden[...], matrix[0]).astype(BF16)

    @pl.when(step < 2)
    def _():
        pairs[...] = out

    @pl.when(step == 2)
    def _():
        queries[...] = out


def project(layer, stream, gain, shift, matrix):
    tokens, width = stream.shape
    whole = pl.BlockSpec((tokens, width), lambda j: (0, 0))
    row = pl.BlockSpec(gain.shape, lambda j: (0, 0))
    return pl.pallas_call(
        functools.partial(project_kernel, layer),
        grid=(3,),
        in_specs=[whole, row, row, pl.BlockSpec((1, width, width), lambda j: (layer, 0, (j + 1) % 3))],
        out_specs=[whole, whole, pl.BlockSpec((tokens, width), lambda j: (0, jnp.minimum(j, 1)))],
        out_shape=[
            pltpu.HBM((tokens, width), BF16),
            pltpu.HBM((tokens, width), BF16),
            pltpu.HBM((tokens, 2 * width), BF16),
        ],
        compiler_params=pltpu.CompilerParams(vmem_limit_bytes=VMEM_BYTES),
        cost_estimate=SMALL_COST,
        name="project",
    )(*in_hbm(stream), gain, shift, *in_hbm(matrix))


def feed_forward_kernel(
    layer, steps, attended, stream, matrix_out, gain, shift, up, down,
    middle, normed, active_ref, slope_ref, out, *rest,
):
    acc = rest[-1]
    step = pl.program_id(0)

    @pl.when(step == 0)
    def _():
        acc[...] = stream[...].astype(F32) + dot_nn(attended[...], matrix_out[0])
        middle[...] = acc[...].astype(BF16)
        unit, unused = normalised(acc[...])
        normed[...] = (unit * gain[layer : layer + 1] + shift[layer : layer + 1]).astype(BF16)

    groups = 4
    rows = normed.shape[0] // groups
    raw = {}
    for group in range(groups + 1):
        if group < groups:
            raw[group] = dot_nn(normed[group * rows : (group + 1) * rows, :], up[0])
        if group > 0:
            span = slice((group - 1) * rows, group * rows)
            active, slope = gelu_and_slope(raw.pop(group - 1))
            active = active.astype(BF16)
            active_ref[span, :] = active
            slope_ref[span, :] = slope.astype(BF16)
            acc[span, :] += dot_nn(active, down[0])

    @pl.when(step == steps - 1)
    def _():
        out[...] = acc[...].astype(out.dtype)
        if len(rest) == 2:
            rest[0][...] = acc[other_block(acc.shape[0] // 2), :].astype(out.dtype)


def other_block(rows):
    return pl.ds(pl.multiple_of((1 - lax.axis_index("seq") // 2) * rows, rows), rows)


def feed_forward(layer, attended, stream, matrix_out, gain, shift, up, down):
    tokens, width = stream.shape
    last = layer == LAYERS - 1
    block = pl.BlockSpec((tokens // 2, width), lambda j: (0, 0))
    hidden = up.shape[2]
    tile = 1024
    steps = hidden // tile
    whole = pl.BlockSpec((tokens, width), lambda j: (0, 0))
    row = pl.BlockSpec(gain.shape, lambda j: (0, 0))
    part = pl.BlockSpec((tokens, tile), lambda j: (0, j))
    return pl.pallas_call(
        functools.partial(feed_forward_kernel, layer, steps),
        grid=(steps,),
        in_specs=[
            whole, whole, pl.BlockSpec((1, width, width), lambda j: (layer, 0, 0)), row, row,
            pl.BlockSpec((1, width, tile), lambda j: (layer, 0, j)),
            pl.BlockSpec((1, tile, width), lambda j: (layer, j, 0)),
        ],
        out_specs=[whole, whole, part, part, whole] + [block] * last,
        out_shape=[
            pltpu.HBM((tokens, width), BF16),
            pltpu.HBM((tokens, width), BF16),
            pltpu.HBM((tokens, hidden), BF16),
            pltpu.HBM((tokens, hidden), BF16),
            pltpu.HBM((tokens, width), BF16),
        ] + [jax.ShapeDtypeStruct((tokens // 2, width), BF16)] * last,
        scratch_shapes=[pltpu.VMEM((tokens, width), F32)],
        compiler_params=pltpu.CompilerParams(vmem_limit_bytes=VMEM_BYTES),
        cost_estimate=SMALL_COST,
        name="feed_forward",
    )(*in_hbm(attended, stream, matrix_out), gain, shift, *in_hbm(up, down))


def feed_back_kernel(
    layer, steps, meta, back_out, slope, up, down, middle, gain, matrix_out, sums_in,
    own, send, back_branch, branch_send, back_attended, grads, acc,
):
    step = pl.program_id(0)
    half = branch_send.shape[1]
    theirs = pl.ds(pl.multiple_of((1 - meta[1]) * half, 128), half)

    @pl.when(step == 0)
    def _():
        acc[...] = jnp.zeros_like(acc)

    back_up = (dot_nt(back_out[...], down[0]) * slope[...].astype(F32)).astype(BF16)

    @pl.when(step < steps // 2)
    def _():
        send[...] = back_up

    @pl.when(step >= steps // 2)
    def _():
        own[...] = back_up

    acc[...] += dot_nt(back_up, up[0])

    @pl.when(step == steps - 1)
    def _():
        back, sums = norm_back(middle[...].astype(F32), gain[layer : layer + 1], acc[...])
        back = back + back_out[...].astype(F32)
        grads[...] = with_rows(sums_in[...], 4 * layer + 2, sums)
        back_branch[...] = back.astype(BF16)
        branch_send[...] = back_branch[:, theirs]
        back_attended[...] = dot_nt(back_branch[...], matrix_out[0]).astype(BF16)


def feed_back(layer, meta, back_out, slope, up, down, middle, gain, matrix_out, sums):
    tokens, width = back_out.shape
    hidden = up.shape[2]
    tile = 512
    steps = hidden // tile
    half = steps // 2

    def place(j, m):
        return jnp.where(j < half, (1 - m[1]) * half + j, m[1] * half + j - half)

    whole = pl.BlockSpec((tokens, width), lambda j, m: (0, 0))
    narrow = pl.BlockSpec((tokens, width // 2), lambda j, m: (0, 0))
    wide = jax.ShapeDtypeStruct((tokens, width), BF16)
    return pl.pallas_call(
        functools.partial(feed_back_kernel, layer, steps),
        grid_spec=pltpu.PrefetchScalarGridSpec(
            num_scalar_prefetch=1,
            grid=(steps,),
            in_specs=[
                whole, pl.BlockSpec((tokens, tile), lambda j, m: (0, place(j, m))),
                pl.BlockSpec((1, width, tile), lambda j, m: (layer, 0, place(j, m))),
                pl.BlockSpec((1, tile, width), lambda j, m: (layer, place(j, m), 0)),
                whole, pl.BlockSpec(gain.shape, lambda j, m: (0, 0)),
                pl.BlockSpec((1, width, width), lambda j, m: (layer, 0, 0)),
                pl.BlockSpec((8, width), lambda j, m: (0, 0)),
            ],
            out_specs=[
                pl.BlockSpec((tokens, tile), lambda j, m: (0, jnp.maximum(j - half, 0))),
                pl.BlockSpec((tokens, tile), lambda j, m: (0, jnp.minimum(j, half - 1))),
                whole, narrow, whole,
                pl.BlockSpec((8, width), lambda j, m: (0, 0)),
            ],
            scratch_shapes=[pltpu.VMEM((tokens, width), F32)],
        ),
        out_shape=[
            jax.ShapeDtypeStruct((tokens, hidden // 2), BF16),
            jax.ShapeDtypeStruct((tokens, hidden // 2), BF16),
            wide, jax.ShapeDtypeStruct((tokens, width // 2), BF16),
            wide, jax.ShapeDtypeStruct((8, width), F32),
        ],
        compiler_params=pltpu.CompilerParams(vmem_limit_bytes=VMEM_BYTES),
        cost_estimate=SMALL_COST,
        name="feed_back",
    )(meta, back_out, *in_hbm(slope, up, down, middle), gain, *in_hbm(matrix_out), sums)


def project_back_kernel(
    layer, meta, back_q, own, got, matrix, stream, gain, back_middle, sums_in,
    mine, theirs, back_out, back_out_send, grads, *rest,
):
    step = pl.program_id(0)
    width = back_q.shape[1]
    table, acc = rest[-2:]

    @pl.when(step == 0)
    def _():
        table[0] = back_q[...]
        for which in range(2):
            table[1 + which] = (own[which].astype(F32) + got[which].astype(F32)).astype(BF16)
        half = width // 2

        @pl.when(meta[1] == 0)
        def _():
            mine[:, :width] = table[0]
            mine[:, width:] = table[1, :, :half]
            theirs[:, :half] = table[1, :, half:]
            theirs[:, half:] = table[2]

        @pl.when(meta[1] == 1)
        def _():
            theirs[:, :width] = table[0]
            theirs[:, width:] = table[1, :, :half]
            mine[:, :half] = table[1, :, half:]
            mine[:, half:] = table[2]

        acc[...] = jnp.zeros_like(acc)

    acc[...] += dot_nt(table[step], matrix[0])

    @pl.when(step == 2)
    def _():
        back, sums = norm_back(stream[...].astype(F32), gain[layer : layer + 1], acc[...])
        back = back + back_middle[...].astype(F32)
        back_out[...] = back.astype(BF16)
        half = width // 2
        back_out_send[...] = back_out[:, pl.ds(pl.multiple_of((1 - meta[1]) * half, 128), half)]
        grads[...] = with_rows(sums_in[...], 4 * layer, sums)
        if len(rest) == 3:
            rest[0][...] = back_out[other_block(back_out.shape[0] // 2), :]


def project_back(layer, meta, back_q, own, got, matrix, stream, gain, back_middle, sums):
    tokens, width = stream.shape
    whole = pl.BlockSpec((tokens, width), lambda j, m: (0, 0))
    both = pl.BlockSpec((2, tokens, width), lambda j, m: (0, 0, 0))
    side = pl.BlockSpec((tokens, 3 * width // 2), lambda j, m: (0, 0))
    return pl.pallas_call(
        functools.partial(project_back_kernel, layer),
        grid_spec=pltpu.PrefetchScalarGridSpec(
            num_scalar_prefetch=1,
            grid=(3,),
            in_specs=[
                whole, both, both, pl.BlockSpec((1, width, width), lambda j, m: (layer, 0, j)),
                whole, pl.BlockSpec(gain.shape, lambda j, m: (0, 0)), whole,
                pl.BlockSpec((8, width), lambda j, m: (0, 0)),
            ],
            out_specs=[side, side, whole, pl.BlockSpec((tokens, width // 2), lambda j, m: (0, 0)),
                       pl.BlockSpec((8, width), lambda j, m: (0, 0))]
            + [pl.BlockSpec((tokens // 2, width), lambda j, m: (0, 0))] * (layer == 0),
            scratch_shapes=[pltpu.VMEM((3, tokens, width), BF16), pltpu.VMEM((tokens, width), F32)],
        ),
        out_shape=[
            jax.ShapeDtypeStruct((tokens, 3 * width // 2), BF16),
            jax.ShapeDtypeStruct((tokens, 3 * width // 2), BF16),
            jax.ShapeDtypeStruct((tokens, width), BF16),
            jax.ShapeDtypeStruct((tokens, width // 2), BF16),
            jax.ShapeDtypeStruct((8, width), F32),
        ] + [jax.ShapeDtypeStruct((tokens // 2, width), BF16)] * (layer == 0),
        compiler_params=pltpu.CompilerParams(vmem_limit_bytes=VMEM_BYTES),
        cost_estimate=SMALL_COST,
        name="project_back",
    )(meta, *in_hbm(back_q, own), got, *in_hbm(matrix, stream), gain, *in_hbm(back_middle), sums)


def weigh_kernel(weight, start, own, got, back_out, back_out_send):
    rows, half = own.shape[0], back_out_send.shape[1]
    place = lax.axis_index("seq")
    core, low = place % 2, ((place + 1) // 2) % 2
    step = lax.broadcasted_iota(jnp.int32, (rows, 1), 0)
    first = place < 2
    for which, block in enumerate((low, 3 - low)):
        span = slice(which * rows, (which + 1) * rows)
        scale = jnp.where(block * rows + step >= start[0], weight[0], 0.0)
        mine = own[...].astype(F32) if which == 0 else got[...].astype(F32)
        other = got[...].astype(F32) if which == 0 else own[...].astype(F32)
        back_out[span, :] = (jnp.where(first, mine, other) * scale).astype(BF16)
    back_out_send[...] = back_out[:, pl.ds(pl.multiple_of((1 - core) * half, 128), half)]


def weigh(weight, start, own, got):
    rows, width = own.shape
    scalar = pl.BlockSpec(memory_space=pltpu.SMEM)
    return pl.pallas_call(
        weigh_kernel,
        in_specs=[scalar, scalar, pl.BlockSpec(memory_space=pltpu.VMEM), pl.BlockSpec(memory_space=pltpu.VMEM)],
        out_specs=[pl.BlockSpec(memory_space=pltpu.VMEM)] * 2,
        out_shape=[
            jax.ShapeDtypeStruct((2 * rows, width), BF16),
            jax.ShapeDtypeStruct((2 * rows, width // 2), BF16),
        ],
        compiler_params=pltpu.CompilerParams(vmem_limit_bytes=VMEM_BYTES),
        cost_estimate=SMALL_COST,
        name="weigh",
    )(weight, start, own, got)


def store_chunks(chips, meta, acc, keep, send):
    rows = acc.shape[0] // chips
    for position in range(chips):
        chunk = acc[pl.ds(pl.multiple_of(meta[2 + position] * rows, 16), rows), :]
        if position < chips // 2:
            keep[position] = chunk
        else:
            send[position - chips // 2] = chunk


def grad_up_kernel(chips, meta, ao, ax, bo, bx, co, cx, do, dx, *refs):
    keep, send, acc = refs[-3:]
    step = pl.program_id(0)

    @pl.when(step < 4)
    def _():
        acc[...] = (dot_tn(ao[...], bo[...]) + dot_tn(ax[...], bx[...])).astype(BF16)

    @pl.when(step == 4)
    def _():
        acc[...] = (dot_tn(co[...], do[...]) + dot_tn(cx[...], dx[...])).astype(BF16)

    store_chunks(chips, meta, acc, keep, send)


def grad_down_kernel(chips, meta, ao, ax, bo, bx, *refs):
    keep, send = refs[-2:]
    rows = keep.shape[1]
    each = ao.shape[1] // rows
    total = (dot_tn(ao[...], bo[...]) + dot_tn(ax[...], bx[...])).astype(BF16)
    for local in range(each):
        position = meta[2 + chips + pl.program_id(0) * each + local]
        chunk = total[local * rows : (local + 1) * rows]

        @pl.when(position < chips // 2)
        def _():
            keep[position] = chunk

        @pl.when(position >= chips // 2)
        def _():
            send[position - chips // 2] = chunk


def grad_qkv_kernel(chips, meta, ao, ax, bo, bx, sums, keep, send, acc, columns):
    wide = bo.shape[1]
    acc[:, :wide] = (dot_tn(ao[...], bo[...]) + dot_tn(ax[...], bx[...])).astype(BF16)
    columns[...] = jnp.concatenate([sums[...], jnp.zeros((120, sums.shape[1]), F32)], 0).T
    acc[:, wide:] = columns[...].astype(BF16)
    store_chunks(chips, meta, acc, keep, send)


def ordered(total, ids, chips):
    split = total.astype(BF16).reshape(chips, total.shape[0] // chips, total.shape[1])
    return jnp.take(split, ids, axis=0)


def gradient_call(kernel, name, chips, grid, in_specs, out_spec, shape, scratch):
    return pl.pallas_call(
        functools.partial(kernel, chips),
        grid_spec=pltpu.PrefetchScalarGridSpec(
            num_scalar_prefetch=1, grid=(grid,), in_specs=in_specs, out_specs=[out_spec] * 2,
            scratch_shapes=scratch,
        ),
        out_shape=[pltpu.HBM(shape, BF16)] * 2,
        compiler_params=pltpu.CompilerParams(vmem_limit_bytes=VMEM_BYTES),
        cost_estimate=SMALL_COST,
        name=name,
    )


def up_gradients(
    meta, chips, normed, normed_x, back_up, back_up_x, attended, attended_x, back_branch, branch_x
):
    tokens, width = normed.shape
    half = width // 2
    rows = width // chips
    if rows % 16 != 0:
        ids = meta[2 : 2 + chips]
        up = dot_tn(normed, back_up) + dot_tn(normed_x, back_up_x)
        own = lax.dynamic_slice_in_dim(back_branch, meta[1] * half, half, 1)
        out = dot_tn(attended, own) + dot_tn(attended_x, branch_x)
        up = ordered(up, ids, chips).reshape(chips, rows, 4, half)
        up = up.transpose(0, 2, 1, 3).reshape(chips, 4 * rows, half)
        both = jnp.concatenate([up, ordered(out, ids, chips)], 1)
        return both[: chips // 2], both[chips // 2 :]
    whole = pl.BlockSpec((tokens, width), lambda j, m: (0, 0))
    fixed = pl.BlockSpec((tokens, half), lambda j, m: (0, 0))
    mine = pl.BlockSpec((tokens, half), lambda j, m: (0, m[1]))
    tile = pl.BlockSpec((tokens, half), lambda j, m: (0, jnp.minimum(j, 3)))
    return gradient_call(
        grad_up_kernel, "gradient_up", chips, 5, [whole, whole, tile, tile, whole, whole, mine, fixed],
        pl.BlockSpec((chips // 2, rows, half), lambda j, m: (0, j, 0)),
        (chips // 2, 5 * rows, half), [pltpu.VMEM((width, half), BF16)],
    )(meta, *in_hbm(normed, normed_x), back_up, back_up_x, *in_hbm(attended, attended_x), back_branch, branch_x)


def down_gradients(meta, chips, active, active_x, back_out, back_out_x):
    tokens, hidden = active.shape
    width = back_out.shape[1]
    half = width // 2
    rows = hidden // chips
    if rows % 64 != 0:
        own = lax.dynamic_slice_in_dim(back_out, meta[1] * half, half, 1)
        down = dot_tn(active, own) + dot_tn(active_x, back_out_x)
        down = ordered(down, meta[2 : 2 + chips], chips)
        return down[: chips // 2], down[chips // 2 :]
    fixed = pl.BlockSpec((tokens, half), lambda j, m: (0, 0))
    mine = pl.BlockSpec((tokens, half), lambda j, m: (0, m[1]))
    tile = pl.BlockSpec((tokens, width), lambda j, m: (0, j))
    return gradient_call(
        grad_down_kernel, "gradient_down", chips, hidden // width, [tile, tile, mine, fixed],
        pl.BlockSpec((chips // 2, rows, half), lambda j, m: (0, 0, 0)), (chips // 2, rows, half), [],
    )(meta, *in_hbm(active, active_x), back_out, back_out_x)


def qkv_gradients(meta, chips, hidden, hidden_x, back_projected, back_projected_x, sums):
    tokens, width = hidden.shape
    wide = back_projected.shape[1]
    rows = width // chips
    if rows % 16 != 0:
        qkv = dot_tn(hidden, back_projected) + dot_tn(hidden_x, back_projected_x)
        table = jnp.pad(sums.T, ((0, 0), (0, 120)))
        both = ordered(jnp.concatenate([qkv, table], -1), meta[2 : 2 + chips], chips)
        return both[: chips // 2], both[chips // 2 :]
    specs = [pl.BlockSpec((tokens, width), lambda j, m: (0, 0))] * 2
    specs += [pl.BlockSpec((tokens, wide), lambda j, m: (0, 0))] * 2
    specs += [pl.BlockSpec((8, width), lambda j, m: (0, 0))]
    return gradient_call(
        grad_qkv_kernel, "gradient_qkv", chips, 1, specs,
        pl.BlockSpec((chips // 2, rows, wide + 128), lambda j, m: (0, 0, 0)),
        (chips // 2, rows, wide + 128),
        [pltpu.VMEM((width, wide + 128), BF16), pltpu.VMEM((width, 128), F32)],
    )(meta, *in_hbm(hidden, hidden_x), back_projected, back_projected_x, sums)


class Exchange:
    def __init__(self, dp):
        self.dp = dp
        self.chips = 2 * dp
        self.bits = int(math.log2(self.chips))
        self.core_pairs = [(s, s ^ 1) for s in range(4)]
        self.mirror_pairs = [(s, 3 - s) for s in range(4)]
        rest = list(range(2, self.bits))
        self.orders = ([1, 0] + rest, [0, 1] + rest[::-1])

    def swap_core(self, value):
        return lax.ppermute(value, "seq", self.core_pairs)

    def mirror(self, value):
        return lax.ppermute(value, "seq", self.mirror_pairs)

    def pairs(self, phase):
        result = []
        for device in range(2 * self.chips):
            chip = (device // 4) * 2 + (device % 4) // 2
            core = device % 2
            other = chip ^ (1 << self.orders[core][phase])
            result.append((device, (other // 2) * 4 + (other % 2) * 2 + core))
        return result

    def tables(self, chip, core):
        index = np.arange(self.chips)
        maps = []
        for order in self.orders:
            value = np.zeros_like(index)
            for phase, bit in enumerate(order):
                value |= ((index >> (self.bits - 1 - phase)) & 1) << bit
            maps.append(value.astype(np.int32))
        ids = chip ^ jnp.where(core == 0, jnp.asarray(maps[0]), jnp.asarray(maps[1]))
        relative = jnp.asarray(index.astype(np.int32)) ^ chip
        places = []
        for order in self.orders:
            place = jnp.zeros_like(relative)
            for phase, bit in enumerate(order):
                place = place | (((relative >> bit) & 1) << (self.bits - 1 - phase))
            places.append(place)
        return ids.astype(jnp.int32), jnp.where(core == 0, places[0], places[1]).astype(jnp.int32)


class Reduction:
    def __init__(self, exchange, keep, send):
        self.exchange, self.parts, self.phase = exchange, [keep], 0
        self.first, self.kind = send, send.dtype

    def message(self):
        if self.phase == 0:
            return self.first
        size = self.parts[-1].shape[0]
        terms = [part[size // 2 : size].astype(F32) for part in self.parts]
        return functools.reduce(jnp.add, terms).astype(self.kind)

    def partner(self, phase):
        dp, seq = lax.axis_index("dp"), lax.axis_index("seq")
        where = []
        for order in self.exchange.orders:
            bit = order[phase]
            if bit == 0:
                where.append((dp, (seq + 2) % 4))
            else:
                size = 1 << (bit - 1)
                where.append((dp + size - 2 * size * ((dp // size) % 2), seq))
        (dp0, seq0), (dp1, seq1) = where
        return dp0 + (seq % 2) * (dp1 - dp0), seq0 + (seq % 2) * (seq1 - seq0)

    def transfer(self, message):
        self.phase += 1
        return lax.ppermute(message, AXES, self.exchange.pairs(self.phase - 1))

    def arrived(self, value):
        self.parts.append(value)

    def complete(self):
        while self.phase < self.exchange.bits:
            self.arrived(self.transfer(self.message()))


def total(parts):
    return functools.reduce(jnp.add, [part[0].astype(F32) for part in parts])


class Move:
    def __init__(self, transfer, value):
        self.transfer, self.value = transfer, value

    def message(self):
        return self.value

    def arrived(self, value):
        self.value = value


def host(run, inputs, *moves):
    count = len(inputs)
    tied = lax.optimization_barrier(tuple(inputs) + tuple(move.message() for move in moves))
    results = tuple(run(*tied[:count]))
    got = tuple(move.transfer(message) for move, message in zip(moves, tied[count:]))
    tied = lax.optimization_barrier(results + got)
    for move, value in zip(moves, tied[len(results) :]):
        move.arrived(value)
    return tied[: len(results)]


def by_core(core, mine, theirs, axis):
    return jnp.where(
        core == 0,
        jnp.concatenate([mine, theirs], axis),
        jnp.concatenate([theirs, mine], axis),
    )


def small_call(kernel, name, shapes, operands, scratch=()):
    def spec(value):
        if value.ndim == 3 and value.dtype == BF16:
            return pl.BlockSpec((1,) + value.shape[1:], lambda i: (0, 0, 0))
        return pl.BlockSpec(value.shape, lambda i: (0,) * value.ndim)

    return pl.pallas_call(
        kernel,
        grid=(1,),
        in_specs=[spec(value) for value in operands],
        out_specs=[spec(shape) for shape in shapes],
        out_shape=shapes,
        scratch_shapes=list(scratch),
        compiler_params=pltpu.CompilerParams(vmem_limit_bytes=VMEM_BYTES),
        cost_estimate=SMALL_COST,
        name=name,
    )(*operands)


def collect(groups):
    counts = [len(parts) for parts, unused in groups]
    units = [unit for unused, unit in groups]
    totals = [parts[0].shape[1:] for parts, unused in groups]
    wide = totals[0][1]
    half = sum(rows for rows, unused in totals) // 2

    def kernel(*refs):
        refs = list(refs)
        core = lax.axis_index("seq") % 2
        mine, theirs = refs[sum(counts) : sum(counts) + 2]
        sums = refs[sum(counts) + 2 :]
        at = 0
        for count, unit, scratch in zip(counts, units, sums):
            parts, refs = refs[:count], refs[count:]
            scratch[...] = functools.reduce(jnp.add, [part[0].astype(F32) for part in parts])
            each = unit // 2
            for start in range(0, scratch.shape[0], unit):
                span = slice(at, at + each)
                mine[span, :] = scratch[pl.ds(pl.multiple_of(start + core * each, 8), each), :]
                theirs[span, :] = scratch[pl.ds(pl.multiple_of(start + (1 - core) * each, 8), each), :]
                at += each

    shape = jax.ShapeDtypeStruct((half, wide), F32)
    operands = in_hbm(*[part for parts, unused in groups for part in parts])
    return small_call(kernel, "collect", [shape, shape], operands, [pltpu.VMEM(t, F32) for t in totals])


def place_mlp(each, mine_a, theirs_a, mine_b, theirs_b):
    half = mine_a.shape[1]

    def kernel(*refs):
        ups, downs, outs = refs[4:]
        core = lax.axis_index("seq") % 2
        for layer in range(2):
            for side, value in ((core, refs[2 * layer]), (1 - core, refs[2 * layer + 1])):
                narrow = pl.ds(pl.multiple_of(side * half, 128), half)
                downs[layer, :, narrow] = value[: 4 * each, :]
                for unit in range(4):
                    lanes = pl.ds(pl.multiple_of(side * 4 * half + unit * half, 128), half)
                    ups[layer, :, lanes] = value[(4 + unit) * each : (5 + unit) * each, :]
                outs[layer, :, narrow] = value[8 * each :, :]

    shapes = [
        jax.ShapeDtypeStruct((2, each, 8 * half), F32), jax.ShapeDtypeStruct((2, 4 * each, 2 * half), F32),
        jax.ShapeDtypeStruct((2, each, 2 * half), F32),
    ]
    return small_call(kernel, "place", shapes, (mine_a, theirs_a, mine_b, theirs_b))


def place_qkv(mine_a, theirs_a, mine_b, theirs_b):
    each, wide = mine_a.shape
    wide -= 128

    def kernel(*refs):
        out, table = refs[4:]
        core = lax.axis_index("seq") % 2
        for layer in range(2):
            for side, value in ((core, refs[2 * layer]), (1 - core, refs[2 * layer + 1])):
                out[layer, :, pl.ds(pl.multiple_of(side * wide, 128), wide)] = value[:, :wide]
        table[...] = refs[0][:, wide:] + refs[1][:, wide:]

    shapes = [jax.ShapeDtypeStruct((2, each, 2 * wide), F32), jax.ShapeDtypeStruct((each, 128), F32)]
    return small_call(kernel, "place_qkv", shapes, (mine_a, theirs_a, mine_b, theirs_b))


def last_exchanges(last, before, up, down, theirs_b):
    keep, message = last.parts[0], last.first
    chunk = keep.shape[1:]
    each, wide = chunk[0] // 2, chunk[1]
    up_rows, down_rows, half = up.parts[0].shape[1], down.parts[0].shape[1], up.parts[0].shape[2]
    mesh = pl.DeviceIdType.MESH

    def kernel(keep, message, *refs):
        refs = list(refs)

        def take(count):
            taken = refs[:count]
            del refs[:count]
            return taken

        before_parts, up_parts, down_parts, (theirs_b,) = take(3), take(4), take(5), take(1)
        mine_a, got_a, got_b, mine_l, got_l, mine_q, got_q = take(7)
        land1, land2, land3, land4, q_land3, q_land4, up_land = take(7)
        send2, send3, send4, q_send3, q_send4, up_send = take(6)
        sums, up_sum, down_sum, swap_q, swap_q_land, swap_a, swap_a_land = take(7)
        send_sem, recv_sem = take(2)
        seq = lax.axis_index("seq")
        core = seq % 2
        other = lax.axis_index("dp"), seq + 1 - 2 * core
        partners = [last.partner(phase) for phase in range(4)]
        barrier = pltpu.get_barrier_semaphore()
        for partner in partners + [other]:
            pl.semaphore_signal(barrier, inc=1, device_id=partner, device_id_type=mesh)
        pl.semaphore_wait(barrier, 5)

        def remote(index, source, target, partner):
            return pltpu.make_async_remote_copy(
                src_ref=source, dst_ref=target, send_sem=send_sem.at[index], recv_sem=recv_sem.at[index],
                device_id=partner, device_id_type=mesh,
            )

        def added(values, kind=BF16):
            return functools.reduce(jnp.add, [value.astype(F32) for value in values]).astype(kind)

        def rows_of(ref, start, count, side):
            return ref[pl.ds(pl.multiple_of(start + side * count, 8), count), :]

        pieces = (slice(4, 8), slice(2, 4), slice(0, 2))
        first = [remote(k, message.at[p], land1.at[p], partners[0]) for k, p in zip((0, 1, 13), pieces)]
        second = [remote(2, send2.at[2:4], land2.at[2:4], partners[1]), remote(3, send2.at[0:2], land2.at[0:2], partners[1])]
        third, fourth = remote(4, send3, land3, partners[2]), remote(5, send4, land4, partners[3])
        q_third, q_fourth = remote(6, q_send3, q_land3, partners[2]), remote(7, q_send4, q_land4, partners[3])
        up_fourth = remote(8, up_send, up_land, partners[3])
        swap_b, swap_own = (remote(9 + k, swap_a.at[k], swap_a_land.at[k], other) for k in range(2))
        swap_qs = [remote(11 + k, swap_q.at[k], swap_q_land.at[k], other) for k in range(2)]

        for copy in first:
            copy.start()
        up_send[...] = added([part[1:2] for part in up_parts])
        up_fourth.start()
        q_send3[...] = added([part[2:4] for part in before_parts])
        q_third.start()
        swap_a[0] = theirs_b[...]
        swap_b.start()
        down_sum[...] = added([part[0] for part in down_parts], F32)
        up_sum[...] = added([part[0] for part in up_parts], F32)
        sums[1] = added([part[0] for part in before_parts], F32)

        first[0].wait()
        send2[...] = added([keep[4:8], land1[4:8]])
        for copy in second:
            copy.start()

        q_third.wait()
        q_send4[...] = added([part[1:2] for part in before_parts] + [q_land3[1:2]])
        q_fourth.start()
        sums[1] = sums[1] + q_land3[0].astype(F32)

        up_fourth.wait()
        up_sum[...] = up_sum[...] + up_land[0].astype(F32)
        at = 0
        for scratch, unit in ((down_sum, 8 * each), (up_sum, 2 * each)):
            count = unit // 2
            for start in range(0, scratch.shape[0], unit):
                mine_a[at : at + count, :] = rows_of(scratch, start, count, core)
                swap_a[1, at : at + count, :] = rows_of(scratch, start, count, 1 - core)
                at += count
        swap_own.start()
        swap_b.wait()
        got_b[...] = swap_a_land[0]

        first[1].wait()
        second[0].wait()
        send3[...] = added([keep[2:4], land1[2:4], land2[2:4]])
        third.start()

        q_fourth.wait()
        sums[1] = sums[1] + q_land4[0].astype(F32)
        mine_q[...] = rows_of(sums.at[1], 0, each, core)
        swap_q[1] = rows_of(sums.at[1], 0, each, 1 - core)
        swap_qs[1].start()
        swap_own.wait()
        got_a[...] = swap_a_land[1]

        first[2].wait()
        second[1].wait()
        sums[0] = added([keep[0], land1[0], land2[0]], F32)
        third.wait()
        send4[...] = added([keep[1:2], land1[1:2], land2[1:2], land3[1:2]])
        fourth.start()
        swap_qs[1].wait()
        got_q[...] = swap_q_land[1]
        sums[0] = sums[0] + land3[0].astype(F32)
        fourth.wait()
        sums[0] = sums[0] + land4[0].astype(F32)
        mine_l[...] = rows_of(sums.at[0], 0, each, core)
        swap_q[0] = rows_of(sums.at[0], 0, each, 1 - core)
        swap_qs[0].start()
        swap_qs[0].wait()
        got_l[...] = swap_q_land[0]

    def leading(count, value):
        return pl.BlockSpec((count,) + value.shape[1:], lambda i: (0, 0, 0))

    long = theirs_b.shape
    flat, out = pl.BlockSpec(long, lambda i: (0, 0)), pl.BlockSpec((each, wide), lambda i: (0, 0))
    up_chunk = (1, up_rows, half)
    return pl.pallas_call(
        kernel,
        grid=(1,),
        in_specs=[leading(8, keep), pl.BlockSpec(memory_space=pl.ANY)]
        + [leading(4, part) for part in before.parts] + [leading(2, part) for part in up.parts]
        + [leading(1, part) for part in down.parts] + [flat],
        out_specs=[flat] * 3 + [out] * 4,
        out_shape=[jax.ShapeDtypeStruct(long, F32)] * 3 + [jax.ShapeDtypeStruct((each, wide), F32)] * 4,
        scratch_shapes=[pltpu.VMEM((size,) + chunk, BF16) for size in (8, 4, 2, 1, 2, 1)]
        + [pltpu.VMEM(up_chunk, BF16)]
        + [pltpu.VMEM((size,) + chunk, BF16) for size in (4, 2, 1, 2, 1)]
        + [
            pltpu.VMEM(up_chunk, BF16),
            pltpu.VMEM((2,) + chunk, F32), pltpu.VMEM(up_chunk[1:], F32), pltpu.VMEM((down_rows, half), F32),
            pltpu.VMEM((2, each, wide), F32), pltpu.VMEM((2, each, wide), F32),
            pltpu.VMEM((2,) + long, F32), pltpu.VMEM((2,) + long, F32),
            pltpu.SemaphoreType.DMA((14,)), pltpu.SemaphoreType.DMA((14,)),
        ],
        compiler_params=pltpu.CompilerParams(
            vmem_limit_bytes=VMEM_BYTES, collective_id=0, has_side_effects=True
        ),
        cost_estimate=SMALL_COST,
        name="last_exchanges",
    )(*in_hbm(keep, message, *before.parts, *up.parts, *down.parts), theirs_b)


def unpack_mlp(share, rows, core, exchange):
    half, each = share.shape[1], rows // 2
    down = share[: 4 * rows].reshape(2, 4 * each, half)
    rest = share[4 * rows :].reshape(share.shape[0] // rows - 4, 2, each, half)

    def pick(which):
        return jnp.concatenate(
            [lax.dynamic_index_in_dim(down, which, 0, False),
             lax.dynamic_index_in_dim(rest, which, 1, False).reshape(-1, half)], 0)

    mine, theirs = pick(core), exchange.swap_core(pick(1 - core))

    def widen(value, start, count):
        value = value[start * each : (start + count) * each].reshape(count, each, half)
        return value.transpose(1, 0, 2).reshape(each, count * half)

    def join(start, count):
        return by_core(core, widen(mine, start, count), widen(theirs, start, count), 1)

    grad_down = by_core(core, mine[: 4 * each], theirs[: 4 * each], 1)
    return grad_down, join(4, 4), join(8, 1)


def unpack_qkv(share, core, exchange):
    rows, wide = share.shape
    split = share.reshape(2, rows // 2, wide)
    mine = lax.dynamic_index_in_dim(split, core, 0, False)
    theirs = exchange.swap_core(lax.dynamic_index_in_dim(split, 1 - core, 0, False))
    wide -= 128
    table = mine[:, wide : wide + 8] + theirs[:, wide : wide + 8]
    return by_core(core, mine[:, :wide], theirs[:, :wide], 1), table


def per_device(
    inputs, cotangent, task_table, type_counts,
    gain_one, bias_one, proj_qkv, proj_out, gain_two, bias_two, proj_up, proj_down,
):
    slots, rows, width = inputs.shape
    length = rows * lax.axis_size("seq")
    exchange = Exchange(lax.axis_size("dp"))
    place = lax.axis_index("seq")
    side, core = place // 2, place % 2
    chip = lax.axis_index("dp") * 2 + side
    low = jnp.minimum(place, 3 - place)
    own_first = place < 2
    flag = low.astype(jnp.int32).reshape(1)

    meta = jnp.concatenate([flag, core.astype(jnp.int32).reshape(1), *exchange.tables(chip, core)])

    def gather_slot(value, got):
        own = lax.dynamic_index_in_dim(value, side, 0, False)
        return jnp.where(own_first, jnp.concatenate([own, got]), jnp.concatenate([got, own]))

    choose = (task_table[:, None] == jnp.arange(TASKS, dtype=jnp.int32)[None, :]).astype(F32)
    targets = (length - type_counts[:, 0]).astype(F32)
    totals = jnp.sum(choose * targets[:, None], 0)
    bits = int(math.log2(exchange.dp))

    for bit in range(bits):
        pairs = [(d, d ^ (1 << bit)) for d in range(exchange.dp)]
        totals = totals + lax.ppermute(totals, "dp", pairs)
    cotangent_own, cotangent_send = (lax.dynamic_index_in_dim(cotangent, s, 0, False) for s in (side, 1 - side))
    got = exchange.mirror(lax.dynamic_index_in_dim(inputs, 1 - side, 0, False))
    got, totals, cotangent_own, cotangent_send = lax.optimization_barrier(
        (got, totals, cotangent_own, cotangent_send)
    )
    stream = gather_slot(inputs, got)
    factor = jnp.sum(totals) / TASKS / totals
    seq_weight = jnp.sum(choose * factor[None, :], 1)
    own_weight = lax.dynamic_index_in_dim(seq_weight, side, 0, False)
    own_start = lax.dynamic_index_in_dim(type_counts[:, 0], side, 0, False)
    chips = exchange.chips
    half = width // 2
    swap, mirror = exchange.swap_core, exchange.mirror

    def forward(layer, stream, moves_project, moves_attention):
        hidden, queries, own = host(
            lambda v: project(layer, v, gain_one, bias_one, proj_qkv), (stream,), *moves_project
        )
        other = swap(own)
        hidden_x = Move(swap, hidden)
        attended, logs = host(
            lambda q, k, kx: attention_forward(flag, q, k, kx), (queries, own, other),
            hidden_x, *moves_attention
        )
        attended_x = Move(swap, attended)
        middle, normed, active, slope, *output = host(
            lambda a, v: feed_forward(layer, a, v, proj_out, gain_two, bias_two, proj_up, proj_down),
            (attended, stream), attended_x,
        )
        moves = Move(swap, normed), Move(swap, active)
        return output, moves, (stream, hidden, hidden_x, queries, own, other, logs, attended, attended_x, middle, normed, active, slope)

    def attention_step(layer, back_attended, moves):
        unused, unused, unused, queries, own, other, logs, attended, unused, unused, unused, unused, unused = kept[layer]
        back_q, back_own, back_other = host(
            lambda b: attention_backward(flag, queries, own, other, b, attended, logs), (back_attended,), *moves
        )
        return back_q, back_own, Move(swap, back_other)

    def project_step(layer, back_q, back_own, back_got, back_branch, sums, moves, beside=lambda: (), ready=()):
        return host(
            lambda q, k, kx, *more: (
                *project_back(layer, meta, q, k, kx, proj_qkv, kept[layer][0], gain_one, back_branch, sums),
                *beside(*more),
            ),
            (back_q, back_own, back_got) + tuple(ready), *moves
        )

    def feed_step(layer, back_out, sums, moves):
        middle, slope = kept[layer][9], kept[layer][12]
        return host(
            lambda b: feed_back(layer, meta, b, slope, proj_up, proj_down, middle, gain_two, proj_out, sums),
            (back_out,), *moves
        )

    def down_step(layer, back_out, back_out_x, active_x, moves):
        active = kept[layer][11]
        return Reduction(exchange, *host(
            lambda b, bx: down_gradients(meta, chips, active, active_x, b, bx), (back_out, back_out_x), *moves
        ))

    def up_step(layer, back_up, back_up_x, back_branch, branch_x, normed_x, moves):
        normed, attended, attended_x = kept[layer][10], kept[layer][7], kept[layer][8].value
        return Reduction(exchange, *host(
            lambda b, bx: up_gradients(
                meta, chips, normed, normed_x, b, bx, attended, attended_x, back_branch, branch_x
            ),
            (back_up, back_up_x), *moves
        ))

    def qkv_step(layer, mine, theirs_x, sums, moves):
        hidden, hidden_x = kept[layer][1], kept[layer][2].value
        return Reduction(exchange, *host(
            lambda b, bx: qkv_gradients(meta, chips, hidden, hidden_x, b, bx, sums), (mine, theirs_x), *moves
        ))

    got_cotangent = Move(mirror, cotangent_send)
    (stream,), moves, saved = forward(0, stream, (), (got_cotangent,))
    kept = [saved]
    back_out, back_out_send = weigh(
        own_weight.reshape(1), own_start.reshape(1), cotangent_own, got_cotangent.value
    )
    back_out_x = Move(swap, back_out_send)
    (stream, stream_send), last_moves, saved = forward(1, stream, moves, (back_out_x,))
    normed_x, active_x = (move.value for move in moves)
    kept.append(saved)
    outputs_move = Move(mirror, stream_send)

    sums = jnp.zeros((8, width), F32)
    back_up, back_up_send, back_branch, branch_send, back_attended, sums = feed_step(
        1, back_out, sums, last_moves + (outputs_move,)
    )
    last_normed_x, last_active_x = (move.value for move in last_moves)
    back_up_x, branch_x = Move(swap, back_up_send), Move(swap, branch_send)
    down1 = down_step(1, back_out, back_out_x.value, last_active_x, (back_up_x, branch_x))
    back_q, back_own, back_got = attention_step(1, back_attended, (down1,))
    up1 = up_step(1, back_up, back_up_x.value, back_branch, branch_x.value, last_normed_x, (down1, back_got))
    mine, theirs, back_out, back_out_send, sums = project_step(
        1, back_q, back_own, back_got.value, back_branch, sums, (up1, down1)
    )
    theirs_x = Move(swap, theirs)
    down0 = down_step(0, back_out, swap(back_out_send), active_x, (theirs_x, up1, down1))
    back_up, back_up_send, back_branch, branch_send, back_attended, sums0 = feed_step(
        0, back_out, sums, (down0, up1)
    )
    back_up_x, branch_x = Move(swap, back_up_send), Move(swap, branch_send)
    qkv1 = qkv_step(1, mine, theirs_x.value, sums, (back_up_x, branch_x, down0, up1))
    up0 = up_step(0, back_up, back_up_x.value, back_branch, branch_x.value, normed_x, (qkv1,))
    back_q, back_own, back_got = attention_step(0, back_attended, (up0, down0))
    unit = width // chips

    def return_slot(value, got):
        own = jnp.where(own_first, value[:rows], value[rows:])
        return jnp.where(side == 0, jnp.stack([own, got]), jnp.stack([got, own]))

    each = unit // 2
    whole_tiles = each % 8 == 0 and exchange.bits == 4
    ready = (outputs_move.value,) + tuple(down1.parts) + tuple(up1.parts)

    def beside(got, *parts):
        count = len(down1.parts)
        return (return_slot(stream, got), *collect([(parts[:count], 8 * each), (parts[count:], unit)]))

    mine, theirs, back_out, back_out_send, sums, back_send, *finished = project_step(
        0, back_q, back_own, swap(back_got.value), back_branch, sums0, (up0, qkv1, down0),
        *((beside, ready) if whole_tiles else ()),
    )
    back_move = Move(mirror, back_send)
    qkv0 = qkv_step(0, mine, swap(theirs), sums, (up0, back_move))
    back_inputs = return_slot(back_out, back_move.value).astype(F32)
    if not whole_tiles:
        for one in (down0, down1, up0, up1, qkv0, qkv1):
            one.complete()
        shares = [jnp.concatenate([total(d.parts), total(u.parts)], 0) for d, u in ((down0, up0), (down1, up1))]
        down, up, out = (
            jnp.stack(value) for value in zip(*(unpack_mlp(share, unit, core, exchange) for share in shares))
        )
        (qkv_a, table), (qkv_b, unused) = (unpack_qkv(total(one.parts), core, exchange) for one in (qkv0, qkv1))
        qkv = jnp.stack([qkv_a, qkv_b])
        outputs = return_slot(stream, outputs_move.value)
    else:
        outputs, mine_b, theirs_b = finished
        mine_a, got_a, got_b, last_q, last_got, mine_q, got_q = last_exchanges(qkv0, qkv1, up0, down0, theirs_b)
        up, down, out = place_mlp(each, mine_a, got_a, mine_b, got_b)
        qkv, table = place_qkv(last_q, last_got, mine_q, got_q)
        table = table[:, :8]
    table = table.T.reshape(LAYERS, 4, each)
    return outputs, back_inputs, table[:, 0], table[:, 1], qkv, out, table[:, 2], table[:, 3], up, down


def solution(mesh):
    tokens = P("dp", "seq", None)
    shared = P(None, AXES)
    in_specs = (tokens, tokens, P("dp"), P("dp", None)) + (P(),) * 8
    out_specs = (
        tokens, tokens, shared, shared, P(None, AXES, None), P(None, AXES, None),
        shared, shared, P(None, AXES, None), P(None, AXES, None),
    )
    return jax.shard_map(
        per_device, mesh=mesh, in_specs=in_specs, out_specs=out_specs, check_vma=False
    )
```

```python
import functools
import math

import jax
import jax.numpy as jnp
import numpy as np
from jax import lax
from jax.experimental import pallas as pl
from jax.experimental.pallas import tpu as pltpu
from jax.sharding import PartitionSpec as P

HEADS = 12
HEAD_DIM = 64
LAYERS = 2
TASKS = 3
AXES = ("dp", "seq")
F32 = jnp.float32
BF16 = jnp.bfloat16
epsilon = 1e-05
PAIRS = 2
VMEM_BYTES = 32 * 1024 * 1024
SMALL_COST = pl.CostEstimate(flops=1000, bytes_accessed=1000, transcendentals=0)


def in_hbm(*values):
    return tuple(pltpu.with_memory_space_constraint(v, pltpu.HBM) for v in values)


def dot_nn(a, b):
    return lax.dot_general(a, b, (((1,), (0,)), ((), ())), preferred_element_type=F32)


def dot_nt(a, b):
    return lax.dot_general(a, b, (((1,), (1,)), ((), ())), preferred_element_type=F32)


def dot_tn(a, b):
    return lax.dot_general(a, b, (((0,), (0,)), ((), ())), preferred_element_type=F32)


def gelu_and_slope(x):
    z = jnp.abs(x) * 0.7071067811865476
    d = 1.0 + 0.3275911 * z
    t = pl.reciprocal(d, approx=True)
    t = t * (2.0 - d * t)
    poly = t * (
        0.254829592
        + t * (-0.284496736 + t * (1.421413741 + t * (-1.453152027 + t * 1.061405429)))
    )
    bell = jnp.exp(-0.5 * x * x)
    tail = 0.5 * poly * bell
    below = jnp.where(x >= 0.0, 1.0 - tail, tail)
    return x * below, below + x * bell * 0.3989422804014327


def head_masks(scale):
    lane = lax.broadcasted_iota(jnp.int32, (1, 2 * HEAD_DIM), 1)
    first = jnp.where(lane < HEAD_DIM, scale, 0.0)
    return first.astype(BF16), (scale - first).astype(BF16)


def stacked(value, masks):
    return jnp.concatenate([value * masks[0], value * masks[1]], 0)


def merged(value):
    rows = value.shape[0] // 2
    lane = lax.broadcasted_iota(jnp.int32, (rows, 2 * HEAD_DIM), 1)
    return jnp.where(lane < HEAD_DIM, value[:rows], value[rows:])


def by_variant(meta, run):
    @pl.when(meta[0] == 0)
    def _():
        run(0)

    @pl.when(meta[0] == 1)
    def _():
        run(1)


def attention_forward_kernel(meta, q_ref, ko_ref, vo_ref, kx_ref, vx_ref, out_ref, lse_ref):
    def run_all(variant):
        for pair in range(PAIRS):
            lanes = (slice(None), slice(pair * 2 * HEAD_DIM, (pair + 1) * 2 * HEAD_DIM))
            refs = [ref.at[lanes] for ref in (q_ref, ko_ref, vo_ref, kx_ref, vx_ref, out_ref)]
            attention_forward_pair(variant, *refs, lse_ref.at[pair])

    by_variant(meta, run_all)


def attention_forward_pair(variant, q_ref, ko_ref, vo_ref, kx_ref, vx_ref, out_ref, lse_ref):
    rows = q_ref.shape[0] // 2
    masks = head_masks(1.0 / math.sqrt(HEAD_DIM))

    def run(variant):
        position = lax.broadcasted_iota(jnp.int32, (2 * rows, rows), 0) % rows
        below = lax.broadcasted_iota(jnp.int32, (2 * rows, rows), 1) <= position
        low, high = slice(0, rows), slice(rows, 2 * rows)
        if variant == 0:
            plan = [
                (low, [(ko_ref, vo_ref, low)]),
                (high, [(ko_ref, vo_ref, low), (kx_ref, vx_ref, low), (kx_ref, vx_ref, high), (ko_ref, vo_ref, high)]),
            ]
        else:
            plan = [
                (low, [(kx_ref, vx_ref, low), (ko_ref, vo_ref, low)]),
                (high, [(ko_ref, vo_ref, low), (kx_ref, vx_ref, low), (ko_ref, vo_ref, high)]),
            ]
        all_scores = []
        for span, parts in plan:
            q2 = stacked(q_ref[span, :], masks)
            all_scores.append([dot_nt(q2, keys[place, :]) for keys, unused, place in parts])
        for (span, parts), scores in zip(plan, all_scores):
            scores[-1] = jnp.where(below, scores[-1], -1e30)
            peak = jnp.max(functools.reduce(jnp.maximum, scores), -1, keepdims=True)
            total, acc = None, None
            for part, (unused, values, place) in zip(scores, parts):
                raised = jnp.exp(part - peak)
                total = raised if total is None else total + raised
                term = dot_nn(raised.astype(BF16), values[place, :])
                acc = term if acc is None else acc + term
            total = jnp.sum(total, -1, keepdims=True)
            out_ref[span, :] = merged(acc / total).astype(BF16)
            log = peak + jnp.log(total)
            lane = lax.broadcasted_iota(jnp.int32, (rows, 2 * HEAD_DIM), 1)
            lse_ref[:, span] = jnp.where(lane == 0, log[:rows], log[rows:]).T[:8, :]

    run(variant)


def attention_forward(meta, queries, own, other):
    tokens = queries.shape[0]
    pairs = HEADS // 2
    wide = 2 * HEAD_DIM * PAIRS

    def at(offset):
        return pl.BlockSpec((tokens, wide), lambda g, m: (0, offset // PAIRS + g))

    return pl.pallas_call(
        attention_forward_kernel,
        grid_spec=pltpu.PrefetchScalarGridSpec(
            num_scalar_prefetch=1,
            grid=(pairs // PAIRS,),
            in_specs=[at(0), at(0), at(pairs), at(0), at(pairs)],
            out_specs=[at(0), pl.BlockSpec((PAIRS, 8, tokens), lambda g, m: (g, 0, 0))],
        ),
        out_shape=[
            pltpu.HBM((tokens, HEADS * HEAD_DIM), BF16),
            pltpu.HBM((pairs, 8, tokens), F32),
        ],
        compiler_params=pltpu.CompilerParams(vmem_limit_bytes=VMEM_BYTES),
        cost_estimate=SMALL_COST,
        name="attention_forward",
    )(meta, *in_hbm(queries, own, own, other, other))


def attention_backward_kernel(
    meta, q_ref, ko_ref, vo_ref, kx_ref, vx_ref, do_ref, o_ref, lse_ref,
    dq_ref, own_ref, other_ref, q4, do4,
):
    def run_all(variant):
        for pair in range(PAIRS):
            lanes = (slice(None), slice(pair * 2 * HEAD_DIM, (pair + 1) * 2 * HEAD_DIM))
            refs = [ref.at[lanes] for ref in (q_ref, ko_ref, vo_ref, kx_ref, vx_ref, do_ref, o_ref)]
            grads = [ref.at[(slice(None),) + lanes] for ref in (own_ref, other_ref)]
            attention_backward_pair(
                variant, *refs, lse_ref.at[pair], dq_ref.at[lanes], *grads, q4.at[pair], do4.at[pair]
            )

    by_variant(meta, run_all)


def attention_backward_pair(
    variant, q_ref, ko_ref, vo_ref, kx_ref, vx_ref, do_ref, o_ref, lse_ref,
    dq_ref, own_ref, other_ref, q4, do4,
):
    rows = q_ref.shape[0] // 2
    scale = 1.0 / math.sqrt(HEAD_DIM)
    scaled, plain = head_masks(scale), head_masks(1.0)
    product = (do_ref[...].astype(F32) * o_ref[...].astype(F32)).T
    first = jnp.sum(product[:HEAD_DIM], 0, keepdims=True)
    second = jnp.sum(product[HEAD_DIM:], 0, keepdims=True)
    logs = lse_ref[...]
    dot_row = jnp.concatenate([first[:, :rows], second[:, :rows], first[:, rows:], second[:, rows:]], 1)
    log_row = jnp.concatenate(
        [logs[0:1, :rows], logs[1:2, :rows], logs[0:1, rows:], logs[1:2, rows:]], 1
    )
    for block in range(2):
        span = slice(block * rows, (block + 1) * rows)
        q4[2 * block * rows : 2 * (block + 1) * rows, :] = stacked(q_ref[span, :], scaled)
        do4[2 * block * rows : 2 * (block + 1) * rows, :] = stacked(do_ref[span, :], plain)

    def run(variant):
        column = lax.broadcasted_iota(jnp.int32, (rows, 2 * rows), 1) % rows
        below = lax.broadcasted_iota(jnp.int32, (rows, 2 * rows), 0) <= column
        low, high = slice(0, rows), slice(rows, 2 * rows)
        both, upper, lower = slice(0, 4 * rows), slice(2 * rows, 4 * rows), slice(0, 2 * rows)
        plan = [(0, low, lower, True), (0, low, upper, False), (1, low, upper, False), (0, high, upper, True)]
        plan.insert(3, (1, high, upper, False) if variant == 0 else (1, low, lower, False))
        keys, values, grads = (ko_ref, kx_ref), (vo_ref, vx_ref), (own_ref, other_ref)
        dq_parts = {}
        sums = {}
        ahead = {}

        def products(index):
            source, place, cols, unused = plan[index]
            ahead[index] = dot_nt(keys[source][place, :], q4[cols, :]), dot_nt(values[source][place, :], do4[cols, :])

        products(0)
        products(1)
        for index, (source, place, cols, diagonal) in enumerate(plan):
            if index + 2 < len(plan):
                products(index + 2)
            scores, back = ahead.pop(index)
            raised = jnp.exp(scores - log_row[:, cols])
            if diagonal:
                raised = jnp.where(below, raised, 0.0)
            slope = (raised * (back - dot_row[:, cols])).astype(BF16)
            slot = (source, place.start)
            terms = dot_nn(slope, q4[cols, :]), dot_nn(raised.astype(BF16), do4[cols, :])
            sums[slot] = tuple(a + b for a, b in zip(sums[slot], terms)) if slot in sums else terms
            term = dot_tn(slope, keys[source][place, :])
            dq_parts[cols.start] = dq_parts[cols.start] + term if cols.start in dq_parts else term
        for block in range(2):
            dq_ref[block * rows : (block + 1) * rows, :] = (
                merged(dq_parts[2 * block * rows]) * scale
            ).astype(BF16)
        for source in range(2):
            for place in (low, high):
                zero = jnp.zeros((rows, 2 * HEAD_DIM), F32)
                for which, value in enumerate(sums.get((source, place.start), (zero, zero))):
                    grads[source][which, place, :] = value.astype(grads[source].dtype)

    run(variant)


def attention_backward(meta, queries, own, other, back_attended, attended, logs):
    tokens = queries.shape[0]
    pairs = HEADS // 2
    wide = 2 * HEAD_DIM * PAIRS
    width = HEADS * HEAD_DIM

    def at(offset):
        return pl.BlockSpec((tokens, wide), lambda g, m: (0, offset // PAIRS + g))

    return pl.pallas_call(
        attention_backward_kernel,
        grid_spec=pltpu.PrefetchScalarGridSpec(
            num_scalar_prefetch=1,
            grid=(pairs // PAIRS,),
            in_specs=[at(0), at(0), at(pairs), at(0), at(pairs), at(0), at(0),
                      pl.BlockSpec((PAIRS, 8, tokens), lambda g, m: (g, 0, 0))],
            out_specs=[at(0)] + [pl.BlockSpec((2, tokens, wide), lambda g, m: (0, 0, g))] * 2,
            scratch_shapes=[pltpu.VMEM((PAIRS, 2 * tokens, 2 * HEAD_DIM), BF16)] * 2,
        ),
        out_shape=[
            jax.ShapeDtypeStruct((tokens, width), BF16),
            pltpu.HBM((2, tokens, width), BF16),
            jax.ShapeDtypeStruct((2, tokens, width), BF16),
        ],
        compiler_params=pltpu.CompilerParams(vmem_limit_bytes=VMEM_BYTES),
        cost_estimate=SMALL_COST,
        name="attention_backward",
    )(meta, *in_hbm(queries, own, own, other, other, back_attended, attended, logs))


def normalised(rows_in):
    average = jnp.mean(rows_in, -1, keepdims=True)
    centred = rows_in - average
    inverse = lax.rsqrt(jnp.mean(centred * centred, -1, keepdims=True) + epsilon)
    return centred * inverse, inverse


def norm_back(rows_in, gain_row, back):
    unit, inverse = normalised(rows_in)
    slope = back * gain_row
    first = jnp.mean(slope, -1, keepdims=True)
    second = jnp.mean(slope * unit, -1, keepdims=True)
    return inverse * (slope - first - unit * second), (
        jnp.sum(back * unit, 0, keepdims=True), jnp.sum(back, 0, keepdims=True))


def with_rows(table, row, sums):
    index = lax.broadcasted_iota(jnp.int32, table.shape, 0)
    return jnp.where(index == row, sums[0], jnp.where(index == row + 1, sums[1], table))


def project_kernel(layer, stream, gain, shift, matrix, hidden, queries, pairs):
    width = stream.shape[1]
    groups = 4
    rows = stream.shape[0] // groups
    for group in range(groups):
        span = slice(group * rows, (group + 1) * rows)
        unit, unused = normalised(stream[span, :].astype(F32))
        hidden[span, :] = (unit * gain[layer : layer + 1] + shift[layer : layer + 1]).astype(BF16)
        pairs[span, :] = dot_nn(hidden[span, :], matrix[0, :, width:]).astype(BF16)
        queries[span, :] = dot_nn(hidden[span, :], matrix[0, :, :width]).astype(BF16)


def project(layer, stream, gain, shift, matrix):
    tokens, width = stream.shape
    whole = pl.BlockSpec((tokens, width), lambda j: (0, 0))
    row = pl.BlockSpec(gain.shape, lambda j: (0, 0))
    return pl.pallas_call(
        functools.partial(project_kernel, layer),
        grid=(1,),
        in_specs=[whole, row, row, pl.BlockSpec((1, width, 3 * width), lambda j: (layer, 0, 0))],
        out_specs=[whole, whole, pl.BlockSpec((tokens, 2 * width), lambda j: (0, 0))],
        out_shape=[
            pltpu.HBM((tokens, width), BF16),
            pltpu.HBM((tokens, width), BF16),
            pltpu.HBM((tokens, 2 * width), BF16),
        ],
        compiler_params=pltpu.CompilerParams(vmem_limit_bytes=VMEM_BYTES),
        cost_estimate=SMALL_COST,
        name="project",
    )(*in_hbm(stream), gain, shift, *in_hbm(matrix))


def feed_forward_kernel(
    layer, steps, attended, stream, matrix_out, gain, shift, up, down,
    middle, normed, active_ref, slope_ref, out, *rest,
):
    acc = rest[-1]
    step = pl.program_id(0)

    @pl.when(step == 0)
    def _():
        acc[...] = stream[...].astype(F32) + dot_nn(attended[...], matrix_out[0])
        middle[...] = acc[...].astype(BF16)
        unit, unused = normalised(acc[...])
        normed[...] = (unit * gain[layer : layer + 1] + shift[layer : layer + 1]).astype(BF16)

    groups = 4
    rows = normed.shape[0] // groups
    raw = {}
    for group in range(groups + 1):
        if group < groups:
            raw[group] = dot_nn(normed[group * rows : (group + 1) * rows, :], up[0])
        if group > 0:
            span = slice((group - 1) * rows, group * rows)
            active, slope = gelu_and_slope(raw.pop(group - 1))
            active = active.astype(BF16)
            active_ref[span, :] = active
            slope_ref[span, :] = slope.astype(BF16)
            acc[span, :] += dot_nn(active, down[0])

    @pl.when(step == steps - 1)
    def _():
        out[...] = acc[...].astype(out.dtype)
        if len(rest) == 2:
            rest[0][...] = acc[other_block(acc.shape[0] // 2), :].astype(out.dtype)


def other_block(rows):
    return pl.ds(pl.multiple_of((1 - lax.axis_index("seq") // 2) * rows, rows), rows)


def feed_forward(layer, attended, stream, matrix_out, gain, shift, up, down):
    tokens, width = stream.shape
    last = layer == LAYERS - 1
    block = pl.BlockSpec((tokens // 2, width), lambda j: (0, 0))
    hidden = up.shape[2]
    tile = 1024
    steps = hidden // tile
    whole = pl.BlockSpec((tokens, width), lambda j: (0, 0))
    row = pl.BlockSpec(gain.shape, lambda j: (0, 0))
    part = pl.BlockSpec((tokens, tile), lambda j: (0, j))
    return pl.pallas_call(
        functools.partial(feed_forward_kernel, layer, steps),
        grid=(steps,),
        in_specs=[
            whole, whole, pl.BlockSpec((1, width, width), lambda j: (layer, 0, 0)), row, row,
            pl.BlockSpec((1, width, tile), lambda j: (layer, 0, j)),
            pl.BlockSpec((1, tile, width), lambda j: (layer, j, 0)),
        ],
        out_specs=[whole, whole, part, part, whole] + [block] * last,
        out_shape=[
            pltpu.HBM((tokens, width), BF16),
            pltpu.HBM((tokens, width), BF16),
            pltpu.HBM((tokens, hidden), BF16),
            pltpu.HBM((tokens, hidden), BF16),
            pltpu.HBM((tokens, width), BF16),
        ] + [jax.ShapeDtypeStruct((tokens // 2, width), BF16)] * last,
        scratch_shapes=[pltpu.VMEM((tokens, width), F32)],
        compiler_params=pltpu.CompilerParams(vmem_limit_bytes=VMEM_BYTES),
        cost_estimate=SMALL_COST,
        name="feed_forward",
    )(*in_hbm(attended, stream, matrix_out), gain, shift, *in_hbm(up, down))


def feed_back_kernel(
    layer, steps, meta, back_out, slope, up, down, middle, gain, matrix_out, sums_in,
    own, send, back_branch, branch_send, back_attended, grads, acc,
):
    step = pl.program_id(0)
    half = branch_send.shape[1]
    theirs = pl.ds(pl.multiple_of((1 - meta[1]) * half, 128), half)

    @pl.when(step == 0)
    def _():
        acc[...] = jnp.zeros_like(acc)

    back_up = (dot_nt(back_out[...], down[0]) * slope[...].astype(F32)).astype(BF16)

    @pl.when(step < steps // 2)
    def _():
        send[...] = back_up

    @pl.when(step >= steps // 2)
    def _():
        own[...] = back_up

    acc[...] += dot_nt(back_up, up[0])

    @pl.when(step == steps - 1)
    def _():
        back, sums = norm_back(middle[...].astype(F32), gain[layer : layer + 1], acc[...])
        back = back + back_out[...].astype(F32)
        grads[...] = with_rows(sums_in[...], 4 * layer + 2, sums)
        back_branch[...] = back.astype(BF16)
        branch_send[...] = back_branch[:, theirs]
        back_attended[...] = dot_nt(back_branch[...], matrix_out[0]).astype(BF16)


def feed_back(layer, meta, back_out, slope, up, down, middle, gain, matrix_out, sums):
    tokens, width = back_out.shape
    hidden = up.shape[2]
    tile = 768
    steps = hidden // tile
    half = steps // 2

    def place(j, m):
        return jnp.where(j < half, (1 - m[1]) * half + j, m[1] * half + j - half)

    whole = pl.BlockSpec((tokens, width), lambda j, m: (0, 0))
    narrow = pl.BlockSpec((tokens, width // 2), lambda j, m: (0, 0))
    wide = jax.ShapeDtypeStruct((tokens, width), BF16)
    return pl.pallas_call(
        functools.partial(feed_back_kernel, layer, steps),
        grid_spec=pltpu.PrefetchScalarGridSpec(
            num_scalar_prefetch=1,
            grid=(steps,),
            in_specs=[
                whole, pl.BlockSpec((tokens, tile), lambda j, m: (0, place(j, m))),
                pl.BlockSpec((1, width, tile), lambda j, m: (layer, 0, place(j, m))),
                pl.BlockSpec((1, tile, width), lambda j, m: (layer, place(j, m), 0)),
                whole, pl.BlockSpec(gain.shape, lambda j, m: (0, 0)),
                pl.BlockSpec((1, width, width), lambda j, m: (layer, 0, 0)),
                pl.BlockSpec((8, width), lambda j, m: (0, 0)),
            ],
            out_specs=[
                pl.BlockSpec((tokens, tile), lambda j, m: (0, jnp.maximum(j - half, 0))),
                pl.BlockSpec((tokens, tile), lambda j, m: (0, jnp.minimum(j, half - 1))),
                whole, narrow, whole,
                pl.BlockSpec((8, width), lambda j, m: (0, 0)),
            ],
            scratch_shapes=[pltpu.VMEM((tokens, width), F32)],
        ),
        out_shape=[
            jax.ShapeDtypeStruct((tokens, hidden // 2), BF16),
            jax.ShapeDtypeStruct((tokens, hidden // 2), BF16),
            wide, jax.ShapeDtypeStruct((tokens, width // 2), BF16),
            wide, jax.ShapeDtypeStruct((8, width), F32),
        ],
        compiler_params=pltpu.CompilerParams(vmem_limit_bytes=VMEM_BYTES),
        cost_estimate=SMALL_COST,
        name="feed_back",
    )(meta, back_out, *in_hbm(slope, up, down, middle), gain, *in_hbm(matrix_out), sums)


def project_back_kernel(
    layer, meta, back_q, own, got, matrix, stream, gain, back_middle, sums_in,
    mine, theirs, back_out, back_out_send, grads, *rest,
):
    width = back_q.shape[1]
    table, acc = rest[-2:]

    def begin():
        table[0] = back_q[...]
        for which in range(2):
            table[1 + which] = (own[which].astype(F32) + got[which].astype(F32)).astype(BF16)
        half = width // 2

        @pl.when(meta[1] == 0)
        def _():
            mine[:, :width] = table[0]
            mine[:, width:] = table[1, :, :half]
            theirs[:, :half] = table[1, :, half:]
            theirs[:, half:] = table[2]

        @pl.when(meta[1] == 1)
        def _():
            theirs[:, :width] = table[0]
            theirs[:, width:] = table[1, :, :half]
            mine[:, :half] = table[1, :, half:]
            mine[:, half:] = table[2]

    begin()
    acc[...] = sum(
        dot_nt(table[which], matrix[0, :, which * width : (which + 1) * width]) for which in range(3)
    )

    def end():
        back, sums = norm_back(stream[...].astype(F32), gain[layer : layer + 1], acc[...])
        back = back + back_middle[...].astype(F32)
        back_out[...] = back.astype(BF16)
        half = width // 2
        back_out_send[...] = back_out[:, pl.ds(pl.multiple_of((1 - meta[1]) * half, 128), half)]
        grads[...] = with_rows(sums_in[...], 4 * layer, sums)
        if len(rest) == 3:
            rest[0][...] = back_out[other_block(back_out.shape[0] // 2), :]

    end()


def project_back(layer, meta, back_q, own, got, matrix, stream, gain, back_middle, sums):
    tokens, width = stream.shape
    whole = pl.BlockSpec((tokens, width), lambda j, m: (0, 0))
    both = pl.BlockSpec((2, tokens, width), lambda j, m: (0, 0, 0))
    side = pl.BlockSpec((tokens, 3 * width // 2), lambda j, m: (0, 0))
    return pl.pallas_call(
        functools.partial(project_back_kernel, layer),
        grid_spec=pltpu.PrefetchScalarGridSpec(
            num_scalar_prefetch=1,
            grid=(1,),
            in_specs=[
                whole, both, both, pl.BlockSpec((1, width, 3 * width), lambda j, m: (layer, 0, 0)),
                whole, pl.BlockSpec(gain.shape, lambda j, m: (0, 0)), whole,
                pl.BlockSpec((8, width), lambda j, m: (0, 0)),
            ],
            out_specs=[side, side, whole, pl.BlockSpec((tokens, width // 2), lambda j, m: (0, 0)),
                       pl.BlockSpec((8, width), lambda j, m: (0, 0))]
            + [pl.BlockSpec((tokens // 2, width), lambda j, m: (0, 0))] * (layer == 0),
            scratch_shapes=[pltpu.VMEM((3, tokens, width), BF16), pltpu.VMEM((tokens, width), F32)],
        ),
        out_shape=[
            jax.ShapeDtypeStruct((tokens, 3 * width // 2), BF16),
            jax.ShapeDtypeStruct((tokens, 3 * width // 2), BF16),
            jax.ShapeDtypeStruct((tokens, width), BF16),
            jax.ShapeDtypeStruct((tokens, width // 2), BF16),
            jax.ShapeDtypeStruct((8, width), F32),
        ] + [jax.ShapeDtypeStruct((tokens // 2, width), BF16)] * (layer == 0),
        compiler_params=pltpu.CompilerParams(vmem_limit_bytes=VMEM_BYTES),
        cost_estimate=SMALL_COST,
        name="project_back",
    )(meta, *in_hbm(back_q, own), got, *in_hbm(matrix, stream), gain, *in_hbm(back_middle), sums)


def weigh_kernel(weight, start, own, got, back_out, back_out_send):
    rows, half = own.shape[0], back_out_send.shape[1]
    place = lax.axis_index("seq")
    core, low = place % 2, ((place + 1) // 2) % 2
    step = lax.broadcasted_iota(jnp.int32, (rows, 1), 0)
    first = place < 2
    for which, block in enumerate((low, 3 - low)):
        span = slice(which * rows, (which + 1) * rows)
        scale = jnp.where(block * rows + step >= start[0], weight[0], 0.0)
        mine = own[...].astype(F32) if which == 0 else got[...].astype(F32)
        other = got[...].astype(F32) if which == 0 else own[...].astype(F32)
        back_out[span, :] = (jnp.where(first, mine, other) * scale).astype(BF16)
    back_out_send[...] = back_out[:, pl.ds(pl.multiple_of((1 - core) * half, 128), half)]


def weigh(weight, start, own, got):
    rows, width = own.shape
    scalar = pl.BlockSpec(memory_space=pltpu.SMEM)
    return pl.pallas_call(
        weigh_kernel,
        in_specs=[scalar, scalar, pl.BlockSpec(memory_space=pltpu.VMEM), pl.BlockSpec(memory_space=pltpu.VMEM)],
        out_specs=[pl.BlockSpec(memory_space=pltpu.VMEM)] * 2,
        out_shape=[
            jax.ShapeDtypeStruct((2 * rows, width), BF16),
            jax.ShapeDtypeStruct((2 * rows, width // 2), BF16),
        ],
        compiler_params=pltpu.CompilerParams(vmem_limit_bytes=VMEM_BYTES),
        cost_estimate=SMALL_COST,
        name="weigh",
    )(weight, start, own, got)


def store_chunks(chips, meta, acc, keep, send):
    rows = acc.shape[0] // chips
    for position in range(chips):
        chunk = acc[pl.ds(pl.multiple_of(meta[2 + position] * rows, 16), rows), :]
        if position < chips // 2:
            keep[position] = chunk
        else:
            send[position - chips // 2] = chunk


def grad_up_kernel(chips, meta, ao, ax, bo, bx, co, cx, do, dx, keep, send, acc):
    step = pl.program_id(0)
    rows, half = acc.shape[0] // chips, do.shape[1]

    @pl.when(step < 2)
    def _():
        acc[...] = (dot_tn(ao[...], bo[...]) + dot_tn(ax[...], bx[...])).astype(BF16)

    @pl.when(step == 2)
    def _():
        acc[:, :half] = (dot_tn(co[...], do[...]) + dot_tn(cx[...], dx[...])).astype(BF16)

    for position in range(chips):
        place = pl.ds(pl.multiple_of(meta[2 + position] * rows, 16), rows)
        target, index = (keep, position) if position < chips // 2 else (send, position - chips // 2)
        target[index, :rows, :] = acc[place, :half]
        target[index, rows:, :] = acc[place, half:]


def grad_down_kernel(chips, meta, ao, ax, bo, bx, *refs):
    keep, send = refs[-2:]
    rows = keep.shape[1]
    each = ao.shape[1] // rows
    total = (dot_tn(ao[...], bo[...]) + dot_tn(ax[...], bx[...])).astype(BF16)
    for local in range(each):
        position = meta[2 + chips + pl.program_id(0) * each + local]
        chunk = total[local * rows : (local + 1) * rows]

        @pl.when(position < chips // 2)
        def _():
            keep[position] = chunk

        @pl.when(position >= chips // 2)
        def _():
            send[position - chips // 2] = chunk


def grad_qkv_kernel(chips, meta, ao, ax, bo, bx, sums, keep, send, acc, columns):
    wide = bo.shape[1]
    acc[:, :wide] = (dot_tn(ao[...], bo[...]) + dot_tn(ax[...], bx[...])).astype(BF16)
    columns[...] = jnp.concatenate([sums[...], jnp.zeros((120, sums.shape[1]), F32)], 0).T
    acc[:, wide:] = columns[...].astype(BF16)
    store_chunks(chips, meta, acc, keep, send)


def ordered(total, ids, chips):
    split = total.astype(BF16).reshape(chips, total.shape[0] // chips, total.shape[1])
    return jnp.take(split, ids, axis=0)


def gradient_call(kernel, name, chips, grid, in_specs, out_spec, shape, scratch):
    return pl.pallas_call(
        functools.partial(kernel, chips),
        grid_spec=pltpu.PrefetchScalarGridSpec(
            num_scalar_prefetch=1, grid=(grid,), in_specs=in_specs, out_specs=[out_spec] * 2,
            scratch_shapes=scratch,
        ),
        out_shape=[pltpu.HBM(shape, BF16)] * 2,
        compiler_params=pltpu.CompilerParams(vmem_limit_bytes=VMEM_BYTES),
        cost_estimate=SMALL_COST,
        name=name,
    )


def up_gradients(
    meta, chips, normed, normed_x, back_up, back_up_x, attended, attended_x, back_branch, branch_x
):
    tokens, width = normed.shape
    half = width // 2
    rows = width // chips
    if rows % 16 != 0:
        ids = meta[2 : 2 + chips]
        up = dot_tn(normed, back_up) + dot_tn(normed_x, back_up_x)
        own = lax.dynamic_slice_in_dim(back_branch, meta[1] * half, half, 1)
        out = dot_tn(attended, own) + dot_tn(attended_x, branch_x)
        up = ordered(up, ids, chips).reshape(chips, rows, 4, half)
        up = up.transpose(0, 2, 1, 3).reshape(chips, 4 * rows, half)
        both = jnp.concatenate([up, ordered(out, ids, chips)], 1)
        return both[: chips // 2], both[chips // 2 :]
    whole = pl.BlockSpec((tokens, width), lambda j, m: (0, 0))
    fixed = pl.BlockSpec((tokens, half), lambda j, m: (0, 0))
    mine = pl.BlockSpec((tokens, half), lambda j, m: (0, m[1]))
    tile = pl.BlockSpec((tokens, 2 * half), lambda j, m: (0, jnp.minimum(j, 1)))
    return gradient_call(
        grad_up_kernel, "gradient_up", chips, 3, [whole, whole, tile, tile, whole, whole, mine, fixed],
        pl.BlockSpec((chips // 2, 2 * rows, half), lambda j, m: (0, j, 0)),
        (chips // 2, 5 * rows, half), [pltpu.VMEM((width, 2 * half), BF16)],
    )(meta, *in_hbm(normed, normed_x), back_up, back_up_x, *in_hbm(attended, attended_x), back_branch, branch_x)


def down_gradients(meta, chips, active, active_x, back_out, back_out_x):
    tokens, hidden = active.shape
    width = back_out.shape[1]
    half = width // 2
    rows = hidden // chips
    if rows % 64 != 0:
        own = lax.dynamic_slice_in_dim(back_out, meta[1] * half, half, 1)
        down = dot_tn(active, own) + dot_tn(active_x, back_out_x)
        down = ordered(down, meta[2 : 2 + chips], chips)
        return down[: chips // 2], down[chips // 2 :]
    fixed = pl.BlockSpec((tokens, half), lambda j, m: (0, 0))
    mine = pl.BlockSpec((tokens, half), lambda j, m: (0, m[1]))
    tile = pl.BlockSpec((tokens, 2 * width), lambda j, m: (0, j))
    return gradient_call(
        grad_down_kernel, "gradient_down", chips, hidden // (2 * width), [tile, tile, mine, fixed],
        pl.BlockSpec((chips // 2, rows, half), lambda j, m: (0, 0, 0)), (chips // 2, rows, half), [],
    )(meta, *in_hbm(active, active_x), back_out, back_out_x)


def qkv_gradients(meta, chips, hidden, hidden_x, back_projected, back_projected_x, sums):
    tokens, width = hidden.shape
    wide = back_projected.shape[1]
    rows = width // chips
    if rows % 16 != 0:
        qkv = dot_tn(hidden, back_projected) + dot_tn(hidden_x, back_projected_x)
        table = jnp.pad(sums.T, ((0, 0), (0, 120)))
        both = ordered(jnp.concatenate([qkv, table], -1), meta[2 : 2 + chips], chips)
        return both[: chips // 2], both[chips // 2 :]
    specs = [pl.BlockSpec((tokens, width), lambda j, m: (0, 0))] * 2
    specs += [pl.BlockSpec((tokens, wide), lambda j, m: (0, 0))] * 2
    specs += [pl.BlockSpec((8, width), lambda j, m: (0, 0))]
    return gradient_call(
        grad_qkv_kernel, "gradient_qkv", chips, 1, specs,
        pl.BlockSpec((chips // 2, rows, wide + 128), lambda j, m: (0, 0, 0)),
        (chips // 2, rows, wide + 128),
        [pltpu.VMEM((width, wide + 128), BF16), pltpu.VMEM((width, 128), F32)],
    )(meta, *in_hbm(hidden, hidden_x), back_projected, back_projected_x, sums)


class Exchange:
    def __init__(self, dp):
        self.dp = dp
        self.chips = 2 * dp
        self.bits = int(math.log2(self.chips))
        self.core_pairs = [(s, s ^ 1) for s in range(4)]
        self.mirror_pairs = [(s, 3 - s) for s in range(4)]
        rest = list(range(2, self.bits))
        self.orders = ([1, 0] + rest, [0, 1] + rest[::-1])

    def swap_core(self, value):
        return lax.ppermute(value, "seq", self.core_pairs)

    def mirror(self, value):
        return lax.ppermute(value, "seq", self.mirror_pairs)

    def pairs(self, phase):
        result = []
        for device in range(2 * self.chips):
            chip = (device // 4) * 2 + (device % 4) // 2
            core = device % 2
            other = chip ^ (1 << self.orders[core][phase])
            result.append((device, (other // 2) * 4 + (other % 2) * 2 + core))
        return result

    def tables(self, chip, core):
        index = np.arange(self.chips)
        maps = []
        for order in self.orders:
            value = np.zeros_like(index)
            for phase, bit in enumerate(order):
                value |= ((index >> (self.bits - 1 - phase)) & 1) << bit
            maps.append(value.astype(np.int32))
        ids = chip ^ jnp.where(core == 0, jnp.asarray(maps[0]), jnp.asarray(maps[1]))
        relative = jnp.asarray(index.astype(np.int32)) ^ chip
        places = []
        for order in self.orders:
            place = jnp.zeros_like(relative)
            for phase, bit in enumerate(order):
                place = place | (((relative >> bit) & 1) << (self.bits - 1 - phase))
            places.append(place)
        return ids.astype(jnp.int32), jnp.where(core == 0, places[0], places[1]).astype(jnp.int32)


class Reduction:
    def __init__(self, exchange, keep, send):
        self.exchange, self.parts, self.phase = exchange, [keep], 0
        self.first, self.kind = send, send.dtype

    def message(self):
        if self.phase == 0:
            return self.first
        size = self.parts[-1].shape[0]
        terms = [part[size // 2 : size].astype(F32) for part in self.parts]
        return functools.reduce(jnp.add, terms).astype(self.kind)

    def partner(self, phase):
        dp, seq = lax.axis_index("dp"), lax.axis_index("seq")
        where = []
        for order in self.exchange.orders:
            bit = order[phase]
            if bit == 0:
                where.append((dp, (seq + 2) % 4))
            else:
                size = 1 << (bit - 1)
                where.append((dp + size - 2 * size * ((dp // size) % 2), seq))
        (dp0, seq0), (dp1, seq1) = where
        return dp0 + (seq % 2) * (dp1 - dp0), seq0 + (seq % 2) * (seq1 - seq0)

    def transfer(self, message):
        self.phase += 1
        return lax.ppermute(message, AXES, self.exchange.pairs(self.phase - 1))

    def arrived(self, value):
        self.parts.append(value)

    def complete(self):
        while self.phase < self.exchange.bits:
            self.arrived(self.transfer(self.message()))


def total(parts):
    return functools.reduce(jnp.add, [part[0].astype(F32) for part in parts])


class Move:
    def __init__(self, transfer, value):
        self.transfer, self.value = transfer, value

    def message(self):
        return self.value

    def arrived(self, value):
        self.value = value


def host(run, inputs, *moves):
    count = len(inputs)
    tied = lax.optimization_barrier(tuple(inputs) + tuple(move.message() for move in moves))
    results = tuple(run(*tied[:count]))
    got = tuple(move.transfer(message) for move, message in zip(moves, tied[count:]))
    tied = lax.optimization_barrier(results + got)
    for move, value in zip(moves, tied[len(results) :]):
        move.arrived(value)
    return tied[: len(results)]


def by_core(core, mine, theirs, axis):
    return jnp.where(
        core == 0,
        jnp.concatenate([mine, theirs], axis),
        jnp.concatenate([theirs, mine], axis),
    )


def small_call(kernel, name, shapes, operands, scratch=()):
    def spec(value):
        if value.ndim == 3 and value.dtype == BF16:
            return pl.BlockSpec((1,) + value.shape[1:], lambda i: (0, 0, 0))
        return pl.BlockSpec(value.shape, lambda i: (0,) * value.ndim)

    return pl.pallas_call(
        kernel,
        grid=(1,),
        in_specs=[spec(value) for value in operands],
        out_specs=[spec(shape) for shape in shapes],
        out_shape=shapes,
        scratch_shapes=list(scratch),
        compiler_params=pltpu.CompilerParams(vmem_limit_bytes=VMEM_BYTES),
        cost_estimate=SMALL_COST,
        name=name,
    )(*operands)


def collect(groups):
    counts = [len(parts) for parts, unused in groups]
    units = [unit for unused, unit in groups]
    totals = [parts[0].shape[1:] for parts, unused in groups]
    wide = totals[0][1]
    half = sum(rows for rows, unused in totals) // 2

    def kernel(*refs):
        refs = list(refs)
        core = lax.axis_index("seq") % 2
        mine, theirs = refs[sum(counts) : sum(counts) + 2]
        sums = refs[sum(counts) + 2 :]
        at = 0
        for count, unit, scratch in zip(counts, units, sums):
            parts, refs = refs[:count], refs[count:]
            scratch[...] = functools.reduce(jnp.add, [part[0].astype(F32) for part in parts])
            each = unit // 2
            for start in range(0, scratch.shape[0], unit):
                span = slice(at, at + each)
                mine[span, :] = scratch[pl.ds(pl.multiple_of(start + core * each, 8), each), :]
                theirs[span, :] = scratch[pl.ds(pl.multiple_of(start + (1 - core) * each, 8), each), :]
                at += each

    shape = jax.ShapeDtypeStruct((half, wide), F32)
    operands = in_hbm(*[part for parts, unused in groups for part in parts])
    return small_call(kernel, "collect", [shape, shape], operands, [pltpu.VMEM(t, F32) for t in totals])


def place_mlp(each, mine_a, theirs_a, mine_b, theirs_b):
    half = mine_a.shape[1]

    def kernel(*refs):
        ups, downs, outs = refs[4:]
        core = lax.axis_index("seq") % 2
        for layer in range(2):
            for side, value in ((core, refs[2 * layer]), (1 - core, refs[2 * layer + 1])):
                narrow = pl.ds(pl.multiple_of(side * half, 128), half)
                downs[layer, :, narrow] = value[: 4 * each, :]
                for unit in range(4):
                    lanes = pl.ds(pl.multiple_of(side * 4 * half + unit * half, 128), half)
                    ups[layer, :, lanes] = value[(4 + unit) * each : (5 + unit) * each, :]
                outs[layer, :, narrow] = value[8 * each :, :]

    shapes = [
        jax.ShapeDtypeStruct((2, each, 8 * half), F32), jax.ShapeDtypeStruct((2, 4 * each, 2 * half), F32),
        jax.ShapeDtypeStruct((2, each, 2 * half), F32),
    ]
    return small_call(kernel, "place", shapes, (mine_a, theirs_a, mine_b, theirs_b))


def place_qkv(mine_a, theirs_a, mine_b, theirs_b):
    each, wide = mine_a.shape
    wide -= 128

    def kernel(*refs):
        out, table = refs[4:]
        core = lax.axis_index("seq") % 2
        for layer in range(2):
            for side, value in ((core, refs[2 * layer]), (1 - core, refs[2 * layer + 1])):
                out[layer, :, pl.ds(pl.multiple_of(side * wide, 128), wide)] = value[:, :wide]
        table[...] = refs[0][:, wide:] + refs[1][:, wide:]

    shapes = [jax.ShapeDtypeStruct((2, each, 2 * wide), F32), jax.ShapeDtypeStruct((each, 128), F32)]
    return small_call(kernel, "place_qkv", shapes, (mine_a, theirs_a, mine_b, theirs_b))


def last_exchanges(last, before, up, down, theirs_b):
    keep, message = last.parts[0], last.first
    chunk = keep.shape[1:]
    each, wide = chunk[0] // 2, chunk[1]
    up_rows, down_rows, half = up.parts[0].shape[1], down.parts[0].shape[1], up.parts[0].shape[2]
    mesh = pl.DeviceIdType.MESH

    def kernel(keep, message, *refs):
        refs = list(refs)

        def take(count):
            taken = refs[:count]
            del refs[:count]
            return taken

        before_parts, up_parts, down_parts, (theirs_b,) = take(3), take(4), take(5), take(1)
        mine_a, got_a, got_b, mine_l, got_l, mine_q, got_q = take(7)
        land1, land2, land3, land4, q_land3, q_land4, up_land = take(7)
        send2, send3, send4, q_send3, q_send4, up_send = take(6)
        sums, up_sum, down_sum, swap_q, swap_q_land, swap_a, swap_a_land = take(7)
        send_sem, recv_sem = take(2)
        seq = lax.axis_index("seq")
        core = seq % 2
        other = lax.axis_index("dp"), seq + 1 - 2 * core
        partners = [last.partner(phase) for phase in range(4)]
        barrier = pltpu.get_barrier_semaphore()
        for partner in partners + [other]:
            pl.semaphore_signal(barrier, inc=1, device_id=partner, device_id_type=mesh)
        pl.semaphore_wait(barrier, 5)

        def remote(index, source, target, partner):
            return pltpu.make_async_remote_copy(
                src_ref=source, dst_ref=target, send_sem=send_sem.at[index], recv_sem=recv_sem.at[index],
                device_id=partner, device_id_type=mesh,
            )

        def added(values, kind=BF16):
            return functools.reduce(jnp.add, [value.astype(F32) for value in values]).astype(kind)

        def rows_of(ref, start, count, side):
            return ref[pl.ds(pl.multiple_of(start + side * count, 8), count), :]

        pieces = (slice(4, 8), slice(2, 4), slice(0, 2))
        first = [remote(k, message.at[p], land1.at[p], partners[0]) for k, p in zip((0, 1, 13), pieces)]
        second = [remote(2, send2.at[2:4], land2.at[2:4], partners[1]), remote(3, send2.at[0:2], land2.at[0:2], partners[1])]
        third, fourth = remote(4, send3, land3, partners[2]), remote(5, send4, land4, partners[3])
        q_third, q_fourth = remote(6, q_send3, q_land3, partners[2]), remote(7, q_send4, q_land4, partners[3])
        up_fourth = remote(8, up_send, up_land, partners[3])
        swap_b, swap_own = (remote(9 + k, swap_a.at[k], swap_a_land.at[k], other) for k in range(2))
        swap_qs = [remote(11 + k, swap_q.at[k], swap_q_land.at[k], other) for k in range(2)]

        for copy in first:
            copy.start()
        up_send[...] = added([part[1:2] for part in up_parts])
        up_fourth.start()
        q_send3[...] = added([part[2:4] for part in before_parts])
        q_third.start()
        swap_a[0] = theirs_b[...]
        swap_b.start()
        down_sum[...] = added([part[0] for part in down_parts], F32)
        up_sum[...] = added([part[0] for part in up_parts], F32)
        sums[1] = added([part[0] for part in before_parts], F32)

        first[0].wait()
        send2[...] = added([keep[4:8], land1[4:8]])
        for copy in second:
            copy.start()

        q_third.wait()
        q_send4[...] = added([part[1:2] for part in before_parts] + [q_land3[1:2]])
        q_fourth.start()
        sums[1] = sums[1] + q_land3[0].astype(F32)

        up_fourth.wait()
        up_sum[...] = up_sum[...] + up_land[0].astype(F32)
        at = 0
        for scratch, unit in ((down_sum, 8 * each), (up_sum, 2 * each)):
            count = unit // 2
            for start in range(0, scratch.shape[0], unit):
                mine_a[at : at + count, :] = rows_of(scratch, start, count, core)
                swap_a[1, at : at + count, :] = rows_of(scratch, start, count, 1 - core)
                at += count
        swap_own.start()
        swap_b.wait()
        got_b[...] = swap_a_land[0]

        first[1].wait()
        second[0].wait()
        send3[...] = added([keep[2:4], land1[2:4], land2[2:4]])
        third.start()

        q_fourth.wait()
        sums[1] = sums[1] + q_land4[0].astype(F32)
        mine_q[...] = rows_of(sums.at[1], 0, each, core)
        swap_q[1] = rows_of(sums.at[1], 0, each, 1 - core)
        swap_qs[1].start()
        swap_own.wait()
        got_a[...] = swap_a_land[1]

        first[2].wait()
        second[1].wait()
        sums[0] = added([keep[0], land1[0], land2[0]], F32)
        third.wait()
        send4[...] = added([keep[1:2], land1[1:2], land2[1:2], land3[1:2]])
        fourth.start()
        swap_qs[1].wait()
        got_q[...] = swap_q_land[1]
        sums[0] = sums[0] + land3[0].astype(F32)
        fourth.wait()
        sums[0] = sums[0] + land4[0].astype(F32)
        mine_l[...] = rows_of(sums.at[0], 0, each, core)
        swap_q[0] = rows_of(sums.at[0], 0, each, 1 - core)
        swap_qs[0].start()
        swap_qs[0].wait()
        got_l[...] = swap_q_land[0]

    def leading(count, value):
        return pl.BlockSpec((count,) + value.shape[1:], lambda i: (0, 0, 0))

    long = theirs_b.shape
    flat, out = pl.BlockSpec(long, lambda i: (0, 0)), pl.BlockSpec((each, wide), lambda i: (0, 0))
    up_chunk = (1, up_rows, half)
    return pl.pallas_call(
        kernel,
        grid=(1,),
        in_specs=[leading(8, keep), pl.BlockSpec(memory_space=pl.ANY)]
        + [leading(4, part) for part in before.parts] + [leading(2, part) for part in up.parts]
        + [leading(1, part) for part in down.parts] + [flat],
        out_specs=[flat] * 3 + [out] * 4,
        out_shape=[jax.ShapeDtypeStruct(long, F32)] * 3 + [jax.ShapeDtypeStruct((each, wide), F32)] * 4,
        scratch_shapes=[pltpu.VMEM((size,) + chunk, BF16) for size in (8, 4, 2, 1, 2, 1)]
        + [pltpu.VMEM(up_chunk, BF16)]
        + [pltpu.VMEM((size,) + chunk, BF16) for size in (4, 2, 1, 2, 1)]
        + [
            pltpu.VMEM(up_chunk, BF16),
            pltpu.VMEM((2,) + chunk, F32), pltpu.VMEM(up_chunk[1:], F32), pltpu.VMEM((down_rows, half), F32),
            pltpu.VMEM((2, each, wide), F32), pltpu.VMEM((2, each, wide), F32),
            pltpu.VMEM((2,) + long, F32), pltpu.VMEM((2,) + long, F32),
            pltpu.SemaphoreType.DMA((14,)), pltpu.SemaphoreType.DMA((14,)),
        ],
        compiler_params=pltpu.CompilerParams(
            vmem_limit_bytes=VMEM_BYTES, collective_id=0, has_side_effects=True
        ),
        cost_estimate=SMALL_COST,
        name="last_exchanges",
    )(*in_hbm(keep, message, *before.parts, *up.parts, *down.parts), theirs_b)


def unpack_mlp(share, rows, core, exchange):
    half, each = share.shape[1], rows // 2
    down = share[: 4 * rows].reshape(2, 4 * each, half)
    rest = share[4 * rows :].reshape(share.shape[0] // rows - 4, 2, each, half)

    def pick(which):
        return jnp.concatenate(
            [lax.dynamic_index_in_dim(down, which, 0, False),
             lax.dynamic_index_in_dim(rest, which, 1, False).reshape(-1, half)], 0)

    mine, theirs = pick(core), exchange.swap_core(pick(1 - core))

    def widen(value, start, count):
        value = value[start * each : (start + count) * each].reshape(count, each, half)
        return value.transpose(1, 0, 2).reshape(each, count * half)

    def join(start, count):
        return by_core(core, widen(mine, start, count), widen(theirs, start, count), 1)

    grad_down = by_core(core, mine[: 4 * each], theirs[: 4 * each], 1)
    return grad_down, join(4, 4), join(8, 1)


def unpack_qkv(share, core, exchange):
    rows, wide = share.shape
    split = share.reshape(2, rows // 2, wide)
    mine = lax.dynamic_index_in_dim(split, core, 0, False)
    theirs = exchange.swap_core(lax.dynamic_index_in_dim(split, 1 - core, 0, False))
    wide -= 128
    table = mine[:, wide : wide + 8] + theirs[:, wide : wide + 8]
    return by_core(core, mine[:, :wide], theirs[:, :wide], 1), table


def per_device(
    inputs, cotangent, task_table, type_counts,
    gain_one, bias_one, proj_qkv, proj_out, gain_two, bias_two, proj_up, proj_down,
):
    slots, rows, width = inputs.shape
    length = rows * lax.axis_size("seq")
    exchange = Exchange(lax.axis_size("dp"))
    place = lax.axis_index("seq")
    side, core = place // 2, place % 2
    chip = lax.axis_index("dp") * 2 + side
    low = jnp.minimum(place, 3 - place)
    own_first = place < 2
    flag = low.astype(jnp.int32).reshape(1)

    meta = jnp.concatenate([flag, core.astype(jnp.int32).reshape(1), *exchange.tables(chip, core)])

    def gather_slot(value, got):
        own = lax.dynamic_index_in_dim(value, side, 0, False)
        return jnp.where(own_first, jnp.concatenate([own, got]), jnp.concatenate([got, own]))

    choose = (task_table[:, None] == jnp.arange(TASKS, dtype=jnp.int32)[None, :]).astype(F32)
    targets = (length - type_counts[:, 0]).astype(F32)
    totals = jnp.sum(choose * targets[:, None], 0)
    bits = int(math.log2(exchange.dp))

    for bit in range(bits):
        pairs = [(d, d ^ (1 << bit)) for d in range(exchange.dp)]
        totals = totals + lax.ppermute(totals, "dp", pairs)
    cotangent_own, cotangent_send = (lax.dynamic_index_in_dim(cotangent, s, 0, False) for s in (side, 1 - side))
    got = exchange.mirror(lax.dynamic_index_in_dim(inputs, 1 - side, 0, False))
    got, totals, cotangent_own, cotangent_send = lax.optimization_barrier(
        (got, totals, cotangent_own, cotangent_send)
    )
    stream = gather_slot(inputs, got)
    factor = jnp.sum(totals) / TASKS / totals
    seq_weight = jnp.sum(choose * factor[None, :], 1)
    own_weight = lax.dynamic_index_in_dim(seq_weight, side, 0, False)
    own_start = lax.dynamic_index_in_dim(type_counts[:, 0], side, 0, False)
    chips = exchange.chips
    half = width // 2
    swap, mirror = exchange.swap_core, exchange.mirror

    def forward(layer, stream, moves_project, moves_attention):
        hidden, queries, own = host(
            lambda v: project(layer, v, gain_one, bias_one, proj_qkv), (stream,), *moves_project
        )
        other = swap(own)
        hidden_x = Move(swap, hidden)
        attended, logs = host(
            lambda q, k, kx: attention_forward(flag, q, k, kx), (queries, own, other),
            hidden_x, *moves_attention
        )
        attended_x = Move(swap, attended)
        middle, normed, active, slope, *output = host(
            lambda a, v: feed_forward(layer, a, v, proj_out, gain_two, bias_two, proj_up, proj_down),
            (attended, stream), attended_x,
        )
        moves = Move(swap, normed), Move(swap, active)
        return output, moves, (stream, hidden, hidden_x, queries, own, other, logs, attended, attended_x, middle, normed, active, slope)

    def attention_step(layer, back_attended, moves):
        unused, unused, unused, queries, own, other, logs, attended, unused, unused, unused, unused, unused = kept[layer]
        back_q, back_own, back_other = host(
            lambda b: attention_backward(flag, queries, own, other, b, attended, logs), (back_attended,), *moves
        )
        return back_q, back_own, Move(swap, back_other)

    def project_step(layer, back_q, back_own, back_got, back_branch, sums, moves, beside=lambda: (), ready=()):
        return host(
            lambda q, k, kx, *more: (
                *project_back(layer, meta, q, k, kx, proj_qkv, kept[layer][0], gain_one, back_branch, sums),
                *beside(*more),
            ),
            (back_q, back_own, back_got) + tuple(ready), *moves
        )

    def feed_step(layer, back_out, sums, moves):
        middle, slope = kept[layer][9], kept[layer][12]
        return host(
            lambda b: feed_back(layer, meta, b, slope, proj_up, proj_down, middle, gain_two, proj_out, sums),
            (back_out,), *moves
        )

    def down_step(layer, back_out, back_out_x, active_x, moves):
        active = kept[layer][11]
        return Reduction(exchange, *host(
            lambda b, bx: down_gradients(meta, chips, active, active_x, b, bx), (back_out, back_out_x), *moves
        ))

    def up_step(layer, back_up, back_up_x, back_branch, branch_x, normed_x, moves):
        normed, attended, attended_x = kept[layer][10], kept[layer][7], kept[layer][8].value
        return Reduction(exchange, *host(
            lambda b, bx: up_gradients(
                meta, chips, normed, normed_x, b, bx, attended, attended_x, back_branch, branch_x
            ),
            (back_up, back_up_x), *moves
        ))

    def qkv_step(layer, mine, theirs_x, sums, moves):
        hidden, hidden_x = kept[layer][1], kept[layer][2].value
        return Reduction(exchange, *host(
            lambda b, bx: qkv_gradients(meta, chips, hidden, hidden_x, b, bx, sums), (mine, theirs_x), *moves
        ))

    got_cotangent = Move(mirror, cotangent_send)
    (stream,), moves, saved = forward(0, stream, (), (got_cotangent,))
    kept = [saved]
    back_out, back_out_send = weigh(
        own_weight.reshape(1), own_start.reshape(1), cotangent_own, got_cotangent.value
    )
    back_out_x = Move(swap, back_out_send)
    (stream, stream_send), last_moves, saved = forward(1, stream, moves, (back_out_x,))
    normed_x, active_x = (move.value for move in moves)
    kept.append(saved)
    outputs_move = Move(mirror, stream_send)

    sums = jnp.zeros((8, width), F32)
    back_up, back_up_send, back_branch, branch_send, back_attended, sums = feed_step(
        1, back_out, sums, last_moves + (outputs_move,)
    )
    last_normed_x, last_active_x = (move.value for move in last_moves)
    back_up_x, branch_x = Move(swap, back_up_send), Move(swap, branch_send)
    down1 = down_step(1, back_out, back_out_x.value, last_active_x, (back_up_x, branch_x))
    back_q, back_own, back_got = attention_step(1, back_attended, (down1,))
    up1 = up_step(1, back_up, back_up_x.value, back_branch, branch_x.value, last_normed_x, (down1, back_got))
    mine, theirs, back_out, back_out_send, sums = project_step(
        1, back_q, back_own, back_got.value, back_branch, sums, (up1, down1)
    )
    theirs_x = Move(swap, theirs)
    down0 = down_step(0, back_out, swap(back_out_send), active_x, (theirs_x, up1, down1))
    back_up, back_up_send, back_branch, branch_send, back_attended, sums0 = feed_step(
        0, back_out, sums, (down0, up1)
    )
    back_up_x, branch_x = Move(swap, back_up_send), Move(swap, branch_send)
    qkv1 = qkv_step(1, mine, theirs_x.value, sums, (back_up_x, branch_x, down0, up1))
    up0 = up_step(0, back_up, back_up_x.value, back_branch, branch_x.value, normed_x, (qkv1,))
    back_q, back_own, back_got = attention_step(0, back_attended, (up0, down0))
    unit = width // chips

    def return_slot(value, got):
        own = jnp.where(own_first, value[:rows], value[rows:])
        return jnp.where(side == 0, jnp.stack([own, got]), jnp.stack([got, own]))

    each = unit // 2
    whole_tiles = each % 8 == 0 and exchange.bits == 4
    ready = (outputs_move.value,) + tuple(down1.parts) + tuple(up1.parts)

    def beside(got, *parts):
        count = len(down1.parts)
        return (return_slot(stream, got), *collect([(parts[:count], 8 * each), (parts[count:], unit)]))

    mine, theirs, back_out, back_out_send, sums, back_send, *finished = project_step(
        0, back_q, back_own, swap(back_got.value), back_branch, sums0, (up0, qkv1, down0),
        *((beside, ready) if whole_tiles else ()),
    )
    back_move = Move(mirror, back_send)
    qkv0 = qkv_step(0, mine, swap(theirs), sums, (up0, back_move))
    back_inputs = return_slot(back_out, back_move.value).astype(F32)
    if not whole_tiles:
        for one in (down0, down1, up0, up1, qkv0, qkv1):
            one.complete()
        shares = [jnp.concatenate([total(d.parts), total(u.parts)], 0) for d, u in ((down0, up0), (down1, up1))]
        down, up, out = (
            jnp.stack(value) for value in zip(*(unpack_mlp(share, unit, core, exchange) for share in shares))
        )
        (qkv_a, table), (qkv_b, unused) = (unpack_qkv(total(one.parts), core, exchange) for one in (qkv0, qkv1))
        qkv = jnp.stack([qkv_a, qkv_b])
        outputs = return_slot(stream, outputs_move.value)
    else:
        outputs, mine_b, theirs_b = finished
        mine_a, got_a, got_b, last_q, last_got, mine_q, got_q = last_exchanges(qkv0, qkv1, up0, down0, theirs_b)
        up, down, out = place_mlp(each, mine_a, got_a, mine_b, got_b)
        qkv, table = place_qkv(last_q, last_got, mine_q, got_q)
        table = table[:, :8]
    table = table.T.reshape(LAYERS, 4, each)
    return outputs, back_inputs, table[:, 0], table[:, 1], qkv, out, table[:, 2], table[:, 3], up, down


def solution(mesh):
    tokens = P("dp", "seq", None)
    shared = P(None, AXES)
    in_specs = (tokens, tokens, P("dp"), P("dp", None)) + (P(),) * 8
    out_specs = (
        tokens, tokens, shared, shared, P(None, AXES, None), P(None, AXES, None),
        shared, shared, P(None, AXES, None), P(None, AXES, None),
    )
    return jax.shard_map(
        per_device, mesh=mesh, in_specs=in_specs, out_specs=out_specs, check_vma=False
    )
```

```python
import functools
import math

import jax
import jax.numpy as jnp
import numpy as np
from jax import lax
from jax.experimental import pallas as pl
from jax.experimental.pallas import tpu as pltpu
from jax.sharding import PartitionSpec as P

HEADS = 12
HEAD_DIM = 64
LAYERS = 2
TASKS = 3
AXES = ("dp", "seq")
F32 = jnp.float32
BF16 = jnp.bfloat16
epsilon = 1e-05
PAIRS = 2
VMEM_BYTES = 32 * 1024 * 1024
SMALL_COST = pl.CostEstimate(flops=1000, bytes_accessed=1000, transcendentals=0)


def in_hbm(*values):
    return tuple(pltpu.with_memory_space_constraint(v, pltpu.HBM) for v in values)


def dot_nn(a, b):
    return lax.dot_general(a, b, (((1,), (0,)), ((), ())), preferred_element_type=F32)


def dot_nt(a, b):
    return lax.dot_general(a, b, (((1,), (1,)), ((), ())), preferred_element_type=F32)


def dot_tn(a, b):
    return lax.dot_general(a, b, (((0,), (0,)), ((), ())), preferred_element_type=F32)


def gelu_and_slope(x):
    z = jnp.abs(x) * 0.7071067811865476
    d = 1.0 + 0.3275911 * z
    t = pl.reciprocal(d, approx=True)
    t = t * (2.0 - d * t)
    poly = t * (
        0.254829592
        + t * (-0.284496736 + t * (1.421413741 + t * (-1.453152027 + t * 1.061405429)))
    )
    bell = jnp.exp(-0.5 * x * x)
    tail = 0.5 * poly * bell
    below = jnp.where(x >= 0.0, 1.0 - tail, tail)
    return x * below, below + x * bell * 0.3989422804014327


def head_masks(scale):
    lane = lax.broadcasted_iota(jnp.int32, (1, 2 * HEAD_DIM), 1)
    first = jnp.where(lane < HEAD_DIM, scale, 0.0)
    return first.astype(BF16), (scale - first).astype(BF16)


def stacked(value, masks):
    return jnp.concatenate([value * masks[0], value * masks[1]], 0)


def merged(value):
    rows = value.shape[0] // 2
    lane = lax.broadcasted_iota(jnp.int32, (rows, 2 * HEAD_DIM), 1)
    return jnp.where(lane < HEAD_DIM, value[:rows], value[rows:])


def by_variant(meta, run):
    @pl.when(meta[0] == 0)
    def _():
        run(0)

    @pl.when(meta[0] == 1)
    def _():
        run(1)


def attention_forward_kernel(meta, q_ref, ko_ref, vo_ref, kx_ref, vx_ref, out_ref, lse_ref):
    def run_all(variant):
        for pair in range(PAIRS):
            lanes = (slice(None), slice(pair * 2 * HEAD_DIM, (pair + 1) * 2 * HEAD_DIM))
            refs = [ref.at[lanes] for ref in (q_ref, ko_ref, vo_ref, kx_ref, vx_ref, out_ref)]
            attention_forward_pair(variant, *refs, lse_ref.at[pair])

    by_variant(meta, run_all)


def attention_forward_pair(variant, q_ref, ko_ref, vo_ref, kx_ref, vx_ref, out_ref, lse_ref):
    rows = q_ref.shape[0] // 2
    masks = head_masks(1.0 / math.sqrt(HEAD_DIM))

    def run(variant):
        position = lax.broadcasted_iota(jnp.int32, (2 * rows, rows), 0) % rows
        below = lax.broadcasted_iota(jnp.int32, (2 * rows, rows), 1) <= position
        low, high = slice(0, rows), slice(rows, 2 * rows)
        if variant == 0:
            plan = [
                (low, [(ko_ref, vo_ref, low)]),
                (high, [(ko_ref, vo_ref, low), (kx_ref, vx_ref, low), (kx_ref, vx_ref, high), (ko_ref, vo_ref, high)]),
            ]
        else:
            plan = [
                (low, [(kx_ref, vx_ref, low), (ko_ref, vo_ref, low)]),
                (high, [(ko_ref, vo_ref, low), (kx_ref, vx_ref, low), (ko_ref, vo_ref, high)]),
            ]
        all_scores = []
        for span, parts in plan:
            q2 = stacked(q_ref[span, :], masks)
            all_scores.append([dot_nt(q2, keys[place, :]) for keys, unused, place in parts])
        for (span, parts), scores in zip(plan, all_scores):
            scores[-1] = jnp.where(below, scores[-1], -1e30)
            peak = jnp.max(functools.reduce(jnp.maximum, scores), -1, keepdims=True)
            total, acc = None, None
            for part, (unused, values, place) in zip(scores, parts):
                raised = jnp.exp(part - peak)
                total = raised if total is None else total + raised
                term = dot_nn(raised.astype(BF16), values[place, :])
                acc = term if acc is None else acc + term
            total = jnp.sum(total, -1, keepdims=True)
            out_ref[span, :] = merged(acc / total).astype(BF16)
            log = peak + jnp.log(total)
            lane = lax.broadcasted_iota(jnp.int32, (rows, 2 * HEAD_DIM), 1)
            lse_ref[:, span] = jnp.where(lane == 0, log[:rows], log[rows:]).T[:8, :]

    run(variant)


def attention_forward(meta, queries, own, other):
    tokens = queries.shape[0]
    pairs = HEADS // 2
    wide = 2 * HEAD_DIM * PAIRS

    def at(offset):
        return pl.BlockSpec((tokens, wide), lambda g, m: (0, offset // PAIRS + g))

    return pl.pallas_call(
        attention_forward_kernel,
        grid_spec=pltpu.PrefetchScalarGridSpec(
            num_scalar_prefetch=1,
            grid=(pairs // PAIRS,),
            in_specs=[at(0), at(0), at(pairs), at(0), at(pairs)],
            out_specs=[at(0), pl.BlockSpec((PAIRS, 8, tokens), lambda g, m: (g, 0, 0))],
        ),
        out_shape=[
            pltpu.HBM((tokens, HEADS * HEAD_DIM), BF16),
            pltpu.HBM((pairs, 8, tokens), F32),
        ],
        compiler_params=pltpu.CompilerParams(vmem_limit_bytes=VMEM_BYTES),
        cost_estimate=SMALL_COST,
        name="attention_forward",
    )(meta, *in_hbm(queries, own, own, other, other))


def attention_backward_kernel(
    meta, q_ref, ko_ref, vo_ref, kx_ref, vx_ref, do_ref, o_ref, lse_ref,
    dq_ref, own_ref, other_ref, q4, do4,
):
    def run_all(variant):
        for pair in range(PAIRS):
            lanes = (slice(None), slice(pair * 2 * HEAD_DIM, (pair + 1) * 2 * HEAD_DIM))
            refs = [ref.at[lanes] for ref in (q_ref, ko_ref, vo_ref, kx_ref, vx_ref, do_ref, o_ref)]
            grads = [ref.at[(slice(None),) + lanes] for ref in (own_ref, other_ref)]
            attention_backward_pair(
                variant, *refs, lse_ref.at[pair], dq_ref.at[lanes], *grads, q4.at[pair], do4.at[pair]
            )

    by_variant(meta, run_all)


def attention_backward_pair(
    variant, q_ref, ko_ref, vo_ref, kx_ref, vx_ref, do_ref, o_ref, lse_ref,
    dq_ref, own_ref, other_ref, q4, do4,
):
    rows = q_ref.shape[0] // 2
    scale = 1.0 / math.sqrt(HEAD_DIM)
    scaled, plain = head_masks(scale), head_masks(1.0)
    product = (do_ref[...].astype(F32) * o_ref[...].astype(F32)).T
    first = jnp.sum(product[:HEAD_DIM], 0, keepdims=True)
    second = jnp.sum(product[HEAD_DIM:], 0, keepdims=True)
    logs = lse_ref[...]
    dot_row = jnp.concatenate([first[:, :rows], second[:, :rows], first[:, rows:], second[:, rows:]], 1)
    log_row = jnp.concatenate(
        [logs[0:1, :rows], logs[1:2, :rows], logs[0:1, rows:], logs[1:2, rows:]], 1
    )
    for block in range(2):
        span = slice(block * rows, (block + 1) * rows)
        q4[2 * block * rows : 2 * (block + 1) * rows, :] = stacked(q_ref[span, :], scaled)
        do4[2 * block * rows : 2 * (block + 1) * rows, :] = stacked(do_ref[span, :], plain)

    def run(variant):
        column = lax.broadcasted_iota(jnp.int32, (rows, 2 * rows), 1) % rows
        below = lax.broadcasted_iota(jnp.int32, (rows, 2 * rows), 0) <= column
        low, high = slice(0, rows), slice(rows, 2 * rows)
        both, upper, lower = slice(0, 4 * rows), slice(2 * rows, 4 * rows), slice(0, 2 * rows)
        plan = [(0, low, lower, True), (0, low, upper, False), (1, low, upper, False), (0, high, upper, True)]
        plan.insert(3, (1, high, upper, False) if variant == 0 else (1, low, lower, False))
        keys, values, grads = (ko_ref, kx_ref), (vo_ref, vx_ref), (own_ref, other_ref)
        dq_parts = {}
        sums = {}
        ahead = {}

        def products(index):
            source, place, cols, unused = plan[index]
            ahead[index] = dot_nt(keys[source][place, :], q4[cols, :]), dot_nt(values[source][place, :], do4[cols, :])

        products(0)
        products(1)
        for index, (source, place, cols, diagonal) in enumerate(plan):
            if index + 2 < len(plan):
                products(index + 2)
            scores, back = ahead.pop(index)
            raised = jnp.exp(scores - log_row[:, cols])
            if diagonal:
                raised = jnp.where(below, raised, 0.0)
            slope = (raised * (back - dot_row[:, cols])).astype(BF16)
            slot = (source, place.start)
            terms = dot_nn(slope, q4[cols, :]), dot_nn(raised.astype(BF16), do4[cols, :])
            sums[slot] = tuple(a + b for a, b in zip(sums[slot], terms)) if slot in sums else terms
            term = dot_tn(slope, keys[source][place, :])
            dq_parts[cols.start] = dq_parts[cols.start] + term if cols.start in dq_parts else term
        for block in range(2):
            dq_ref[block * rows : (block + 1) * rows, :] = (
                merged(dq_parts[2 * block * rows]) * scale
            ).astype(BF16)
        for source in range(2):
            for place in (low, high):
                zero = jnp.zeros((rows, 2 * HEAD_DIM), F32)
                for which, value in enumerate(sums.get((source, place.start), (zero, zero))):
                    grads[source][which, place, :] = value.astype(grads[source].dtype)

    run(variant)


def attention_backward(meta, queries, own, other, back_attended, attended, logs):
    tokens = queries.shape[0]
    pairs = HEADS // 2
    wide = 2 * HEAD_DIM * PAIRS
    width = HEADS * HEAD_DIM

    def at(offset):
        return pl.BlockSpec((tokens, wide), lambda g, m: (0, offset // PAIRS + g))

    return pl.pallas_call(
        attention_backward_kernel,
        grid_spec=pltpu.PrefetchScalarGridSpec(
            num_scalar_prefetch=1,
            grid=(pairs // PAIRS,),
            in_specs=[at(0), at(0), at(pairs), at(0), at(pairs), at(0), at(0),
                      pl.BlockSpec((PAIRS, 8, tokens), lambda g, m: (g, 0, 0))],
            out_specs=[at(0)] + [pl.BlockSpec((2, tokens, wide), lambda g, m: (0, 0, g))] * 2,
            scratch_shapes=[pltpu.VMEM((PAIRS, 2 * tokens, 2 * HEAD_DIM), BF16)] * 2,
        ),
        out_shape=[
            jax.ShapeDtypeStruct((tokens, width), BF16),
            pltpu.HBM((2, tokens, width), BF16),
            jax.ShapeDtypeStruct((2, tokens, width), BF16),
        ],
        compiler_params=pltpu.CompilerParams(vmem_limit_bytes=VMEM_BYTES),
        cost_estimate=SMALL_COST,
        name="attention_backward",
    )(meta, *in_hbm(queries, own, own, other, other, back_attended, attended, logs))


def normalised(rows_in):
    average = jnp.mean(rows_in, -1, keepdims=True)
    centred = rows_in - average
    inverse = lax.rsqrt(jnp.mean(centred * centred, -1, keepdims=True) + epsilon)
    return centred * inverse, inverse


def norm_back(rows_in, gain_row, back):
    unit, inverse = normalised(rows_in)
    slope = back * gain_row
    first = jnp.mean(slope, -1, keepdims=True)
    second = jnp.mean(slope * unit, -1, keepdims=True)
    return inverse * (slope - first - unit * second), (
        jnp.sum(back * unit, 0, keepdims=True), jnp.sum(back, 0, keepdims=True))


def with_rows(table, row, sums):
    index = lax.broadcasted_iota(jnp.int32, table.shape, 0)
    return jnp.where(index == row, sums[0], jnp.where(index == row + 1, sums[1], table))


def project_kernel(layer, stream, gain, shift, matrix, hidden, queries, pairs):
    width = stream.shape[1]
    groups = 4
    rows = stream.shape[0] // groups
    for group in range(groups):
        span = slice(group * rows, (group + 1) * rows)
        unit, unused = normalised(stream[span, :].astype(F32))
        hidden[span, :] = (unit * gain[layer : layer + 1] + shift[layer : layer + 1]).astype(BF16)
        pairs[span, :] = dot_nn(hidden[span, :], matrix[0, :, width:]).astype(BF16)
        queries[span, :] = dot_nn(hidden[span, :], matrix[0, :, :width]).astype(BF16)


def project(layer, stream, gain, shift, matrix):
    tokens, width = stream.shape
    whole = pl.BlockSpec((tokens, width), lambda j: (0, 0))
    row = pl.BlockSpec(gain.shape, lambda j: (0, 0))
    return pl.pallas_call(
        functools.partial(project_kernel, layer),
        grid=(1,),
        in_specs=[whole, row, row, pl.BlockSpec((1, width, 3 * width), lambda j: (layer, 0, 0))],
        out_specs=[whole, whole, pl.BlockSpec((tokens, 2 * width), lambda j: (0, 0))],
        out_shape=[
            pltpu.HBM((tokens, width), BF16),
            pltpu.HBM((tokens, width), BF16),
            pltpu.HBM((tokens, 2 * width), BF16),
        ],
        compiler_params=pltpu.CompilerParams(vmem_limit_bytes=VMEM_BYTES),
        cost_estimate=SMALL_COST,
        name="project",
    )(*in_hbm(stream), gain, shift, *in_hbm(matrix))


def feed_forward_kernel(
    layer, steps, attended, stream, matrix_out, gain, shift, up, down,
    middle, normed, active_ref, slope_ref, out, *rest,
):
    acc = rest[-1]
    step = pl.program_id(0)

    @pl.when(step == 0)
    def _():
        acc[...] = stream[...].astype(F32) + dot_nn(attended[...], matrix_out[0])
        middle[...] = acc[...].astype(BF16)
        unit, unused = normalised(acc[...])
        normed[...] = (unit * gain[layer : layer + 1] + shift[layer : layer + 1]).astype(BF16)

    groups = 4
    rows = normed.shape[0] // groups
    raw = {}
    for group in range(groups + 1):
        if group < groups:
            raw[group] = dot_nn(normed[group * rows : (group + 1) * rows, :], up[0])
        if group > 0:
            span = slice((group - 1) * rows, group * rows)
            active, slope = gelu_and_slope(raw.pop(group - 1))
            active = active.astype(BF16)
            active_ref[span, :] = active
            slope_ref[span, :] = slope.astype(BF16)
            acc[span, :] += dot_nn(active, down[0])

    @pl.when(step == steps - 1)
    def _():
        out[...] = acc[...].astype(out.dtype)
        if len(rest) == 2:
            rest[0][...] = acc[other_block(acc.shape[0] // 2), :].astype(out.dtype)


def other_block(rows):
    return pl.ds(pl.multiple_of((1 - lax.axis_index("seq") // 2) * rows, rows), rows)


def feed_forward(layer, attended, stream, matrix_out, gain, shift, up, down):
    tokens, width = stream.shape
    last = layer == LAYERS - 1
    block = pl.BlockSpec((tokens // 2, width), lambda j: (0, 0))
    hidden = up.shape[2]
    tile = 1024
    steps = hidden // tile
    whole = pl.BlockSpec((tokens, width), lambda j: (0, 0))
    row = pl.BlockSpec(gain.shape, lambda j: (0, 0))
    part = pl.BlockSpec((tokens, tile), lambda j: (0, j))
    return pl.pallas_call(
        functools.partial(feed_forward_kernel, layer, steps),
        grid=(steps,),
        in_specs=[
            whole, whole, pl.BlockSpec((1, width, width), lambda j: (layer, 0, 0)), row, row,
            pl.BlockSpec((1, width, tile), lambda j: (layer, 0, j)),
            pl.BlockSpec((1, tile, width), lambda j: (layer, j, 0)),
        ],
        out_specs=[whole, whole, part, part, whole] + [block] * last,
        out_shape=[
            pltpu.HBM((tokens, width), BF16),
            pltpu.HBM((tokens, width), BF16),
            pltpu.HBM((tokens, hidden), BF16),
            pltpu.HBM((tokens, hidden), BF16),
            pltpu.HBM((tokens, width), BF16),
        ] + [jax.ShapeDtypeStruct((tokens // 2, width), BF16)] * last,
        scratch_shapes=[pltpu.VMEM((tokens, width), F32)],
        compiler_params=pltpu.CompilerParams(vmem_limit_bytes=VMEM_BYTES),
        cost_estimate=SMALL_COST,
        name="feed_forward",
    )(*in_hbm(attended, stream, matrix_out), gain, shift, *in_hbm(up, down))


def feed_back_kernel(
    layer, steps, meta, back_out, slope, up, down, middle, gain, matrix_out, sums_in,
    own, send, back_branch, branch_send, back_attended, grads, acc,
):
    step = pl.program_id(0)
    half = branch_send.shape[1]
    theirs = pl.ds(pl.multiple_of((1 - meta[1]) * half, 128), half)

    @pl.when(step == 0)
    def _():
        acc[...] = jnp.zeros_like(acc)

    back_up = (dot_nt(back_out[...], down[0]) * slope[...].astype(F32)).astype(BF16)

    @pl.when(step < steps // 2)
    def _():
        send[...] = back_up

    @pl.when(step >= steps // 2)
    def _():
        own[...] = back_up

    acc[...] += dot_nt(back_up, up[0])

    @pl.when(step == steps - 1)
    def _():
        back, sums = norm_back(middle[...].astype(F32), gain[layer : layer + 1], acc[...])
        back = back + back_out[...].astype(F32)
        grads[...] = with_rows(sums_in[...], 4 * layer + 2, sums)
        back_branch[...] = back.astype(BF16)
        branch_send[...] = back_branch[:, theirs]
        back_attended[...] = dot_nt(back_branch[...], matrix_out[0]).astype(BF16)


def feed_back(layer, meta, back_out, slope, up, down, middle, gain, matrix_out, sums):
    tokens, width = back_out.shape
    hidden = up.shape[2]
    tile = 768
    steps = hidden // tile
    half = steps // 2

    def place(j, m):
        return jnp.where(j < half, (1 - m[1]) * half + j, m[1] * half + j - half)

    whole = pl.BlockSpec((tokens, width), lambda j, m: (0, 0))
    narrow = pl.BlockSpec((tokens, width // 2), lambda j, m: (0, 0))
    wide = jax.ShapeDtypeStruct((tokens, width), BF16)
    return pl.pallas_call(
        functools.partial(feed_back_kernel, layer, steps),
        grid_spec=pltpu.PrefetchScalarGridSpec(
            num_scalar_prefetch=1,
            grid=(steps,),
            in_specs=[
                whole, pl.BlockSpec((tokens, tile), lambda j, m: (0, place(j, m))),
                pl.BlockSpec((1, width, tile), lambda j, m: (layer, 0, place(j, m))),
                pl.BlockSpec((1, tile, width), lambda j, m: (layer, place(j, m), 0)),
                whole, pl.BlockSpec(gain.shape, lambda j, m: (0, 0)),
                pl.BlockSpec((1, width, width), lambda j, m: (layer, 0, 0)),
                pl.BlockSpec((8, width), lambda j, m: (0, 0)),
            ],
            out_specs=[
                pl.BlockSpec((tokens, tile), lambda j, m: (0, jnp.maximum(j - half, 0))),
                pl.BlockSpec((tokens, tile), lambda j, m: (0, jnp.minimum(j, half - 1))),
                whole, narrow, whole,
                pl.BlockSpec((8, width), lambda j, m: (0, 0)),
            ],
            scratch_shapes=[pltpu.VMEM((tokens, width), F32)],
        ),
        out_shape=[
            jax.ShapeDtypeStruct((tokens, hidden // 2), BF16),
            jax.ShapeDtypeStruct((tokens, hidden // 2), BF16),
            wide, jax.ShapeDtypeStruct((tokens, width // 2), BF16),
            wide, jax.ShapeDtypeStruct((8, width), F32),
        ],
        compiler_params=pltpu.CompilerParams(vmem_limit_bytes=VMEM_BYTES),
        cost_estimate=SMALL_COST,
        name="feed_back",
    )(meta, back_out, *in_hbm(slope, up, down, middle), gain, *in_hbm(matrix_out), sums)


def project_back_kernel(
    layer, meta, back_q, own, got, matrix, stream, gain, back_middle, sums_in,
    mine, theirs, back_out, back_out_send, grads, *rest,
):
    width = back_q.shape[1]
    table, acc = rest[-2:]

    def begin():
        table[0] = back_q[...]
        for which in range(2):
            table[1 + which] = (own[which].astype(F32) + got[which].astype(F32)).astype(BF16)
        half = width // 2

        @pl.when(meta[1] == 0)
        def _():
            mine[:, :width] = table[0]
            mine[:, width:] = table[1, :, :half]
            theirs[:, :half] = table[1, :, half:]
            theirs[:, half:] = table[2]

        @pl.when(meta[1] == 1)
        def _():
            theirs[:, :width] = table[0]
            theirs[:, width:] = table[1, :, :half]
            mine[:, :half] = table[1, :, half:]
            mine[:, half:] = table[2]

    begin()
    acc[...] = sum(
        dot_nt(table[which], matrix[0, :, which * width : (which + 1) * width]) for which in range(3)
    )

    def end():
        back, sums = norm_back(stream[...].astype(F32), gain[layer : layer + 1], acc[...])
        back = back + back_middle[...].astype(F32)
        back_out[...] = back.astype(BF16)
        half = width // 2
        back_out_send[...] = back_out[:, pl.ds(pl.multiple_of((1 - meta[1]) * half, 128), half)]
        grads[...] = with_rows(sums_in[...], 4 * layer, sums)
        if len(rest) == 3:
            rest[0][...] = back_out[other_block(back_out.shape[0] // 2), :]

    end()


def project_back(layer, meta, back_q, own, got, matrix, stream, gain, back_middle, sums):
    tokens, width = stream.shape
    whole = pl.BlockSpec((tokens, width), lambda j, m: (0, 0))
    both = pl.BlockSpec((2, tokens, width), lambda j, m: (0, 0, 0))
    side = pl.BlockSpec((tokens, 3 * width // 2), lambda j, m: (0, 0))
    return pl.pallas_call(
        functools.partial(project_back_kernel, layer),
        grid_spec=pltpu.PrefetchScalarGridSpec(
            num_scalar_prefetch=1,
            grid=(1,),
            in_specs=[
                whole, both, both, pl.BlockSpec((1, width, 3 * width), lambda j, m: (layer, 0, 0)),
                whole, pl.BlockSpec(gain.shape, lambda j, m: (0, 0)), whole,
                pl.BlockSpec((8, width), lambda j, m: (0, 0)),
            ],
            out_specs=[side, side, whole, pl.BlockSpec((tokens, width // 2), lambda j, m: (0, 0)),
                       pl.BlockSpec((8, width), lambda j, m: (0, 0))]
            + [pl.BlockSpec((tokens // 2, width), lambda j, m: (0, 0))] * (layer == 0),
            scratch_shapes=[pltpu.VMEM((3, tokens, width), BF16), pltpu.VMEM((tokens, width), F32)],
        ),
        out_shape=[
            jax.ShapeDtypeStruct((tokens, 3 * width // 2), BF16),
            jax.ShapeDtypeStruct((tokens, 3 * width // 2), BF16),
            jax.ShapeDtypeStruct((tokens, width), BF16),
            jax.ShapeDtypeStruct((tokens, width // 2), BF16),
            jax.ShapeDtypeStruct((8, width), F32),
        ] + [jax.ShapeDtypeStruct((tokens // 2, width), BF16)] * (layer == 0),
        compiler_params=pltpu.CompilerParams(vmem_limit_bytes=VMEM_BYTES),
        cost_estimate=SMALL_COST,
        name="project_back",
    )(meta, *in_hbm(back_q, own), got, *in_hbm(matrix, stream), gain, *in_hbm(back_middle), sums)


def weigh_kernel(weight, start, own, got, back_out, back_out_send):
    rows, half = own.shape[0], back_out_send.shape[1]
    place = lax.axis_index("seq")
    core, low = place % 2, ((place + 1) // 2) % 2
    step = lax.broadcasted_iota(jnp.int32, (rows, 1), 0)
    first = place < 2
    for which, block in enumerate((low, 3 - low)):
        span = slice(which * rows, (which + 1) * rows)
        scale = jnp.where(block * rows + step >= start[0], weight[0], 0.0)
        mine = own[...].astype(F32) if which == 0 else got[...].astype(F32)
        other = got[...].astype(F32) if which == 0 else own[...].astype(F32)
        back_out[span, :] = (jnp.where(first, mine, other) * scale).astype(BF16)
    back_out_send[...] = back_out[:, pl.ds(pl.multiple_of((1 - core) * half, 128), half)]


def weigh(weight, start, own, got):
    rows, width = own.shape
    scalar = pl.BlockSpec(memory_space=pltpu.SMEM)
    return pl.pallas_call(
        weigh_kernel,
        in_specs=[scalar, scalar, pl.BlockSpec(memory_space=pltpu.VMEM), pl.BlockSpec(memory_space=pltpu.VMEM)],
        out_specs=[pl.BlockSpec(memory_space=pltpu.VMEM)] * 2,
        out_shape=[
            jax.ShapeDtypeStruct((2 * rows, width), BF16),
            jax.ShapeDtypeStruct((2 * rows, width // 2), BF16),
        ],
        compiler_params=pltpu.CompilerParams(vmem_limit_bytes=VMEM_BYTES),
        cost_estimate=SMALL_COST,
        name="weigh",
    )(weight, start, own, got)


def store_chunks(chips, meta, acc, keep, send):
    rows = acc.shape[0] // chips
    for position in range(chips):
        chunk = acc[pl.ds(pl.multiple_of(meta[2 + position] * rows, 16), rows), :]
        if position < chips // 2:
            keep[position] = chunk
        else:
            send[position - chips // 2] = chunk


def grad_up_kernel(chips, meta, ao, ax, bo, bx, co, cx, do, dx, keep, send, acc):
    step = pl.program_id(0)
    rows, half = acc.shape[0] // chips, do.shape[1]

    @pl.when(step < 2)
    def _():
        acc[...] = (dot_tn(ao[...], bo[...]) + dot_tn(ax[...], bx[...])).astype(BF16)

    @pl.when(step == 2)
    def _():
        acc[:, :half] = (dot_tn(co[...], do[...]) + dot_tn(cx[...], dx[...])).astype(BF16)

    for position in range(chips):
        place = pl.ds(pl.multiple_of(meta[2 + position] * rows, 16), rows)
        target, index = (keep, position) if position < chips // 2 else (send, position - chips // 2)
        target[index, :rows, :] = acc[place, :half]
        target[index, rows:, :] = acc[place, half:]


def grad_down_kernel(chips, meta, ao, ax, bo, bx, *refs):
    keep, send = refs[-2:]
    rows = keep.shape[1]
    each = ao.shape[1] // rows
    total = (dot_tn(ao[...], bo[...]) + dot_tn(ax[...], bx[...])).astype(BF16)
    for local in range(each):
        position = meta[2 + chips + pl.program_id(0) * each + local]
        chunk = total[local * rows : (local + 1) * rows]

        @pl.when(position < chips // 2)
        def _():
            keep[position] = chunk

        @pl.when(position >= chips // 2)
        def _():
            send[position - chips // 2] = chunk


def grad_qkv_kernel(chips, meta, ao, ax, bo, bx, sums, keep, send, acc, columns):
    wide = bo.shape[1]
    acc[:, :wide] = (dot_tn(ao[...], bo[...]) + dot_tn(ax[...], bx[...])).astype(BF16)
    columns[...] = jnp.concatenate([sums[...], jnp.zeros((120, sums.shape[1]), F32)], 0).T
    acc[:, wide:] = columns[...].astype(BF16)
    store_chunks(chips, meta, acc, keep, send)


def ordered(total, ids, chips):
    split = total.astype(BF16).reshape(chips, total.shape[0] // chips, total.shape[1])
    return jnp.take(split, ids, axis=0)


def gradient_call(kernel, name, chips, grid, in_specs, out_spec, shape, scratch):
    return pl.pallas_call(
        functools.partial(kernel, chips),
        grid_spec=pltpu.PrefetchScalarGridSpec(
            num_scalar_prefetch=1, grid=(grid,), in_specs=in_specs, out_specs=[out_spec] * 2,
            scratch_shapes=scratch,
        ),
        out_shape=[pltpu.HBM(shape, BF16)] * 2,
        compiler_params=pltpu.CompilerParams(vmem_limit_bytes=VMEM_BYTES),
        cost_estimate=SMALL_COST,
        name=name,
    )


def up_gradients(
    meta, chips, normed, normed_x, back_up, back_up_x, attended, attended_x, back_branch, branch_x
):
    tokens, width = normed.shape
    half = width // 2
    rows = width // chips
    if rows % 16 != 0:
        ids = meta[2 : 2 + chips]
        up = dot_tn(normed, back_up) + dot_tn(normed_x, back_up_x)
        own = lax.dynamic_slice_in_dim(back_branch, meta[1] * half, half, 1)
        out = dot_tn(attended, own) + dot_tn(attended_x, branch_x)
        up = ordered(up, ids, chips).reshape(chips, rows, 4, half)
        up = up.transpose(0, 2, 1, 3).reshape(chips, 4 * rows, half)
        both = jnp.concatenate([up, ordered(out, ids, chips)], 1)
        return both[: chips // 2], both[chips // 2 :]
    whole = pl.BlockSpec((tokens, width), lambda j, m: (0, 0))
    fixed = pl.BlockSpec((tokens, half), lambda j, m: (0, 0))
    mine = pl.BlockSpec((tokens, half), lambda j, m: (0, m[1]))
    tile = pl.BlockSpec((tokens, 2 * half), lambda j, m: (0, jnp.minimum(j, 1)))
    return gradient_call(
        grad_up_kernel, "gradient_up", chips, 3, [whole, whole, tile, tile, whole, whole, mine, fixed],
        pl.BlockSpec((chips // 2, 2 * rows, half), lambda j, m: (0, j, 0)),
        (chips // 2, 5 * rows, half), [pltpu.VMEM((width, 2 * half), BF16)],
    )(meta, *in_hbm(normed, normed_x), back_up, back_up_x, *in_hbm(attended, attended_x), back_branch, branch_x)


def down_gradients(meta, chips, active, active_x, back_out, back_out_x):
    tokens, hidden = active.shape
    width = back_out.shape[1]
    half = width // 2
    rows = hidden // chips
    if rows % 64 != 0:
        own = lax.dynamic_slice_in_dim(back_out, meta[1] * half, half, 1)
        down = dot_tn(active, own) + dot_tn(active_x, back_out_x)
        down = ordered(down, meta[2 : 2 + chips], chips)
        return down[: chips // 2], down[chips // 2 :]
    fixed = pl.BlockSpec((tokens, half), lambda j, m: (0, 0))
    mine = pl.BlockSpec((tokens, half), lambda j, m: (0, m[1]))
    tile = pl.BlockSpec((tokens, 2 * width), lambda j, m: (0, j))
    return gradient_call(
        grad_down_kernel, "gradient_down", chips, hidden // (2 * width), [tile, tile, mine, fixed],
        pl.BlockSpec((chips // 2, rows, half), lambda j, m: (0, 0, 0)), (chips // 2, rows, half), [],
    )(meta, *in_hbm(active, active_x), back_out, back_out_x)


def qkv_gradients(meta, chips, hidden, hidden_x, back_projected, back_projected_x, sums):
    tokens, width = hidden.shape
    wide = back_projected.shape[1]
    rows = width // chips
    if rows % 16 != 0:
        qkv = dot_tn(hidden, back_projected) + dot_tn(hidden_x, back_projected_x)
        table = jnp.pad(sums.T, ((0, 0), (0, 120)))
        both = ordered(jnp.concatenate([qkv, table], -1), meta[2 : 2 + chips], chips)
        return both[: chips // 2], both[chips // 2 :]
    specs = [pl.BlockSpec((tokens, width), lambda j, m: (0, 0))] * 2
    specs += [pl.BlockSpec((tokens, wide), lambda j, m: (0, 0))] * 2
    specs += [pl.BlockSpec((8, width), lambda j, m: (0, 0))]
    return gradient_call(
        grad_qkv_kernel, "gradient_qkv", chips, 1, specs,
        pl.BlockSpec((chips // 2, rows, wide + 128), lambda j, m: (0, 0, 0)),
        (chips // 2, rows, wide + 128),
        [pltpu.VMEM((width, wide + 128), BF16), pltpu.VMEM((width, 128), F32)],
    )(meta, *in_hbm(hidden, hidden_x), back_projected, back_projected_x, sums)


class Exchange:
    def __init__(self, dp):
        self.dp = dp
        self.chips = 2 * dp
        self.bits = int(math.log2(self.chips))
        self.core_pairs = [(s, s ^ 1) for s in range(4)]
        self.mirror_pairs = [(s, 3 - s) for s in range(4)]
        rest = list(range(2, self.bits))
        self.orders = ([1, 0] + rest, [0, 1] + rest[::-1])

    def swap_core(self, value):
        return lax.ppermute(value, "seq", self.core_pairs)

    def mirror(self, value):
        return lax.ppermute(value, "seq", self.mirror_pairs)

    def pairs(self, phase):
        result = []
        for device in range(2 * self.chips):
            chip = (device // 4) * 2 + (device % 4) // 2
            core = device % 2
            other = chip ^ (1 << self.orders[core][phase])
            result.append((device, (other // 2) * 4 + (other % 2) * 2 + core))
        return result

    def tables(self, chip, core):
        index = np.arange(self.chips)
        maps = []
        for order in self.orders:
            value = np.zeros_like(index)
            for phase, bit in enumerate(order):
                value |= ((index >> (self.bits - 1 - phase)) & 1) << bit
            maps.append(value.astype(np.int32))
        ids = chip ^ jnp.where(core == 0, jnp.asarray(maps[0]), jnp.asarray(maps[1]))
        relative = jnp.asarray(index.astype(np.int32)) ^ chip
        places = []
        for order in self.orders:
            place = jnp.zeros_like(relative)
            for phase, bit in enumerate(order):
                place = place | (((relative >> bit) & 1) << (self.bits - 1 - phase))
            places.append(place)
        return ids.astype(jnp.int32), jnp.where(core == 0, places[0], places[1]).astype(jnp.int32)


class Reduction:
    def __init__(self, exchange, keep, send):
        self.exchange, self.parts, self.phase = exchange, [keep], 0
        self.first, self.kind = send, send.dtype

    def message(self):
        if self.phase == 0:
            return self.first
        size = self.parts[-1].shape[0]
        terms = [part[size // 2 : size].astype(F32) for part in self.parts]
        return functools.reduce(jnp.add, terms).astype(self.kind)

    def partner(self, phase):
        dp, seq = lax.axis_index("dp"), lax.axis_index("seq")
        where = []
        for order in self.exchange.orders:
            bit = order[phase]
            if bit == 0:
                where.append((dp, (seq + 2) % 4))
            else:
                size = 1 << (bit - 1)
                where.append((dp + size - 2 * size * ((dp // size) % 2), seq))
        (dp0, seq0), (dp1, seq1) = where
        return dp0 + (seq % 2) * (dp1 - dp0), seq0 + (seq % 2) * (seq1 - seq0)

    def transfer(self, message):
        self.phase += 1
        return lax.ppermute(message, AXES, self.exchange.pairs(self.phase - 1))

    def arrived(self, value):
        self.parts.append(value)

    def complete(self):
        while self.phase < self.exchange.bits:
            self.arrived(self.transfer(self.message()))


def total(parts):
    return functools.reduce(jnp.add, [part[0].astype(F32) for part in parts])


class Move:
    def __init__(self, transfer, value):
        self.transfer, self.value = transfer, value

    def message(self):
        return self.value

    def arrived(self, value):
        self.value = value


def host(run, inputs, *moves):
    count = len(inputs)
    tied = lax.optimization_barrier(tuple(inputs) + tuple(move.message() for move in moves))
    results = tuple(run(*tied[:count]))
    got = tuple(move.transfer(message) for move, message in zip(moves, tied[count:]))
    tied = lax.optimization_barrier(results + got)
    for move, value in zip(moves, tied[len(results) :]):
        move.arrived(value)
    return tied[: len(results)]


def by_core(core, mine, theirs, axis):
    return jnp.where(
        core == 0,
        jnp.concatenate([mine, theirs], axis),
        jnp.concatenate([theirs, mine], axis),
    )


def small_call(kernel, name, shapes, operands, scratch=()):
    def spec(value):
        if value.ndim == 3 and value.dtype == BF16:
            return pl.BlockSpec((1,) + value.shape[1:], lambda i: (0, 0, 0))
        return pl.BlockSpec(value.shape, lambda i: (0,) * value.ndim)

    return pl.pallas_call(
        kernel,
        grid=(1,),
        in_specs=[spec(value) for value in operands],
        out_specs=[spec(shape) for shape in shapes],
        out_shape=shapes,
        scratch_shapes=list(scratch),
        compiler_params=pltpu.CompilerParams(vmem_limit_bytes=VMEM_BYTES),
        cost_estimate=SMALL_COST,
        name=name,
    )(*operands)


def collect(groups):
    counts = [len(parts) for parts, unused in groups]
    units = [unit for unused, unit in groups]
    totals = [parts[0].shape[1:] for parts, unused in groups]
    wide = totals[0][1]
    half = sum(rows for rows, unused in totals) // 2

    def kernel(*refs):
        refs = list(refs)
        core = lax.axis_index("seq") % 2
        mine, theirs = refs[sum(counts) : sum(counts) + 2]
        sums = refs[sum(counts) + 2 :]
        at = 0
        for count, unit, scratch in zip(counts, units, sums):
            parts, refs = refs[:count], refs[count:]
            scratch[...] = functools.reduce(jnp.add, [part[0].astype(F32) for part in parts])
            each = unit // 2
            for start in range(0, scratch.shape[0], unit):
                span = slice(at, at + each)
                mine[span, :] = scratch[pl.ds(pl.multiple_of(start + core * each, 8), each), :]
                theirs[span, :] = scratch[pl.ds(pl.multiple_of(start + (1 - core) * each, 8), each), :]
                at += each

    shape = jax.ShapeDtypeStruct((half, wide), F32)
    operands = in_hbm(*[part for parts, unused in groups for part in parts])
    return small_call(kernel, "collect", [shape, shape], operands, [pltpu.VMEM(t, F32) for t in totals])


def place_mlp(each, mine_a, theirs_a, mine_b, theirs_b):
    half = mine_a.shape[1]

    def kernel(*refs):
        ups, downs, outs = refs[4:]
        core = lax.axis_index("seq") % 2
        for layer in range(2):
            for side, value in ((core, refs[2 * layer]), (1 - core, refs[2 * layer + 1])):
                narrow = pl.ds(pl.multiple_of(side * half, 128), half)
                downs[layer, :, narrow] = value[: 4 * each, :]
                for unit in range(4):
                    lanes = pl.ds(pl.multiple_of(side * 4 * half + unit * half, 128), half)
                    ups[layer, :, lanes] = value[(4 + unit) * each : (5 + unit) * each, :]
                outs[layer, :, narrow] = value[8 * each :, :]

    shapes = [
        jax.ShapeDtypeStruct((2, each, 8 * half), F32), jax.ShapeDtypeStruct((2, 4 * each, 2 * half), F32),
        jax.ShapeDtypeStruct((2, each, 2 * half), F32),
    ]
    return small_call(kernel, "place", shapes, (mine_a, theirs_a, mine_b, theirs_b))


def place_qkv(mine_a, theirs_a, mine_b, theirs_b):
    each, wide = mine_a.shape
    wide -= 128

    def kernel(*refs):
        out, table = refs[4:]
        core = lax.axis_index("seq") % 2
        for layer in range(2):
            for side, value in ((core, refs[2 * layer]), (1 - core, refs[2 * layer + 1])):
                out[layer, :, pl.ds(pl.multiple_of(side * wide, 128), wide)] = value[:, :wide]
        table[...] = refs[0][:, wide:] + refs[1][:, wide:]

    shapes = [jax.ShapeDtypeStruct((2, each, 2 * wide), F32), jax.ShapeDtypeStruct((each, 128), F32)]
    return small_call(kernel, "place_qkv", shapes, (mine_a, theirs_a, mine_b, theirs_b))


def last_exchanges(last, before, up, down, theirs_b):
    keep, message = last.parts[0], last.first
    chunk = keep.shape[1:]
    each, wide = chunk[0] // 2, chunk[1]
    up_rows, down_rows, half = up.parts[0].shape[1], down.parts[0].shape[1], up.parts[0].shape[2]
    mesh = pl.DeviceIdType.MESH

    loaded = [(8, keep)] + [(4, v) for v in before.parts] + [(2, v) for v in up.parts] + [(1, v) for v in down.parts]
    buffers = [pltpu.VMEM((size,) + value.shape[1:], BF16) for size, value in loaded]

    def kernel(*refs):
        refs = list(refs)

        def take(count):
            taken = refs[:count]
            del refs[:count]
            return taken

        given, (message, theirs_b) = take(len(loaded)), take(2)
        mine_a, got_a, got_b, mine_l, got_l, mine_q, got_q = take(7)
        land1, land2, land3, land4, q_land3, q_land4, up_land = take(7)
        send2, send3, send4, q_send3, q_send4, up_send = take(6)
        sums, up_sum, down_sum, swap_q, swap_q_land, swap_a, swap_a_land = take(7)
        send_sem, recv_sem, load_sem = take(3)
        held = take(len(loaded))
        keep, before_parts, up_parts, down_parts = held[0], held[1:4], held[4:8], held[8:]
        loads = [
            pltpu.make_async_copy(ref.at[0 : loaded[k][0]], held[k], load_sem.at[k]) for k, ref in enumerate(given)
        ]
        for load in loads:
            load.start()
        seq = lax.axis_index("seq")
        core = seq % 2
        other = lax.axis_index("dp"), seq + 1 - 2 * core
        partners = [last.partner(phase) for phase in range(4)]
        barrier = pltpu.get_barrier_semaphore()
        for partner in partners + [other]:
            pl.semaphore_signal(barrier, inc=1, device_id=partner, device_id_type=mesh)
        pl.semaphore_wait(barrier, 5)

        def remote(index, source, target, partner):
            return pltpu.make_async_remote_copy(
                src_ref=source, dst_ref=target, send_sem=send_sem.at[index], recv_sem=recv_sem.at[index],
                device_id=partner, device_id_type=mesh,
            )

        def added(values, kind=BF16):
            return functools.reduce(jnp.add, [value.astype(F32) for value in values]).astype(kind)

        def rows_of(ref, start, count, side):
            return ref[pl.ds(pl.multiple_of(start + side * count, 8), count), :]

        pieces = (slice(4, 8), slice(2, 4), slice(0, 2))
        first = [remote(k, message.at[p], land1.at[p], partners[0]) for k, p in zip((0, 1, 13), pieces)]
        second = [remote(2, send2.at[2:4], land2.at[2:4], partners[1]), remote(3, send2.at[0:2], land2.at[0:2], partners[1])]
        third, fourth = remote(4, send3, land3, partners[2]), remote(5, send4, land4, partners[3])
        q_third, q_fourth = remote(6, q_send3, q_land3, partners[2]), remote(7, q_send4, q_land4, partners[3])
        up_fourth = remote(8, up_send, up_land, partners[3])
        swap_b, swap_own = (remote(9 + k, swap_a.at[k], swap_a_land.at[k], other) for k in range(2))
        swap_qs = [remote(11 + k, swap_q.at[k], swap_q_land.at[k], other) for k in range(2)]

        for copy in first:
            copy.start()
        for load in loads:
            load.wait()
        up_send[...] = added([part[1:2] for part in up_parts])
        up_fourth.start()
        q_send3[...] = added([part[2:4] for part in before_parts])
        q_third.start()
        swap_a[0] = theirs_b[...]
        swap_b.start()
        down_sum[...] = added([part[0] for part in down_parts], F32)
        up_sum[...] = added([part[0] for part in up_parts], F32)
        sums[1] = added([part[0] for part in before_parts], F32)

        first[0].wait()
        send2[...] = added([keep[4:8], land1[4:8]])
        for copy in second:
            copy.start()

        q_third.wait()
        q_send4[...] = added([part[1:2] for part in before_parts] + [q_land3[1:2]])
        q_fourth.start()
        sums[1] = sums[1] + q_land3[0].astype(F32)

        up_fourth.wait()
        up_sum[...] = up_sum[...] + up_land[0].astype(F32)
        at = 0
        for scratch, unit in ((down_sum, 8 * each), (up_sum, 2 * each)):
            count = unit // 2
            for start in range(0, scratch.shape[0], unit):
                mine_a[at : at + count, :] = rows_of(scratch, start, count, core)
                swap_a[1, at : at + count, :] = rows_of(scratch, start, count, 1 - core)
                at += count
        swap_own.start()
        swap_b.wait()
        got_b[...] = swap_a_land[0]

        first[1].wait()
        second[0].wait()
        send3[...] = added([keep[2:4], land1[2:4], land2[2:4]])
        third.start()

        q_fourth.wait()
        sums[1] = sums[1] + q_land4[0].astype(F32)
        mine_q[...] = rows_of(sums.at[1], 0, each, core)
        swap_q[1] = rows_of(sums.at[1], 0, each, 1 - core)
        swap_qs[1].start()
        swap_own.wait()
        got_a[...] = swap_a_land[1]

        first[2].wait()
        second[1].wait()
        sums[0] = added([keep[0], land1[0], land2[0]], F32)
        third.wait()
        send4[...] = added([keep[1:2], land1[1:2], land2[1:2], land3[1:2]])
        fourth.start()
        swap_qs[1].wait()
        got_q[...] = swap_q_land[1]
        sums[0] = sums[0] + land3[0].astype(F32)
        fourth.wait()
        sums[0] = sums[0] + land4[0].astype(F32)
        mine_l[...] = rows_of(sums.at[0], 0, each, core)
        swap_q[0] = rows_of(sums.at[0], 0, each, 1 - core)
        swap_qs[0].start()
        swap_qs[0].wait()
        got_l[...] = swap_q_land[0]

    long = theirs_b.shape
    flat, out = pl.BlockSpec(long, lambda i: (0, 0)), pl.BlockSpec((each, wide), lambda i: (0, 0))
    up_chunk = (1, up_rows, half)
    return pl.pallas_call(
        kernel,
        grid=(1,),
        in_specs=[pl.BlockSpec(memory_space=pl.ANY)] * (len(loaded) + 1) + [flat],
        out_specs=[flat] * 3 + [out] * 4,
        out_shape=[jax.ShapeDtypeStruct(long, F32)] * 3 + [jax.ShapeDtypeStruct((each, wide), F32)] * 4,
        scratch_shapes=[pltpu.VMEM((size,) + chunk, BF16) for size in (8, 4, 2, 1, 2, 1)]
        + [pltpu.VMEM(up_chunk, BF16)]
        + [pltpu.VMEM((size,) + chunk, BF16) for size in (4, 2, 1, 2, 1)]
        + [
            pltpu.VMEM(up_chunk, BF16),
            pltpu.VMEM((2,) + chunk, F32), pltpu.VMEM(up_chunk[1:], F32), pltpu.VMEM((down_rows, half), F32),
            pltpu.VMEM((2, each, wide), F32), pltpu.VMEM((2, each, wide), F32),
            pltpu.VMEM((2,) + long, F32), pltpu.VMEM((2,) + long, F32),
            pltpu.SemaphoreType.DMA((14,)), pltpu.SemaphoreType.DMA((14,)),
            pltpu.SemaphoreType.DMA((len(loaded),)),
        ] + buffers,
        compiler_params=pltpu.CompilerParams(
            vmem_limit_bytes=VMEM_BYTES, collective_id=0, has_side_effects=True
        ),
        cost_estimate=SMALL_COST,
        name="last_exchanges",
    )(*in_hbm(*[value for unused, value in loaded], message), theirs_b)


def unpack_mlp(share, rows, core, exchange):
    half, each = share.shape[1], rows // 2
    down = share[: 4 * rows].reshape(2, 4 * each, half)
    rest = share[4 * rows :].reshape(share.shape[0] // rows - 4, 2, each, half)

    def pick(which):
        return jnp.concatenate(
            [lax.dynamic_index_in_dim(down, which, 0, False),
             lax.dynamic_index_in_dim(rest, which, 1, False).reshape(-1, half)], 0)

    mine, theirs = pick(core), exchange.swap_core(pick(1 - core))

    def widen(value, start, count):
        value = value[start * each : (start + count) * each].reshape(count, each, half)
        return value.transpose(1, 0, 2).reshape(each, count * half)

    def join(start, count):
        return by_core(core, widen(mine, start, count), widen(theirs, start, count), 1)

    grad_down = by_core(core, mine[: 4 * each], theirs[: 4 * each], 1)
    return grad_down, join(4, 4), join(8, 1)


def unpack_qkv(share, core, exchange):
    rows, wide = share.shape
    split = share.reshape(2, rows // 2, wide)
    mine = lax.dynamic_index_in_dim(split, core, 0, False)
    theirs = exchange.swap_core(lax.dynamic_index_in_dim(split, 1 - core, 0, False))
    wide -= 128
    table = mine[:, wide : wide + 8] + theirs[:, wide : wide + 8]
    return by_core(core, mine[:, :wide], theirs[:, :wide], 1), table


def per_device(
    inputs, cotangent, task_table, type_counts,
    gain_one, bias_one, proj_qkv, proj_out, gain_two, bias_two, proj_up, proj_down,
):
    slots, rows, width = inputs.shape
    length = rows * lax.axis_size("seq")
    exchange = Exchange(lax.axis_size("dp"))
    place = lax.axis_index("seq")
    side, core = place // 2, place % 2
    chip = lax.axis_index("dp") * 2 + side
    low = jnp.minimum(place, 3 - place)
    own_first = place < 2
    flag = low.astype(jnp.int32).reshape(1)

    meta = jnp.concatenate([flag, core.astype(jnp.int32).reshape(1), *exchange.tables(chip, core)])

    def gather_slot(value, got):
        own = lax.dynamic_index_in_dim(value, side, 0, False)
        return jnp.where(own_first, jnp.concatenate([own, got]), jnp.concatenate([got, own]))

    choose = (task_table[:, None] == jnp.arange(TASKS, dtype=jnp.int32)[None, :]).astype(F32)
    targets = (length - type_counts[:, 0]).astype(F32)
    totals = jnp.sum(choose * targets[:, None], 0)
    bits = int(math.log2(exchange.dp))

    for bit in range(bits):
        pairs = [(d, d ^ (1 << bit)) for d in range(exchange.dp)]
        totals = totals + lax.ppermute(totals, "dp", pairs)
    cotangent_own, cotangent_send = (lax.dynamic_index_in_dim(cotangent, s, 0, False) for s in (side, 1 - side))
    got = exchange.mirror(lax.dynamic_index_in_dim(inputs, 1 - side, 0, False))
    got, totals, cotangent_own, cotangent_send = lax.optimization_barrier(
        (got, totals, cotangent_own, cotangent_send)
    )
    stream = gather_slot(inputs, got)
    factor = jnp.sum(totals) / TASKS / totals
    seq_weight = jnp.sum(choose * factor[None, :], 1)
    own_weight = lax.dynamic_index_in_dim(seq_weight, side, 0, False)
    own_start = lax.dynamic_index_in_dim(type_counts[:, 0], side, 0, False)
    chips = exchange.chips
    half = width // 2
    swap, mirror = exchange.swap_core, exchange.mirror

    def forward(layer, stream, moves_project, moves_attention):
        hidden, queries, own = host(
            lambda v: project(layer, v, gain_one, bias_one, proj_qkv), (stream,), *moves_project
        )
        other = swap(own)
        hidden_x = Move(swap, hidden)
        attended, logs = host(
            lambda q, k, kx: attention_forward(flag, q, k, kx), (queries, own, other),
            hidden_x, *moves_attention
        )
        attended_x = Move(swap, attended)
        middle, normed, active, slope, *output = host(
            lambda a, v: feed_forward(layer, a, v, proj_out, gain_two, bias_two, proj_up, proj_down),
            (attended, stream), attended_x,
        )
        moves = Move(swap, normed), Move(swap, active)
        return output, moves, (stream, hidden, hidden_x, queries, own, other, logs, attended, attended_x, middle, normed, active, slope)

    def attention_step(layer, back_attended, moves):
        unused, unused, unused, queries, own, other, logs, attended, unused, unused, unused, unused, unused = kept[layer]
        back_q, back_own, back_other = host(
            lambda b: attention_backward(flag, queries, own, other, b, attended, logs), (back_attended,), *moves
        )
        return back_q, back_own, Move(swap, back_other)

    def project_step(layer, back_q, back_own, back_got, back_branch, sums, moves, beside=lambda: (), ready=()):
        return host(
            lambda q, k, kx, *more: (
                *project_back(layer, meta, q, k, kx, proj_qkv, kept[layer][0], gain_one, back_branch, sums),
                *beside(*more),
            ),
            (back_q, back_own, back_got) + tuple(ready), *moves
        )

    def feed_step(layer, back_out, sums, moves):
        middle, slope = kept[layer][9], kept[layer][12]
        return host(
            lambda b: feed_back(layer, meta, b, slope, proj_up, proj_down, middle, gain_two, proj_out, sums),
            (back_out,), *moves
        )

    def down_step(layer, back_out, back_out_x, active_x, moves):
        active = kept[layer][11]
        return Reduction(exchange, *host(
            lambda b, bx: down_gradients(meta, chips, active, active_x, b, bx), (back_out, back_out_x), *moves
        ))

    def up_step(layer, back_up, back_up_x, back_branch, branch_x, normed_x, moves):
        normed, attended, attended_x = kept[layer][10], kept[layer][7], kept[layer][8].value
        return Reduction(exchange, *host(
            lambda b, bx: up_gradients(
                meta, chips, normed, normed_x, b, bx, attended, attended_x, back_branch, branch_x
            ),
            (back_up, back_up_x), *moves
        ))

    def qkv_step(layer, mine, theirs_x, sums, moves):
        hidden, hidden_x = kept[layer][1], kept[layer][2].value
        return Reduction(exchange, *host(
            lambda b, bx: qkv_gradients(meta, chips, hidden, hidden_x, b, bx, sums), (mine, theirs_x), *moves
        ))

    got_cotangent = Move(mirror, cotangent_send)
    (stream,), moves, saved = forward(0, stream, (), (got_cotangent,))
    kept = [saved]
    back_out, back_out_send = weigh(
        own_weight.reshape(1), own_start.reshape(1), cotangent_own, got_cotangent.value
    )
    back_out_x = Move(swap, back_out_send)
    (stream, stream_send), last_moves, saved = forward(1, stream, moves, (back_out_x,))
    normed_x, active_x = (move.value for move in moves)
    kept.append(saved)
    outputs_move = Move(mirror, stream_send)

    sums = jnp.zeros((8, width), F32)
    back_up, back_up_send, back_branch, branch_send, back_attended, sums = feed_step(
        1, back_out, sums, last_moves + (outputs_move,)
    )
    last_normed_x, last_active_x = (move.value for move in last_moves)
    back_up_x, branch_x = Move(swap, back_up_send), Move(swap, branch_send)
    down1 = down_step(1, back_out, back_out_x.value, last_active_x, (back_up_x, branch_x))
    back_q, back_own, back_got = attention_step(1, back_attended, (down1,))
    up1 = up_step(1, back_up, back_up_x.value, back_branch, branch_x.value, last_normed_x, (down1, back_got))
    mine, theirs, back_out, back_out_send, sums = project_step(
        1, back_q, back_own, back_got.value, back_branch, sums, (up1, down1)
    )
    theirs_x = Move(swap, theirs)
    down0 = down_step(0, back_out, swap(back_out_send), active_x, (theirs_x, up1, down1))
    back_up, back_up_send, back_branch, branch_send, back_attended, sums0 = feed_step(
        0, back_out, sums, (down0, up1)
    )
    back_up_x, branch_x = Move(swap, back_up_send), Move(swap, branch_send)
    qkv1 = qkv_step(1, mine, theirs_x.value, sums, (back_up_x, branch_x, down0, up1))
    up0 = up_step(0, back_up, back_up_x.value, back_branch, branch_x.value, normed_x, (qkv1,))
    back_q, back_own, back_got = attention_step(0, back_attended, (up0, down0))
    unit = width // chips

    def return_slot(value, got):
        own = jnp.where(own_first, value[:rows], value[rows:])
        return jnp.where(side == 0, jnp.stack([own, got]), jnp.stack([got, own]))

    each = unit // 2
    whole_tiles = each % 8 == 0 and exchange.bits == 4
    ready = (outputs_move.value,) + tuple(down1.parts) + tuple(up1.parts)

    def beside(got, *parts):
        count = len(down1.parts)
        return (return_slot(stream, got), *collect([(parts[:count], 8 * each), (parts[count:], unit)]))

    mine, theirs, back_out, back_out_send, sums, back_send, *finished = project_step(
        0, back_q, back_own, swap(back_got.value), back_branch, sums0, (up0, qkv1, down0),
        *((beside, ready) if whole_tiles else ()),
    )
    back_move = Move(mirror, back_send)
    qkv0 = qkv_step(0, mine, swap(theirs), sums, (up0, back_move))
    back_inputs = return_slot(back_out, back_move.value).astype(F32)
    if not whole_tiles:
        for one in (down0, down1, up0, up1, qkv0, qkv1):
            one.complete()
        shares = [jnp.concatenate([total(d.parts), total(u.parts)], 0) for d, u in ((down0, up0), (down1, up1))]
        down, up, out = (
            jnp.stack(value) for value in zip(*(unpack_mlp(share, unit, core, exchange) for share in shares))
        )
        (qkv_a, table), (qkv_b, unused) = (unpack_qkv(total(one.parts), core, exchange) for one in (qkv0, qkv1))
        qkv = jnp.stack([qkv_a, qkv_b])
        outputs = return_slot(stream, outputs_move.value)
    else:
        outputs, mine_b, theirs_b = finished
        mine_a, got_a, got_b, last_q, last_got, mine_q, got_q = last_exchanges(qkv0, qkv1, up0, down0, theirs_b)
        up, down, out = place_mlp(each, mine_a, got_a, mine_b, got_b)
        qkv, table = place_qkv(last_q, last_got, mine_q, got_q)
        table = table[:, :8]
    table = table.T.reshape(LAYERS, 4, each)
    return outputs, back_inputs, table[:, 0], table[:, 1], qkv, out, table[:, 2], table[:, 3], up, down


def solution(mesh):
    tokens = P("dp", "seq", None)
    shared = P(None, AXES)
    in_specs = (tokens, tokens, P("dp"), P("dp", None)) + (P(),) * 8
    out_specs = (
        tokens, tokens, shared, shared, P(None, AXES, None), P(None, AXES, None),
        shared, shared, P(None, AXES, None), P(None, AXES, None),
    )
    return jax.shard_map(
        per_device, mesh=mesh, in_specs=in_specs, out_specs=out_specs, check_vma=False
    )
```

```python
import functools
import math

import jax
import jax.numpy as jnp
import numpy as np
from jax import lax
from jax.experimental import pallas as pl
from jax.experimental.pallas import tpu as pltpu
from jax.sharding import PartitionSpec as P

HEADS = 12
HEAD_DIM = 64
LAYERS = 2
TASKS = 3
AXES = ("dp", "seq")
F32 = jnp.float32
BF16 = jnp.bfloat16
epsilon = 1e-05
PAIRS = 2
VMEM_BYTES = 32 * 1024 * 1024
SMALL_COST = pl.CostEstimate(flops=1000, bytes_accessed=1000, transcendentals=0)


def in_hbm(*values):
    return tuple(pltpu.with_memory_space_constraint(v, pltpu.HBM) for v in values)


def dot_nn(a, b):
    return lax.dot_general(a, b, (((1,), (0,)), ((), ())), preferred_element_type=F32)


def dot_nt(a, b):
    return lax.dot_general(a, b, (((1,), (1,)), ((), ())), preferred_element_type=F32)


def dot_tn(a, b):
    return lax.dot_general(a, b, (((0,), (0,)), ((), ())), preferred_element_type=F32)


def gelu_and_slope(x):
    z = jnp.abs(x) * 0.7071067811865476
    d = 1.0 + 0.3275911 * z
    t = pl.reciprocal(d, approx=True)
    t = t * (2.0 - d * t)
    poly = t * (
        0.254829592
        + t * (-0.284496736 + t * (1.421413741 + t * (-1.453152027 + t * 1.061405429)))
    )
    bell = jnp.exp(-0.5 * x * x)
    tail = 0.5 * poly * bell
    below = jnp.where(x >= 0.0, 1.0 - tail, tail)
    return x * below, below + x * bell * 0.3989422804014327


def head_masks(scale):
    lane = lax.broadcasted_iota(jnp.int32, (1, 2 * HEAD_DIM), 1)
    first = jnp.where(lane < HEAD_DIM, scale, 0.0)
    return first.astype(BF16), (scale - first).astype(BF16)


def stacked(value, masks):
    return jnp.concatenate([value * masks[0], value * masks[1]], 0)


def merged(value):
    rows = value.shape[0] // 2
    lane = lax.broadcasted_iota(jnp.int32, (rows, 2 * HEAD_DIM), 1)
    return jnp.where(lane < HEAD_DIM, value[:rows], value[rows:])


def by_variant(meta, run):
    @pl.when(meta[0] == 0)
    def _():
        run(0)

    @pl.when(meta[0] == 1)
    def _():
        run(1)


def attention_forward_kernel(meta, q_ref, ko_ref, vo_ref, kx_ref, vx_ref, out_ref, lse_ref):
    def run_all(variant):
        for pair in range(PAIRS):
            lanes = (slice(None), slice(pair * 2 * HEAD_DIM, (pair + 1) * 2 * HEAD_DIM))
            refs = [ref.at[lanes] for ref in (q_ref, ko_ref, vo_ref, kx_ref, vx_ref, out_ref)]
            attention_forward_pair(variant, *refs, lse_ref.at[pair])

    by_variant(meta, run_all)


def attention_forward_pair(variant, q_ref, ko_ref, vo_ref, kx_ref, vx_ref, out_ref, lse_ref):
    rows = q_ref.shape[0] // 2
    masks = head_masks(1.0 / math.sqrt(HEAD_DIM))

    def run(variant):
        position = lax.broadcasted_iota(jnp.int32, (2 * rows, rows), 0) % rows
        below = lax.broadcasted_iota(jnp.int32, (2 * rows, rows), 1) <= position
        low, high = slice(0, rows), slice(rows, 2 * rows)
        if variant == 0:
            plan = [
                (low, [(ko_ref, vo_ref, low)]),
                (high, [(ko_ref, vo_ref, low), (kx_ref, vx_ref, low), (kx_ref, vx_ref, high), (ko_ref, vo_ref, high)]),
            ]
        else:
            plan = [
                (low, [(kx_ref, vx_ref, low), (ko_ref, vo_ref, low)]),
                (high, [(ko_ref, vo_ref, low), (kx_ref, vx_ref, low), (ko_ref, vo_ref, high)]),
            ]
        all_scores = []
        for span, parts in plan:
            q2 = stacked(q_ref[span, :], masks)
            all_scores.append([dot_nt(q2, keys[place, :]) for keys, unused, place in parts])
        for (span, parts), scores in zip(plan, all_scores):
            scores[-1] = jnp.where(below, scores[-1], -1e30)
            peak = jnp.max(functools.reduce(jnp.maximum, scores), -1, keepdims=True)
            total, acc = None, None
            for part, (unused, values, place) in zip(scores, parts):
                raised = jnp.exp(part - peak)
                total = raised if total is None else total + raised
                term = dot_nn(raised.astype(BF16), values[place, :])
                acc = term if acc is None else acc + term
            total = jnp.sum(total, -1, keepdims=True)
            out_ref[span, :] = merged(acc / total).astype(BF16)
            log = peak + jnp.log(total)
            lane = lax.broadcasted_iota(jnp.int32, (rows, 2 * HEAD_DIM), 1)
            lse_ref[:, span] = jnp.where(lane == 0, log[:rows], log[rows:]).T[:8, :]

    run(variant)


def attention_forward(meta, queries, own, other):
    tokens = queries.shape[0]
    pairs = HEADS // 2
    wide = 2 * HEAD_DIM * PAIRS

    def at(offset):
        return pl.BlockSpec((tokens, wide), lambda g, m: (0, offset // PAIRS + g))

    return pl.pallas_call(
        attention_forward_kernel,
        grid_spec=pltpu.PrefetchScalarGridSpec(
            num_scalar_prefetch=1,
            grid=(pairs // PAIRS,),
            in_specs=[at(0), at(0), at(pairs), at(0), at(pairs)],
            out_specs=[at(0), pl.BlockSpec((PAIRS, 8, tokens), lambda g, m: (g, 0, 0))],
        ),
        out_shape=[
            pltpu.HBM((tokens, HEADS * HEAD_DIM), BF16),
            pltpu.HBM((pairs, 8, tokens), F32),
        ],
        compiler_params=pltpu.CompilerParams(vmem_limit_bytes=VMEM_BYTES),
        cost_estimate=SMALL_COST,
        name="attention_forward",
    )(meta, *in_hbm(queries, own, own, other, other))


def attention_backward_kernel(
    meta, q_ref, ko_ref, vo_ref, kx_ref, vx_ref, do_ref, o_ref, lse_ref,
    dq_ref, own_ref, other_ref, q4, do4,
):
    def run_all(variant):
        for pair in range(PAIRS):
            lanes = (slice(None), slice(pair * 2 * HEAD_DIM, (pair + 1) * 2 * HEAD_DIM))
            refs = [ref.at[lanes] for ref in (q_ref, ko_ref, vo_ref, kx_ref, vx_ref, do_ref, o_ref)]
            grads = [ref.at[(slice(None),) + lanes] for ref in (own_ref, other_ref)]
            attention_backward_pair(
                variant, *refs, lse_ref.at[pair], dq_ref.at[lanes], *grads, q4.at[pair], do4.at[pair]
            )

    by_variant(meta, run_all)


def attention_backward_pair(
    variant, q_ref, ko_ref, vo_ref, kx_ref, vx_ref, do_ref, o_ref, lse_ref,
    dq_ref, own_ref, other_ref, q4, do4,
):
    rows = q_ref.shape[0] // 2
    scale = 1.0 / math.sqrt(HEAD_DIM)
    scaled, plain = head_masks(scale), head_masks(1.0)
    product = (do_ref[...].astype(F32) * o_ref[...].astype(F32)).T
    first = jnp.sum(product[:HEAD_DIM], 0, keepdims=True)
    second = jnp.sum(product[HEAD_DIM:], 0, keepdims=True)
    logs = lse_ref[...]
    dot_row = jnp.concatenate([first[:, :rows], second[:, :rows], first[:, rows:], second[:, rows:]], 1)
    log_row = jnp.concatenate(
        [logs[0:1, :rows], logs[1:2, :rows], logs[0:1, rows:], logs[1:2, rows:]], 1
    )
    for block in range(2):
        span = slice(block * rows, (block + 1) * rows)
        q4[2 * block * rows : 2 * (block + 1) * rows, :] = stacked(q_ref[span, :], scaled)
        do4[2 * block * rows : 2 * (block + 1) * rows, :] = stacked(do_ref[span, :], plain)

    def run(variant):
        column = lax.broadcasted_iota(jnp.int32, (rows, 2 * rows), 1) % rows
        below = lax.broadcasted_iota(jnp.int32, (rows, 2 * rows), 0) <= column
        low, high = slice(0, rows), slice(rows, 2 * rows)
        both, upper, lower = slice(0, 4 * rows), slice(2 * rows, 4 * rows), slice(0, 2 * rows)
        plan = [(0, low, lower, True), (0, low, upper, False), (1, low, upper, False), (0, high, upper, True)]
        plan.insert(3, (1, high, upper, False) if variant == 0 else (1, low, lower, False))
        keys, values, grads = (ko_ref, kx_ref), (vo_ref, vx_ref), (own_ref, other_ref)
        dq_parts = {}
        sums = {}
        ahead = {}

        def products(index):
            source, place, cols, unused = plan[index]
            ahead[index] = dot_nt(keys[source][place, :], q4[cols, :]), dot_nt(values[source][place, :], do4[cols, :])

        products(0)
        products(1)
        for index, (source, place, cols, diagonal) in enumerate(plan):
            if index + 2 < len(plan):
                products(index + 2)
            scores, back = ahead.pop(index)
            raised = jnp.exp(scores - log_row[:, cols])
            if diagonal:
                raised = jnp.where(below, raised, 0.0)
            slope = (raised * (back - dot_row[:, cols])).astype(BF16)
            slot = (source, place.start)
            terms = dot_nn(slope, q4[cols, :]), dot_nn(raised.astype(BF16), do4[cols, :])
            sums[slot] = tuple(a + b for a, b in zip(sums[slot], terms)) if slot in sums else terms
            term = dot_tn(slope, keys[source][place, :])
            dq_parts[cols.start] = dq_parts[cols.start] + term if cols.start in dq_parts else term
        for block in range(2):
            dq_ref[block * rows : (block + 1) * rows, :] = (
                merged(dq_parts[2 * block * rows]) * scale
            ).astype(BF16)
        for source in range(2):
            for place in (low, high):
                zero = jnp.zeros((rows, 2 * HEAD_DIM), F32)
                for which, value in enumerate(sums.get((source, place.start), (zero, zero))):
                    grads[source][which, place, :] = value.astype(grads[source].dtype)

    run(variant)


def attention_backward(meta, queries, own, other, back_attended, attended, logs):
    tokens = queries.shape[0]
    pairs = HEADS // 2
    wide = 2 * HEAD_DIM * PAIRS
    width = HEADS * HEAD_DIM

    def at(offset):
        return pl.BlockSpec((tokens, wide), lambda g, m: (0, offset // PAIRS + g))

    return pl.pallas_call(
        attention_backward_kernel,
        grid_spec=pltpu.PrefetchScalarGridSpec(
            num_scalar_prefetch=1,
            grid=(pairs // PAIRS,),
            in_specs=[at(0), at(0), at(pairs), at(0), at(pairs), at(0), at(0),
                      pl.BlockSpec((PAIRS, 8, tokens), lambda g, m: (g, 0, 0))],
            out_specs=[at(0)] + [pl.BlockSpec((2, tokens, wide), lambda g, m: (0, 0, g))] * 2,
            scratch_shapes=[pltpu.VMEM((PAIRS, 2 * tokens, 2 * HEAD_DIM), BF16)] * 2,
        ),
        out_shape=[
            jax.ShapeDtypeStruct((tokens, width), BF16),
            pltpu.HBM((2, tokens, width), BF16),
            jax.ShapeDtypeStruct((2, tokens, width), BF16),
        ],
        compiler_params=pltpu.CompilerParams(vmem_limit_bytes=VMEM_BYTES),
        cost_estimate=SMALL_COST,
        name="attention_backward",
    )(meta, *in_hbm(queries, own, own, other, other, back_attended, attended, logs))


def normalised(rows_in):
    average = jnp.mean(rows_in, -1, keepdims=True)
    centred = rows_in - average
    inverse = lax.rsqrt(jnp.mean(centred * centred, -1, keepdims=True) + epsilon)
    return centred * inverse, inverse


def norm_back(rows_in, gain_row, back):
    unit, inverse = normalised(rows_in)
    slope = back * gain_row
    first = jnp.mean(slope, -1, keepdims=True)
    second = jnp.mean(slope * unit, -1, keepdims=True)
    return inverse * (slope - first - unit * second), (
        jnp.sum(back * unit, 0, keepdims=True), jnp.sum(back, 0, keepdims=True))


def with_rows(table, row, sums):
    index = lax.broadcasted_iota(jnp.int32, table.shape, 0)
    return jnp.where(index == row, sums[0], jnp.where(index == row + 1, sums[1], table))


def project_kernel(layer, stream, gain, shift, matrix, hidden, queries, pairs):
    width = stream.shape[1]
    groups = 4
    rows = stream.shape[0] // groups
    for group in range(groups):
        span = slice(group * rows, (group + 1) * rows)
        unit, unused = normalised(stream[span, :].astype(F32))
        hidden[span, :] = (unit * gain[layer : layer + 1] + shift[layer : layer + 1]).astype(BF16)
        pairs[span, :] = dot_nn(hidden[span, :], matrix[0, :, width:]).astype(BF16)
        queries[span, :] = dot_nn(hidden[span, :], matrix[0, :, :width]).astype(BF16)


def project(layer, stream, gain, shift, matrix):
    tokens, width = stream.shape
    whole = pl.BlockSpec((tokens, width), lambda j: (0, 0))
    row = pl.BlockSpec(gain.shape, lambda j: (0, 0))
    return pl.pallas_call(
        functools.partial(project_kernel, layer),
        grid=(1,),
        in_specs=[whole, row, row, pl.BlockSpec((1, width, 3 * width), lambda j: (layer, 0, 0))],
        out_specs=[whole, whole, pl.BlockSpec((tokens, 2 * width), lambda j: (0, 0))],
        out_shape=[
            pltpu.HBM((tokens, width), BF16),
            pltpu.HBM((tokens, width), BF16),
            pltpu.HBM((tokens, 2 * width), BF16),
        ],
        compiler_params=pltpu.CompilerParams(vmem_limit_bytes=VMEM_BYTES),
        cost_estimate=SMALL_COST,
        name="project",
    )(*in_hbm(stream), gain, shift, *in_hbm(matrix))


def feed_forward_kernel(
    layer, steps, attended, stream, matrix_out, gain, shift, up, down,
    middle, normed, active_ref, slope_ref, out, *rest,
):
    acc = rest[-1]
    step = pl.program_id(0)

    @pl.when(step == 0)
    def _():
        acc[...] = stream[...].astype(F32) + dot_nn(attended[...], matrix_out[0])
        middle[...] = acc[...].astype(BF16)
        unit, unused = normalised(acc[...])
        normed[...] = (unit * gain[layer : layer + 1] + shift[layer : layer + 1]).astype(BF16)

    groups = 4
    rows = normed.shape[0] // groups
    raw = {}
    for group in range(groups + 1):
        if group < groups:
            raw[group] = dot_nn(normed[group * rows : (group + 1) * rows, :], up[0])
        if group > 0:
            span = slice((group - 1) * rows, group * rows)
            active, slope = gelu_and_slope(raw.pop(group - 1))
            active = active.astype(BF16)
            active_ref[span, :] = active
            slope_ref[span, :] = slope.astype(BF16)
            acc[span, :] += dot_nn(active, down[0])

    @pl.when(step == steps - 1)
    def _():
        out[...] = acc[...].astype(out.dtype)
        if len(rest) == 2:
            rest[0][...] = acc[other_block(acc.shape[0] // 2), :].astype(out.dtype)


def other_block(rows):
    return pl.ds(pl.multiple_of((1 - lax.axis_index("seq") // 2) * rows, rows), rows)


def feed_forward(layer, attended, stream, matrix_out, gain, shift, up, down):
    tokens, width = stream.shape
    last = layer == LAYERS - 1
    block = pl.BlockSpec((tokens // 2, width), lambda j: (0, 0))
    hidden = up.shape[2]
    tile = 1024
    steps = hidden // tile
    whole = pl.BlockSpec((tokens, width), lambda j: (0, 0))
    row = pl.BlockSpec(gain.shape, lambda j: (0, 0))
    part = pl.BlockSpec((tokens, tile), lambda j: (0, j))
    return pl.pallas_call(
        functools.partial(feed_forward_kernel, layer, steps),
        grid=(steps,),
        in_specs=[
            whole, whole, pl.BlockSpec((1, width, width), lambda j: (layer, 0, 0)), row, row,
            pl.BlockSpec((1, width, tile), lambda j: (layer, 0, j)),
            pl.BlockSpec((1, tile, width), lambda j: (layer, j, 0)),
        ],
        out_specs=[whole, whole, part, part, whole] + [block] * last,
        out_shape=[
            pltpu.HBM((tokens, width), BF16),
            pltpu.HBM((tokens, width), BF16),
            pltpu.HBM((tokens, hidden), BF16),
            pltpu.HBM((tokens, hidden), BF16),
            pltpu.HBM((tokens, width), BF16),
        ] + [jax.ShapeDtypeStruct((tokens // 2, width), BF16)] * last,
        scratch_shapes=[pltpu.VMEM((tokens, width), F32)],
        compiler_params=pltpu.CompilerParams(vmem_limit_bytes=VMEM_BYTES),
        cost_estimate=SMALL_COST,
        name="feed_forward",
    )(*in_hbm(attended, stream, matrix_out), gain, shift, *in_hbm(up, down))


def feed_back_kernel(
    layer, steps, meta, back_out, slope, up, down, middle, gain, matrix_out, sums_in,
    own, send, back_branch, branch_send, back_attended, grads, acc,
):
    step = pl.program_id(0)
    half = branch_send.shape[1]
    theirs = pl.ds(pl.multiple_of((1 - meta[1]) * half, 128), half)

    @pl.when(step == 0)
    def _():
        acc[...] = jnp.zeros_like(acc)

    back_up = (dot_nt(back_out[...], down[0]) * slope[...].astype(F32)).astype(BF16)

    @pl.when(step < steps // 2)
    def _():
        send[...] = back_up

    @pl.when(step >= steps // 2)
    def _():
        own[...] = back_up

    acc[...] += dot_nt(back_up, up[0])

    @pl.when(step == steps - 1)
    def _():
        back, sums = norm_back(middle[...].astype(F32), gain[layer : layer + 1], acc[...])
        back = back + back_out[...].astype(F32)
        grads[...] = with_rows(sums_in[...], 4 * layer + 2, sums)
        back_branch[...] = back.astype(BF16)
        branch_send[...] = back_branch[:, theirs]
        back_attended[...] = dot_nt(back_branch[...], matrix_out[0]).astype(BF16)


def feed_back(layer, meta, back_out, slope, up, down, middle, gain, matrix_out, sums):
    tokens, width = back_out.shape
    hidden = up.shape[2]
    tile = 768
    steps = hidden // tile
    half = steps // 2

    def place(j, m):
        return jnp.where(j < half, (1 - m[1]) * half + j, m[1] * half + j - half)

    whole = pl.BlockSpec((tokens, width), lambda j, m: (0, 0))
    narrow = pl.BlockSpec((tokens, width // 2), lambda j, m: (0, 0))
    wide = jax.ShapeDtypeStruct((tokens, width), BF16)
    return pl.pallas_call(
        functools.partial(feed_back_kernel, layer, steps),
        grid_spec=pltpu.PrefetchScalarGridSpec(
            num_scalar_prefetch=1,
            grid=(steps,),
            in_specs=[
                whole, pl.BlockSpec((tokens, tile), lambda j, m: (0, place(j, m))),
                pl.BlockSpec((1, width, tile), lambda j, m: (layer, 0, place(j, m))),
                pl.BlockSpec((1, tile, width), lambda j, m: (layer, place(j, m), 0)),
                whole, pl.BlockSpec(gain.shape, lambda j, m: (0, 0)),
                pl.BlockSpec((1, width, width), lambda j, m: (layer, 0, 0)),
                pl.BlockSpec((8, width), lambda j, m: (0, 0)),
            ],
            out_specs=[
                pl.BlockSpec((tokens, tile), lambda j, m: (0, jnp.maximum(j - half, 0))),
                pl.BlockSpec((tokens, tile), lambda j, m: (0, jnp.minimum(j, half - 1))),
                whole, narrow, whole,
                pl.BlockSpec((8, width), lambda j, m: (0, 0)),
            ],
            scratch_shapes=[pltpu.VMEM((tokens, width), F32)],
        ),
        out_shape=[
            jax.ShapeDtypeStruct((tokens, hidden // 2), BF16),
            jax.ShapeDtypeStruct((tokens, hidden // 2), BF16),
            wide, jax.ShapeDtypeStruct((tokens, width // 2), BF16),
            wide, jax.ShapeDtypeStruct((8, width), F32),
        ],
        compiler_params=pltpu.CompilerParams(vmem_limit_bytes=VMEM_BYTES),
        cost_estimate=SMALL_COST,
        name="feed_back",
    )(meta, back_out, *in_hbm(slope, up, down, middle), gain, *in_hbm(matrix_out), sums)


def project_back_kernel(
    layer, meta, back_q, own, got, matrix, stream, gain, back_middle, sums_in,
    mine, theirs, back_out, back_out_send, grads, *rest,
):
    width = back_q.shape[1]
    table, acc = rest[-2:]

    def begin():
        table[0] = back_q[...]
        for which in range(2):
            table[1 + which] = (own[which].astype(F32) + got[which].astype(F32)).astype(BF16)
        half = width // 2

        @pl.when(meta[1] == 0)
        def _():
            mine[:, :width] = table[0]
            mine[:, width:] = table[1, :, :half]
            theirs[:, :half] = table[1, :, half:]
            theirs[:, half:] = table[2]

        @pl.when(meta[1] == 1)
        def _():
            theirs[:, :width] = table[0]
            theirs[:, width:] = table[1, :, :half]
            mine[:, :half] = table[1, :, half:]
            mine[:, half:] = table[2]

    begin()
    acc[...] = sum(
        dot_nt(table[which], matrix[0, :, which * width : (which + 1) * width]) for which in range(3)
    )

    def end():
        back, sums = norm_back(stream[...].astype(F32), gain[layer : layer + 1], acc[...])
        back = back + back_middle[...].astype(F32)
        back_out[...] = back.astype(BF16)
        half = width // 2
        back_out_send[...] = back_out[:, pl.ds(pl.multiple_of((1 - meta[1]) * half, 128), half)]
        grads[...] = with_rows(sums_in[...], 4 * layer, sums)
        if len(rest) == 3:
            rest[0][...] = back_out[other_block(back_out.shape[0] // 2), :]

    end()


def project_back(layer, meta, back_q, own, got, matrix, stream, gain, back_middle, sums):
    tokens, width = stream.shape
    whole = pl.BlockSpec((tokens, width), lambda j, m: (0, 0))
    both = pl.BlockSpec((2, tokens, width), lambda j, m: (0, 0, 0))
    side = pl.BlockSpec((tokens, 3 * width // 2), lambda j, m: (0, 0))
    return pl.pallas_call(
        functools.partial(project_back_kernel, layer),
        grid_spec=pltpu.PrefetchScalarGridSpec(
            num_scalar_prefetch=1,
            grid=(1,),
            in_specs=[
                whole, both, both, pl.BlockSpec((1, width, 3 * width), lambda j, m: (layer, 0, 0)),
                whole, pl.BlockSpec(gain.shape, lambda j, m: (0, 0)), whole,
                pl.BlockSpec((8, width), lambda j, m: (0, 0)),
            ],
            out_specs=[side, side, whole, pl.BlockSpec((tokens, width // 2), lambda j, m: (0, 0)),
                       pl.BlockSpec((8, width), lambda j, m: (0, 0))]
            + [pl.BlockSpec((tokens // 2, width), lambda j, m: (0, 0))] * (layer == 0),
            scratch_shapes=[pltpu.VMEM((3, tokens, width), BF16), pltpu.VMEM((tokens, width), F32)],
        ),
        out_shape=[
            jax.ShapeDtypeStruct((tokens, 3 * width // 2), BF16),
            jax.ShapeDtypeStruct((tokens, 3 * width // 2), BF16),
            jax.ShapeDtypeStruct((tokens, width), BF16),
            jax.ShapeDtypeStruct((tokens, width // 2), BF16),
            jax.ShapeDtypeStruct((8, width), F32),
        ] + [jax.ShapeDtypeStruct((tokens // 2, width), BF16)] * (layer == 0),
        compiler_params=pltpu.CompilerParams(vmem_limit_bytes=VMEM_BYTES),
        cost_estimate=SMALL_COST,
        name="project_back",
    )(meta, *in_hbm(back_q, own), got, *in_hbm(matrix, stream), gain, *in_hbm(back_middle), sums)


def weigh_kernel(weight, start, own, got, back_out, back_out_send):
    rows, half = own.shape[0], back_out_send.shape[1]
    place = lax.axis_index("seq")
    core, low = place % 2, ((place + 1) // 2) % 2
    step = lax.broadcasted_iota(jnp.int32, (rows, 1), 0)
    first = place < 2
    for which, block in enumerate((low, 3 - low)):
        span = slice(which * rows, (which + 1) * rows)
        scale = jnp.where(block * rows + step >= start[0], weight[0], 0.0)
        mine = own[...].astype(F32) if which == 0 else got[...].astype(F32)
        other = got[...].astype(F32) if which == 0 else own[...].astype(F32)
        back_out[span, :] = (jnp.where(first, mine, other) * scale).astype(BF16)
    back_out_send[...] = back_out[:, pl.ds(pl.multiple_of((1 - core) * half, 128), half)]


def weigh(weight, start, own, got):
    rows, width = own.shape
    scalar = pl.BlockSpec(memory_space=pltpu.SMEM)
    return pl.pallas_call(
        weigh_kernel,
        in_specs=[scalar, scalar, pl.BlockSpec(memory_space=pltpu.VMEM), pl.BlockSpec(memory_space=pltpu.VMEM)],
        out_specs=[pl.BlockSpec(memory_space=pltpu.VMEM)] * 2,
        out_shape=[
            jax.ShapeDtypeStruct((2 * rows, width), BF16),
            jax.ShapeDtypeStruct((2 * rows, width // 2), BF16),
        ],
        compiler_params=pltpu.CompilerParams(vmem_limit_bytes=VMEM_BYTES),
        cost_estimate=SMALL_COST,
        name="weigh",
    )(weight, start, own, got)


def store_chunks(chips, meta, acc, keep, send):
    rows = acc.shape[0] // chips
    for position in range(chips):
        chunk = acc[pl.ds(pl.multiple_of(meta[2 + position] * rows, 16), rows), :]
        if position < chips // 2:
            keep[position] = chunk
        else:
            send[position - chips // 2] = chunk


def grad_up_kernel(chips, meta, ao, ax, bo, bx, co, cx, do, dx, keep, send, acc):
    step = pl.program_id(0)
    rows, half = acc.shape[0] // chips, do.shape[1]

    @pl.when(step < 2)
    def _():
        acc[...] = (dot_tn(ao[...], bo[...]) + dot_tn(ax[...], bx[...])).astype(BF16)

    @pl.when(step == 2)
    def _():
        acc[:, :half] = (dot_tn(co[...], do[...]) + dot_tn(cx[...], dx[...])).astype(BF16)

    for position in range(chips):
        place = pl.ds(pl.multiple_of(meta[2 + position] * rows, 16), rows)
        target, index = (keep, position) if position < chips // 2 else (send, position - chips // 2)
        target[index, :rows, :] = acc[place, :half]
        target[index, rows:, :] = acc[place, half:]


def grad_down_kernel(chips, meta, ao, ax, bo, bx, *refs):
    keep, send = refs[-2:]
    rows = keep.shape[1]
    each = ao.shape[1] // rows
    total = (dot_tn(ao[...], bo[...]) + dot_tn(ax[...], bx[...])).astype(BF16)
    for local in range(each):
        position = meta[2 + chips + pl.program_id(0) * each + local]
        chunk = total[local * rows : (local + 1) * rows]

        @pl.when(position < chips // 2)
        def _():
            keep[position] = chunk

        @pl.when(position >= chips // 2)
        def _():
            send[position - chips // 2] = chunk


def grad_qkv_kernel(chips, meta, ao, ax, bo, bx, sums, keep, send, acc, columns):
    wide = bo.shape[1]
    acc[:, :wide] = (dot_tn(ao[...], bo[...]) + dot_tn(ax[...], bx[...])).astype(BF16)
    columns[...] = jnp.concatenate([sums[...], jnp.zeros((120, sums.shape[1]), F32)], 0).T
    acc[:, wide:] = columns[...].astype(BF16)
    store_chunks(chips, meta, acc, keep, send)


def ordered(total, ids, chips):
    split = total.astype(BF16).reshape(chips, total.shape[0] // chips, total.shape[1])
    return jnp.take(split, ids, axis=0)


def gradient_call(kernel, name, chips, grid, in_specs, out_spec, shape, scratch):
    return pl.pallas_call(
        functools.partial(kernel, chips),
        grid_spec=pltpu.PrefetchScalarGridSpec(
            num_scalar_prefetch=1, grid=(grid,), in_specs=in_specs, out_specs=[out_spec] * 2,
            scratch_shapes=scratch,
        ),
        out_shape=[pltpu.HBM(shape, BF16)] * 2,
        compiler_params=pltpu.CompilerParams(vmem_limit_bytes=VMEM_BYTES),
        cost_estimate=SMALL_COST,
        name=name,
    )


def up_gradients(
    meta, chips, normed, normed_x, back_up, back_up_x, attended, attended_x, back_branch, branch_x
):
    tokens, width = normed.shape
    half = width // 2
    rows = width // chips
    if rows % 16 != 0:
        ids = meta[2 : 2 + chips]
        up = dot_tn(normed, back_up) + dot_tn(normed_x, back_up_x)
        own = lax.dynamic_slice_in_dim(back_branch, meta[1] * half, half, 1)
        out = dot_tn(attended, own) + dot_tn(attended_x, branch_x)
        up = ordered(up, ids, chips).reshape(chips, rows, 4, half)
        up = up.transpose(0, 2, 1, 3).reshape(chips, 4 * rows, half)
        both = jnp.concatenate([up, ordered(out, ids, chips)], 1)
        return both[: chips // 2], both[chips // 2 :]
    whole = pl.BlockSpec((tokens, width), lambda j, m: (0, 0))
    fixed = pl.BlockSpec((tokens, half), lambda j, m: (0, 0))
    mine = pl.BlockSpec((tokens, half), lambda j, m: (0, m[1]))
    tile = pl.BlockSpec((tokens, 2 * half), lambda j, m: (0, jnp.minimum(j, 1)))
    return gradient_call(
        grad_up_kernel, "gradient_up", chips, 3, [whole, whole, tile, tile, whole, whole, mine, fixed],
        pl.BlockSpec((chips // 2, 2 * rows, half), lambda j, m: (0, j, 0)),
        (chips // 2, 5 * rows, half), [pltpu.VMEM((width, 2 * half), BF16)],
    )(meta, *in_hbm(normed, normed_x), back_up, back_up_x, *in_hbm(attended, attended_x), back_branch, branch_x)


def down_gradients(meta, chips, active, active_x, back_out, back_out_x):
    tokens, hidden = active.shape
    width = back_out.shape[1]
    half = width // 2
    rows = hidden // chips
    if rows % 64 != 0:
        own = lax.dynamic_slice_in_dim(back_out, meta[1] * half, half, 1)
        down = dot_tn(active, own) + dot_tn(active_x, back_out_x)
        down = ordered(down, meta[2 : 2 + chips], chips)
        return down[: chips // 2], down[chips // 2 :]
    fixed = pl.BlockSpec((tokens, half), lambda j, m: (0, 0))
    mine = pl.BlockSpec((tokens, half), lambda j, m: (0, m[1]))
    tile = pl.BlockSpec((tokens, 2 * width), lambda j, m: (0, j))
    return gradient_call(
        grad_down_kernel, "gradient_down", chips, hidden // (2 * width), [tile, tile, mine, fixed],
        pl.BlockSpec((chips // 2, rows, half), lambda j, m: (0, 0, 0)), (chips // 2, rows, half), [],
    )(meta, *in_hbm(active, active_x), back_out, back_out_x)


def qkv_gradients(meta, chips, hidden, hidden_x, back_projected, back_projected_x, sums):
    tokens, width = hidden.shape
    wide = back_projected.shape[1]
    rows = width // chips
    if rows % 16 != 0:
        qkv = dot_tn(hidden, back_projected) + dot_tn(hidden_x, back_projected_x)
        table = jnp.pad(sums.T, ((0, 0), (0, 120)))
        both = ordered(jnp.concatenate([qkv, table], -1), meta[2 : 2 + chips], chips)
        return both[: chips // 2], both[chips // 2 :]
    specs = [pl.BlockSpec((tokens, width), lambda j, m: (0, 0))] * 2
    specs += [pl.BlockSpec((tokens, wide), lambda j, m: (0, 0))] * 2
    specs += [pl.BlockSpec((8, width), lambda j, m: (0, 0))]
    return gradient_call(
        grad_qkv_kernel, "gradient_qkv", chips, 1, specs,
        pl.BlockSpec((chips // 2, rows, wide + 128), lambda j, m: (0, 0, 0)),
        (chips // 2, rows, wide + 128),
        [pltpu.VMEM((width, wide + 128), BF16), pltpu.VMEM((width, 128), F32)],
    )(meta, *in_hbm(hidden, hidden_x), back_projected, back_projected_x, sums)


class Exchange:
    def __init__(self, dp):
        self.dp = dp
        self.chips = 2 * dp
        self.bits = int(math.log2(self.chips))
        self.core_pairs = [(s, s ^ 1) for s in range(4)]
        self.mirror_pairs = [(s, 3 - s) for s in range(4)]
        rest = list(range(2, self.bits))
        self.orders = ([1, 0] + rest, [0, 1] + rest[::-1])

    def swap_core(self, value):
        return lax.ppermute(value, "seq", self.core_pairs)

    def mirror(self, value):
        return lax.ppermute(value, "seq", self.mirror_pairs)

    def pairs(self, phase):
        result = []
        for device in range(2 * self.chips):
            chip = (device // 4) * 2 + (device % 4) // 2
            core = device % 2
            other = chip ^ (1 << self.orders[core][phase])
            result.append((device, (other // 2) * 4 + (other % 2) * 2 + core))
        return result

    def tables(self, chip, core):
        index = np.arange(self.chips)
        maps = []
        for order in self.orders:
            value = np.zeros_like(index)
            for phase, bit in enumerate(order):
                value |= ((index >> (self.bits - 1 - phase)) & 1) << bit
            maps.append(value.astype(np.int32))
        ids = chip ^ jnp.where(core == 0, jnp.asarray(maps[0]), jnp.asarray(maps[1]))
        relative = jnp.asarray(index.astype(np.int32)) ^ chip
        places = []
        for order in self.orders:
            place = jnp.zeros_like(relative)
            for phase, bit in enumerate(order):
                place = place | (((relative >> bit) & 1) << (self.bits - 1 - phase))
            places.append(place)
        return ids.astype(jnp.int32), jnp.where(core == 0, places[0], places[1]).astype(jnp.int32)


class Reduction:
    def __init__(self, exchange, keep, send):
        self.exchange, self.parts, self.phase = exchange, [keep], 0
        self.first, self.kind = send, send.dtype

    def message(self):
        if self.phase == 0:
            return self.first
        size = self.parts[-1].shape[0]
        terms = [part[size // 2 : size].astype(F32) for part in self.parts]
        return functools.reduce(jnp.add, terms).astype(self.kind)

    def partner(self, phase):
        dp, seq = lax.axis_index("dp"), lax.axis_index("seq")
        where = []
        for order in self.exchange.orders:
            bit = order[phase]
            if bit == 0:
                where.append((dp, (seq + 2) % 4))
            else:
                size = 1 << (bit - 1)
                where.append((dp + size - 2 * size * ((dp // size) % 2), seq))
        (dp0, seq0), (dp1, seq1) = where
        return dp0 + (seq % 2) * (dp1 - dp0), seq0 + (seq % 2) * (seq1 - seq0)

    def transfer(self, message):
        self.phase += 1
        return lax.ppermute(message, AXES, self.exchange.pairs(self.phase - 1))

    def arrived(self, value):
        self.parts.append(value)

    def complete(self):
        while self.phase < self.exchange.bits:
            self.arrived(self.transfer(self.message()))


def total(parts):
    return functools.reduce(jnp.add, [part[0].astype(F32) for part in parts])


class Move:
    def __init__(self, transfer, value):
        self.transfer, self.value = transfer, value

    def message(self):
        return self.value

    def arrived(self, value):
        self.value = value


def host(run, inputs, *moves):
    count = len(inputs)
    tied = lax.optimization_barrier(tuple(inputs) + tuple(move.message() for move in moves))
    results = tuple(run(*tied[:count]))
    got = tuple(move.transfer(message) for move, message in zip(moves, tied[count:]))
    tied = lax.optimization_barrier(results + got)
    for move, value in zip(moves, tied[len(results) :]):
        move.arrived(value)
    return tied[: len(results)]


def by_core(core, mine, theirs, axis):
    return jnp.where(
        core == 0,
        jnp.concatenate([mine, theirs], axis),
        jnp.concatenate([theirs, mine], axis),
    )


def small_call(kernel, name, shapes, operands, scratch=()):
    def spec(value):
        if value.ndim == 3 and value.dtype == BF16:
            return pl.BlockSpec((1,) + value.shape[1:], lambda i: (0, 0, 0))
        return pl.BlockSpec(value.shape, lambda i: (0,) * value.ndim)

    return pl.pallas_call(
        kernel,
        grid=(1,),
        in_specs=[spec(value) for value in operands],
        out_specs=[spec(shape) for shape in shapes],
        out_shape=shapes,
        scratch_shapes=list(scratch),
        compiler_params=pltpu.CompilerParams(vmem_limit_bytes=VMEM_BYTES),
        cost_estimate=SMALL_COST,
        name=name,
    )(*operands)


def collect(groups):
    counts = [len(parts) for parts, unused in groups]
    units = [unit for unused, unit in groups]
    totals = [parts[0].shape[1:] for parts, unused in groups]
    wide = totals[0][1]
    half = sum(rows for rows, unused in totals) // 2

    def kernel(*refs):
        refs = list(refs)
        core = lax.axis_index("seq") % 2
        mine, theirs = refs[sum(counts) : sum(counts) + 2]
        sums = refs[sum(counts) + 2 :]
        at = 0
        for count, unit, scratch in zip(counts, units, sums):
            parts, refs = refs[:count], refs[count:]
            scratch[...] = functools.reduce(jnp.add, [part[0].astype(F32) for part in parts])
            each = unit // 2
            for start in range(0, scratch.shape[0], unit):
                span = slice(at, at + each)
                mine[span, :] = scratch[pl.ds(pl.multiple_of(start + core * each, 8), each), :]
                theirs[span, :] = scratch[pl.ds(pl.multiple_of(start + (1 - core) * each, 8), each), :]
                at += each

    shape = jax.ShapeDtypeStruct((half, wide), F32)
    operands = in_hbm(*[part for parts, unused in groups for part in parts])
    return small_call(kernel, "collect", [shape, shape], operands, [pltpu.VMEM(t, F32) for t in totals])


def place_mlp(each, mine_a, theirs_a, mine_b, theirs_b):
    half = mine_a.shape[1]

    def kernel(*refs):
        ups, downs, outs = refs[4:]
        core = lax.axis_index("seq") % 2
        for layer in range(2):
            for side, value in ((core, refs[2 * layer]), (1 - core, refs[2 * layer + 1])):
                narrow = pl.ds(pl.multiple_of(side * half, 128), half)
                downs[layer, :, narrow] = value[: 4 * each, :]
                for unit in range(4):
                    lanes = pl.ds(pl.multiple_of(side * 4 * half + unit * half, 128), half)
                    ups[layer, :, lanes] = value[(4 + unit) * each : (5 + unit) * each, :]
                outs[layer, :, narrow] = value[8 * each :, :]

    shapes = [
        jax.ShapeDtypeStruct((2, each, 8 * half), F32), jax.ShapeDtypeStruct((2, 4 * each, 2 * half), F32),
        jax.ShapeDtypeStruct((2, each, 2 * half), F32),
    ]
    return small_call(kernel, "place", shapes, (mine_a, theirs_a, mine_b, theirs_b))


def place_qkv(mine_a, theirs_a, mine_b, theirs_b):
    each, wide = mine_a.shape
    wide -= 128

    def kernel(*refs):
        out, table = refs[4:]
        core = lax.axis_index("seq") % 2
        for layer in range(2):
            for side, value in ((core, refs[2 * layer]), (1 - core, refs[2 * layer + 1])):
                out[layer, :, pl.ds(pl.multiple_of(side * wide, 128), wide)] = value[:, :wide]
        table[...] = refs[0][:, wide:] + refs[1][:, wide:]

    shapes = [jax.ShapeDtypeStruct((2, each, 2 * wide), F32), jax.ShapeDtypeStruct((each, 128), F32)]
    return small_call(kernel, "place_qkv", shapes, (mine_a, theirs_a, mine_b, theirs_b))


def last_exchanges(last, before, up, down, theirs_b):
    keep, message = last.parts[0], last.first
    chunk = keep.shape[1:]
    each, wide = chunk[0] // 2, chunk[1]
    up_rows, down_rows, half = up.parts[0].shape[1], down.parts[0].shape[1], up.parts[0].shape[2]
    mesh = pl.DeviceIdType.MESH

    loaded = [(8, keep)] + [(4, v) for v in before.parts] + [(2, v) for v in up.parts] + [(1, v) for v in down.parts]
    buffers = [pltpu.VMEM((size,) + value.shape[1:], BF16) for size, value in loaded]

    def kernel(*refs):
        refs = list(refs)

        def take(count):
            taken = refs[:count]
            del refs[:count]
            return taken

        given, (message, theirs_b) = take(len(loaded)), take(2)
        mine_a, got_a, got_b, mine_l, got_l, mine_q, got_q = take(7)
        land1, land2, land3, land4, q_land3, q_land4, up_land = take(7)
        send2, send3, send4, q_send3, q_send4, up_send = take(6)
        sums, up_sum, down_sum, swap_q, swap_q_land, swap_a, swap_a_land = take(7)
        send_sem, recv_sem, load_sem = take(3)
        held = take(len(loaded))
        keep, before_parts, up_parts, down_parts = held[0], held[1:4], held[4:8], held[8:]
        loads = [
            pltpu.make_async_copy(ref.at[0 : loaded[k][0]], held[k], load_sem.at[k]) for k, ref in enumerate(given)
        ]
        for load in loads:
            load.start()
        seq = lax.axis_index("seq")
        core = seq % 2
        other = lax.axis_index("dp"), seq + 1 - 2 * core
        partners = [last.partner(phase) for phase in range(4)]
        barrier = pltpu.get_barrier_semaphore()
        for partner in partners + [other]:
            pl.semaphore_signal(barrier, inc=1, device_id=partner, device_id_type=mesh)
        pl.semaphore_wait(barrier, 5)

        def remote(index, source, target, partner):
            return pltpu.make_async_remote_copy(
                src_ref=source, dst_ref=target, send_sem=send_sem.at[index], recv_sem=recv_sem.at[index],
                device_id=partner, device_id_type=mesh,
            )

        def added(values, kind=BF16):
            return functools.reduce(jnp.add, [value.astype(F32) for value in values]).astype(kind)

        def rows_of(ref, start, count, side):
            return ref[pl.ds(pl.multiple_of(start + side * count, 8), count), :]

        pieces = (slice(4, 8), slice(2, 4), slice(0, 2))
        first = [remote(k, message.at[p], land1.at[p], partners[0]) for k, p in zip((0, 1, 13), pieces)]
        second = [remote(2, send2.at[2:4], land2.at[2:4], partners[1]), remote(3, send2.at[0:2], land2.at[0:2], partners[1])]
        third = [remote(k, send3.at[p], land3.at[p], partners[2]) for k, p in ((4, slice(1, 2)), (14, slice(0, 1)))]
        fourth = remote(5, send4, land4, partners[3])
        q_third, q_fourth = remote(6, q_send3, q_land3, partners[2]), remote(7, q_send4, q_land4, partners[3])
        up_fourth = remote(8, up_send, up_land, partners[3])
        swap_b, swap_own = (remote(9 + k, swap_a.at[k], swap_a_land.at[k], other) for k in range(2))
        swap_qs = [remote(11 + k, swap_q.at[k], swap_q_land.at[k], other) for k in range(2)]

        for copy in first:
            copy.start()
        for load in loads:
            load.wait()
        up_send[...] = added([part[1:2] for part in up_parts])
        up_fourth.start()
        q_send3[...] = added([part[2:4] for part in before_parts])
        q_third.start()
        swap_a[0] = theirs_b[...]
        swap_b.start()
        down_sum[...] = added([part[0] for part in down_parts], F32)
        up_sum[...] = added([part[0] for part in up_parts], F32)
        sums[1] = added([part[0] for part in before_parts], F32)

        first[0].wait()
        send2[...] = added([keep[4:8], land1[4:8]])
        for copy in second:
            copy.start()

        q_third.wait()
        q_send4[...] = added([part[1:2] for part in before_parts] + [q_land3[1:2]])
        q_fourth.start()
        sums[1] = sums[1] + q_land3[0].astype(F32)

        up_fourth.wait()
        up_sum[...] = up_sum[...] + up_land[0].astype(F32)
        at = 0
        for scratch, unit in ((down_sum, 8 * each), (up_sum, 2 * each)):
            count = unit // 2
            for start in range(0, scratch.shape[0], unit):
                mine_a[at : at + count, :] = rows_of(scratch, start, count, core)
                swap_a[1, at : at + count, :] = rows_of(scratch, start, count, 1 - core)
                at += count
        swap_own.start()
        swap_b.wait()
        got_b[...] = swap_a_land[0]

        first[1].wait()
        second[0].wait()
        send3[...] = added([keep[2:4], land1[2:4], land2[2:4]])
        for copy in third:
            copy.start()

        q_fourth.wait()
        sums[1] = sums[1] + q_land4[0].astype(F32)
        mine_q[...] = rows_of(sums.at[1], 0, each, core)
        swap_q[1] = rows_of(sums.at[1], 0, each, 1 - core)
        swap_qs[1].start()
        swap_own.wait()
        got_a[...] = swap_a_land[1]

        first[2].wait()
        second[1].wait()
        sums[0] = added([keep[0], land1[0], land2[0]], F32)
        third[0].wait()
        send4[...] = added([keep[1:2], land1[1:2], land2[1:2], land3[1:2]])
        fourth.start()
        swap_qs[1].wait()
        got_q[...] = swap_q_land[1]
        third[1].wait()
        sums[0] = sums[0] + land3[0].astype(F32)
        fourth.wait()
        sums[0] = sums[0] + land4[0].astype(F32)
        mine_l[...] = rows_of(sums.at[0], 0, each, core)
        swap_q[0] = rows_of(sums.at[0], 0, each, 1 - core)
        swap_qs[0].start()
        swap_qs[0].wait()
        got_l[...] = swap_q_land[0]

    long = theirs_b.shape
    flat, out = pl.BlockSpec(long, lambda i: (0, 0)), pl.BlockSpec((each, wide), lambda i: (0, 0))
    up_chunk = (1, up_rows, half)
    return pl.pallas_call(
        kernel,
        grid=(1,),
        in_specs=[pl.BlockSpec(memory_space=pl.ANY)] * (len(loaded) + 1) + [flat],
        out_specs=[flat] * 3 + [out] * 4,
        out_shape=[jax.ShapeDtypeStruct(long, F32)] * 3 + [jax.ShapeDtypeStruct((each, wide), F32)] * 4,
        scratch_shapes=[pltpu.VMEM((size,) + chunk, BF16) for size in (8, 4, 2, 1, 2, 1)]
        + [pltpu.VMEM(up_chunk, BF16)]
        + [pltpu.VMEM((size,) + chunk, BF16) for size in (4, 2, 1, 2, 1)]
        + [
            pltpu.VMEM(up_chunk, BF16),
            pltpu.VMEM((2,) + chunk, F32), pltpu.VMEM(up_chunk[1:], F32), pltpu.VMEM((down_rows, half), F32),
            pltpu.VMEM((2, each, wide), F32), pltpu.VMEM((2, each, wide), F32),
            pltpu.VMEM((2,) + long, F32), pltpu.VMEM((2,) + long, F32),
            pltpu.SemaphoreType.DMA((15,)), pltpu.SemaphoreType.DMA((15,)),
            pltpu.SemaphoreType.DMA((len(loaded),)),
        ] + buffers,
        compiler_params=pltpu.CompilerParams(
            vmem_limit_bytes=VMEM_BYTES, collective_id=0, has_side_effects=True
        ),
        cost_estimate=SMALL_COST,
        name="last_exchanges",
    )(*in_hbm(*[value for unused, value in loaded], message), theirs_b)


def unpack_mlp(share, rows, core, exchange):
    half, each = share.shape[1], rows // 2
    down = share[: 4 * rows].reshape(2, 4 * each, half)
    rest = share[4 * rows :].reshape(share.shape[0] // rows - 4, 2, each, half)

    def pick(which):
        return jnp.concatenate(
            [lax.dynamic_index_in_dim(down, which, 0, False),
             lax.dynamic_index_in_dim(rest, which, 1, False).reshape(-1, half)], 0)

    mine, theirs = pick(core), exchange.swap_core(pick(1 - core))

    def widen(value, start, count):
        value = value[start * each : (start + count) * each].reshape(count, each, half)
        return value.transpose(1, 0, 2).reshape(each, count * half)

    def join(start, count):
        return by_core(core, widen(mine, start, count), widen(theirs, start, count), 1)

    grad_down = by_core(core, mine[: 4 * each], theirs[: 4 * each], 1)
    return grad_down, join(4, 4), join(8, 1)


def unpack_qkv(share, core, exchange):
    rows, wide = share.shape
    split = share.reshape(2, rows // 2, wide)
    mine = lax.dynamic_index_in_dim(split, core, 0, False)
    theirs = exchange.swap_core(lax.dynamic_index_in_dim(split, 1 - core, 0, False))
    wide -= 128
    table = mine[:, wide : wide + 8] + theirs[:, wide : wide + 8]
    return by_core(core, mine[:, :wide], theirs[:, :wide], 1), table


def per_device(
    inputs, cotangent, task_table, type_counts,
    gain_one, bias_one, proj_qkv, proj_out, gain_two, bias_two, proj_up, proj_down,
):
    slots, rows, width = inputs.shape
    length = rows * lax.axis_size("seq")
    exchange = Exchange(lax.axis_size("dp"))
    place = lax.axis_index("seq")
    side, core = place // 2, place % 2
    chip = lax.axis_index("dp") * 2 + side
    low = jnp.minimum(place, 3 - place)
    own_first = place < 2
    flag = low.astype(jnp.int32).reshape(1)

    meta = jnp.concatenate([flag, core.astype(jnp.int32).reshape(1), *exchange.tables(chip, core)])

    def gather_slot(value, got):
        own = lax.dynamic_index_in_dim(value, side, 0, False)
        return jnp.where(own_first, jnp.concatenate([own, got]), jnp.concatenate([got, own]))

    choose = (task_table[:, None] == jnp.arange(TASKS, dtype=jnp.int32)[None, :]).astype(F32)
    targets = (length - type_counts[:, 0]).astype(F32)
    totals = jnp.sum(choose * targets[:, None], 0)
    bits = int(math.log2(exchange.dp))

    for bit in range(bits):
        pairs = [(d, d ^ (1 << bit)) for d in range(exchange.dp)]
        totals = totals + lax.ppermute(totals, "dp", pairs)
    cotangent_own, cotangent_send = (lax.dynamic_index_in_dim(cotangent, s, 0, False) for s in (side, 1 - side))
    got = exchange.mirror(lax.dynamic_index_in_dim(inputs, 1 - side, 0, False))
    got, totals, cotangent_own, cotangent_send = lax.optimization_barrier(
        (got, totals, cotangent_own, cotangent_send)
    )
    stream = gather_slot(inputs, got)
    factor = jnp.sum(totals) / TASKS / totals
    seq_weight = jnp.sum(choose * factor[None, :], 1)
    own_weight = lax.dynamic_index_in_dim(seq_weight, side, 0, False)
    own_start = lax.dynamic_index_in_dim(type_counts[:, 0], side, 0, False)
    chips = exchange.chips
    half = width // 2
    swap, mirror = exchange.swap_core, exchange.mirror

    def forward(layer, stream, moves_project, moves_attention):
        hidden, queries, own = host(
            lambda v: project(layer, v, gain_one, bias_one, proj_qkv), (stream,), *moves_project
        )
        other = swap(own)
        hidden_x = Move(swap, hidden)
        attended, logs = host(
            lambda q, k, kx: attention_forward(flag, q, k, kx), (queries, own, other),
            hidden_x, *moves_attention
        )
        attended_x = Move(swap, attended)
        middle, normed, active, slope, *output = host(
            lambda a, v: feed_forward(layer, a, v, proj_out, gain_two, bias_two, proj_up, proj_down),
            (attended, stream), attended_x,
        )
        moves = Move(swap, normed), Move(swap, active)
        return output, moves, (stream, hidden, hidden_x, queries, own, other, logs, attended, attended_x, middle, normed, active, slope)

    def attention_step(layer, back_attended, moves):
        unused, unused, unused, queries, own, other, logs, attended, unused, unused, unused, unused, unused = kept[layer]
        back_q, back_own, back_other = host(
            lambda b: attention_backward(flag, queries, own, other, b, attended, logs), (back_attended,), *moves
        )
        return back_q, back_own, Move(swap, back_other)

    def project_step(layer, back_q, back_own, back_got, back_branch, sums, moves, beside=lambda: (), ready=()):
        return host(
            lambda q, k, kx, *more: (
                *project_back(layer, meta, q, k, kx, proj_qkv, kept[layer][0], gain_one, back_branch, sums),
                *beside(*more),
            ),
            (back_q, back_own, back_got) + tuple(ready), *moves
        )

    def feed_step(layer, back_out, sums, moves):
        middle, slope = kept[layer][9], kept[layer][12]
        return host(
            lambda b: feed_back(layer, meta, b, slope, proj_up, proj_down, middle, gain_two, proj_out, sums),
            (back_out,), *moves
        )

    def down_step(layer, back_out, back_out_x, active_x, moves):
        active = kept[layer][11]
        return Reduction(exchange, *host(
            lambda b, bx: down_gradients(meta, chips, active, active_x, b, bx), (back_out, back_out_x), *moves
        ))

    def up_step(layer, back_up, back_up_x, back_branch, branch_x, normed_x, moves):
        normed, attended, attended_x = kept[layer][10], kept[layer][7], kept[layer][8].value
        return Reduction(exchange, *host(
            lambda b, bx: up_gradients(
                meta, chips, normed, normed_x, b, bx, attended, attended_x, back_branch, branch_x
            ),
            (back_up, back_up_x), *moves
        ))

    def qkv_step(layer, mine, theirs_x, sums, moves):
        hidden, hidden_x = kept[layer][1], kept[layer][2].value
        return Reduction(exchange, *host(
            lambda b, bx: qkv_gradients(meta, chips, hidden, hidden_x, b, bx, sums), (mine, theirs_x), *moves
        ))

    got_cotangent = Move(mirror, cotangent_send)
    (stream,), moves, saved = forward(0, stream, (), (got_cotangent,))
    kept = [saved]
    back_out, back_out_send = weigh(
        own_weight.reshape(1), own_start.reshape(1), cotangent_own, got_cotangent.value
    )
    back_out_x = Move(swap, back_out_send)
    (stream, stream_send), last_moves, saved = forward(1, stream, moves, (back_out_x,))
    normed_x, active_x = (move.value for move in moves)
    kept.append(saved)
    outputs_move = Move(mirror, stream_send)

    sums = jnp.zeros((8, width), F32)
    back_up, back_up_send, back_branch, branch_send, back_attended, sums = feed_step(
        1, back_out, sums, last_moves + (outputs_move,)
    )
    last_normed_x, last_active_x = (move.value for move in last_moves)
    back_up_x, branch_x = Move(swap, back_up_send), Move(swap, branch_send)
    down1 = down_step(1, back_out, back_out_x.value, last_active_x, (back_up_x, branch_x))
    back_q, back_own, back_got = attention_step(1, back_attended, (down1,))
    up1 = up_step(1, back_up, back_up_x.value, back_branch, branch_x.value, last_normed_x, (down1, back_got))
    mine, theirs, back_out, back_out_send, sums = project_step(
        1, back_q, back_own, back_got.value, back_branch, sums, (up1, down1)
    )
    theirs_x = Move(swap, theirs)
    down0 = down_step(0, back_out, swap(back_out_send), active_x, (theirs_x, up1, down1))
    back_up, back_up_send, back_branch, branch_send, back_attended, sums0 = feed_step(
        0, back_out, sums, (down0, up1)
    )
    back_up_x, branch_x = Move(swap, back_up_send), Move(swap, branch_send)
    qkv1 = qkv_step(1, mine, theirs_x.value, sums, (back_up_x, branch_x, down0, up1))
    up0 = up_step(0, back_up, back_up_x.value, back_branch, branch_x.value, normed_x, (qkv1,))
    back_q, back_own, back_got = attention_step(0, back_attended, (up0, down0))
    unit = width // chips

    def return_slot(value, got):
        own = jnp.where(own_first, value[:rows], value[rows:])
        return jnp.where(side == 0, jnp.stack([own, got]), jnp.stack([got, own]))

    each = unit // 2
    whole_tiles = each % 8 == 0 and exchange.bits == 4
    ready = (outputs_move.value,) + tuple(down1.parts) + tuple(up1.parts)

    def beside(got, *parts):
        count = len(down1.parts)
        return (return_slot(stream, got), *collect([(parts[:count], 8 * each), (parts[count:], unit)]))

    mine, theirs, back_out, back_out_send, sums, back_send, *finished = project_step(
        0, back_q, back_own, swap(back_got.value), back_branch, sums0, (up0, qkv1, down0),
        *((beside, ready) if whole_tiles else ()),
    )
    back_move = Move(mirror, back_send)
    qkv0 = qkv_step(0, mine, swap(theirs), sums, (up0, back_move))
    back_inputs = return_slot(back_out, back_move.value).astype(F32)
    if not whole_tiles:
        for one in (down0, down1, up0, up1, qkv0, qkv1):
            one.complete()
        shares = [jnp.concatenate([total(d.parts), total(u.parts)], 0) for d, u in ((down0, up0), (down1, up1))]
        down, up, out = (
            jnp.stack(value) for value in zip(*(unpack_mlp(share, unit, core, exchange) for share in shares))
        )
        (qkv_a, table), (qkv_b, unused) = (unpack_qkv(total(one.parts), core, exchange) for one in (qkv0, qkv1))
        qkv = jnp.stack([qkv_a, qkv_b])
        outputs = return_slot(stream, outputs_move.value)
    else:
        outputs, mine_b, theirs_b = finished
        mine_a, got_a, got_b, last_q, last_got, mine_q, got_q = last_exchanges(qkv0, qkv1, up0, down0, theirs_b)
        up, down, out = place_mlp(each, mine_a, got_a, mine_b, got_b)
        qkv, table = place_qkv(last_q, last_got, mine_q, got_q)
        table = table[:, :8]
    table = table.T.reshape(LAYERS, 4, each)
    return outputs, back_inputs, table[:, 0], table[:, 1], qkv, out, table[:, 2], table[:, 3], up, down


def solution(mesh):
    tokens = P("dp", "seq", None)
    shared = P(None, AXES)
    in_specs = (tokens, tokens, P("dp"), P("dp", None)) + (P(),) * 8
    out_specs = (
        tokens, tokens, shared, shared, P(None, AXES, None), P(None, AXES, None),
        shared, shared, P(None, AXES, None), P(None, AXES, None),
    )
    return jax.shard_map(
        per_device, mesh=mesh, in_specs=in_specs, out_specs=out_specs, check_vma=False
    )
```
